32 devices in a mesh: batch: 4 (over y, core), blk: 8 (over z, x).
Axes of the slice: x: 2, y: 2, z: 4, core: 2. Of those that a mesh axis runs over, the one named last changes fastest.
Arguments:
- tokens: bfloat16 [8, 2048, 1536], P('batch', 'blk'), may hold values from -6 to 6
- cotangent: bfloat16 [8, 2048, 1536], P('batch', 'blk'), may hold values from -6 to 6
- lengths: int32 [8, 6], P('batch'), may hold values from 1 to 1024, 2048 in all within a row
- unit_owner: int32 [36], replicated, may hold values from 0 to 35, each once
- step_count: int32 [1], replicated, may hold values from 1 to 20
- master: float32 [1536, 36, 512], P('blk', 'batch'), may hold values from -0.15625 to 0.15625
- first: float32 [1536, 36, 512], P('blk', 'batch'), may hold values from -80 to 80
- second: float32 [1536, 36, 512], P('blk', 'batch'), may hold values from 861.7984 to 3440.64
- bases: float32 [1536, 36, 1536], P('blk', 'batch'), may hold values from -0.0612372436 to 0.8612372
- small: float32 [3456], replicated, may hold values from -0.4 to 1.5
- small_first: float32 [3456], replicated, may hold values from -80 to 80
- small_second: float32 [3456], replicated, may hold values from 861.7984 to 3440.64
Outputs:
- block_out: bfloat16 [8, 2048, 1536], P('batch', 'blk')
- input_grad: bfloat16 [8, 2048, 1536], P('batch', 'blk')
- new_master: float32 [1536, 36, 512], P('blk', 'batch')
- new_first: float32 [1536, 36, 512], P('blk', 'batch')
- new_second: float32 [1536, 36, 512], P('blk', 'batch')
- small_grads: float32 [3456], replicated
- new_small: float32 [3456], replicated
- new_small_first: float32 [3456], replicated
- new_small_second: float32 [3456], replicated
The draws below stay inside these ranges and needn't reach their ends.
Inputs may be any that keep to these rules, and one draw needn't show every extreme that they name: `lengths`: each row's entries sum to 2048; the last entry counts the padding positions at the row's end, the others are documents. Each slot holds exactly one unit: unit u lies in slot unit_owner[u], and slot s lies with batch index s // 9.
All inputs are finite; a program needn't handle non-finite values.
Results may differ from the reference program's by a relative error of at most 0.029.
Values may be sent and summed in bfloat16 or wider, within the bound.
A program may use at most 448 MiB of HBM per device.

```python
import math
import jax
import jax.numpy as jnp
import numpy as np
from jax import lax

D = 1536
H = 12
HD = 64
VD = 128
FF = 4096
UW = 512
LEN = 2048
NDOC = 6
NROWS = 8
UNITS = 36
SMALL = 3456


def draw_bases(key, part):
    places = jnp.arange(D, dtype=jnp.int32)
    diagonal = (places[:, None, None] == places[None, None, :]).astype(jnp.float32)
    noise = jax.random.truncated_normal(key, -4.0, 4.0, (D, UNITS, D), jnp.float32)
    return 0.8 * diagonal + 0.6 * noise / D ** 0.5


def draw_small(key, part):
    gain_key = jax.random.fold_in(key, 101)
    mixer_key = jax.random.fold_in(key, 202)
    gains = jnp.exp(jax.random.uniform(gain_key, (2 * D + VD,), jnp.float32, -0.4, 0.4))
    mixers = 0.1 * jax.random.truncated_normal(mixer_key, -4.0, 4.0, (4 * HD,), jnp.float32)
    return jnp.concatenate([gains, mixers])


def level_of(stream_key, extent, split, low, largest):
    loudness, own = 1.0, jax.random.fold_in(stream_key, 6)
    for dim, parts in split:
        draws = jnp.exp(jax.random.uniform(jax.random.fold_in(own, dim), (parts,), jnp.float32, low / len(split), largest / len(split)))
        loudness = loudness * jnp.repeat(draws, extent[dim] // parts).reshape([-1 if axis == dim else 1 for axis in range(len(extent))])
    return loudness


def profile(number_of, total, bound, lean):
    weights = [(1 << 20) // math.isqrt(rank ** lean) + 1 for rank in range(2, number_of + 1)]
    surplus, holding = total - bound - (number_of - 1), [1] * (number_of - 1)
    while surplus > 0:
        free = [i for i in range(number_of - 1) if holding[i] < bound]
        mass, budget = sum([weights[i] for i in free]), surplus
        for i in free:
            addition = min(bound - holding[i], max(1, budget * weights[i] // mass), surplus)
            holding[i] = holding[i] + addition
            surplus = surplus - addition
    return np.array([bound] + holding)


def ragged_sizes(rng, amount, total, limit, lean):
    if amount == 2:
        one = jax.random.randint(rng, (), max(1, total - limit), min(limit, total - 1) + 1)
        return jnp.stack([one, total - one])
    tallies = jnp.asarray(profile(amount, total, limit, lean), jnp.int32)
    twos = (amount - 1) // 2
    donor, taker = tallies[1:1 + 2 * twos:2], tallies[2:2 + 2 * twos:2]
    room = jnp.minimum(donor - 1, limit - taker)
    shifted = jax.random.randint(jax.random.fold_in(rng, 1), (twos,), 0, 1 << 20) % (room + 1)
    tallies = tallies.at[1:1 + 2 * twos:2].set(donor - shifted).at[2:2 + 2 * twos:2].set(taker + shifted)
    return tallies[jax.random.permutation(jax.random.fold_in(rng, 2), amount)]


def gaussian(own_key, dims, spread, reach, cuts=(), kind=jnp.bfloat16):
    values = jax.random.normal(own_key, dims, jnp.float32) * spread
    if len(cuts) > 0:
        values = level_of(own_key, dims, cuts, -0.22, 0.18) * values
    return jnp.clip(values, min=-reach, max=reach).astype(kind)


def setup_inputs(seed: int = 0) -> dict:
    streams_of = jax.random.split(jax.random.key(seed), 13)
    return {
        "tokens": gaussian(streams_of[0], (NROWS, LEN, D), 1.0, 6.0, ((0, 4), (1, 8))),
        "cotangent": gaussian(streams_of[1], (NROWS, LEN, D), 1.0, 6.0, ((0, 4), (1, 8))),
        "lengths": jax.vmap(lambda own: ragged_sizes(own, NDOC, LEN, LEN // 2, 1))(jax.random.split(streams_of[2], NROWS)).reshape((NROWS, NDOC)).astype(jnp.int32),
        "unit_owner": jax.random.permutation(streams_of[3], UNITS).astype(jnp.int32),
        "step_count": jax.random.randint(streams_of[4], (1,), 1, 21).astype(jnp.int32),
        "master": gaussian(streams_of[5], (D, UNITS, UW), D ** -0.5, 0.15625, ((0, 8), (1, 4)), jnp.float32),
        "first": gaussian(streams_of[6], (D, UNITS, UW), (0.111 * (NROWS * LEN) ** 0.5), 80.0, ((0, 8), (1, 4)), jnp.float32),
        "second": jnp.clip(jnp.exp(math.log(3440.64) - 1.3843914 * jax.random.uniform(streams_of[7], (D, UNITS, UW), jnp.float32) ** level_of(streams_of[7], (D, UNITS, UW), ((0, 8), (1, 4)), -0.2, 0.2)), 861.7984, 3440.64),
        "bases": draw_bases(jax.random.fold_in(streams_of[12], 71), 0),
        "small": draw_small(jax.random.fold_in(streams_of[12], 71), 0),
        "small_first": gaussian(streams_of[10], (SMALL,), (0.111 * (NROWS * LEN) ** 0.5), 80.0, (), jnp.float32),
        "small_second": jnp.clip(jnp.exp(jax.random.uniform(streams_of[11], (SMALL,), jnp.float32, math.log(861.7984), math.log(3440.64))), 861.7984, 3440.64),
    }


@jax.custom_vjp
def low(v):
    return lax.optimization_barrier(v.astype(jnp.bfloat16)).astype(jnp.float32)

@jax.custom_vjp
def low_back(v):
    return v

def low_keep(v):
    return (low(v), None)

def low_pass(kept, grad):
    return (grad,)

def back_keep(v):
    return (v, None)

def back_low(kept, grad):
    return (low(grad),)
low.defvjp(low_keep, low_pass)
low_back.defvjp(back_keep, back_low)
norm_epsilon = 1e-05
lambda_start = 0.2
rope_base = 10000.0
masked_fill = -1000000000.0
beta_one = 0.9
beta_two = 0.95
adam_epsilon = 1e-08
weight_decay = 0.01
small_rate = 1.0
highest = lax.Precision.HIGHEST

def root_norm(values, gain):
    return values * lax.rsqrt(lax.optimization_barrier(jnp.mean(values * values, axis=-1, keepdims=True)) + norm_epsilon) * gain

def mix_value(mixers):
    return jnp.exp(jnp.sum(mixers[0] * mixers[1])) - jnp.exp(jnp.sum(mixers[2] * mixers[3])) + lambda_start

def head_mix(maps_out, head_gain, mixer):
    combined = maps_out[:, :, 0] - mixer * maps_out[:, :, 1]
    normed = combined * lax.rsqrt(lax.optimization_barrier(jnp.mean(combined * combined, axis=-1, keepdims=True)) + norm_epsilon) * head_gain * (1.0 - lambda_start)
    rows_count, heads, positions, width = normed.shape
    return jnp.transpose(normed, (0, 2, 1, 3)).reshape(rows_count, positions, heads * width)

def document_places(lengths, places):
    ends = jnp.cumsum(lengths, axis=1)
    starts = ends - lengths
    segment = lax.optimization_barrier(jnp.sum((places[None, :, None] >= ends[:, None, :]).astype(jnp.int32), axis=2))
    chosen = segment[:, :, None] == jnp.arange(lengths.shape[1], dtype=jnp.int32)[None, None, :]
    offset = lax.optimization_barrier(jnp.sum(jnp.where(chosen, starts[:, None, :], 0), axis=2))
    return (segment, places[None, :] - offset)

def allowed(seg_query, place_query, seg_key, place_key, last):
    same = seg_query[:, :, None] == seg_key[:, None, :]
    causal = place_key[None, None, :] <= place_query[None, :, None]
    itself = place_key[None, None, :] == place_query[None, :, None]
    return same & causal & ((seg_query[:, :, None] < last) | itself)

def turn_tables(position):
    rates = rope_base ** (-2.0 * jnp.arange(HD // 2, dtype=jnp.float32) / HD)
    angle = position.astype(jnp.float32)[..., None] * rates
    return (jnp.cos(angle), jnp.sin(angle))

def rotate(values, cosine, sine):
    half = values.shape[-1] // 2
    front = values[..., :half]
    back = values[..., half:]
    return jnp.concatenate([front * cosine - back * sine, back * cosine + front * sine], axis=-1)

def row_forward(row, lengths_row, weights, small):
    gain_one = small[:D]
    gain_two = small[D:2 * D]
    head_gain = small[2 * D:2 * D + VD]
    mixer = mix_value(small[2 * D + VD:].reshape(4, HD))
    places = jnp.arange(LEN, dtype=jnp.int32)
    segment, position = document_places(lengths_row[None, :], places)
    mask = allowed(segment, places, segment, places, NDOC - 1)[0]
    cosine, sine = turn_tables(position[0])
    cosine = cosine[:, None, None, :]
    sine = sine[:, None, None, :]
    normed = low(root_norm(row, gain_one))
    query = low(rotate(low_back(jnp.dot(normed, weights[:, :D], precision=highest)).reshape(LEN, H, 2, HD), cosine, sine))
    keys = low(rotate(low_back(jnp.dot(normed, weights[:, D:2 * D], precision=highest)).reshape(LEN, H, 2, HD), cosine, sine))
    values = low(low_back(jnp.dot(normed, weights[:, 2 * D:3 * D], precision=highest))).reshape(LEN, H, VD)
    results = []
    for half in range(2):
        scores = jnp.einsum('qhd,khd->hqk', query[:, :, half], keys[:, :, half], precision=highest) * HD ** (-0.5)
        scores = jnp.where(mask[None], low_back(scores), masked_fill)
        shares = jax.nn.softmax(scores, axis=-1)
        results.append(low_back(jnp.einsum('hqk,khe->hqe', low(shares), values, precision=highest)))
    maps_out = jnp.stack(results, axis=1)[None]
    mixed = low(head_mix(maps_out, head_gain, mixer))[0]
    middle = row + low_back(jnp.dot(mixed, weights[:, 3 * D:4 * D].T, precision=highest))
    normed_two = low(root_norm(middle, gain_two))
    gate = low_back(jnp.dot(normed_two, weights[:, 4 * D:4 * D + FF], precision=highest))
    up = low_back(jnp.dot(normed_two, weights[:, 4 * D + FF:4 * D + 2 * FF], precision=highest))
    hidden = low(jax.nn.silu(gate) * up)
    return middle + low_back(jnp.dot(hidden, weights[:, 4 * D + 2 * FF:].T, precision=highest))

def forward(tokens32, weights, small, lengths):
    row_function = jax.checkpoint(row_forward)

    def step(carry, pair):
        return (carry, row_function(pair[0], pair[1], weights, small))
    unused, results = lax.scan(step, jnp.zeros((), jnp.float32), (tokens32, lengths))
    return results

def adam_step(first_new, second_new, steps_done):
    return first_new / (1.0 - beta_one ** steps_done) / (jnp.sqrt(second_new / (1.0 - beta_two ** steps_done)) + adam_epsilon)

def reference(tokens, cotangent, lengths, unit_owner, step_count, master, first, second, bases, small, small_first, small_second):
    learn_rate = 2.0 / D ** 0.5
    weights = low(jnp.take(master, unit_owner, axis=1).reshape(D, UNITS * UW))

    def run_rows(inputs, matrix, parameters):
        return forward(inputs, matrix, parameters, lengths)
    result, pullback = jax.vjp(run_rows, tokens.astype(jnp.float32), weights, small)
    input_grad, weight_grad, small_grads = pullback(cotangent.astype(jnp.float32))
    slot_order = jnp.argsort(unit_owner)
    grads = jnp.take(weight_grad.reshape(D, UNITS, UW), slot_order, axis=1)
    turned = jnp.einsum('ksa,ksn->asn', bases, grads, precision=highest)
    steps_done = step_count[0].astype(jnp.float32)
    new_first = beta_one * first + (1.0 - beta_one) * turned
    new_second = beta_two * second + (1.0 - beta_two) * turned * turned
    normalized = adam_step(new_first, new_second, steps_done)
    update = jnp.einsum('ksa,asn->ksn', bases, normalized, precision=highest)
    new_master = master - learn_rate * (update + weight_decay * master)
    new_small_first = beta_one * small_first + (1.0 - beta_one) * small_grads
    new_small_second = beta_two * small_second + (1.0 - beta_two) * small_grads * small_grads
    new_small = small - small_rate * adam_step(new_small_first, new_small_second, steps_done)
    return (result.astype(jnp.bfloat16), input_grad.astype(jnp.bfloat16), new_master, new_first, new_second, small_grads, new_small, new_small_first, new_small_second)
```

```python
import functools

import jax
import jax.numpy as jnp
from jax import lax
from jax.experimental import pallas as pl
from jax.experimental.pallas import tpu as pltpu
from jax.sharding import PartitionSpec as P

D = 1536
H = 12
HD = 64
VD = 128
FF = 4096
UW = 512
NDOC = 6
UNITS = 36


norm_epsilon = 1e-05
lambda_start = 0.2
rope_base = 10000.0
masked_fill = -1000000000.0
beta_one = 0.9
beta_two = 0.95
adam_epsilon = 1e-08
weight_decay = 0.01
small_rate = 1.0


def from_behind(shard, axis, by):
    count = lax.axis_size(axis)
    return lax.ppermute(shard, axis, [(i, (i + by) % count) for i in range(count)])


def root_norm(values, gain):
    return (
        values * lax.rsqrt(jnp.mean(values * values, axis=-1, keepdims=True) + norm_epsilon) * gain
    )


def mix_value(mixers):
    return (
        jnp.exp(jnp.sum(mixers[0] * mixers[1]))
        - jnp.exp(jnp.sum(mixers[2] * mixers[3]))
        + lambda_start
    )


def head_mix(maps_out, head_gain, mixer):
    combined = maps_out[:, :, 0] - mixer * maps_out[:, :, 1]
    normed = (
        combined
        * lax.rsqrt(jnp.mean(combined * combined, axis=-1, keepdims=True) + norm_epsilon)
        * head_gain
        * (1.0 - lambda_start)
    )
    rows_count, heads, positions, width = normed.shape
    return jnp.transpose(normed, (0, 2, 1, 3)).reshape(rows_count, positions, heads * width)


def gated_unit(gate, up):
    return jax.nn.silu(gate) * up


def doc_ends(lengths):
    count = lengths.shape[1]
    ends = [lengths[:, 0]]
    for j in range(1, count):
        ends.append(ends[-1] + lengths[:, j])
    return jnp.stack(ends, axis=1)


def document_places(lengths, places):
    ends = doc_ends(lengths)
    starts = ends - lengths
    segment = jnp.sum((places[None, :, None] >= ends[:, None, :]).astype(jnp.int32), axis=2)
    chosen = segment[:, :, None] == jnp.arange(lengths.shape[1], dtype=jnp.int32)[None, None, :]
    offset = jnp.sum(jnp.where(chosen, starts[:, None, :], 0), axis=2)
    return (segment, places[None, :] - offset)


def allowed(seg_query, place_query, seg_key, place_key, last):
    same = seg_query[:, :, None] == seg_key[:, None, :]
    causal = place_key[None, None, :] <= place_query[None, :, None]
    itself = place_key[None, None, :] == place_query[None, :, None]
    return same & causal & ((seg_query[:, :, None] < last) | itself)


def turn_tables(position):
    rates = rope_base ** (-2.0 * jnp.arange(HD // 2, dtype=jnp.float32) / HD)
    angle = position.astype(jnp.float32)[..., None] * rates
    return (jnp.cos(angle), jnp.sin(angle))


def rotate(values, cosine, sine):
    half = values.shape[-1] // 2
    front = values[..., :half]
    back = values[..., half:]
    return jnp.concatenate([front * cosine - back * sine, back * cosine + front * sine], axis=-1)


def adam_step(first_new, second_new, steps_done):
    return (
        first_new
        / (1.0 - beta_one**steps_done)
        / (jnp.sqrt(second_new / (1.0 - beta_two**steps_done)) + adam_epsilon)
    )


def take_units(stacked, order):
    parts = [lax.dynamic_slice_in_dim(stacked, order[i], 1, axis=1) for i in range(UNITS)]
    return jnp.concatenate(parts, axis=1)


def inverse_order(owner):
    numbers = jnp.arange(UNITS, dtype=jnp.int32)
    return jnp.sum(jnp.where(owner[None, :] == numbers[:, None], numbers[None, :], 0), axis=1)


def contract_rows(left, right):
    return lax.dot_general(
        left, right, (((1,), (1,)), ((), ())), preferred_element_type=jnp.float32
    )


def any_mesh(
    tokens,
    cotangent,
    lengths,
    unit_owner,
    step_count,
    master,
    first,
    second,
    bases,
    small,
    small_first,
    small_second,
):
    rows_count, seq_part, width = tokens.shape
    token_count = rows_count * seq_part
    axis_count = lax.axis_size("blk")
    axis_place = lax.axis_index("blk")
    rows_part = master.shape[0]
    scale = HD ** (-0.5)
    highest = lax.Precision.HIGHEST
    learn_rate = 2.0 / D**0.5
    every_slot = lax.all_gather(master.astype(jnp.bfloat16), "batch", axis=1, tiled=True)
    by_unit = take_units(every_slot, unit_owner).reshape(rows_part, UNITS * UW)
    attention_whole = lax.all_gather(by_unit[:, : 4 * D], "blk", axis=0, tiled=True)
    gate_whole = lax.all_gather(by_unit[:, 4 * D : 4 * D + 2 * FF], "blk", axis=0, tiled=True)
    down_whole = lax.all_gather(by_unit[:, 4 * D + 2 * FF :], "blk", axis=0, tiled=True)
    places = axis_place * seq_part + jnp.arange(seq_part, dtype=jnp.int32)
    segment, position = document_places(lengths, places)
    cosine, sine = turn_tables(position)
    cosine = cosine[:, :, None, None, :]
    sine = sine[:, :, None, None, :]
    residual = tokens.astype(jnp.float32)
    gain_one = small[:D]
    gain_two = small[D : 2 * D]
    head_gain = small[2 * D : 2 * D + VD]
    mixer, mixer_back = jax.vjp(mix_value, small[2 * D + VD :].reshape(4, HD))
    normed_exact, norm_one_back = jax.vjp(root_norm, residual, gain_one)
    normed_one = normed_exact.astype(jnp.bfloat16).reshape(token_count, D)
    projected = jnp.dot(normed_one, attention_whole[:, : 3 * D], preferred_element_type=jnp.float32)
    query = rotate(projected[:, :D].reshape(rows_count, seq_part, H, 2, HD), cosine, sine).astype(
        jnp.bfloat16
    )
    key_own = (
        rotate(projected[:, D : 2 * D].reshape(rows_count, seq_part, H, 2, HD), cosine, sine)
        .astype(jnp.bfloat16)
        .reshape(rows_count, seq_part, D)
    )
    value_own = projected[:, 2 * D :].astype(jnp.bfloat16).reshape(rows_count, seq_part, D)
    best = jnp.full((rows_count, H, 2, seq_part), masked_fill, jnp.float32)
    key_piece = lax.all_gather(key_own, "blk", axis=1, tiled=True)
    value_piece = lax.all_gather(value_own, "blk", axis=1, tiled=True)
    count = key_piece.shape[1]
    key_places = jnp.arange(count, dtype=jnp.int32)
    key_segment, unused = document_places(lengths, key_places)
    mask = allowed(segment, places, key_segment, key_places, NDOC - 1)[:, None, None]
    keys = key_piece.reshape(rows_count, count, H, 2, HD)
    values = value_piece.reshape(rows_count, count, H, VD)
    scores = (
        jnp.einsum("rqhcd,rkhcd->rhcqk", query, keys, preferred_element_type=jnp.float32) * scale
    )
    scores = jnp.where(mask, scores, masked_fill)
    top = jnp.maximum(best, jnp.max(scores, axis=-1))
    shares = jnp.where(mask, jnp.exp(scores - top[..., None]), 0.0)
    mass = jnp.sum(shares, axis=-1)
    summed = jnp.einsum(
        "rhcqk,rkhe->rhcqe", shares.astype(jnp.bfloat16), values, preferred_element_type=jnp.float32
    )
    best, mass, summed = (top, mass, summed)
    maps_out = summed / mass[..., None]
    log_mass = best + jnp.log(mass)
    mixed_exact, mix_back = jax.vjp(head_mix, maps_out, head_gain, mixer)
    mixed = mixed_exact.astype(jnp.bfloat16).reshape(token_count, D)
    middle = residual.reshape(token_count, D) + contract_rows(mixed, attention_whole[:, 3 * D :])
    normed_two_exact, norm_two_back = jax.vjp(root_norm, middle, gain_two)
    normed_two = normed_two_exact.astype(jnp.bfloat16)
    gate_up = jnp.dot(normed_two, gate_whole, preferred_element_type=jnp.float32)
    hidden_exact, gated_back = jax.vjp(gated_unit, gate_up[:, :FF], gate_up[:, FF:])
    hidden = hidden_exact.astype(jnp.bfloat16)
    result = middle + contract_rows(hidden, down_whole)
    block_out = result.astype(jnp.bfloat16).reshape(rows_count, seq_part, D)
    output_grad = cotangent.reshape(token_count, D)
    hidden_grad = jnp.dot(output_grad, down_whole, preferred_element_type=jnp.float32)
    gate_grad, up_grad = gated_back(hidden_grad)
    gate_up_grad = jnp.concatenate([gate_grad, up_grad], axis=1).astype(jnp.bfloat16)
    normed_two_grad = contract_rows(gate_up_grad, gate_whole)
    middle_part, gain_two_grad = norm_two_back(normed_two_grad)
    middle_grad = output_grad.astype(jnp.float32) + middle_part
    middle_low = middle_grad.astype(jnp.bfloat16)
    mixed_grad = jnp.dot(
        middle_low, attention_whole[:, 3 * D :], preferred_element_type=jnp.float32
    )
    maps_grad, head_gain_grad, mixer_grad = mix_back(mixed_grad.reshape(rows_count, seq_part, D))
    maps_low = maps_grad.astype(jnp.bfloat16)
    offset_term = jnp.sum(maps_low.astype(jnp.float32) * maps_out, axis=-1)

    def circle(turn_index, carry):
        moving, moving_grad, query_grad = carry
        source = (axis_place - turn_index) % axis_count
        key_places = source * seq_part + jnp.arange(seq_part, dtype=jnp.int32)
        key_segment, unused = document_places(lengths, key_places)
        mask = allowed(segment, places, key_segment, key_places, NDOC - 1)[:, None, None]
        keys = moving[0].astype(jnp.bfloat16).reshape(rows_count, seq_part, H, 2, HD)
        values = moving[1].astype(jnp.bfloat16).reshape(rows_count, seq_part, H, VD)
        scores = (
            jnp.einsum("rqhcd,rkhcd->rhcqk", query, keys, preferred_element_type=jnp.float32)
            * scale
        )
        shares = jnp.where(mask, jnp.exp(scores - log_mass[..., None]), 0.0)
        value_term = jnp.einsum(
            "rhcqk,rhcqe->rkhe",
            shares.astype(jnp.bfloat16),
            maps_low,
            preferred_element_type=jnp.float32,
        )
        share_grad = jnp.einsum(
            "rhcqe,rkhe->rhcqk", maps_low, values, preferred_element_type=jnp.float32
        )
        score_low = (shares * (share_grad - offset_term[..., None])).astype(jnp.bfloat16)
        query_grad = query_grad + jnp.einsum(
            "rhcqk,rkhcd->rqhcd", score_low, keys, preferred_element_type=jnp.float32
        )
        key_term = jnp.einsum(
            "rhcqk,rqhcd->rkhcd", score_low, query, preferred_element_type=jnp.float32
        )
        update = jnp.stack(
            [key_term.reshape(rows_count, seq_part, D), value_term.reshape(rows_count, seq_part, D)]
        )
        moving_grad = moving_grad + update
        moving, moving_grad = (
            from_behind(moving.astype(jnp.bfloat16), "blk", 1).astype(moving.dtype),
            from_behind(moving_grad.astype(jnp.bfloat16), "blk", 1).astype(moving_grad.dtype),
        )
        return (moving, moving_grad, query_grad)

    circle_start = (
        jnp.stack([key_own, value_own]).astype(jnp.float32),
        jnp.zeros((2, rows_count, seq_part, D), jnp.float32),
        jnp.zeros((rows_count, seq_part, H, 2, HD), jnp.float32),
    )
    moving, moving_grad, query_grad = lax.fori_loop(0, axis_count, circle, circle_start)
    key_grad = moving_grad[0].reshape(rows_count, seq_part, H, 2, HD) * scale
    query_pre = rotate(query_grad * scale, cosine, -sine).reshape(token_count, D)
    key_pre = rotate(key_grad, cosine, -sine).reshape(token_count, D)
    projected_grad = jnp.concatenate(
        [query_pre, key_pre, moving_grad[1].reshape(token_count, D)], axis=1
    ).astype(jnp.bfloat16)
    normed_one_grad = contract_rows(projected_grad, attention_whole[:, : 3 * D])
    residual_part, gain_one_grad = norm_one_back(normed_one_grad.reshape(rows_count, seq_part, D))
    input_grad = (middle_grad.reshape(rows_count, seq_part, D) + residual_part).astype(jnp.bfloat16)
    (mixers_grad,) = mixer_back(mixer_grad)
    small_local = jnp.concatenate(
        [gain_one_grad, gain_two_grad, head_gain_grad, mixers_grad.reshape(-1)]
    )
    small_grads = lax.psum(small_local, ("batch", "blk"))
    right_side = jnp.concatenate([projected_grad, mixed, gate_up_grad, hidden], axis=1)
    left_sides = (normed_one, middle_low, normed_two, output_grad)
    bounds = (0, 3 * D, 4 * D, 4 * D + 2 * FF, 4 * D + 3 * FF)
    slot_order = inverse_order(unit_owner)
    parts = []
    for group in range(4):
        left_rows = left_sides[group]
        parts.append(
            lax.dot_general(
                left_rows,
                right_side[:, bounds[group] : bounds[group + 1]],
                (((0,), (0,)), ((), ())),
                preferred_element_type=jnp.float32,
            )
        )
    row_sums = lax.psum_scatter(
        jnp.concatenate(parts, axis=1).astype(jnp.bfloat16), "blk", scatter_dimension=0, tiled=True
    ).astype(jnp.float32)
    placed = take_units(row_sums.reshape(rows_part, UNITS, UW), slot_order)
    grad_slots = lax.psum_scatter(
        placed.astype(jnp.bfloat16), "batch", scatter_dimension=1, tiled=True
    ).astype(jnp.float32)
    columns = bases
    turned = lax.psum_scatter(
        jnp.einsum("ksa,ksn->asn", columns, grad_slots, precision=highest).astype(jnp.bfloat16),
        "blk",
        scatter_dimension=0,
        tiled=True,
    ).astype(jnp.float32)
    steps_done = step_count[0].astype(jnp.float32)
    new_first = beta_one * first + (1.0 - beta_one) * turned
    new_second = beta_two * second + (1.0 - beta_two) * turned * turned
    normalized = adam_step(new_first, new_second, steps_done)
    columns = bases
    update = jnp.zeros_like(master) + jnp.einsum(
        "ksa,asn->ksn",
        columns,
        lax.all_gather(normalized.astype(jnp.bfloat16), "blk", axis=0, tiled=True).astype(
            jnp.float32
        ),
        precision=highest,
    )
    new_master = master - learn_rate * (update + weight_decay * master)
    new_small_first = beta_one * small_first + (1.0 - beta_one) * small_grads
    new_small_second = beta_two * small_second + (1.0 - beta_two) * small_grads * small_grads
    new_small = small - small_rate * adam_step(new_small_first, new_small_second, steps_done)
    return (
        block_out,
        input_grad,
        new_master,
        new_first,
        new_second,
        small_grads,
        new_small,
        new_small_first,
        new_small_second,
    )


BF = jnp.bfloat16
F32 = jnp.float32
TILE = 256
HEADS = 3
QW = HEADS * VD
FQ = FF // 4
VMEM_LIMIT = 56 * 2**20


def params(**more):
    return pltpu.CompilerParams(vmem_limit_bytes=VMEM_LIMIT, **more)


def dot_last(left, right):
    return lax.dot_general(left, right, (((1,), (1,)), ((), ())), preferred_element_type=F32)


def dot_first(left, right):
    return lax.dot_general(left, right, (((0,), (0,)), ((), ())), preferred_element_type=F32)


def dot_plain(left, right):
    return jnp.dot(left, right, preferred_element_type=F32)


def swap_core(piece):
    return lax.ppermute(piece, "batch", [(i, i ^ 1) for i in range(4)])


def swap_y(piece):
    return lax.ppermute(piece, "batch", [(i, i ^ 2) for i in range(4)])


LOOP = (0, 2, 4, 6, 7, 5, 3, 1)


def ring_up(piece):
    return lax.ppermute(piece, "blk", [(LOOP[i], LOOP[(i + 1) % 8]) for i in range(8)])


def ring_down(piece):
    return lax.ppermute(piece, "blk", [(LOOP[(i + 1) % 8], LOOP[i]) for i in range(8)])


def sum_everywhere(values):
    values = values + swap_core(values)
    values = values + swap_y(values)
    for bit in (1, 2, 4):
        values = values + lax.ppermute(values, "blk", [(i, i ^ bit) for i in range(8)])
    return values


def after(values, earlier):
    return lax.optimization_barrier((values, earlier))[0]


def ring_place(blk):
    return jnp.where(blk % 2 == 0, blk // 2, 7 - blk // 2)


def ring_owner(place):
    place = place % 8
    return jnp.where(place < 4, 2 * place, 2 * (7 - place) + 1)


def put(whole, piece, index, axis):
    return lax.dynamic_update_slice_in_dim(whole, jnp.expand_dims(piece, axis), index, axis)


def batch_pieces(piece):
    far = swap_y(piece)
    return (piece, swap_core(piece), far, swap_core(far))


def batch_gather(piece, me, axis):
    pieces = batch_pieces(piece)
    shape = piece.shape[:axis] + (4,) + piece.shape[axis:]
    whole = jnp.zeros(shape, piece.dtype)
    for other in range(4):
        whole = put(whole, pieces[other], me ^ other, axis)
    return whole


def batch_scatter(partial, me, axis):
    shape = partial.shape
    split = partial.reshape(shape[:axis] + (2, 2) + shape[axis + 1 :])
    y, core = me // 2, me % 2

    def pick(array, index, at):
        return lax.dynamic_index_in_dim(array, index, at, keepdims=False)

    near = pick(split, core, axis + 1).astype(F32) + swap_core(pick(split, 1 - core, axis + 1)).astype(F32)
    far = swap_y(pick(near, 1 - y, axis).astype(BF))
    return pick(near, y, axis) + far.astype(F32)


def ring_gather(shard, blk, axis):
    half = shard.shape[axis] // 2
    place = ring_place(blk)
    shape = shard.shape[:axis] + (8,) + shard.shape[axis:]
    whole = put(jnp.zeros(shape, shard.dtype), shard, blk, axis)
    up = lax.slice_in_dim(shard, 0, half, axis=axis)
    down = lax.slice_in_dim(shard, half, 2 * half, axis=axis)

    def store(whole, piece, owner, begin):
        starts = [0] * len(shape)
        starts[axis] = owner
        starts[axis + 1] = begin
        return lax.dynamic_update_slice(whole, jnp.expand_dims(piece, axis), starts)

    for step in range(1, 8):
        up, down = ring_up(up), ring_down(down)
        whole = store(whole, up, ring_owner(place - step), 0)
        whole = store(whole, down, ring_owner(place + step), half)
    return whole


def ring_scatter(part_of, blk):
    place = ring_place(blk)
    up, down = part_of(ring_owner(place - 1), 0), part_of(ring_owner(place + 1), 1)
    for step in range(1, 8):
        up, down = ring_up(up.astype(BF)), ring_down(down.astype(BF))
        up = up.astype(F32) + part_of(ring_owner(place - 1 - step), 0).astype(F32)
        down = down.astype(F32) + part_of(ring_owner(place + 1 + step), 1).astype(F32)
    return up, down


def to_rows(tokens):
    rows, count, width = tokens.shape
    pieces = tokens.reshape(rows, 4, count // 4, width)
    pieces = lax.all_to_all(pieces, "batch", 1, 0, tiled=True)
    return lax.all_to_all(pieces.reshape(8, count // 4, width), "blk", 0, 0, tiled=True)


def from_rows(tokens):
    count, width = tokens.shape[1:]
    pieces = lax.all_to_all(tokens, "blk", 0, 0, tiled=True)
    pieces = lax.all_to_all(pieces.reshape(8, 1, count, width), "batch", 0, 1, tiled=True)
    return pieces.reshape(2, 4 * count, width)


def attention_pieces(me):
    pieces = []
    for matrix in range(4):
        for j in range(HEADS):
            block = HEADS * me + j
            pieces.append((3 * matrix + block // 4, block % 4, HEADS * matrix + j))
    return pieces


def pick_kernel(place_ref, me_ref, own, core, far, far_core, attn_ref, ffn_ref, sems):
    me = me_ref[0]
    waits = []

    def begin(unit, source, target, sem):
        at = place_ref[unit]
        for other, ref in enumerate((own, core, far, far_core)):

            @pl.when(at // 9 == other)
            def start():
                pltpu.make_async_copy(source(ref.at[at % 9]), target, sem).start()

        waits.append(pltpu.make_async_copy(source(own.at[0]), target, sem))

    for i, (unit, block, packed) in enumerate(attention_pieces(me)):
        column = pl.multiple_of(block * 128, 128)
        begin(unit, lambda r, c=column: r.at[:, pl.ds(c, 128)], attn_ref.at[:, pl.ds(packed * 128, 128)], sems.at[i])
    for i in range(6):
        unit = 12 + 8 * (i // 2) + 2 * me + i % 2
        begin(unit, lambda r: r, ffn_ref.at[:, pl.ds(i * UW, UW)], sems.at[12 + i])
    for wait in waits:
        wait.wait()


def pick_units(place, me, pieces):
    rows = pieces[0].shape[1]
    hbm = pl.BlockSpec(memory_space=pl.ANY)
    smem = pl.BlockSpec(memory_space=pltpu.SMEM)
    vmem = pl.BlockSpec(memory_space=pltpu.VMEM)
    return pl.pallas_call(
        pick_kernel,
        in_specs=[smem, smem, hbm, hbm, hbm, hbm],
        out_specs=[vmem, vmem],
        out_shape=[
            jax.ShapeDtypeStruct((rows, 4 * QW), BF),
            jax.ShapeDtypeStruct((rows, 6 * UW), BF),
        ],
        scratch_shapes=[pltpu.SemaphoreType.DMA((18,))],
        compiler_params=params(),
        name="pick_units",
    )(place, me.reshape(1), *pieces)


def place_kernel(unit_ref, me_ref, *refs):
    attn, ffn, out_ref, sems = refs[:4], refs[4:8], refs[8], refs[9]
    me = me_ref[0]
    waits = []
    for i in range(9):
        unit = unit_ref[i]
        of_attn = unit < 12
        f = jnp.maximum(unit - 12, 0)
        for q in range(4):
            block = (unit % 3) * 4 + q
            source = jnp.where(of_attn, block // HEADS, (f % 8) // 2) ^ me
            column = jnp.where(
                of_attn, (unit // 3) * QW + (block % HEADS) * 128, (f // 8) * FQ + (f % 2) * UW + q * 128
            )
            column = pl.multiple_of(column, 128)
            target, sem = out_ref.at[i, :, pl.ds(q * 128, 128)], sems.at[i, q]
            for other in range(4):
                for mine, pieces in ((of_attn, attn), (jnp.logical_not(of_attn), ffn)):

                    @pl.when(mine & (source == other))
                    def start(ref=pieces[other], column=column, target=target, sem=sem):
                        pltpu.make_async_copy(ref.at[:, pl.ds(column, 128)], target, sem).start()

            waits.append(pltpu.make_async_copy(attn[0].at[:, pl.ds(0, 128)], target, sem))
    for wait in waits:
        wait.wait()


def place_units(units, me, attn_pieces, ffn_pieces):
    rows = attn_pieces[0].shape[0]
    hbm = pl.BlockSpec(memory_space=pl.ANY)
    smem = pl.BlockSpec(memory_space=pltpu.SMEM)
    return pl.pallas_call(
        place_kernel,
        in_specs=[smem, smem] + [hbm] * 8,
        out_specs=pl.BlockSpec(memory_space=pltpu.VMEM),
        out_shape=jax.ShapeDtypeStruct((9, rows, UW), BF),
        scratch_shapes=[pltpu.SemaphoreType.DMA((9, 4))],
        compiler_params=params(),
        name="place_units",
    )(units, me.reshape(1), *attn_pieces, *ffn_pieces)


def turn(values, cosine, sine, lane):
    partner = jnp.where(lane % HD < HD // 2, pltpu.roll(values, 96, 1), pltpu.roll(values, 32, 1))
    return values * cosine + partner * sine


def project_kernel(x_ref, w_ref, gain_ref, cos_ref, sin_ref, n_ref, q_ref, k_ref, v_ref):
    x = x_ref[...].astype(F32)
    r = lax.rsqrt(jnp.mean(x * x, axis=-1, keepdims=True) + norm_epsilon)
    n = (x * r * gain_ref[...]).astype(BF)
    n_ref[...] = n
    lane = lax.broadcasted_iota(jnp.int32, (x.shape[0], VD), 1)
    cosine, sine = cos_ref[...], sin_ref[...]
    out = dot_plain(n, w_ref[...])
    for h in range(HEADS):
        at = slice(h * VD, (h + 1) * VD)
        q = turn(out[:, h * VD : (h + 1) * VD], cosine, sine, lane)
        q_ref[:, at] = (q.astype(BF).astype(F32) * HD**-0.5).astype(BF)
        k = turn(out[:, QW + h * VD : QW + (h + 1) * VD], cosine, sine, lane)
        k_ref[:, at] = k.astype(BF)
    v_ref[...] = out[:, 2 * QW :].astype(BF)


def project(x, weights, gain, cosine, sine):
    count = x.shape[0]
    rows = lambda w: pl.BlockSpec((TILE, w), lambda i: (i, 0))
    fixed = lambda h, w: pl.BlockSpec((h, w), lambda i: (0, 0), pipeline_mode=pl.Buffered(1))
    narrow = jax.ShapeDtypeStruct((count, QW), BF)
    return pl.pallas_call(
        project_kernel,
        grid=(count // TILE,),
        in_specs=[rows(D), fixed(D, 3 * QW), fixed(1, D), rows(VD), rows(VD)],
        out_specs=[rows(D), rows(QW), rows(QW), rows(QW)],
        out_shape=[jax.ShapeDtypeStruct((count, D), BF), narrow, narrow, narrow],
        compiler_params=params(),
        cost_estimate=pl.CostEstimate(
            flops=2 * count * D * 3 * QW, bytes_accessed=count * D * 6 + 6 * D * QW, transcendentals=0
        ),
        name="project",
    )(x, weights, gain, cosine, sine)


def split_halves(q):
    lane = lax.broadcasted_iota(jnp.int32, q.shape, 1)
    zero = jnp.zeros_like(q)
    return jnp.concatenate([jnp.where(lane < HD, q, zero), jnp.where(lane >= HD, q, zero)], axis=0)


def block_mask(j, i, start):
    key = j * TILE + lax.broadcasted_iota(jnp.int32, (TILE, 2 * TILE), 0)
    query = i * TILE + lax.broadcasted_iota(jnp.int32, (TILE, TILE), 1)
    query = jnp.concatenate([query, query], axis=1)
    return (key >= start) & (key <= query)


def attend_kernel(low_ref, lam_ref, q_ref, k_ref, v_ref, start_ref, gain_ref, a_ref, maps_ref, log_ref, vt_ref):
    i = pl.program_id(1)

    @pl.when(i == 0)
    def turn_values():
        for j in range(vt_ref.shape[0]):
            vt_ref[j] = v_ref[j * TILE : (j + 1) * TILE, :].astype(F32).T.astype(BF)

    q = split_halves(q_ref[...])
    start = jnp.concatenate([start_ref[...], start_ref[...]], axis=1)

    def step(j, carry):
        top, mass, total = carry
        keys = k_ref[pl.ds(pl.multiple_of(j * TILE, TILE), TILE), :]
        scores = jnp.where(block_mask(j, i, start), dot_last(keys, q), masked_fill)
        new = jnp.maximum(top, jnp.max(scores, axis=0, keepdims=True))
        shares = jnp.exp(scores - new)
        keep = jnp.exp(top - new)
        mass = mass * keep + jnp.sum(shares, axis=0, keepdims=True)
        total = total * keep + dot_plain(vt_ref[j], shares.astype(BF))
        return new, mass, total

    first = (
        jnp.full((1, 2 * TILE), masked_fill, F32),
        jnp.zeros((1, 2 * TILE), F32),
        jnp.zeros((VD, 2 * TILE), F32),
    )
    top, mass, total = lax.fori_loop(low_ref[i], i + 1, step, first)
    maps = total / mass
    one, two = maps[:, :TILE], maps[:, TILE:]
    maps_ref[0, 0] = one
    maps_ref[0, 1] = two
    log_ref[0, 0] = top + jnp.log(mass)
    mixed = one - lam_ref[0] * two
    r = lax.rsqrt(jnp.mean(mixed * mixed, axis=0, keepdims=True) + norm_epsilon)
    a_ref[...] = (mixed * r * gain_ref[...] * (1.0 - lambda_start)).T.astype(BF)


def attend(low, lam, q, k, v, start, gain):
    count = q.shape[0]
    blocks = count // TILE
    smem = pl.BlockSpec(memory_space=pltpu.SMEM)
    return pl.pallas_call(
        attend_kernel,
        grid=(HEADS, blocks),
        in_specs=[
            smem,
            smem,
            pl.BlockSpec((TILE, VD), lambda h, i: (i, h)),
            pl.BlockSpec((count, VD), lambda h, i: (0, h)),
            pl.BlockSpec((count, VD), lambda h, i: (0, h)),
            pl.BlockSpec((1, TILE), lambda h, i: (0, i)),
            pl.BlockSpec((VD, 1), lambda h, i: (0, 0)),
        ],
        out_specs=[
            pl.BlockSpec((TILE, VD), lambda h, i: (i, h)),
            pl.BlockSpec((1, 2, VD, TILE), lambda h, i: (h, 0, 0, i)),
            pl.BlockSpec((1, 1, 1, 2 * TILE), lambda h, i: (h, i, 0, 0)),
        ],
        out_shape=[
            jax.ShapeDtypeStruct((count, QW), BF),
            jax.ShapeDtypeStruct((HEADS, 2, VD, count), F32),
            jax.ShapeDtypeStruct((HEADS, blocks, 1, 2 * TILE), F32),
        ],
        scratch_shapes=[pltpu.VMEM((blocks, VD, TILE), BF)],
        compiler_params=params(),
        cost_estimate=pl.CostEstimate(
            flops=8 * count * count * VD * HEADS, bytes_accessed=count * QW * 16, transcendentals=count * count * HEADS
        ),
        name="attend",
    )(low, lam, q, k, v, start, gain)


def attend_back_kernel(
    low_ref, lam_ref, q_ref, k_ref, v_ref, start_ref, gain_ref, maps_ref, log_ref, da_ref, cosq_ref, sinq_ref,
    cosk_ref, sink_ref, dq_ref, dk_ref, dv_ref, dgain_ref, dlam_ref, kt_ref, dk_sum, dv_sum, dq_sum,
):
    i = pl.program_id(1)
    blocks = kt_ref.shape[0]

    @pl.when(i == 0)
    def begin():
        for j in range(blocks):
            kt_ref[j] = k_ref[j * TILE : (j + 1) * TILE, :].astype(F32).T.astype(BF)
        dk_sum[...] = jnp.zeros_like(dk_sum)
        dv_sum[...] = jnp.zeros_like(dv_sum)
        dgain_ref[...] = jnp.zeros_like(dgain_ref)
        dlam_ref[...] = jnp.zeros_like(dlam_ref)

    lam = lam_ref[0]
    q = split_halves(q_ref[...])
    start = jnp.concatenate([start_ref[...], start_ref[...]], axis=1)
    log_mass = log_ref[0, 0]
    one, two = maps_ref[0, 0], maps_ref[0, 1]
    mixed = one - lam * two
    r = lax.rsqrt(jnp.mean(mixed * mixed, axis=0, keepdims=True) + norm_epsilon)
    t = mixed * r
    da = da_ref[...].T * (1.0 - lambda_start)
    dgain_ref[0] += da * t
    e = da * gain_ref[...]
    dmixed = r * (e - t * jnp.mean(e * t, axis=0, keepdims=True))
    dlam_ref[0] -= jnp.sum(dmixed * two, axis=0, keepdims=True)
    dmaps = jnp.concatenate([dmixed, -lam * dmixed], axis=1).astype(BF)
    maps = jnp.concatenate([one, two], axis=1)
    offset = jnp.sum(dmaps.astype(F32) * maps, axis=0, keepdims=True)
    dq_sum[...] = jnp.zeros_like(dq_sum)

    def step(j, carry):
        at = pl.ds(pl.multiple_of(j * TILE, TILE), TILE)
        keys, values = k_ref[at, :], v_ref[at, :]
        scores = dot_last(keys, q)
        shares = jnp.where(block_mask(j, i, start), jnp.exp(scores - log_mass), 0.0)
        dshares = dot_plain(values, dmaps)
        dscores = (shares * (dshares - offset)).astype(BF)
        dv_sum[at, :] += dot_last(shares.astype(BF), dmaps)
        dk_sum[at, :] += dot_plain(dscores, q)
        dq_sum[...] += dot_plain(kt_ref[j], dscores)
        return carry

    lax.fori_loop(low_ref[i], i + 1, step, 0)
    lane = lax.broadcasted_iota(jnp.int32, (TILE, VD), 1)
    dq = jnp.concatenate([dq_sum[:HD, :TILE], dq_sum[HD:, TILE:]], axis=0).T * HD**-0.5
    dq_ref[...] = turn(dq, cosq_ref[...], -sinq_ref[...], lane).astype(BF)

    @pl.when(i == blocks - 1)
    def finish():
        for j in range(blocks):
            at = slice(j * TILE, (j + 1) * TILE)
            dk_ref[at, :] = turn(dk_sum[at, :], cosk_ref[at, :], -sink_ref[at, :], lane).astype(BF)
        dv_ref[...] = dv_sum[...].astype(BF)


def attend_back(low, lam, q, k, v, start, gain, maps, log_mass, da, cosine, sine):
    count = q.shape[0]
    blocks = count // TILE
    smem = pl.BlockSpec(memory_space=pltpu.SMEM)
    tile = pl.BlockSpec((TILE, VD), lambda h, i: (i, h))
    whole = pl.BlockSpec((count, VD), lambda h, i: (0, h))
    table = pl.BlockSpec((TILE, VD), lambda h, i: (i, 0))
    full_table = pl.BlockSpec((count, VD), lambda h, i: (0, 0), pipeline_mode=pl.Buffered(1))
    narrow = jax.ShapeDtypeStruct((count, QW), BF)
    return pl.pallas_call(
        attend_back_kernel,
        grid=(HEADS, blocks),
        in_specs=[
            smem,
            smem,
            tile,
            whole,
            whole,
            pl.BlockSpec((1, TILE), lambda h, i: (0, i)),
            pl.BlockSpec((VD, 1), lambda h, i: (0, 0)),
            pl.BlockSpec((1, 2, VD, TILE), lambda h, i: (h, 0, 0, i)),
            pl.BlockSpec((1, 1, 1, 2 * TILE), lambda h, i: (h, i, 0, 0)),
            tile,
            table,
            table,
            full_table,
            full_table,
        ],
        out_specs=[
            tile,
            whole,
            whole,
            pl.BlockSpec((1, VD, TILE), lambda h, i: (h, 0, 0)),
            pl.BlockSpec((1, 1, TILE), lambda h, i: (h, 0, 0)),
        ],
        out_shape=[
            narrow,
            narrow,
            narrow,
            jax.ShapeDtypeStruct((HEADS, VD, TILE), F32),
            jax.ShapeDtypeStruct((HEADS, 1, TILE), F32),
        ],
        scratch_shapes=[
            pltpu.VMEM((blocks, VD, TILE), BF),
            pltpu.VMEM((count, VD), F32),
            pltpu.VMEM((count, VD), F32),
            pltpu.VMEM((VD, 2 * TILE), F32),
        ],
        compiler_params=params(),
        cost_estimate=pl.CostEstimate(
            flops=20 * count * count * VD * HEADS, bytes_accessed=count * QW * 24, transcendentals=count * count * HEADS
        ),
        name="attend_back",
    )(low, lam, q, k, v, start, gain, maps, log_mass, da, cosine, sine, cosine, sine)


def middle_kernel(me_ref, x_ref, gain_ref, *refs):
    a_refs, w_refs, (n_ref, own_ref, sum_ref) = refs[:4], refs[4:8], refs[8:]
    x1 = x_ref[...].astype(F32)
    for a_ref, w_ref in zip(a_refs, w_refs):
        x1 += dot_last(a_ref[...], w_ref[...])
    sum_ref[...] = x1
    r = lax.rsqrt(jnp.mean(x1 * x1, axis=-1, keepdims=True) + norm_epsilon)
    n_ref[...] = (x1 * r * gain_ref[...]).astype(BF)
    part = TILE // 4
    own_ref[0] = sum_ref[pl.ds(pl.multiple_of(me_ref[0] * part, part), part), :]


def middle(me, a, x, weights, gain):
    count = x.shape[0]
    rows = pl.BlockSpec((TILE, D), lambda i: (i, 0))
    return pl.pallas_call(
        middle_kernel,
        grid=(count // TILE,),
        in_specs=[
            pl.BlockSpec(memory_space=pltpu.SMEM),
            rows,
            pl.BlockSpec((1, D), lambda i: (0, 0)),
        ]
        + [pl.BlockSpec((TILE, QW), lambda i: (i, 0))] * 4
        + [pl.BlockSpec((D, QW), lambda i: (0, 0), pipeline_mode=pl.Buffered(1))] * 4,
        out_specs=[rows, pl.BlockSpec((1, TILE // 4, D), lambda i: (i, 0, 0))],
        out_shape=[
            jax.ShapeDtypeStruct((count, D), BF),
            jax.ShapeDtypeStruct((count // TILE, TILE // 4, D), F32),
        ],
        scratch_shapes=[pltpu.VMEM((TILE, D), F32)],
        compiler_params=params(),
        cost_estimate=pl.CostEstimate(
            flops=2 * count * D * D, bytes_accessed=count * D * 7 + 2 * D * D, transcendentals=0
        ),
        name="middle",
    )(me.reshape(1), x, gain, *a, *weights)


def feed_kernel(n_ref, dy_ref, w_ref, act_ref, out_ref, dn_ref):
    n, dy = n_ref[...], dy_ref[...]
    wg, wu, wd = w_ref[:, :FQ], w_ref[:, FQ : 2 * FQ], w_ref[:, 2 * FQ :]
    gate = dot_plain(n, wg)
    up = dot_plain(n, wu)
    dhidden = dot_plain(dy, wd)
    share = 1.0 / (1.0 + jnp.exp(-gate))
    silu = gate * share
    hidden = (silu * up).astype(BF)
    dup = (dhidden * silu).astype(BF)
    dgate = (dhidden * up * (share * (1.0 + gate * (1.0 - share)))).astype(BF)
    act_ref[:, :FQ] = dgate
    act_ref[:, FQ : 2 * FQ] = dup
    act_ref[:, 2 * FQ :] = hidden
    out_ref[...] = dot_last(hidden, wd).astype(BF)
    dn_ref[...] = (dot_last(dgate, wg) + dot_last(dup, wu)).astype(BF)


def feed(n, dy, weights):
    count = n.shape[0]
    rows = lambda w: pl.BlockSpec((TILE, w), lambda i: (i, 0))
    shape = lambda w: jax.ShapeDtypeStruct((count, w), BF)
    return pl.pallas_call(
        feed_kernel,
        grid=(count // TILE,),
        in_specs=[rows(D), rows(D), pl.BlockSpec((D, 3 * FQ), lambda i: (0, 0), pipeline_mode=pl.Buffered(1))],
        out_specs=[rows(3 * FQ), rows(D), rows(D)],
        out_shape=[shape(3 * FQ), shape(D), shape(D)],
        compiler_params=params(),
        cost_estimate=pl.CostEstimate(
            flops=12 * count * D * FQ, bytes_accessed=count * (8 * D + 6 * FQ) + 6 * D * FQ, transcendentals=count * FQ
        ),
        name="feed",
    )(n, dy, weights)


def row_tables(lengths, row, count):
    everyone = jnp.stack(batch_pieces(lengths))
    holder = (row // 2) ^ lax.axis_index("batch")
    mine = jnp.sum(jnp.where(jnp.arange(4)[:, None, None] == holder, everyone, 0), axis=0)
    mine = jnp.where(row % 2 == 0, mine[:1], mine[1:])
    ends = doc_ends(mine)[0]
    places = jnp.arange(count, dtype=jnp.int32)
    begin = jnp.sum(jnp.where(places[:, None] >= ends[None, :], mine, 0), axis=1)
    start = jnp.where(places >= ends[NDOC - 2], places, begin)
    low = start.reshape(-1, TILE)[:, 0] // TILE
    cosine, sine = turn_tables(places - begin)
    cosine = jnp.tile(cosine, (1, 4))
    sine = jnp.tile(jnp.concatenate([-sine, sine], axis=1), (1, 2))
    return start, low, cosine, sine


def row_groups(
    tokens,
    cotangent,
    lengths,
    unit_owner,
    step_count,
    master,
    first,
    second,
    bases,
    small,
    small_first,
    small_second,
):
    me, blk = lax.axis_index("batch"), lax.axis_index("blk")
    count = tokens.shape[1] * 8
    learn_rate = 2.0 / D**0.5
    slots = lambda array: jnp.transpose(array, (1, 0, 2))
    master_slots = slots(master)

    place = ((unit_owner // 9) ^ me) * 9 + unit_owner % 9
    attn_shard, ffn_shard = pick_units(place, me, batch_pieces(master_slots.astype(BF)))
    attn = ring_gather(attn_shard, blk, 0).reshape(D, 4 * QW)
    attn_out = batch_pieces(attn[:, 3 * QW :])
    ffn_shard = after(ffn_shard, attn)
    ffn = ring_gather(ffn_shard, blk, 0).reshape(D, 6 * UW)

    x_own = to_rows(tokens)
    dy_own = to_rows(cotangent)
    x = batch_gather(x_own, me, 1).reshape(count, D)
    dy = batch_gather(dy_own, me, 1).reshape(count, D)
    start, low, cosine, sine = row_tables(lengths, blk, count)
    start = start.reshape(1, count)

    gain_one = small[:D].reshape(1, D)
    gain_two = small[D : 2 * D].reshape(1, D)
    head_gain = small[2 * D : 2 * D + VD].reshape(VD, 1)
    mixer, mixer_back = jax.vjp(mix_value, small[2 * D + VD :].reshape(4, HD))
    lam = mixer.reshape(1)

    n1, q, k, v = project(x, attn, gain_one, cosine, sine)
    a_own, maps, log_mass = attend(low, lam, q, k, v, start, head_gain)
    a = batch_pieces(a_own)
    n2, x1 = middle(me, a, x, attn_out, gain_two)
    acts, out_part, dn2_part = feed(n2, dy, ffn)

    groups = (8, 4, count // 32, D)
    dn2 = batch_scatter(dn2_part.reshape(groups), me, 1)
    r2 = lax.rsqrt(jnp.mean(x1 * x1, axis=-1, keepdims=True) + norm_epsilon)
    t2 = x1 * r2
    e2 = dn2 * gain_two
    dx1 = dy_own.astype(F32) + r2 * (e2 - t2 * jnp.mean(e2 * t2, axis=-1, keepdims=True))
    gain_two_grad = jnp.sum(dn2 * t2, axis=(0, 1))
    dx1_low = batch_gather(dx1.astype(BF), me, 1).reshape(count, D)
    da = dot_plain(dx1_low, attn[:, 3 * QW :])
    dq, dk, dv, head_gain_sums, mixer_sums = attend_back(
        low, lam, q, k, v, start, head_gain, maps, log_mass, da, cosine, sine
    )
    dqkv = jnp.concatenate([dq, dk, dv], axis=1)
    dn1_part = dot_last(dqkv, attn[:, : 3 * QW]).astype(BF)
    dn1 = batch_scatter(dn1_part.reshape(groups), me, 1)
    x_f = x_own.astype(F32)
    r1 = lax.rsqrt(jnp.mean(x_f * x_f, axis=-1, keepdims=True) + norm_epsilon)
    t1 = x_f * r1
    e1 = dn1 * gain_one
    dx = dx1 + r1 * (e1 - t1 * jnp.mean(e1 * t1, axis=-1, keepdims=True))
    gain_one_grad = jnp.sum(dn1 * t1, axis=(0, 1))
    input_grad = from_rows(dx.astype(BF))
    out = batch_scatter(out_part.reshape(groups), me, 1)
    block_out = from_rows((x1 + out).astype(BF))

    (mixers_grad,) = mixer_back(jnp.sum(mixer_sums))
    small_local = jnp.concatenate(
        [gain_one_grad, gain_two_grad, jnp.sum(head_gain_sums, axis=(0, 2)), mixers_grad.reshape(-1)]
    )
    small_grads = sum_everywhere(small_local)

    part = D // 8

    def scatter_rows(grad):
        def part_of(owner, half):
            return lax.dynamic_slice_in_dim(grad, owner * part + half * part // 2, part // 2, axis=0)

        return jnp.concatenate(ring_scatter(part_of, blk), axis=0).astype(BF)

    ffn_grad = jnp.concatenate(
        [dot_first(n2, acts[:, : 2 * FQ]).astype(BF), dot_first(dy, acts[:, 2 * FQ :]).astype(BF)], axis=1
    )
    attn_grad = jnp.concatenate(
        [dot_first(n1, dqkv).astype(BF), dot_first(dx1_low, a_own).astype(BF)], axis=1
    )
    ffn_sums = scatter_rows(ffn_grad)
    attn_sums = scatter_rows(attn_grad)

    unit_of = inverse_order(unit_owner)
    units = lax.dynamic_slice_in_dim(unit_of, me * 9, 9)
    grads = place_units(units, me, batch_pieces(attn_sums), batch_pieces(ffn_sums))

    base = slots(bases).astype(BF)
    turned_part = jnp.einsum("sja,sjn->san", base, grads, preferred_element_type=F32).astype(BF)

    def turned_of(owner, half):
        return lax.dynamic_slice_in_dim(turned_part, owner * part + half * part // 2, part // 2, axis=1)

    turned = jnp.concatenate(ring_scatter(turned_of, blk), axis=1)
    steps_done = step_count[0].astype(F32)
    new_first = beta_one * slots(first) + (1.0 - beta_one) * turned
    new_second = beta_two * slots(second) + (1.0 - beta_two) * turned * turned
    normalized = adam_step(new_first, new_second, steps_done).astype(BF)
    every_step = ring_gather(normalized, blk, 1).reshape(9, D, UW)
    update = jnp.einsum("sja,san->sjn", base, every_step, preferred_element_type=F32)
    new_master = master_slots - learn_rate * (update + weight_decay * master_slots)
    new_small_first = beta_one * small_first + (1.0 - beta_one) * small_grads
    new_small_second = beta_two * small_second + (1.0 - beta_two) * small_grads * small_grads
    new_small = small - small_rate * adam_step(new_small_first, new_small_second, steps_done)
    return (
        block_out,
        input_grad,
        slots(new_master),
        slots(new_first),
        slots(new_second),
        small_grads,
        new_small,
        new_small_first,
        new_small_second,
    )


def solution(mesh):
    in_specs = (
        P("batch", "blk", None),
        P("batch", "blk", None),
        P("batch", None),
        P(),
        P(),
        P("blk", "batch", None),
        P("blk", "batch", None),
        P("blk", "batch", None),
        P("blk", "batch", None),
        P(),
        P(),
        P(),
    )
    out_specs = (
        P("batch", "blk", None),
        P("batch", "blk", None),
        P("blk", "batch", None),
        P("blk", "batch", None),
        P("blk", "batch", None),
        P(),
        P(),
        P(),
        P(),
    )
    by_rows = mesh.shape["blk"] == 8 and mesh.shape["batch"] == 4
    body = row_groups if by_rows else any_mesh
    return jax.shard_map(body, mesh=mesh, in_specs=in_specs, out_specs=out_specs, check_vma=False)
```

```python
import functools

import jax
import jax.numpy as jnp
from jax import lax
from jax.experimental import pallas as pl
from jax.experimental.pallas import tpu as pltpu
from jax.sharding import PartitionSpec as P

D = 1536
H = 12
HD = 64
VD = 128
FF = 4096
UW = 512
NDOC = 6
UNITS = 36


norm_epsilon = 1e-05
lambda_start = 0.2
rope_base = 10000.0
masked_fill = -1000000000.0
beta_one = 0.9
beta_two = 0.95
adam_epsilon = 1e-08
weight_decay = 0.01
small_rate = 1.0


def from_behind(shard, axis, by):
    count = lax.axis_size(axis)
    return lax.ppermute(shard, axis, [(i, (i + by) % count) for i in range(count)])


def root_norm(values, gain):
    return (
        values * lax.rsqrt(jnp.mean(values * values, axis=-1, keepdims=True) + norm_epsilon) * gain
    )


def mix_value(mixers):
    return (
        jnp.exp(jnp.sum(mixers[0] * mixers[1]))
        - jnp.exp(jnp.sum(mixers[2] * mixers[3]))
        + lambda_start
    )


def head_mix(maps_out, head_gain, mixer):
    combined = maps_out[:, :, 0] - mixer * maps_out[:, :, 1]
    normed = (
        combined
        * lax.rsqrt(jnp.mean(combined * combined, axis=-1, keepdims=True) + norm_epsilon)
        * head_gain
        * (1.0 - lambda_start)
    )
    rows_count, heads, positions, width = normed.shape
    return jnp.transpose(normed, (0, 2, 1, 3)).reshape(rows_count, positions, heads * width)


def gated_unit(gate, up):
    return jax.nn.silu(gate) * up


def doc_ends(lengths):
    count = lengths.shape[1]
    ends = [lengths[:, 0]]
    for j in range(1, count):
        ends.append(ends[-1] + lengths[:, j])
    return jnp.stack(ends, axis=1)


def document_places(lengths, places):
    ends = doc_ends(lengths)
    starts = ends - lengths
    segment = jnp.sum((places[None, :, None] >= ends[:, None, :]).astype(jnp.int32), axis=2)
    chosen = segment[:, :, None] == jnp.arange(lengths.shape[1], dtype=jnp.int32)[None, None, :]
    offset = jnp.sum(jnp.where(chosen, starts[:, None, :], 0), axis=2)
    return (segment, places[None, :] - offset)


def allowed(seg_query, place_query, seg_key, place_key, last):
    same = seg_query[:, :, None] == seg_key[:, None, :]
    causal = place_key[None, None, :] <= place_query[None, :, None]
    itself = place_key[None, None, :] == place_query[None, :, None]
    return same & causal & ((seg_query[:, :, None] < last) | itself)


def turn_tables(position):
    rates = rope_base ** (-2.0 * jnp.arange(HD // 2, dtype=jnp.float32) / HD)
    angle = position.astype(jnp.float32)[..., None] * rates
    return (jnp.cos(angle), jnp.sin(angle))


def rotate(values, cosine, sine):
    half = values.shape[-1] // 2
    front = values[..., :half]
    back = values[..., half:]
    return jnp.concatenate([front * cosine - back * sine, back * cosine + front * sine], axis=-1)


def adam_step(first_new, second_new, steps_done):
    return (
        first_new
        / (1.0 - beta_one**steps_done)
        / (jnp.sqrt(second_new / (1.0 - beta_two**steps_done)) + adam_epsilon)
    )


def take_units(stacked, order):
    parts = [lax.dynamic_slice_in_dim(stacked, order[i], 1, axis=1) for i in range(UNITS)]
    return jnp.concatenate(parts, axis=1)


def inverse_order(owner):
    numbers = jnp.arange(UNITS, dtype=jnp.int32)
    return jnp.sum(jnp.where(owner[None, :] == numbers[:, None], numbers[None, :], 0), axis=1)


def contract_rows(left, right):
    return lax.dot_general(
        left, right, (((1,), (1,)), ((), ())), preferred_element_type=jnp.float32
    )


def any_mesh(
    tokens,
    cotangent,
    lengths,
    unit_owner,
    step_count,
    master,
    first,
    second,
    bases,
    small,
    small_first,
    small_second,
):
    rows_count, seq_part, width = tokens.shape
    token_count = rows_count * seq_part
    axis_count = lax.axis_size("blk")
    axis_place = lax.axis_index("blk")
    rows_part = master.shape[0]
    scale = HD ** (-0.5)
    highest = lax.Precision.HIGHEST
    learn_rate = 2.0 / D**0.5
    every_slot = lax.all_gather(master.astype(jnp.bfloat16), "batch", axis=1, tiled=True)
    by_unit = take_units(every_slot, unit_owner).reshape(rows_part, UNITS * UW)
    attention_whole = lax.all_gather(by_unit[:, : 4 * D], "blk", axis=0, tiled=True)
    gate_whole = lax.all_gather(by_unit[:, 4 * D : 4 * D + 2 * FF], "blk", axis=0, tiled=True)
    down_whole = lax.all_gather(by_unit[:, 4 * D + 2 * FF :], "blk", axis=0, tiled=True)
    places = axis_place * seq_part + jnp.arange(seq_part, dtype=jnp.int32)
    segment, position = document_places(lengths, places)
    cosine, sine = turn_tables(position)
    cosine = cosine[:, :, None, None, :]
    sine = sine[:, :, None, None, :]
    residual = tokens.astype(jnp.float32)
    gain_one = small[:D]
    gain_two = small[D : 2 * D]
    head_gain = small[2 * D : 2 * D + VD]
    mixer, mixer_back = jax.vjp(mix_value, small[2 * D + VD :].reshape(4, HD))
    normed_exact, norm_one_back = jax.vjp(root_norm, residual, gain_one)
    normed_one = normed_exact.astype(jnp.bfloat16).reshape(token_count, D)
    projected = jnp.dot(normed_one, attention_whole[:, : 3 * D], preferred_element_type=jnp.float32)
    query = rotate(projected[:, :D].reshape(rows_count, seq_part, H, 2, HD), cosine, sine).astype(
        jnp.bfloat16
    )
    key_own = (
        rotate(projected[:, D : 2 * D].reshape(rows_count, seq_part, H, 2, HD), cosine, sine)
        .astype(jnp.bfloat16)
        .reshape(rows_count, seq_part, D)
    )
    value_own = projected[:, 2 * D :].astype(jnp.bfloat16).reshape(rows_count, seq_part, D)
    best = jnp.full((rows_count, H, 2, seq_part), masked_fill, jnp.float32)
    key_piece = lax.all_gather(key_own, "blk", axis=1, tiled=True)
    value_piece = lax.all_gather(value_own, "blk", axis=1, tiled=True)
    count = key_piece.shape[1]
    key_places = jnp.arange(count, dtype=jnp.int32)
    key_segment, unused = document_places(lengths, key_places)
    mask = allowed(segment, places, key_segment, key_places, NDOC - 1)[:, None, None]
    keys = key_piece.reshape(rows_count, count, H, 2, HD)
    values = value_piece.reshape(rows_count, count, H, VD)
    scores = (
        jnp.einsum("rqhcd,rkhcd->rhcqk", query, keys, preferred_element_type=jnp.float32) * scale
    )
    scores = jnp.where(mask, scores, masked_fill)
    top = jnp.maximum(best, jnp.max(scores, axis=-1))
    shares = jnp.where(mask, jnp.exp(scores - top[..., None]), 0.0)
    mass = jnp.sum(shares, axis=-1)
    summed = jnp.einsum(
        "rhcqk,rkhe->rhcqe", shares.astype(jnp.bfloat16), values, preferred_element_type=jnp.float32
    )
    best, mass, summed = (top, mass, summed)
    maps_out = summed / mass[..., None]
    log_mass = best + jnp.log(mass)
    mixed_exact, mix_back = jax.vjp(head_mix, maps_out, head_gain, mixer)
    mixed = mixed_exact.astype(jnp.bfloat16).reshape(token_count, D)
    middle = residual.reshape(token_count, D) + contract_rows(mixed, attention_whole[:, 3 * D :])
    normed_two_exact, norm_two_back = jax.vjp(root_norm, middle, gain_two)
    normed_two = normed_two_exact.astype(jnp.bfloat16)
    gate_up = jnp.dot(normed_two, gate_whole, preferred_element_type=jnp.float32)
    hidden_exact, gated_back = jax.vjp(gated_unit, gate_up[:, :FF], gate_up[:, FF:])
    hidden = hidden_exact.astype(jnp.bfloat16)
    result = middle + contract_rows(hidden, down_whole)
    block_out = result.astype(jnp.bfloat16).reshape(rows_count, seq_part, D)
    output_grad = cotangent.reshape(token_count, D)
    hidden_grad = jnp.dot(output_grad, down_whole, preferred_element_type=jnp.float32)
    gate_grad, up_grad = gated_back(hidden_grad)
    gate_up_grad = jnp.concatenate([gate_grad, up_grad], axis=1).astype(jnp.bfloat16)
    normed_two_grad = contract_rows(gate_up_grad, gate_whole)
    middle_part, gain_two_grad = norm_two_back(normed_two_grad)
    middle_grad = output_grad.astype(jnp.float32) + middle_part
    middle_low = middle_grad.astype(jnp.bfloat16)
    mixed_grad = jnp.dot(
        middle_low, attention_whole[:, 3 * D :], preferred_element_type=jnp.float32
    )
    maps_grad, head_gain_grad, mixer_grad = mix_back(mixed_grad.reshape(rows_count, seq_part, D))
    maps_low = maps_grad.astype(jnp.bfloat16)
    offset_term = jnp.sum(maps_low.astype(jnp.float32) * maps_out, axis=-1)

    def circle(turn_index, carry):
        moving, moving_grad, query_grad = carry
        source = (axis_place - turn_index) % axis_count
        key_places = source * seq_part + jnp.arange(seq_part, dtype=jnp.int32)
        key_segment, unused = document_places(lengths, key_places)
        mask = allowed(segment, places, key_segment, key_places, NDOC - 1)[:, None, None]
        keys = moving[0].astype(jnp.bfloat16).reshape(rows_count, seq_part, H, 2, HD)
        values = moving[1].astype(jnp.bfloat16).reshape(rows_count, seq_part, H, VD)
        scores = (
            jnp.einsum("rqhcd,rkhcd->rhcqk", query, keys, preferred_element_type=jnp.float32)
            * scale
        )
        shares = jnp.where(mask, jnp.exp(scores - log_mass[..., None]), 0.0)
        value_term = jnp.einsum(
            "rhcqk,rhcqe->rkhe",
            shares.astype(jnp.bfloat16),
            maps_low,
            preferred_element_type=jnp.float32,
        )
        share_grad = jnp.einsum(
            "rhcqe,rkhe->rhcqk", maps_low, values, preferred_element_type=jnp.float32
        )
        score_low = (shares * (share_grad - offset_term[..., None])).astype(jnp.bfloat16)
        query_grad = query_grad + jnp.einsum(
            "rhcqk,rkhcd->rqhcd", score_low, keys, preferred_element_type=jnp.float32
        )
        key_term = jnp.einsum(
            "rhcqk,rqhcd->rkhcd", score_low, query, preferred_element_type=jnp.float32
        )
        update = jnp.stack(
            [key_term.reshape(rows_count, seq_part, D), value_term.reshape(rows_count, seq_part, D)]
        )
        moving_grad = moving_grad + update
        moving, moving_grad = (
            from_behind(moving.astype(jnp.bfloat16), "blk", 1).astype(moving.dtype),
            from_behind(moving_grad.astype(jnp.bfloat16), "blk", 1).astype(moving_grad.dtype),
        )
        return (moving, moving_grad, query_grad)

    circle_start = (
        jnp.stack([key_own, value_own]).astype(jnp.float32),
        jnp.zeros((2, rows_count, seq_part, D), jnp.float32),
        jnp.zeros((rows_count, seq_part, H, 2, HD), jnp.float32),
    )
    moving, moving_grad, query_grad = lax.fori_loop(0, axis_count, circle, circle_start)
    key_grad = moving_grad[0].reshape(rows_count, seq_part, H, 2, HD) * scale
    query_pre = rotate(query_grad * scale, cosine, -sine).reshape(token_count, D)
    key_pre = rotate(key_grad, cosine, -sine).reshape(token_count, D)
    projected_grad = jnp.concatenate(
        [query_pre, key_pre, moving_grad[1].reshape(token_count, D)], axis=1
    ).astype(jnp.bfloat16)
    normed_one_grad = contract_rows(projected_grad, attention_whole[:, : 3 * D])
    residual_part, gain_one_grad = norm_one_back(normed_one_grad.reshape(rows_count, seq_part, D))
    input_grad = (middle_grad.reshape(rows_count, seq_part, D) + residual_part).astype(jnp.bfloat16)
    (mixers_grad,) = mixer_back(mixer_grad)
    small_local = jnp.concatenate(
        [gain_one_grad, gain_two_grad, head_gain_grad, mixers_grad.reshape(-1)]
    )
    small_grads = lax.psum(small_local, ("batch", "blk"))
    right_side = jnp.concatenate([projected_grad, mixed, gate_up_grad, hidden], axis=1)
    left_sides = (normed_one, middle_low, normed_two, output_grad)
    bounds = (0, 3 * D, 4 * D, 4 * D + 2 * FF, 4 * D + 3 * FF)
    slot_order = inverse_order(unit_owner)
    parts = []
    for group in range(4):
        left_rows = left_sides[group]
        parts.append(
            lax.dot_general(
                left_rows,
                right_side[:, bounds[group] : bounds[group + 1]],
                (((0,), (0,)), ((), ())),
                preferred_element_type=jnp.float32,
            )
        )
    row_sums = lax.psum_scatter(
        jnp.concatenate(parts, axis=1).astype(jnp.bfloat16), "blk", scatter_dimension=0, tiled=True
    ).astype(jnp.float32)
    placed = take_units(row_sums.reshape(rows_part, UNITS, UW), slot_order)
    grad_slots = lax.psum_scatter(
        placed.astype(jnp.bfloat16), "batch", scatter_dimension=1, tiled=True
    ).astype(jnp.float32)
    columns = bases
    turned = lax.psum_scatter(
        jnp.einsum("ksa,ksn->asn", columns, grad_slots, precision=highest).astype(jnp.bfloat16),
        "blk",
        scatter_dimension=0,
        tiled=True,
    ).astype(jnp.float32)
    steps_done = step_count[0].astype(jnp.float32)
    new_first = beta_one * first + (1.0 - beta_one) * turned
    new_second = beta_two * second + (1.0 - beta_two) * turned * turned
    normalized = adam_step(new_first, new_second, steps_done)
    columns = bases
    update = jnp.zeros_like(master) + jnp.einsum(
        "ksa,asn->ksn",
        columns,
        lax.all_gather(normalized.astype(jnp.bfloat16), "blk", axis=0, tiled=True).astype(
            jnp.float32
        ),
        precision=highest,
    )
    new_master = master - learn_rate * (update + weight_decay * master)
    new_small_first = beta_one * small_first + (1.0 - beta_one) * small_grads
    new_small_second = beta_two * small_second + (1.0 - beta_two) * small_grads * small_grads
    new_small = small - small_rate * adam_step(new_small_first, new_small_second, steps_done)
    return (
        block_out,
        input_grad,
        new_master,
        new_first,
        new_second,
        small_grads,
        new_small,
        new_small_first,
        new_small_second,
    )


BF = jnp.bfloat16
F32 = jnp.float32
TILE = 256
HEADS = 3
QW = HEADS * VD
FQ = FF // 4
VMEM_LIMIT = 56 * 2**20


def params(**more):
    return pltpu.CompilerParams(vmem_limit_bytes=VMEM_LIMIT, **more)


def dot_last(left, right):
    return lax.dot_general(left, right, (((1,), (1,)), ((), ())), preferred_element_type=F32)


def dot_first(left, right):
    return lax.dot_general(left, right, (((0,), (0,)), ((), ())), preferred_element_type=F32)


def dot_plain(left, right):
    return jnp.dot(left, right, preferred_element_type=F32)


def swap_core(piece):
    return lax.ppermute(piece, "batch", [(i, i ^ 1) for i in range(4)])


def swap_y(piece):
    return lax.ppermute(piece, "batch", [(i, i ^ 2) for i in range(4)])


LOOP = (0, 2, 4, 6, 7, 5, 3, 1)


def ring_up(piece):
    return lax.ppermute(piece, "blk", [(LOOP[i], LOOP[(i + 1) % 8]) for i in range(8)])


def ring_down(piece):
    return lax.ppermute(piece, "blk", [(LOOP[(i + 1) % 8], LOOP[i]) for i in range(8)])


def sum_everywhere(values):
    values = values + swap_core(values)
    values = values + swap_y(values)
    for bit in (1, 2, 4):
        values = values + lax.ppermute(values, "blk", [(i, i ^ bit) for i in range(8)])
    return values


def after(values, earlier):
    return lax.optimization_barrier((values, earlier))[0]


def ring_place(blk):
    return jnp.where(blk % 2 == 0, blk // 2, 7 - blk // 2)


def ring_owner(place):
    place = place % 8
    return jnp.where(place < 4, 2 * place, 2 * (7 - place) + 1)


def put(whole, piece, index, axis):
    return lax.dynamic_update_slice_in_dim(whole, jnp.expand_dims(piece, axis), index, axis)


def batch_pieces(piece):
    far = swap_y(piece)
    return (piece, swap_core(piece), far, swap_core(far))


def batch_gather(piece, me, axis):
    pieces = batch_pieces(piece)
    shape = piece.shape[:axis] + (4,) + piece.shape[axis:]
    whole = jnp.zeros(shape, piece.dtype)
    for other in range(4):
        whole = put(whole, pieces[other], me ^ other, axis)
    return whole


def batch_scatter(partial, me, axis):
    shape = partial.shape
    split = partial.reshape(shape[:axis] + (2, 2) + shape[axis + 1 :])
    y, core = me // 2, me % 2

    def pick(array, index, at):
        return lax.dynamic_index_in_dim(array, index, at, keepdims=False)

    near = pick(split, core, axis + 1).astype(F32) + swap_core(pick(split, 1 - core, axis + 1)).astype(F32)
    far = swap_y(pick(near, 1 - y, axis).astype(BF))
    return pick(near, y, axis) + far.astype(F32)


def ring_gather(shard, blk, axis, waits=()):
    half = shard.shape[axis] // 2
    place = ring_place(blk)
    shape = shard.shape[:axis] + (8,) + shard.shape[axis:]
    whole = put(jnp.zeros(shape, shard.dtype), shard, blk, axis)
    up = lax.slice_in_dim(shard, 0, half, axis=axis)
    down = lax.slice_in_dim(shard, half, 2 * half, axis=axis)

    def store(whole, piece, owner, begin):
        starts = [0] * len(shape)
        starts[axis] = owner
        starts[axis + 1] = begin
        return lax.dynamic_update_slice(whole, jnp.expand_dims(piece, axis), starts)

    for step in range(1, 8):
        for at, arrays in waits:
            if at == step:
                up, down = after((up, down), arrays)
        up, down = ring_up(up), ring_down(down)
        whole = store(whole, up, ring_owner(place - step), 0)
        whole = store(whole, down, ring_owner(place + step), half)
    return whole


def ring_scatter(part_of, blk):
    place = ring_place(blk)
    up, down = part_of(ring_owner(place - 1), 0), part_of(ring_owner(place + 1), 1)
    states = []
    for step in range(1, 8):
        up, down = ring_up(up.astype(BF)), ring_down(down.astype(BF))
        up = (up.astype(F32) + part_of(ring_owner(place - 1 - step), 0).astype(F32)).astype(BF)
        down = (down.astype(F32) + part_of(ring_owner(place + 1 + step), 1).astype(F32)).astype(BF)
        states.append((up, down))
    return states


def swap_blk(piece, bit):
    return lax.ppermute(piece, "blk", [(i, i ^ bit) for i in range(8)])


def choose(flag, zero, one):
    return jnp.where(flag == 0, zero, one)


def to_batch(tokens, me):
    rows, count, width = tokens.shape
    pieces = tokens.reshape(rows, 4, count // 4, width)
    whole = jnp.zeros((4, rows, count // 4, width), tokens.dtype)
    for other in range(4):
        piece = lax.dynamic_index_in_dim(pieces, me ^ other, 1, keepdims=False)
        if other:
            piece = lax.ppermute(piece, "batch", [(i, i ^ other) for i in range(4)])
        whole = put(whole, piece, me ^ other, 0)
    return whole.reshape(8, count // 4, width)


def to_rows(pieces):
    return lax.all_to_all(pieces, "blk", 0, 0, tiled=True)


def from_rows(tokens, me):
    count, width = tokens.shape[1:]
    pieces = lax.all_to_all(tokens, "blk", 0, 0, tiled=True).reshape(4, 2, count, width)
    whole = jnp.zeros((2, 4, count, width), tokens.dtype)
    for other in range(4):
        piece = lax.dynamic_index_in_dim(pieces, me ^ other, 0, keepdims=False)
        if other:
            piece = lax.ppermute(piece, "batch", [(i, i ^ other) for i in range(4)])
        whole = put(whole, piece, me ^ other, 1)
    return whole.reshape(2, 4 * count, width)


def attention_pieces(me):
    pieces = []
    for matrix in range(4):
        for j in range(HEADS):
            block = HEADS * me + j
            pieces.append((3 * matrix + block // 4, block % 4, HEADS * matrix + j))
    return pieces


def pick_kernel(place_ref, me_ref, own, core, far, far_core, attn_ref, ffn_ref, sems):
    me = me_ref[0]
    waits = []

    def begin(unit, source, target, sem):
        at = place_ref[unit]
        for other, ref in enumerate((own, core, far, far_core)):

            @pl.when(at // 9 == other)
            def start():
                pltpu.make_async_copy(source(ref.at[at % 9]), target, sem).start()

        waits.append(pltpu.make_async_copy(source(own.at[0]), target, sem))

    for i, (unit, block, packed) in enumerate(attention_pieces(me)):
        column = pl.multiple_of(block * 128, 128)
        begin(unit, lambda r, c=column: r.at[:, pl.ds(c, 128)], attn_ref.at[:, pl.ds(packed * 128, 128)], sems.at[i])
    for i in range(6):
        unit = 12 + 8 * (i // 2) + 2 * me + i % 2
        begin(unit, lambda r: r, ffn_ref.at[:, pl.ds(i * UW, UW)], sems.at[12 + i])
    for wait in waits:
        wait.wait()


def pick_units(place, me, pieces):
    rows = pieces[0].shape[1]
    hbm = pl.BlockSpec(memory_space=pl.ANY)
    smem = pl.BlockSpec(memory_space=pltpu.SMEM)
    vmem = pl.BlockSpec(memory_space=pltpu.VMEM)
    return pl.pallas_call(
        pick_kernel,
        in_specs=[smem, smem, hbm, hbm, hbm, hbm],
        out_specs=[vmem, vmem],
        out_shape=[
            jax.ShapeDtypeStruct((rows, 4 * QW), BF),
            jax.ShapeDtypeStruct((rows, 6 * UW), BF),
        ],
        scratch_shapes=[pltpu.SemaphoreType.DMA((18,))],
        compiler_params=params(),
        name="pick_units",
    )(place, me.reshape(1), *pieces)


def place_kernel(unit_ref, me_ref, *refs):
    attn, ffn, out_ref, sems = refs[:4], refs[4:8], refs[8], refs[9]
    me = me_ref[0]
    waits = []
    for i in range(9):
        unit = unit_ref[i]
        of_attn = unit < 12
        f = jnp.maximum(unit - 12, 0)
        for q in range(4):
            block = (unit % 3) * 4 + q
            source = jnp.where(of_attn, block // HEADS, (f % 8) // 2) ^ me
            column = jnp.where(
                of_attn, (unit // 3) * QW + (block % HEADS) * 128, (f // 8) * FQ + (f % 2) * UW + q * 128
            )
            column = pl.multiple_of(column, 128)
            target, sem = out_ref.at[i, :, pl.ds(q * 128, 128)], sems.at[i, q]
            for other in range(4):
                for mine, pieces in ((of_attn, attn), (jnp.logical_not(of_attn), ffn)):

                    @pl.when(mine & (source == other))
                    def start(ref=pieces[other], column=column, target=target, sem=sem):
                        pltpu.make_async_copy(ref.at[:, pl.ds(column, 128)], target, sem).start()

            waits.append(pltpu.make_async_copy(attn[0].at[:, pl.ds(0, 128)], target, sem))
    for wait in waits:
        wait.wait()


def place_units(units, me, attn_pieces, ffn_pieces):
    rows = attn_pieces[0].shape[0]
    hbm = pl.BlockSpec(memory_space=pl.ANY)
    smem = pl.BlockSpec(memory_space=pltpu.SMEM)
    return pl.pallas_call(
        place_kernel,
        in_specs=[smem, smem] + [hbm] * 8,
        out_specs=pl.BlockSpec(memory_space=pltpu.VMEM),
        out_shape=jax.ShapeDtypeStruct((9, rows, UW), BF),
        scratch_shapes=[pltpu.SemaphoreType.DMA((9, 4))],
        compiler_params=params(),
        name="place_units",
    )(units, me.reshape(1), *attn_pieces, *ffn_pieces)


def turn(values, cosine, sine, lane):
    partner = jnp.where(lane % HD < HD // 2, pltpu.roll(values, 96, 1), pltpu.roll(values, 32, 1))
    return values * cosine + partner * sine


def project_kernel(x_ref, w_ref, gain_ref, cos_ref, sin_ref, n_ref, q_ref, k_ref, v_ref):
    x = x_ref[...].astype(F32)
    r = lax.rsqrt(jnp.mean(x * x, axis=-1, keepdims=True) + norm_epsilon)
    n = (x * r * gain_ref[...]).astype(BF)
    n_ref[...] = n
    lane = lax.broadcasted_iota(jnp.int32, (x.shape[0], VD), 1)
    cosine, sine = cos_ref[...], sin_ref[...]
    out = dot_plain(n, w_ref[...])
    for h in range(HEADS):
        at = slice(h * VD, (h + 1) * VD)
        q = turn(out[:, h * VD : (h + 1) * VD], cosine, sine, lane)
        q_ref[:, at] = (q.astype(BF).astype(F32) * HD**-0.5).astype(BF)
        k = turn(out[:, QW + h * VD : QW + (h + 1) * VD], cosine, sine, lane)
        k_ref[:, at] = k.astype(BF)
    v_ref[...] = out[:, 2 * QW :].astype(BF)


def project(x, weights, gain, cosine, sine):
    count = x.shape[0]
    rows = lambda w: pl.BlockSpec((TILE, w), lambda i: (i, 0))
    fixed = lambda h, w: pl.BlockSpec((h, w), lambda i: (0, 0), pipeline_mode=pl.Buffered(1))
    narrow = jax.ShapeDtypeStruct((count, QW), BF)
    return pl.pallas_call(
        project_kernel,
        grid=(count // TILE,),
        in_specs=[rows(D), fixed(D, 3 * QW), fixed(1, D), rows(VD), rows(VD)],
        out_specs=[rows(D), rows(QW), rows(QW), rows(QW)],
        out_shape=[jax.ShapeDtypeStruct((count, D), BF), narrow, narrow, narrow],
        compiler_params=params(),
        cost_estimate=pl.CostEstimate(
            flops=2 * count * D * 3 * QW, bytes_accessed=count * D * 6 + 6 * D * QW, transcendentals=0
        ),
        name="project",
    )(x, weights, gain, cosine, sine)


def split_halves(q):
    lane = lax.broadcasted_iota(jnp.int32, q.shape, 1)
    zero = jnp.zeros_like(q)
    return jnp.concatenate([jnp.where(lane < HD, q, zero), jnp.where(lane >= HD, q, zero)], axis=0)


def block_mask(j, i, start):
    key = j * TILE + lax.broadcasted_iota(jnp.int32, (TILE, 2 * TILE), 0)
    query = i * TILE + lax.broadcasted_iota(jnp.int32, (TILE, TILE), 1)
    query = jnp.concatenate([query, query], axis=1)
    return (key >= start) & (key <= query)


def attend_kernel(low_ref, lam_ref, q_ref, k_ref, v_ref, start_ref, gain_ref, a_ref, maps_ref, log_ref, vt_ref):
    i = pl.program_id(1)

    @pl.when(i == 0)
    def turn_values():
        for j in range(vt_ref.shape[0]):
            vt_ref[j] = v_ref[j * TILE : (j + 1) * TILE, :].astype(F32).T.astype(BF)

    q = split_halves(q_ref[...])
    start = jnp.concatenate([start_ref[...], start_ref[...]], axis=1)

    def step(j, carry):
        top, mass, total = carry
        keys = k_ref[pl.ds(pl.multiple_of(j * TILE, TILE), TILE), :]
        scores = jnp.where(block_mask(j, i, start), dot_last(keys, q), masked_fill)
        new = jnp.maximum(top, jnp.max(scores, axis=0, keepdims=True))
        shares = jnp.exp(scores - new)
        keep = jnp.exp(top - new)
        mass = mass * keep + jnp.sum(shares, axis=0, keepdims=True)
        total = total * keep + dot_plain(vt_ref[j], shares.astype(BF))
        return new, mass, total

    first = (
        jnp.full((1, 2 * TILE), masked_fill, F32),
        jnp.zeros((1, 2 * TILE), F32),
        jnp.zeros((VD, 2 * TILE), F32),
    )
    top, mass, total = lax.fori_loop(low_ref[i], i + 1, step, first)
    maps = total / mass
    one, two = maps[:, :TILE], maps[:, TILE:]
    maps_ref[0, 0] = one
    maps_ref[0, 1] = two
    log_ref[0, 0] = top + jnp.log(mass)
    mixed = one - lam_ref[0] * two
    r = lax.rsqrt(jnp.mean(mixed * mixed, axis=0, keepdims=True) + norm_epsilon)
    a_ref[...] = (mixed * r * gain_ref[...] * (1.0 - lambda_start)).T.astype(BF)


def attend(low, lam, q, k, v, start, gain):
    count = q.shape[0]
    blocks = count // TILE
    smem = pl.BlockSpec(memory_space=pltpu.SMEM)
    return pl.pallas_call(
        attend_kernel,
        grid=(HEADS, blocks),
        in_specs=[
            smem,
            smem,
            pl.BlockSpec((TILE, VD), lambda h, i: (i, h)),
            pl.BlockSpec((count, VD), lambda h, i: (0, h)),
            pl.BlockSpec((count, VD), lambda h, i: (0, h)),
            pl.BlockSpec((1, TILE), lambda h, i: (0, i)),
            pl.BlockSpec((VD, 1), lambda h, i: (0, 0)),
        ],
        out_specs=[
            pl.BlockSpec((TILE, VD), lambda h, i: (i, h)),
            pl.BlockSpec((1, 2, VD, TILE), lambda h, i: (h, 0, 0, i)),
            pl.BlockSpec((1, 1, 1, 2 * TILE), lambda h, i: (h, i, 0, 0)),
        ],
        out_shape=[
            jax.ShapeDtypeStruct((count, QW), BF),
            jax.ShapeDtypeStruct((HEADS, 2, VD, count), F32),
            jax.ShapeDtypeStruct((HEADS, blocks, 1, 2 * TILE), F32),
        ],
        scratch_shapes=[pltpu.VMEM((blocks, VD, TILE), BF)],
        compiler_params=params(),
        cost_estimate=pl.CostEstimate(
            flops=8 * count * count * VD * HEADS, bytes_accessed=count * QW * 16, transcendentals=count * count * HEADS
        ),
        name="attend",
    )(low, lam, q, k, v, start, gain)


def attend_back_kernel(
    low_ref, lam_ref, q_ref, k_ref, v_ref, start_ref, gain_ref, maps_ref, log_ref, da_ref, cosq_ref, sinq_ref,
    cosk_ref, sink_ref, dq_ref, dk_ref, dv_ref, dgain_ref, dlam_ref, kt_ref, dk_sum, dv_sum, dq_sum,
):
    i = pl.program_id(1)
    blocks = kt_ref.shape[0]

    @pl.when(i == 0)
    def begin():
        for j in range(blocks):
            kt_ref[j] = k_ref[j * TILE : (j + 1) * TILE, :].astype(F32).T.astype(BF)
        dk_sum[...] = jnp.zeros_like(dk_sum)
        dv_sum[...] = jnp.zeros_like(dv_sum)
        dgain_ref[...] = jnp.zeros_like(dgain_ref)
        dlam_ref[...] = jnp.zeros_like(dlam_ref)

    lam = lam_ref[0]
    q = split_halves(q_ref[...])
    start = jnp.concatenate([start_ref[...], start_ref[...]], axis=1)
    log_mass = log_ref[0, 0]
    one, two = maps_ref[0, 0], maps_ref[0, 1]
    mixed = one - lam * two
    r = lax.rsqrt(jnp.mean(mixed * mixed, axis=0, keepdims=True) + norm_epsilon)
    t = mixed * r
    da = da_ref[...].T * (1.0 - lambda_start)
    dgain_ref[0] += da * t
    e = da * gain_ref[...]
    dmixed = r * (e - t * jnp.mean(e * t, axis=0, keepdims=True))
    dlam_ref[0] -= jnp.sum(dmixed * two, axis=0, keepdims=True)
    dmaps = jnp.concatenate([dmixed, -lam * dmixed], axis=1).astype(BF)
    maps = jnp.concatenate([one, two], axis=1)
    offset = jnp.sum(dmaps.astype(F32) * maps, axis=0, keepdims=True)
    dq_sum[...] = jnp.zeros_like(dq_sum)

    def step(j, carry):
        at = pl.ds(pl.multiple_of(j * TILE, TILE), TILE)
        keys, values = k_ref[at, :], v_ref[at, :]
        scores = dot_last(keys, q)
        shares = jnp.where(block_mask(j, i, start), jnp.exp(scores - log_mass), 0.0)
        dshares = dot_plain(values, dmaps)
        dscores = (shares * (dshares - offset)).astype(BF)
        dv_sum[at, :] += dot_last(shares.astype(BF), dmaps)
        dk_sum[at, :] += dot_plain(dscores, q)
        dq_sum[...] += dot_plain(kt_ref[j], dscores)
        return carry

    lax.fori_loop(low_ref[i], i + 1, step, 0)
    lane = lax.broadcasted_iota(jnp.int32, (TILE, VD), 1)
    dq = jnp.concatenate([dq_sum[:HD, :TILE], dq_sum[HD:, TILE:]], axis=0).T * HD**-0.5
    dq_ref[...] = turn(dq, cosq_ref[...], -sinq_ref[...], lane).astype(BF)

    @pl.when(i == blocks - 1)
    def finish():
        for j in range(blocks):
            at = slice(j * TILE, (j + 1) * TILE)
            dk_ref[at, :] = turn(dk_sum[at, :], cosk_ref[at, :], -sink_ref[at, :], lane).astype(BF)
        dv_ref[...] = dv_sum[...].astype(BF)


def attend_back(low, lam, q, k, v, start, gain, maps, log_mass, da, cosine, sine):
    count = q.shape[0]
    blocks = count // TILE
    smem = pl.BlockSpec(memory_space=pltpu.SMEM)
    tile = pl.BlockSpec((TILE, VD), lambda h, i: (i, h))
    whole = pl.BlockSpec((count, VD), lambda h, i: (0, h))
    table = pl.BlockSpec((TILE, VD), lambda h, i: (i, 0))
    full_table = pl.BlockSpec((count, VD), lambda h, i: (0, 0), pipeline_mode=pl.Buffered(1))
    narrow = jax.ShapeDtypeStruct((count, QW), BF)
    return pl.pallas_call(
        attend_back_kernel,
        grid=(HEADS, blocks),
        in_specs=[
            smem,
            smem,
            tile,
            whole,
            whole,
            pl.BlockSpec((1, TILE), lambda h, i: (0, i)),
            pl.BlockSpec((VD, 1), lambda h, i: (0, 0)),
            pl.BlockSpec((1, 2, VD, TILE), lambda h, i: (h, 0, 0, i)),
            pl.BlockSpec((1, 1, 1, 2 * TILE), lambda h, i: (h, i, 0, 0)),
            tile,
            table,
            table,
            full_table,
            full_table,
        ],
        out_specs=[
            tile,
            whole,
            whole,
            pl.BlockSpec((1, VD, TILE), lambda h, i: (h, 0, 0)),
            pl.BlockSpec((1, 1, TILE), lambda h, i: (h, 0, 0)),
        ],
        out_shape=[
            narrow,
            narrow,
            narrow,
            jax.ShapeDtypeStruct((HEADS, VD, TILE), F32),
            jax.ShapeDtypeStruct((HEADS, 1, TILE), F32),
        ],
        scratch_shapes=[
            pltpu.VMEM((blocks, VD, TILE), BF),
            pltpu.VMEM((count, VD), F32),
            pltpu.VMEM((count, VD), F32),
            pltpu.VMEM((VD, 2 * TILE), F32),
        ],
        compiler_params=params(),
        cost_estimate=pl.CostEstimate(
            flops=20 * count * count * VD * HEADS, bytes_accessed=count * QW * 24, transcendentals=count * count * HEADS
        ),
        name="attend_back",
    )(low, lam, q, k, v, start, gain, maps, log_mass, da, cosine, sine, cosine, sine)


def middle_kernel(me_ref, x_ref, gain_ref, *refs):
    a_refs, w_refs, (n_ref, own_ref, sum_ref) = refs[:4], refs[4:8], refs[8:]
    x1 = x_ref[...].astype(F32)
    for a_ref, w_ref in zip(a_refs, w_refs):
        x1 += dot_last(a_ref[...], w_ref[...])
    sum_ref[...] = x1
    r = lax.rsqrt(jnp.mean(x1 * x1, axis=-1, keepdims=True) + norm_epsilon)
    n_ref[...] = (x1 * r * gain_ref[...]).astype(BF)
    part = TILE // 4
    own_ref[0] = sum_ref[pl.ds(pl.multiple_of(me_ref[0] * part, part), part), :]


def middle(me, a, x, weights, gain):
    count = x.shape[0]
    rows = pl.BlockSpec((TILE, D), lambda i: (i, 0))
    return pl.pallas_call(
        middle_kernel,
        grid=(count // TILE,),
        in_specs=[
            pl.BlockSpec(memory_space=pltpu.SMEM),
            rows,
            pl.BlockSpec((1, D), lambda i: (0, 0)),
        ]
        + [pl.BlockSpec((TILE, QW), lambda i: (i, 0))] * 4
        + [pl.BlockSpec((D, QW), lambda i: (0, 0), pipeline_mode=pl.Buffered(1))] * 4,
        out_specs=[rows, pl.BlockSpec((1, TILE // 4, D), lambda i: (i, 0, 0))],
        out_shape=[
            jax.ShapeDtypeStruct((count, D), BF),
            jax.ShapeDtypeStruct((count // TILE, TILE // 4, D), F32),
        ],
        scratch_shapes=[pltpu.VMEM((TILE, D), F32)],
        compiler_params=params(),
        cost_estimate=pl.CostEstimate(
            flops=2 * count * D * D, bytes_accessed=count * D * 7 + 2 * D * D, transcendentals=0
        ),
        name="middle",
    )(me.reshape(1), x, gain, *a, *weights)


MESH = pl.DeviceIdType.MESH


def greet(devices):
    barrier = pltpu.get_barrier_semaphore()
    for device in devices:
        pl.semaphore_signal(barrier, inc=1, device_id=device, device_id_type=MESH)
    pl.semaphore_wait(barrier, len(devices))


def remote(source, target, sems, at, device):
    return pltpu.make_async_remote_copy(
        src_ref=source,
        dst_ref=target,
        send_sem=sems.at[0, at],
        recv_sem=sems.at[1, at],
        device_id=device,
        device_id_type=MESH,
    )


def feed_kernel(
    n_ref, dy_ref, w_ref, x1_ref, dyo_ref, wo_ref, gain_ref, act_ref, out_ref, dx_ref, low_ref, da_ref, dgain_ref,
    part, near_in, near, far_in, gathered, s_near, s_far, s_y, s_core, s_relay,
):
    i = pl.program_id(0)
    me = lax.axis_index("batch")
    y, core = me // 2, me % 2
    to_core = {"batch": y * 2 + 1 - core}
    to_y = {"batch": (1 - y) * 2 + core}
    blocks = part.shape[0]

    def near_copy(b):
        return remote(part.at[b, :, 1 - core], near_in.at[b], s_near, b, to_core)

    def far_copy(b):
        return remote(near.at[b], far_in.at[b], s_far, b, to_y)

    def own_copy(b, sems, device):
        return remote(gathered.at[b, me], gathered.at[b, me], sems, b, device)

    def relay_copy(b):
        slab = (1 - y) * 2 + core
        return remote(gathered.at[b, slab], gathered.at[b, slab], s_relay, b, to_core)

    @pl.when(i == 0)
    def begin():
        greet((to_core, to_y))
        dgain_ref[...] = jnp.zeros_like(dgain_ref)

    @pl.when((i >= 1) & (i < blocks + 1))
    def send_far():
        b = i - 1
        near_copy(b).wait_recv()
        both = part[b, 1 - y, core].astype(F32) + near_in[b, 1 - y].astype(F32)
        near[b] = both.astype(BF)
        far_copy(b).start()

    @pl.when((i >= 2) & (i < blocks + 2))
    def send_own():
        b = i - 2
        far_copy(b).wait_recv()
        dn = part[b, y, core].astype(F32) + near_in[b, y].astype(F32) + far_in[b].astype(F32)
        x1 = x1_ref[0]
        r = lax.rsqrt(jnp.mean(x1 * x1, axis=-1, keepdims=True) + norm_epsilon)
        t = x1 * r
        e = dn * gain_ref[...]
        dx = dyo_ref[0].astype(F32) + r * (e - t * jnp.mean(e * t, axis=-1, keepdims=True))
        dgain_ref[...] += jnp.sum(dn * t, axis=0, keepdims=True)
        dx_ref[0] = dx
        gathered[b, me] = dx.astype(BF)
        own_copy(b, s_y, to_y).start()
        own_copy(b, s_core, to_core).start()

    @pl.when((i >= 3) & (i < blocks + 3))
    def send_relay():
        b = i - 3
        own_copy(b, s_y, to_y).wait_recv()
        relay_copy(b).start()

    @pl.when(i >= 4)
    def use():
        b = i - 4
        own_copy(b, s_core, to_core).wait_recv()
        relay_copy(b).wait_recv()
        whole = jnp.concatenate([gathered[b, other] for other in range(4)], axis=0)
        low_ref[...] = whole
        da_ref[...] = dot_plain(whole, wo_ref[...])

    @pl.when(i < blocks)
    def compute():
        n, dy = n_ref[...], dy_ref[...]
        wg, wu, wd = w_ref[:, :FQ], w_ref[:, FQ : 2 * FQ], w_ref[:, 2 * FQ :]
        gate = dot_plain(n, wg)
        up = dot_plain(n, wu)
        dhidden = dot_plain(dy, wd)
        share = 1.0 / (1.0 + jnp.exp(-gate))
        silu = gate * share
        hidden = (silu * up).astype(BF)
        dup = (dhidden * silu).astype(BF)
        dgate = (dhidden * up * (share * (1.0 + gate * (1.0 - share)))).astype(BF)
        act_ref[:, :FQ] = dgate
        act_ref[:, FQ : 2 * FQ] = dup
        act_ref[:, 2 * FQ :] = hidden
        dn = (dot_last(dgate, wg) + dot_last(dup, wu)).astype(BF)
        size = dn.shape[0] // 4
        for other in range(4):
            part[i, other // 2, other % 2] = dn[other * size : (other + 1) * size]
        near_copy(i).start()
        out_ref[...] = dot_last(hidden, wd).astype(BF)

    @pl.when(i == blocks + 3)
    def finish():
        for b in range(blocks):
            near_copy(b).wait_send()
            far_copy(b).wait_send()
            own_copy(b, s_y, to_y).wait_send()
            own_copy(b, s_core, to_core).wait_send()
            relay_copy(b).wait_send()


def feed(n, dy, weights, x1, dy_own, attn, gain):
    count = n.shape[0]
    blocks = count // TILE
    size = TILE // 4
    late = lambda lag: lambda i: (jnp.clip(i - lag, 0, blocks - 1), 0)
    late3 = lambda lag: lambda i: (jnp.clip(i - lag, 0, blocks - 1), 0, 0)
    rows = lambda w, lag: pl.BlockSpec((TILE, w), late(lag))
    own = pl.BlockSpec((1, size, D), late3(2))
    shape = lambda w, kind=BF: jax.ShapeDtypeStruct((count, w), kind)
    sems = pltpu.SemaphoreType.DMA((2, blocks))
    return pl.pallas_call(
        feed_kernel,
        grid=(blocks + 4,),
        in_specs=[
            rows(D, 0),
            rows(D, 0),
            pl.BlockSpec((D, 3 * FQ), lambda i: (0, 0), pipeline_mode=pl.Buffered(1)),
            own,
            own,
            pl.BlockSpec((D, QW), lambda i: (0, 3), pipeline_mode=pl.Buffered(1)),
            pl.BlockSpec((1, D), lambda i: (0, 0)),
        ],
        out_specs=[
            rows(3 * FQ, 0),
            rows(D, 0),
            own,
            rows(D, 4),
            rows(QW, 4),
            pl.BlockSpec((1, D), lambda i: (0, 0)),
        ],
        out_shape=[
            shape(3 * FQ),
            shape(D),
            jax.ShapeDtypeStruct((blocks, size, D), F32),
            shape(D),
            shape(QW, F32),
            jax.ShapeDtypeStruct((1, D), F32),
        ],
        scratch_shapes=[
            pltpu.VMEM((blocks, 2, 2, size, D), BF),
            pltpu.VMEM((blocks, 2, size, D), BF),
            pltpu.VMEM((blocks, size, D), BF),
            pltpu.VMEM((blocks, size, D), BF),
            pltpu.VMEM((blocks, 4, size, D), BF),
            sems,
            sems,
            sems,
            sems,
            sems,
        ],
        compiler_params=params(collective_id=1, has_side_effects=True),
        cost_estimate=pl.CostEstimate(
            flops=12 * count * D * FQ, bytes_accessed=count * (8 * D + 6 * FQ) + 6 * D * FQ, transcendentals=count * FQ
        ),
        name="feed",
    )(n, dy, weights, x1, dy_own, attn, gain)


def rotate_kernel(
    g_ref, base_ref, other_ref, first_ref, second_ref, master_ref, scale_ref, new_first_ref, new_second_ref,
    new_master_ref, g, base, other, firsts, seconds, masters, g_in, part, x_in, near, z_in, far, p_in, step, steps,
    back, back_in, steps_own, load, store, s_g, s_x, s_z, s_p, s_step, s_back, s_up, s_side,
):
    blk = lax.axis_index("blk")
    zh, zl, xx = blk // 4, (blk // 2) % 2, blk % 2
    to_x = {"blk": blk + 1 - 2 * xx}
    to_z = {"blk": blk + 4 - 8 * zh}
    to_pair = {"blk": blk + 2 - 4 * zl}
    count = g.shape[0]
    half = UW // 2
    own = pl.ds(pl.multiple_of(zl * half, half), half)
    away = pl.ds(pl.multiple_of((1 - zl) * half, half), half)
    block = 4 * zh + xx
    loads = [
        (g_ref, g), (base_ref, base), (other_ref, other), (first_ref, firsts), (second_ref, seconds), (master_ref, masters),
    ]
    stores = [(firsts, new_first_ref), (seconds, new_second_ref), (masters, new_master_ref)]

    def loading(i, s):
        return pltpu.make_async_copy(loads[i][0].at[s], loads[i][1].at[s], load.at[i, s])

    def storing(i, s):
        return pltpu.make_async_copy(stores[i][0].at[s], stores[i][1].at[s], store.at[i, s])

    def send_g(s):
        return remote(g.at[s, :, away], g_in.at[s], s_g, s, to_pair)

    def send_x(s):
        return remote(part.at[s % 3, :, 1 - xx], x_in.at[s], s_x, s, to_x)

    def send_z(s):
        return remote(near.at[s % 3, 1 - zh], z_in.at[s], s_z, s, to_z)

    def send_p(s):
        return remote(far.at[s % 3], p_in.at[s], s_p, s, to_pair)

    def step_pair(s):
        return remote(step.at[s, :, away], steps.at[s, block + 2 * zl], s_step, s, to_pair)

    def step_z(s, a):
        return remote(steps.at[s, block + 2 * a], steps.at[s, block + 2 * a], s_up, 2 * s + a, to_z)

    def step_x(s, a):
        at = 2 * a + xx
        return remote(steps.at[s, at], steps.at[s, at], s_side, 4 * s + a, to_x)

    def send_back(s):
        return remote(back.at[s % 3], back_in.at[s], s_back, s, to_pair)

    for i in range(len(loads)):
        for s in range(count):
            loading(i, s).start()
    greet((to_x, to_z, to_pair))
    for s in range(count):
        loading(0, s).wait()
        send_g(s).start()

    rows = base.shape[1]

    def tick(t, carry):
        def stage(lag, act):
            @pl.when((t >= lag) & (t < count + lag))
            def run():
                act(t - lag)

        def finish(s):
            send_back(s).wait_recv()
            loading(5, s).wait()
            for at, update in ((own, steps_own[s % 2]), (away, back_in[s].astype(F32))):
                value = masters[s, :, at]
                masters[s, :, at] = value - scale_ref[0] * (update + weight_decay * value)
            storing(2, s).start()

        def update(s):
            for a in range(4):
                step_x(s, a).wait_recv()
            whole = jnp.concatenate([steps[s, b] for b in range(8)], axis=0)
            steps_own[s % 2] = dot_plain(base[s], whole)

            @pl.when(s >= 3)
            def reuse():
                send_back(s - 3).wait_send()

            back[s % 3] = dot_plain(other[s], whole).astype(BF)
            send_back(s).start()

        def relay_x(s):
            for a in range(2):
                step_z(s, a).wait_recv()
            for a in range(4):
                step_x(s, a).start()

        def relay_z(s):
            step_pair(s).wait_recv()
            for a in range(2):
                step_z(s, a).start()

        def adam(s):
            send_p(s).wait_recv()
            loading(3, s).wait()
            loading(4, s).wait()
            mine = near[s % 3, zh, zl].astype(F32) + z_in[s, zl].astype(F32)
            for at, turned in ((own, mine), (away, p_in[s].astype(F32))):
                new_first = beta_one * firsts[s, :, at] + (1.0 - beta_one) * turned
                new_second = beta_two * seconds[s, :, at] + (1.0 - beta_two) * turned * turned
                firsts[s, :, at] = new_first
                seconds[s, :, at] = new_second
                moved = new_first / scale_ref[1] / (jnp.sqrt(new_second / scale_ref[2]) + adam_epsilon)
                step[s, :, at] = moved.astype(BF)
            storing(0, s).start()
            storing(1, s).start()
            steps[s, block + 2 * zl] = step[s, :, own]
            step_pair(s).start()

        def send_far(s):
            send_z(s).wait_recv()

            @pl.when(s >= 3)
            def reuse():
                send_p(s - 3).wait_send()

            far[s % 3] = (near[s % 3, zh, 1 - zl].astype(F32) + z_in[s, 1 - zl].astype(F32)).astype(BF)
            send_p(s).start()

        def send_near(s):
            send_x(s).wait_recv()

            @pl.when(s >= 3)
            def reuse():
                send_z(s - 3).wait_send()

            for a in range(2):
                for b in range(2):
                    at = 2 * a + b
                    total = part[s % 3, at, xx].astype(F32) + x_in[s, at].astype(F32)
                    near[s % 3, a, b] = total.astype(BF)
            send_z(s).start()

        def turn_slot(s):
            loading(1, s).wait()
            loading(2, s).wait()
            send_g(s).wait_recv()

            @pl.when(s >= 3)
            def reuse():
                send_x(s - 3).wait_send()

            turned = dot_first(base[s], g[s, :, own]) + dot_first(other[s], g_in[s])
            for b in range(8):
                part[s % 3, b // 2, b % 2] = turned[b * rows : (b + 1) * rows].astype(BF)
            send_x(s).start()

        stage(7, finish)
        stage(6, update)
        stage(5, relay_x)
        stage(4, relay_z)
        stage(3, adam)
        stage(2, send_far)
        stage(1, send_near)
        stage(0, turn_slot)
        return carry

    lax.fori_loop(0, count + 7, tick, 0)
    for s in range(count):
        send_g(s).wait_send()
        step_pair(s).wait_send()
        for a in range(2):
            step_z(s, a).wait_send()
        for a in range(4):
            step_x(s, a).wait_send()
        for i in range(3):
            storing(i, s).wait()
    for s in range(count - 3, count):
        send_x(s).wait_send()
        send_z(s).wait_send()
        send_p(s).wait_send()
        send_back(s).wait_send()


def rotate_slots(grads, base, other, first, second, master, scales):
    count, rows, width = grads.shape
    half = width // 2
    hbm = pl.BlockSpec(memory_space=pl.ANY)
    shape = jax.ShapeDtypeStruct(master.shape, F32)
    sems = lambda n: pltpu.SemaphoreType.DMA((2, n))
    return pl.pallas_call(
        rotate_kernel,
        in_specs=[hbm] * 6 + [pl.BlockSpec(memory_space=pltpu.SMEM)],
        out_specs=[hbm] * 3,
        out_shape=[shape] * 3,
        scratch_shapes=[
            pltpu.VMEM((count, rows, width), BF),
            pltpu.VMEM((count, rows, D), BF),
            pltpu.VMEM((count, rows, D), BF),
            pltpu.VMEM((count, rows, width), F32),
            pltpu.VMEM((count, rows, width), F32),
            pltpu.VMEM((count, rows, width), F32),
            pltpu.VMEM((count, rows, half), BF),
            pltpu.VMEM((3, 4, 2, rows, half), BF),
            pltpu.VMEM((count, 4, rows, half), BF),
            pltpu.VMEM((3, 2, 2, rows, half), BF),
            pltpu.VMEM((count, 2, rows, half), BF),
            pltpu.VMEM((3, rows, half), BF),
            pltpu.VMEM((count, rows, half), BF),
            pltpu.VMEM((count, rows, width), BF),
            pltpu.VMEM((count, 8, rows, half), BF),
            pltpu.VMEM((3, rows, half), BF),
            pltpu.VMEM((count, rows, half), BF),
            pltpu.VMEM((2, rows, half), F32),
            pltpu.SemaphoreType.DMA((6, count)),
            pltpu.SemaphoreType.DMA((3, count)),
            sems(count),
            sems(count),
            sems(count),
            sems(count),
            sems(count),
            sems(count),
            sems(2 * count),
            sems(4 * count),
        ],
        compiler_params=params(collective_id=2, has_side_effects=True),
        name="rotate_slots",
    )(grads, base, other, first, second, master, scales)


def row_tables(lengths, row, count):
    everyone = jnp.stack(batch_pieces(lengths))
    holder = (row // 2) ^ lax.axis_index("batch")
    mine = jnp.sum(jnp.where(jnp.arange(4)[:, None, None] == holder, everyone, 0), axis=0)
    mine = jnp.where(row % 2 == 0, mine[:1], mine[1:])
    ends = doc_ends(mine)[0]
    places = jnp.arange(count, dtype=jnp.int32)
    begin = jnp.sum(jnp.where(places[:, None] >= ends[None, :], mine, 0), axis=1)
    start = jnp.where(places >= ends[NDOC - 2], places, begin)
    low = start.reshape(-1, TILE)[:, 0] // TILE
    cosine, sine = turn_tables(places - begin)
    cosine = jnp.tile(cosine, (1, 4))
    sine = jnp.tile(jnp.concatenate([-sine, sine], axis=1), (1, 2))
    return start, low, cosine, sine


def row_groups(
    tokens,
    cotangent,
    lengths,
    unit_owner,
    step_count,
    master,
    first,
    second,
    bases,
    small,
    small_first,
    small_second,
):
    me, blk = lax.axis_index("batch"), lax.axis_index("blk")
    count = tokens.shape[1] * 8
    learn_rate = 2.0 / D**0.5
    slots = lambda array: jnp.transpose(array, (1, 0, 2))
    master_slots = slots(master)

    groups = (8, 4, count // 32, D)
    zh, zl, xx = blk // 4, (blk // 2) % 2, blk % 2

    x_parts = to_batch(tokens, me)
    place = ((unit_owner // 9) ^ me) * 9 + unit_owner % 9
    attn_shard, ffn_shard = pick_units(place, me, batch_pieces(master_slots.astype(BF)))
    x_own = to_rows(x_parts)
    start, low, cosine, sine = row_tables(lengths, blk, count)
    start = start.reshape(1, count)
    base = slots(bases).astype(BF)
    attn = ring_gather(attn_shard, blk, 0).reshape(D, 4 * QW)
    x = batch_gather(x_own, me, 1).reshape(count, D)
    dy_own = to_rows(after(to_batch(after(cotangent, attn_shard), me), attn))
    dy = batch_gather(dy_own, me, 1).reshape(count, D)
    attn_out = batch_pieces(attn[:, 3 * QW :])

    gain_one = small[:D].reshape(1, D)
    gain_two = small[D : 2 * D].reshape(1, D)
    head_gain = small[2 * D : 2 * D + VD].reshape(VD, 1)
    mixer, mixer_back = jax.vjp(mix_value, small[2 * D + VD :].reshape(4, HD))
    lam = mixer.reshape(1)

    n1, q, k, v = project(x, attn, gain_one, cosine, sine)
    a_own, maps, log_mass = attend(low, lam, q, k, v, start, head_gain)
    a = batch_pieces(a_own)
    ffn = lax.all_gather(ffn_shard, "blk", axis=0, tiled=True)
    base_other = swap_blk(after(base, attn), 2)
    n2, x1 = middle(me, a, x, attn_out, gain_two)
    acts, out_part, dx1, dx1_low, da, gain_two_grad = feed(n2, dy, ffn, x1, dy_own, attn, gain_two)
    gain_two_grad = gain_two_grad.reshape(D)

    part = D // 8

    def scatter_rows(grad):
        def part_of(owner, half):
            return lax.dynamic_slice_in_dim(grad, owner * part + half * part // 2, part // 2, axis=0)

        return ring_scatter(part_of, blk)

    ffn_grad = jnp.concatenate(
        [dot_first(n2, acts[:, : 2 * FQ]).astype(BF), dot_first(dy, acts[:, 2 * FQ :]).astype(BF)], axis=1
    )
    ffn_sums = lax.psum_scatter(ffn_grad, "blk", scatter_dimension=0, tiled=True)

    out_grad = dot_first(dx1_low, a_own).astype(BF)
    da, out_grad = after((da, out_grad), base_other)
    dq, dk, dv, head_gain_sums, mixer_sums = attend_back(
        low, lam, q, k, v, start, head_gain, maps, log_mass, da, cosine, sine
    )
    dqkv = jnp.concatenate([dq, dk, dv], axis=1)
    attn_states = scatter_rows(jnp.concatenate([dot_first(n1, dqkv).astype(BF), out_grad], axis=1))
    ffn_pieces = batch_pieces(ffn_sums)

    dn1_part = dot_last(after(dqkv, attn_states[0]), attn[:, : 3 * QW]).astype(BF)
    dn1 = batch_scatter(dn1_part.reshape(groups), me, 1)
    x_f = x_own.astype(F32)
    r1 = lax.rsqrt(jnp.mean(x_f * x_f, axis=-1, keepdims=True) + norm_epsilon)
    t1 = x_f * r1
    e1 = dn1 * gain_one
    dx = dx1 + r1 * (e1 - t1 * jnp.mean(e1 * t1, axis=-1, keepdims=True))
    gain_one_grad = jnp.sum(dn1 * t1, axis=(0, 1))
    input_grad = from_rows(dx.astype(BF), me)
    out = batch_scatter(out_part.reshape(groups), me, 1)
    block_out = from_rows((x1 + out).astype(BF), me)

    (mixers_grad,) = mixer_back(jnp.sum(mixer_sums))
    small_local = jnp.concatenate(
        [gain_one_grad, gain_two_grad, jnp.sum(head_gain_sums, axis=(0, 2)), mixers_grad.reshape(-1)]
    )
    small_grads = sum_everywhere(small_local)

    unit_of = inverse_order(unit_owner)
    units = lax.dynamic_slice_in_dim(unit_of, me * 9, 9)
    attn_pieces = batch_pieces(jnp.concatenate(attn_states[6], axis=0))
    grads = place_units(units, me, attn_pieces, ffn_pieces)

    steps_done = step_count[0].astype(F32)
    scales = jnp.stack([jnp.float32(learn_rate), 1.0 - beta_one**steps_done, 1.0 - beta_two**steps_done])
    new_first, new_second, new_master = rotate_slots(
        grads, base, base_other, slots(first), slots(second), master_slots, scales
    )
    new_small_first = beta_one * small_first + (1.0 - beta_one) * small_grads
    new_small_second = beta_two * small_second + (1.0 - beta_two) * small_grads * small_grads
    new_small = small - small_rate * adam_step(new_small_first, new_small_second, steps_done)
    return (
        block_out,
        input_grad,
        slots(new_master),
        slots(new_first),
        slots(new_second),
        small_grads,
        new_small,
        new_small_first,
        new_small_second,
    )


def solution(mesh):
    in_specs = (
        P("batch", "blk", None),
        P("batch", "blk", None),
        P("batch", None),
        P(),
        P(),
        P("blk", "batch", None),
        P("blk", "batch", None),
        P("blk", "batch", None),
        P("blk", "batch", None),
        P(),
        P(),
        P(),
    )
    out_specs = (
        P("batch", "blk", None),
        P("batch", "blk", None),
        P("blk", "batch", None),
        P("blk", "batch", None),
        P("blk", "batch", None),
        P(),
        P(),
        P(),
        P(),
    )
    by_rows = mesh.shape["blk"] == 8 and mesh.shape["batch"] == 4
    body = row_groups if by_rows else any_mesh
    return jax.shard_map(body, mesh=mesh, in_specs=in_specs, out_specs=out_specs, check_vma=False)
```

```python
import functools

import jax
import jax.numpy as jnp
from jax import lax
from jax.experimental import pallas as pl
from jax.experimental.pallas import tpu as pltpu
from jax.sharding import PartitionSpec as P

D = 1536
H = 12
HD = 64
VD = 128
FF = 4096
UW = 512
NDOC = 6
UNITS = 36


norm_epsilon = 1e-05
lambda_start = 0.2
rope_base = 10000.0
masked_fill = -1000000000.0
beta_one = 0.9
beta_two = 0.95
adam_epsilon = 1e-08
weight_decay = 0.01
small_rate = 1.0


def from_behind(shard, axis, by):
    count = lax.axis_size(axis)
    return lax.ppermute(shard, axis, [(i, (i + by) % count) for i in range(count)])


def root_norm(values, gain):
    return (
        values * lax.rsqrt(jnp.mean(values * values, axis=-1, keepdims=True) + norm_epsilon) * gain
    )


def mix_value(mixers):
    return (
        jnp.exp(jnp.sum(mixers[0] * mixers[1]))
        - jnp.exp(jnp.sum(mixers[2] * mixers[3]))
        + lambda_start
    )


def head_mix(maps_out, head_gain, mixer):
    combined = maps_out[:, :, 0] - mixer * maps_out[:, :, 1]
    normed = (
        combined
        * lax.rsqrt(jnp.mean(combined * combined, axis=-1, keepdims=True) + norm_epsilon)
        * head_gain
        * (1.0 - lambda_start)
    )
    rows_count, heads, positions, width = normed.shape
    return jnp.transpose(normed, (0, 2, 1, 3)).reshape(rows_count, positions, heads * width)


def gated_unit(gate, up):
    return jax.nn.silu(gate) * up


def doc_ends(lengths):
    count = lengths.shape[1]
    ends = [lengths[:, 0]]
    for j in range(1, count):
        ends.append(ends[-1] + lengths[:, j])
    return jnp.stack(ends, axis=1)


def document_places(lengths, places):
    ends = doc_ends(lengths)
    starts = ends - lengths
    segment = jnp.sum((places[None, :, None] >= ends[:, None, :]).astype(jnp.int32), axis=2)
    chosen = segment[:, :, None] == jnp.arange(lengths.shape[1], dtype=jnp.int32)[None, None, :]
    offset = jnp.sum(jnp.where(chosen, starts[:, None, :], 0), axis=2)
    return (segment, places[None, :] - offset)


def allowed(seg_query, place_query, seg_key, place_key, last):
    same = seg_query[:, :, None] == seg_key[:, None, :]
    causal = place_key[None, None, :] <= place_query[None, :, None]
    itself = place_key[None, None, :] == place_query[None, :, None]
    return same & causal & ((seg_query[:, :, None] < last) | itself)


def turn_tables(position):
    rates = rope_base ** (-2.0 * jnp.arange(HD // 2, dtype=jnp.float32) / HD)
    angle = position.astype(jnp.float32)[..., None] * rates
    return (jnp.cos(angle), jnp.sin(angle))


def rotate(values, cosine, sine):
    half = values.shape[-1] // 2
    front = values[..., :half]
    back = values[..., half:]
    return jnp.concatenate([front * cosine - back * sine, back * cosine + front * sine], axis=-1)


def adam_step(first_new, second_new, steps_done):
    return (
        first_new
        / (1.0 - beta_one**steps_done)
        / (jnp.sqrt(second_new / (1.0 - beta_two**steps_done)) + adam_epsilon)
    )


def take_units(stacked, order):
    parts = [lax.dynamic_slice_in_dim(stacked, order[i], 1, axis=1) for i in range(UNITS)]
    return jnp.concatenate(parts, axis=1)


def inverse_order(owner):
    numbers = jnp.arange(UNITS, dtype=jnp.int32)
    return jnp.sum(jnp.where(owner[None, :] == numbers[:, None], numbers[None, :], 0), axis=1)


def contract_rows(left, right):
    return lax.dot_general(
        left, right, (((1,), (1,)), ((), ())), preferred_element_type=jnp.float32
    )


def any_mesh(
    tokens,
    cotangent,
    lengths,
    unit_owner,
    step_count,
    master,
    first,
    second,
    bases,
    small,
    small_first,
    small_second,
):
    rows_count, seq_part, width = tokens.shape
    token_count = rows_count * seq_part
    axis_count = lax.axis_size("blk")
    axis_place = lax.axis_index("blk")
    rows_part = master.shape[0]
    scale = HD ** (-0.5)
    highest = lax.Precision.HIGHEST
    learn_rate = 2.0 / D**0.5
    every_slot = lax.all_gather(master.astype(jnp.bfloat16), "batch", axis=1, tiled=True)
    by_unit = take_units(every_slot, unit_owner).reshape(rows_part, UNITS * UW)
    attention_whole = lax.all_gather(by_unit[:, : 4 * D], "blk", axis=0, tiled=True)
    gate_whole = lax.all_gather(by_unit[:, 4 * D : 4 * D + 2 * FF], "blk", axis=0, tiled=True)
    down_whole = lax.all_gather(by_unit[:, 4 * D + 2 * FF :], "blk", axis=0, tiled=True)
    places = axis_place * seq_part + jnp.arange(seq_part, dtype=jnp.int32)
    segment, position = document_places(lengths, places)
    cosine, sine = turn_tables(position)
    cosine = cosine[:, :, None, None, :]
    sine = sine[:, :, None, None, :]
    residual = tokens.astype(jnp.float32)
    gain_one = small[:D]
    gain_two = small[D : 2 * D]
    head_gain = small[2 * D : 2 * D + VD]
    mixer, mixer_back = jax.vjp(mix_value, small[2 * D + VD :].reshape(4, HD))
    normed_exact, norm_one_back = jax.vjp(root_norm, residual, gain_one)
    normed_one = normed_exact.astype(jnp.bfloat16).reshape(token_count, D)
    projected = jnp.dot(normed_one, attention_whole[:, : 3 * D], preferred_element_type=jnp.float32)
    query = rotate(projected[:, :D].reshape(rows_count, seq_part, H, 2, HD), cosine, sine).astype(
        jnp.bfloat16
    )
    key_own = (
        rotate(projected[:, D : 2 * D].reshape(rows_count, seq_part, H, 2, HD), cosine, sine)
        .astype(jnp.bfloat16)
        .reshape(rows_count, seq_part, D)
    )
    value_own = projected[:, 2 * D :].astype(jnp.bfloat16).reshape(rows_count, seq_part, D)
    best = jnp.full((rows_count, H, 2, seq_part), masked_fill, jnp.float32)
    key_piece = lax.all_gather(key_own, "blk", axis=1, tiled=True)
    value_piece = lax.all_gather(value_own, "blk", axis=1, tiled=True)
    count = key_piece.shape[1]
    key_places = jnp.arange(count, dtype=jnp.int32)
    key_segment, unused = document_places(lengths, key_places)
    mask = allowed(segment, places, key_segment, key_places, NDOC - 1)[:, None, None]
    keys = key_piece.reshape(rows_count, count, H, 2, HD)
    values = value_piece.reshape(rows_count, count, H, VD)
    scores = (
        jnp.einsum("rqhcd,rkhcd->rhcqk", query, keys, preferred_element_type=jnp.float32) * scale
    )
    scores = jnp.where(mask, scores, masked_fill)
    top = jnp.maximum(best, jnp.max(scores, axis=-1))
    shares = jnp.where(mask, jnp.exp(scores - top[..., None]), 0.0)
    mass = jnp.sum(shares, axis=-1)
    summed = jnp.einsum(
        "rhcqk,rkhe->rhcqe", shares.astype(jnp.bfloat16), values, preferred_element_type=jnp.float32
    )
    best, mass, summed = (top, mass, summed)
    maps_out = summed / mass[..., None]
    log_mass = best + jnp.log(mass)
    mixed_exact, mix_back = jax.vjp(head_mix, maps_out, head_gain, mixer)
    mixed = mixed_exact.astype(jnp.bfloat16).reshape(token_count, D)
    middle = residual.reshape(token_count, D) + contract_rows(mixed, attention_whole[:, 3 * D :])
    normed_two_exact, norm_two_back = jax.vjp(root_norm, middle, gain_two)
    normed_two = normed_two_exact.astype(jnp.bfloat16)
    gate_up = jnp.dot(normed_two, gate_whole, preferred_element_type=jnp.float32)
    hidden_exact, gated_back = jax.vjp(gated_unit, gate_up[:, :FF], gate_up[:, FF:])
    hidden = hidden_exact.astype(jnp.bfloat16)
    result = middle + contract_rows(hidden, down_whole)
    block_out = result.astype(jnp.bfloat16).reshape(rows_count, seq_part, D)
    output_grad = cotangent.reshape(token_count, D)
    hidden_grad = jnp.dot(output_grad, down_whole, preferred_element_type=jnp.float32)
    gate_grad, up_grad = gated_back(hidden_grad)
    gate_up_grad = jnp.concatenate([gate_grad, up_grad], axis=1).astype(jnp.bfloat16)
    normed_two_grad = contract_rows(gate_up_grad, gate_whole)
    middle_part, gain_two_grad = norm_two_back(normed_two_grad)
    middle_grad = output_grad.astype(jnp.float32) + middle_part
    middle_low = middle_grad.astype(jnp.bfloat16)
    mixed_grad = jnp.dot(
        middle_low, attention_whole[:, 3 * D :], preferred_element_type=jnp.float32
    )
    maps_grad, head_gain_grad, mixer_grad = mix_back(mixed_grad.reshape(rows_count, seq_part, D))
    maps_low = maps_grad.astype(jnp.bfloat16)
    offset_term = jnp.sum(maps_low.astype(jnp.float32) * maps_out, axis=-1)

    def circle(turn_index, carry):
        moving, moving_grad, query_grad = carry
        source = (axis_place - turn_index) % axis_count
        key_places = source * seq_part + jnp.arange(seq_part, dtype=jnp.int32)
        key_segment, unused = document_places(lengths, key_places)
        mask = allowed(segment, places, key_segment, key_places, NDOC - 1)[:, None, None]
        keys = moving[0].astype(jnp.bfloat16).reshape(rows_count, seq_part, H, 2, HD)
        values = moving[1].astype(jnp.bfloat16).reshape(rows_count, seq_part, H, VD)
        scores = (
            jnp.einsum("rqhcd,rkhcd->rhcqk", query, keys, preferred_element_type=jnp.float32)
            * scale
        )
        shares = jnp.where(mask, jnp.exp(scores - log_mass[..., None]), 0.0)
        value_term = jnp.einsum(
            "rhcqk,rhcqe->rkhe",
            shares.astype(jnp.bfloat16),
            maps_low,
            preferred_element_type=jnp.float32,
        )
        share_grad = jnp.einsum(
            "rhcqe,rkhe->rhcqk", maps_low, values, preferred_element_type=jnp.float32
        )
        score_low = (shares * (share_grad - offset_term[..., None])).astype(jnp.bfloat16)
        query_grad = query_grad + jnp.einsum(
            "rhcqk,rkhcd->rqhcd", score_low, keys, preferred_element_type=jnp.float32
        )
        key_term = jnp.einsum(
            "rhcqk,rqhcd->rkhcd", score_low, query, preferred_element_type=jnp.float32
        )
        update = jnp.stack(
            [key_term.reshape(rows_count, seq_part, D), value_term.reshape(rows_count, seq_part, D)]
        )
        moving_grad = moving_grad + update
        moving, moving_grad = (
            from_behind(moving.astype(jnp.bfloat16), "blk", 1).astype(moving.dtype),
            from_behind(moving_grad.astype(jnp.bfloat16), "blk", 1).astype(moving_grad.dtype),
        )
        return (moving, moving_grad, query_grad)

    circle_start = (
        jnp.stack([key_own, value_own]).astype(jnp.float32),
        jnp.zeros((2, rows_count, seq_part, D), jnp.float32),
        jnp.zeros((rows_count, seq_part, H, 2, HD), jnp.float32),
    )
    moving, moving_grad, query_grad = lax.fori_loop(0, axis_count, circle, circle_start)
    key_grad = moving_grad[0].reshape(rows_count, seq_part, H, 2, HD) * scale
    query_pre = rotate(query_grad * scale, cosine, -sine).reshape(token_count, D)
    key_pre = rotate(key_grad, cosine, -sine).reshape(token_count, D)
    projected_grad = jnp.concatenate(
        [query_pre, key_pre, moving_grad[1].reshape(token_count, D)], axis=1
    ).astype(jnp.bfloat16)
    normed_one_grad = contract_rows(projected_grad, attention_whole[:, : 3 * D])
    residual_part, gain_one_grad = norm_one_back(normed_one_grad.reshape(rows_count, seq_part, D))
    input_grad = (middle_grad.reshape(rows_count, seq_part, D) + residual_part).astype(jnp.bfloat16)
    (mixers_grad,) = mixer_back(mixer_grad)
    small_local = jnp.concatenate(
        [gain_one_grad, gain_two_grad, head_gain_grad, mixers_grad.reshape(-1)]
    )
    small_grads = lax.psum(small_local, ("batch", "blk"))
    right_side = jnp.concatenate([projected_grad, mixed, gate_up_grad, hidden], axis=1)
    left_sides = (normed_one, middle_low, normed_two, output_grad)
    bounds = (0, 3 * D, 4 * D, 4 * D + 2 * FF, 4 * D + 3 * FF)
    slot_order = inverse_order(unit_owner)
    parts = []
    for group in range(4):
        left_rows = left_sides[group]
        parts.append(
            lax.dot_general(
                left_rows,
                right_side[:, bounds[group] : bounds[group + 1]],
                (((0,), (0,)), ((), ())),
                preferred_element_type=jnp.float32,
            )
        )
    row_sums = lax.psum_scatter(
        jnp.concatenate(parts, axis=1).astype(jnp.bfloat16), "blk", scatter_dimension=0, tiled=True
    ).astype(jnp.float32)
    placed = take_units(row_sums.reshape(rows_part, UNITS, UW), slot_order)
    grad_slots = lax.psum_scatter(
        placed.astype(jnp.bfloat16), "batch", scatter_dimension=1, tiled=True
    ).astype(jnp.float32)
    columns = bases
    turned = lax.psum_scatter(
        jnp.einsum("ksa,ksn->asn", columns, grad_slots, precision=highest).astype(jnp.bfloat16),
        "blk",
        scatter_dimension=0,
        tiled=True,
    ).astype(jnp.float32)
    steps_done = step_count[0].astype(jnp.float32)
    new_first = beta_one * first + (1.0 - beta_one) * turned
    new_second = beta_two * second + (1.0 - beta_two) * turned * turned
    normalized = adam_step(new_first, new_second, steps_done)
    columns = bases
    update = jnp.zeros_like(master) + jnp.einsum(
        "ksa,asn->ksn",
        columns,
        lax.all_gather(normalized.astype(jnp.bfloat16), "blk", axis=0, tiled=True).astype(
            jnp.float32
        ),
        precision=highest,
    )
    new_master = master - learn_rate * (update + weight_decay * master)
    new_small_first = beta_one * small_first + (1.0 - beta_one) * small_grads
    new_small_second = beta_two * small_second + (1.0 - beta_two) * small_grads * small_grads
    new_small = small - small_rate * adam_step(new_small_first, new_small_second, steps_done)
    return (
        block_out,
        input_grad,
        new_master,
        new_first,
        new_second,
        small_grads,
        new_small,
        new_small_first,
        new_small_second,
    )


BF = jnp.bfloat16
F32 = jnp.float32
TILE = 256
HEADS = 3
QW = HEADS * VD
FQ = FF // 4
VMEM_LIMIT = 56 * 2**20


def params(**more):
    return pltpu.CompilerParams(vmem_limit_bytes=VMEM_LIMIT, **more)


def dot_last(left, right):
    return lax.dot_general(left, right, (((1,), (1,)), ((), ())), preferred_element_type=F32)


def dot_first(left, right):
    return lax.dot_general(left, right, (((0,), (0,)), ((), ())), preferred_element_type=F32)


def dot_plain(left, right):
    return jnp.dot(left, right, preferred_element_type=F32)


def swap_core(piece):
    return lax.ppermute(piece, "batch", [(i, i ^ 1) for i in range(4)])


def swap_y(piece):
    return lax.ppermute(piece, "batch", [(i, i ^ 2) for i in range(4)])


def sum_everywhere(values):
    values = values + swap_core(values)
    values = values + swap_y(values)
    for bit in (1, 2, 4):
        values = values + lax.ppermute(values, "blk", [(i, i ^ bit) for i in range(8)])
    return values


def after(values, earlier):
    return lax.optimization_barrier((values, earlier))[0]


def ring_place(blk):
    side = blk % 2
    return (1 - side) * (blk // 2) + side * (7 - blk // 2)


def ring_owner(place):
    place = (place + 16) % 8
    side = place // 4
    return 2 * ((1 - side) * place + side * (7 - place)) + side


def batch_pieces(piece):
    far = swap_y(piece)
    return (piece, swap_core(piece), far, swap_core(far))


def pick(array, index, axis):
    return lax.dynamic_index_in_dim(array, index, axis, keepdims=False)


def near_sum(partial, me):
    split = partial.reshape(partial.shape[:1] + (2, 2) + partial.shape[2:])
    core = me % 2
    return (pick(split, core, 2).astype(F32) + swap_core(pick(split, 1 - core, 2)).astype(F32)).astype(BF)


def far_sum(near, me):
    y = me // 2
    return pick(near, y, 1).astype(F32) + swap_y(pick(near, 1 - y, 1)).astype(F32)


def swap_blk(piece, bit):
    return lax.ppermute(piece, "blk", [(i, i ^ bit) for i in range(8)])


MESH = pl.DeviceIdType.MESH


def greet(devices):
    barrier = pltpu.get_barrier_semaphore()
    for device in devices:
        pl.semaphore_signal(barrier, inc=1, device_id=device, device_id_type=MESH)
    pl.semaphore_wait(barrier, len(devices))


def greet_all():
    barrier = pltpu.get_barrier_semaphore()
    me, blk = lax.axis_index("batch"), lax.axis_index("blk")

    def signal(n, carry):
        at = (me * 8 + blk + n) % 32
        pl.semaphore_signal(barrier, inc=1, device_id=(at // 8, at % 8), device_id_type=MESH)
        return carry

    lax.fori_loop(1, 32, signal, 0)
    pl.semaphore_wait(barrier, 31)


def remote(source, target, sems, at, device):
    return pltpu.make_async_remote_copy(
        src_ref=source,
        dst_ref=target,
        send_sem=sems.at[0, at],
        recv_sem=sems.at[1, at],
        device_id=device,
        device_id_type=MESH,
    )


def scatter_rows_copies(source, target, sems, me, blk):
    size = target.shape[1]

    def each(act):
        for i in range(2):
            for j in range(4):
                piece = source.at[i, pl.ds(j * size, size)]
                here = (me == j) & (blk == 2 * me + i)

                @pl.when(here)
                def stay():
                    act(pltpu.make_async_copy(piece, target.at[blk], sems.at[0, 4 * i + j]), True)

                @pl.when(jnp.logical_not(here))
                def go():
                    act(
                        pltpu.make_async_remote_copy(
                            src_ref=piece,
                            dst_ref=target.at[blk],
                            send_sem=sems.at[0, 4 * i + j],
                            recv_sem=sems.at[1, blk],
                            device_id=(j, 2 * me + i),
                            device_id_type=MESH,
                        ),
                        False,
                    )

    def start():
        each(lambda copy, local: copy.start())

    def wait_sent():
        each(lambda copy, local: copy.wait() if local else copy.wait_send())

    def wait_arrived():
        for k in range(8):

            @pl.when((blk != k) | (me != blk // 2))
            def arrived():
                pltpu.make_async_remote_copy(
                    src_ref=source.at[0, pl.ds(0, size)],
                    dst_ref=target.at[k],
                    send_sem=sems.at[0, 0],
                    recv_sem=sems.at[1, k],
                    device_id=(me, blk),
                    device_id_type=MESH,
                ).wait_recv()

    return start, wait_sent, wait_arrived


def begin_kernel(master_ref, tokens_ref, pieces_ref, x_ref, s_core, s_y, s_relay, s_x):
    me, blk = lax.axis_index("batch"), lax.axis_index("blk")
    y, core = me // 2, me % 2
    to_core = {"batch": y * 2 + 1 - core}
    to_y = {"batch": (1 - y) * 2 + core}
    x_start, x_sent, x_arrived = scatter_rows_copies(tokens_ref, x_ref, s_x, me, blk)

    def copies(c):
        at = pl.ds(3 * c, 3)
        return (
            lambda: remote(master_ref.at[at], pieces_ref.at[0, at], s_core, c, to_core),
            lambda: remote(master_ref.at[at], pieces_ref.at[1, at], s_y, c, to_y),
            lambda: remote(pieces_ref.at[1, at], pieces_ref.at[2, at], s_relay, c, to_core),
        )

    greet_all()
    for c in range(3):
        copies(c)[1]().start()
    for c in range(3):
        copies(c)[0]().start()
    x_start()
    for c in range(3):
        copies(c)[1]().wait_recv()
        copies(c)[2]().start()
    for c in range(3):
        near, far, relay = copies(c)
        near().wait()
        far().wait_send()
        relay().wait()
    x_sent()
    x_arrived()


def begin(master, tokens):
    hbm = pl.BlockSpec(memory_space=pl.ANY)
    size = tokens.shape[1] // 4
    sems = lambda n: pltpu.SemaphoreType.DMA((2, n))
    return pl.pallas_call(
        begin_kernel,
        in_specs=[hbm, hbm],
        out_specs=[hbm, hbm],
        out_shape=[
            jax.ShapeDtypeStruct((3,) + master.shape, BF),
            jax.ShapeDtypeStruct((8, size, D), BF),
        ],
        scratch_shapes=[sems(3), sems(3), sems(3), sems(8)],
        compiler_params=params(collective_id=3, has_side_effects=True),
        name="begin",
    )(master, tokens)


def gather_kernel(
    shard_ref, down_ref, x_ref, grad_ref, attn_ref, downs_ref, xs_ref, dy_ref, dys_ref, s_local, s_up, s_down, s_up2,
    s_down2, s_x, s_dy, s_dys,
):
    me, blk = lax.axis_index("batch"), lax.axis_index("blk")
    y, core = me // 2, me % 2
    to_core = {"batch": y * 2 + 1 - core}
    to_y = {"batch": (1 - y) * 2 + core}
    place = ring_place(blk)
    after_me, before_me = {"blk": ring_owner(place + 1)}, {"blk": ring_owner(place - 1)}
    half = shard_ref.shape[0] // 2
    sub = half // 2
    far_slab = (1 - y) * 2 + core

    def ring(t, up, part, second=False):
        owner = ring_owner(place - t) if up else ring_owner(place + t)
        at = pl.ds((0 if up else half) + part * sub, sub)
        target = (downs_ref if second else attn_ref).at[owner, at]
        source = (down_ref if second else shard_ref).at[at] if t == 0 else target
        sems = (s_up2 if up else s_down2) if second else (s_up if up else s_down)
        return remote(source, target, sems, 2 * t + part, after_me if up else before_me)

    def spread(source, whole, sems, c):
        at = pl.ds(4 * c, 4)
        return (
            lambda: remote(source.at[at], whole.at[at, me], sems, c, to_core),
            lambda: remote(source.at[at], whole.at[at, me], sems, 2 + c, to_y),
            lambda: remote(whole.at[at, far_slab], whole.at[at, far_slab], sems, 4 + c, to_core),
        )

    dy_start, dy_sent, dy_arrived = scatter_rows_copies(grad_ref, dy_ref, s_dy, me, blk)
    locals_ = [
        pltpu.make_async_copy(shard_ref, attn_ref.at[blk], s_local.at[0]),
        pltpu.make_async_copy(x_ref, xs_ref.at[:, me], s_local.at[1]),
        pltpu.make_async_copy(dy_ref, dys_ref.at[:, me], s_local.at[2]),
        pltpu.make_async_copy(down_ref, downs_ref.at[blk], s_local.at[3]),
    ]
    greet_all()
    for part in range(2):
        ring(0, True, part).start()
        ring(0, False, part).start()
    for c in range(2):
        spread(x_ref, xs_ref, s_x, c)[1]().start()
        spread(x_ref, xs_ref, s_x, c)[0]().start()
    locals_[0].start()
    locals_[1].start()
    locals_[3].start()
    dy_start()
    for t in range(1, 7):
        for part in range(2):
            for up in (True, False):
                ring(t - 1, up, part).wait_recv()
                ring(t, up, part).start()
        if t in (4, 5):
            copies = spread(x_ref, xs_ref, s_x, t - 4)
            copies[1]().wait_recv()
            copies[2]().start()
        if t == 5:
            dy_arrived()
            dy_sent()
            for c in range(2):
                spread(dy_ref, dys_ref, s_dys, c)[1]().start()
                spread(dy_ref, dys_ref, s_dys, c)[0]().start()
            locals_[2].start()
    for part in range(2):
        for up in (True, False):
            ring(0, up, part, True).start()
            ring(6, up, part).wait_recv()
    for t in range(1, 7):
        for part in range(2):
            for up in (True, False):
                ring(t - 1, up, part, True).wait_recv()
                ring(t, up, part, True).start()
        if t in (3, 5):
            copies = spread(dy_ref, dys_ref, s_dys, (t - 3) // 2)
            copies[1]().wait_recv()
            copies[2]().start()
    for part in range(2):
        for up in (True, False):
            ring(6, up, part, True).wait_recv()
    for t in range(7):
        for part in range(2):
            for up in (True, False):
                ring(t, up, part).wait_send()
                ring(t, up, part, True).wait_send()
    for source, whole, sems in ((x_ref, xs_ref, s_x), (dy_ref, dys_ref, s_dys)):
        for c in range(2):
            near, far, relay = spread(source, whole, sems, c)
            near().wait()
            far().wait_send()
            relay().wait()
    for copy in locals_:
        copy.wait()


def gather(shard, down, x, cotangent):
    hbm = pl.BlockSpec(memory_space=pl.ANY)
    size = x.shape[1]
    sems = lambda n: pltpu.SemaphoreType.DMA((2, n))
    whole = jax.ShapeDtypeStruct((8, 4, size, D), BF)
    return pl.pallas_call(
        gather_kernel,
        in_specs=[hbm] * 4,
        out_specs=[hbm] * 5,
        out_shape=[
            jax.ShapeDtypeStruct((8,) + shard.shape, BF),
            jax.ShapeDtypeStruct((8,) + down.shape, BF),
            whole,
            jax.ShapeDtypeStruct((8, size, D), BF),
            whole,
        ],
        scratch_shapes=[pltpu.SemaphoreType.DMA((4,))] + [sems(14)] * 4 + [sems(6), sems(8), sems(6)],
        compiler_params=params(collective_id=4, has_side_effects=True),
        name="gather",
    )(shard, down, x, cotangent)


def attention_pieces(me):
    pieces = []
    for matrix in range(4):
        for j in range(HEADS):
            block = HEADS * me + j
            pieces.append((3 * matrix + block // 4, block % 4, HEADS * matrix + j))
    return pieces


def pick_kernel(place_ref, me_ref, own, pieces, attn_ref, ffn_ref, down_ref, sems):
    me = me_ref[0]
    waits = []

    def begin(unit, source, target, sem):
        at = place_ref[unit]
        for other, ref in enumerate((own, pieces.at[0], pieces.at[1], pieces.at[2])):

            @pl.when(at // 9 == other)
            def start():
                pltpu.make_async_copy(source(ref.at[at % 9]), target, sem).start()

        waits.append(pltpu.make_async_copy(source(own.at[0]), target, sem))

    for i, (unit, block, packed) in enumerate(attention_pieces(me)):
        column = pl.multiple_of(block * 128, 128)
        begin(unit, lambda r, c=column: r.at[:, pl.ds(c, 128)], attn_ref.at[:, pl.ds(packed * 128, 128)], sems.at[i])
    for i in range(6):
        unit = 12 + 8 * (i // 2) + 2 * me + i % 2
        target = ffn_ref.at[:, pl.ds(i * UW, UW)] if i < 4 else down_ref.at[:, pl.ds((i - 4) * UW, UW)]
        begin(unit, lambda r: r, target, sems.at[12 + i])
    for wait in waits:
        wait.wait()


def pick_units(place, me, own, pieces):
    rows = own.shape[1]
    hbm = pl.BlockSpec(memory_space=pl.ANY)
    smem = pl.BlockSpec(memory_space=pltpu.SMEM)
    vmem = pl.BlockSpec(memory_space=pltpu.VMEM)
    return pl.pallas_call(
        pick_kernel,
        in_specs=[smem, smem, hbm, hbm],
        out_specs=[vmem, vmem, vmem],
        out_shape=[
            jax.ShapeDtypeStruct((rows, 4 * QW), BF),
            jax.ShapeDtypeStruct((rows, 4 * UW), BF),
            jax.ShapeDtypeStruct((rows, 2 * UW), BF),
        ],
        scratch_shapes=[pltpu.SemaphoreType.DMA((18,))],
        compiler_params=params(),
        name="pick_units",
    )(place, me.reshape(1), own, pieces)


def place_kernel(unit_ref, me_ref, attn, gate_up, down, out_ref, sems):
    me = me_ref[0]
    waits = []
    for i in range(9):
        unit = unit_ref[i]
        f = jnp.maximum(unit - 12, 0)
        for q in range(4):
            block = (unit % 3) * 4 + q
            low = f % 16
            choices = (
                (unit < 12, attn, block // HEADS, (unit // 3) * QW + (block % HEADS) * 128),
                ((unit >= 12) & (unit < 28), gate_up, (low % 8) // 2, (low // 8) * FQ + (low % 2) * UW + q * 128),
                (unit >= 28, down, (f % 8) // 2, (f % 2) * UW + q * 128),
            )
            target, sem = out_ref.at[i, :, pl.ds(q * 128, 128)], sems.at[i, q]
            for chosen, pieces, holder, column in choices:

                @pl.when(chosen)
                def start(pieces=pieces, holder=holder, column=column, target=target, sem=sem):
                    source = pieces.at[holder ^ me, :, pl.ds(pl.multiple_of(column, 128), 128)]
                    pltpu.make_async_copy(source, target, sem).start()

            waits.append(pltpu.make_async_copy(attn.at[0, :, pl.ds(0, 128)], target, sem))
    for wait in waits:
        wait.wait()


def place_units(units, me, attn_pieces, gate_up_pieces, down_pieces):
    rows = attn_pieces.shape[1]
    hbm = pl.BlockSpec(memory_space=pl.ANY)
    smem = pl.BlockSpec(memory_space=pltpu.SMEM)
    return pl.pallas_call(
        place_kernel,
        in_specs=[smem, smem] + [hbm] * 3,
        out_specs=pl.BlockSpec(memory_space=pltpu.VMEM),
        out_shape=jax.ShapeDtypeStruct((9, rows, UW), BF),
        scratch_shapes=[pltpu.SemaphoreType.DMA((9, 4))],
        compiler_params=params(),
        name="place_units",
    )(units, me.reshape(1), attn_pieces, gate_up_pieces, down_pieces)


def turn(values, cosine, sine, lane):
    partner = jnp.where(lane % HD < HD // 2, pltpu.roll(values, 96, 1), pltpu.roll(values, 32, 1))
    return values * cosine + partner * sine


def project_kernel(x_ref, w_ref, gain_ref, cos_ref, sin_ref, n_ref, q_ref, k_ref, v_ref):
    x = x_ref[...].astype(F32)
    r = lax.rsqrt(jnp.mean(x * x, axis=-1, keepdims=True) + norm_epsilon)
    n = (x * r * gain_ref[...]).astype(BF)
    n_ref[...] = n
    lane = lax.broadcasted_iota(jnp.int32, (x.shape[0], VD), 1)
    cosine, sine = cos_ref[...], sin_ref[...]
    out = dot_plain(n, w_ref[...])
    for h in range(HEADS):
        at = slice(h * VD, (h + 1) * VD)
        q = turn(out[:, h * VD : (h + 1) * VD], cosine, sine, lane)
        q_ref[:, at] = (q.astype(BF).astype(F32) * HD**-0.5).astype(BF)
        k = turn(out[:, QW + h * VD : QW + (h + 1) * VD], cosine, sine, lane)
        k_ref[:, at] = k.astype(BF)
    v_ref[...] = out[:, 2 * QW :].astype(BF)


def project(x, weights, gain, cosine, sine):
    count = x.shape[0]
    rows = lambda w: pl.BlockSpec((TILE, w), lambda i: (i, 0))
    fixed = lambda h, w: pl.BlockSpec((h, w), lambda i: (0, 0), pipeline_mode=pl.Buffered(1))
    narrow = jax.ShapeDtypeStruct((count, QW), BF)
    return pl.pallas_call(
        project_kernel,
        grid=(count // TILE,),
        in_specs=[rows(D), fixed(D, 3 * QW), fixed(1, D), rows(VD), rows(VD)],
        out_specs=[rows(D), rows(QW), rows(QW), rows(QW)],
        out_shape=[jax.ShapeDtypeStruct((count, D), BF), narrow, narrow, narrow],
        compiler_params=params(),
        cost_estimate=pl.CostEstimate(
            flops=2 * count * D * 3 * QW, bytes_accessed=count * D * 6 + 6 * D * QW, transcendentals=0
        ),
        name="project",
    )(x, weights, gain, cosine, sine)


def split_halves(q):
    lane = lax.broadcasted_iota(jnp.int32, q.shape, 1)
    zero = jnp.zeros_like(q)
    return jnp.concatenate([jnp.where(lane < HD, q, zero), jnp.where(lane >= HD, q, zero)], axis=0)


def block_mask(j, i, start):
    key = j * TILE + lax.broadcasted_iota(jnp.int32, (TILE, 2 * TILE), 0)
    query = i * TILE + lax.broadcasted_iota(jnp.int32, (TILE, TILE), 1)
    query = jnp.concatenate([query, query], axis=1)
    return (key >= start) & (key <= query)


def attend_kernel(low_ref, lam_ref, q_ref, k_ref, v_ref, start_ref, gain_ref, a_ref, maps_ref, log_ref, vt_ref):
    i = pl.program_id(1)

    @pl.when(i == 0)
    def turn_values():
        for j in range(vt_ref.shape[0]):
            vt_ref[j] = v_ref[j * TILE : (j + 1) * TILE, :].astype(F32).T.astype(BF)

    q = split_halves(q_ref[...])
    start = jnp.concatenate([start_ref[...], start_ref[...]], axis=1)

    def step(j, carry):
        top, mass, total = carry
        keys = k_ref[pl.ds(pl.multiple_of(j * TILE, TILE), TILE), :]
        scores = jnp.where(block_mask(j, i, start), dot_last(keys, q), masked_fill)
        new = jnp.maximum(top, jnp.max(scores, axis=0, keepdims=True))
        shares = jnp.exp(scores - new)
        keep = jnp.exp(top - new)
        mass = mass * keep + jnp.sum(shares, axis=0, keepdims=True)
        total = total * keep + dot_plain(vt_ref[j], shares.astype(BF))
        return new, mass, total

    first = (
        jnp.full((1, 2 * TILE), masked_fill, F32),
        jnp.zeros((1, 2 * TILE), F32),
        jnp.zeros((VD, 2 * TILE), F32),
    )
    top, mass, total = lax.fori_loop(low_ref[i], i + 1, step, first)
    maps = total / mass
    one, two = maps[:, :TILE], maps[:, TILE:]
    maps_ref[0, 0] = one
    maps_ref[0, 1] = two
    log_ref[0, 0] = top + jnp.log(mass)
    mixed = one - lam_ref[0] * two
    r = lax.rsqrt(jnp.mean(mixed * mixed, axis=0, keepdims=True) + norm_epsilon)
    a_ref[...] = (mixed * r * gain_ref[...] * (1.0 - lambda_start)).T.astype(BF)


def attend(low, lam, q, k, v, start, gain):
    count = q.shape[0]
    blocks = count // TILE
    smem = pl.BlockSpec(memory_space=pltpu.SMEM)
    return pl.pallas_call(
        attend_kernel,
        grid=(HEADS, blocks),
        in_specs=[
            smem,
            smem,
            pl.BlockSpec((TILE, VD), lambda h, i: (i, h)),
            pl.BlockSpec((count, VD), lambda h, i: (0, h)),
            pl.BlockSpec((count, VD), lambda h, i: (0, h)),
            pl.BlockSpec((1, TILE), lambda h, i: (0, i)),
            pl.BlockSpec((VD, 1), lambda h, i: (0, 0)),
        ],
        out_specs=[
            pl.BlockSpec((TILE, VD), lambda h, i: (i, h)),
            pl.BlockSpec((1, 2, VD, TILE), lambda h, i: (h, 0, 0, i)),
            pl.BlockSpec((1, 1, 1, 2 * TILE), lambda h, i: (h, i, 0, 0)),
        ],
        out_shape=[
            jax.ShapeDtypeStruct((count, QW), BF),
            jax.ShapeDtypeStruct((HEADS, 2, VD, count), F32),
            jax.ShapeDtypeStruct((HEADS, blocks, 1, 2 * TILE), F32),
        ],
        scratch_shapes=[pltpu.VMEM((blocks, VD, TILE), BF)],
        compiler_params=params(),
        cost_estimate=pl.CostEstimate(
            flops=8 * count * count * VD * HEADS, bytes_accessed=count * QW * 16, transcendentals=count * count * HEADS
        ),
        name="attend",
    )(low, lam, q, k, v, start, gain)


def attend_back_kernel(
    low_ref, lam_ref, q_ref, k_ref, v_ref, start_ref, gain_ref, maps_ref, log_ref, da_ref, cosq_ref, sinq_ref,
    cosk_ref, sink_ref, dq_ref, dk_ref, dv_ref, dgain_ref, dlam_ref, kt_ref, dk_sum, dv_sum, dq_sum,
):
    i = pl.program_id(1)
    blocks = kt_ref.shape[0]

    @pl.when(i == 0)
    def begin():
        for j in range(blocks):
            kt_ref[j] = k_ref[j * TILE : (j + 1) * TILE, :].astype(F32).T.astype(BF)
        dk_sum[...] = jnp.zeros_like(dk_sum)
        dv_sum[...] = jnp.zeros_like(dv_sum)
        dgain_ref[...] = jnp.zeros_like(dgain_ref)
        dlam_ref[...] = jnp.zeros_like(dlam_ref)

    lam = lam_ref[0]
    q = split_halves(q_ref[...])
    start = jnp.concatenate([start_ref[...], start_ref[...]], axis=1)
    log_mass = log_ref[0, 0]
    one, two = maps_ref[0, 0], maps_ref[0, 1]
    mixed = one - lam * two
    r = lax.rsqrt(jnp.mean(mixed * mixed, axis=0, keepdims=True) + norm_epsilon)
    t = mixed * r
    da = da_ref[...].T * (1.0 - lambda_start)
    dgain_ref[0] += da * t
    e = da * gain_ref[...]
    dmixed = r * (e - t * jnp.mean(e * t, axis=0, keepdims=True))
    dlam_ref[0] -= jnp.sum(dmixed * two, axis=0, keepdims=True)
    dmaps = jnp.concatenate([dmixed, -lam * dmixed], axis=1).astype(BF)
    maps = jnp.concatenate([one, two], axis=1)
    offset = jnp.sum(dmaps.astype(F32) * maps, axis=0, keepdims=True)
    dq_sum[...] = jnp.zeros_like(dq_sum)

    def step(j, carry):
        at = pl.ds(pl.multiple_of(j * TILE, TILE), TILE)
        keys, values = k_ref[at, :], v_ref[at, :]
        scores = dot_last(keys, q)
        shares = jnp.where(block_mask(j, i, start), jnp.exp(scores - log_mass), 0.0)
        dshares = dot_plain(values, dmaps)
        dscores = (shares * (dshares - offset)).astype(BF)
        dv_sum[at, :] += dot_last(shares.astype(BF), dmaps)
        dk_sum[at, :] += dot_plain(dscores, q)
        dq_sum[...] += dot_plain(kt_ref[j], dscores)
        return carry

    lax.fori_loop(low_ref[i], i + 1, step, 0)
    lane = lax.broadcasted_iota(jnp.int32, (TILE, VD), 1)
    dq = jnp.concatenate([dq_sum[:HD, :TILE], dq_sum[HD:, TILE:]], axis=0).T * HD**-0.5
    dq_ref[...] = turn(dq, cosq_ref[...], -sinq_ref[...], lane).astype(BF)

    @pl.when(i == blocks - 1)
    def finish():
        for j in range(blocks):
            at = slice(j * TILE, (j + 1) * TILE)
            dk_ref[at, :] = turn(dk_sum[at, :], cosk_ref[at, :], -sink_ref[at, :], lane).astype(BF)
        dv_ref[...] = dv_sum[...].astype(BF)


def attend_back(low, lam, q, k, v, start, gain, maps, log_mass, da, cosine, sine):
    count = q.shape[0]
    blocks = count // TILE
    smem = pl.BlockSpec(memory_space=pltpu.SMEM)
    tile = pl.BlockSpec((TILE, VD), lambda h, i: (i, h))
    whole = pl.BlockSpec((count, VD), lambda h, i: (0, h))
    table = pl.BlockSpec((TILE, VD), lambda h, i: (i, 0))
    full_table = pl.BlockSpec((count, VD), lambda h, i: (0, 0), pipeline_mode=pl.Buffered(1))
    narrow = jax.ShapeDtypeStruct((count, QW), BF)
    return pl.pallas_call(
        attend_back_kernel,
        grid=(HEADS, blocks),
        in_specs=[
            smem,
            smem,
            tile,
            whole,
            whole,
            pl.BlockSpec((1, TILE), lambda h, i: (0, i)),
            pl.BlockSpec((VD, 1), lambda h, i: (0, 0)),
            pl.BlockSpec((1, 2, VD, TILE), lambda h, i: (h, 0, 0, i)),
            pl.BlockSpec((1, 1, 1, 2 * TILE), lambda h, i: (h, i, 0, 0)),
            tile,
            table,
            table,
            full_table,
            full_table,
        ],
        out_specs=[
            tile,
            whole,
            whole,
            pl.BlockSpec((1, VD, TILE), lambda h, i: (h, 0, 0)),
            pl.BlockSpec((1, 1, TILE), lambda h, i: (h, 0, 0)),
        ],
        out_shape=[
            narrow,
            narrow,
            narrow,
            jax.ShapeDtypeStruct((HEADS, VD, TILE), F32),
            jax.ShapeDtypeStruct((HEADS, 1, TILE), F32),
        ],
        scratch_shapes=[
            pltpu.VMEM((blocks, VD, TILE), BF),
            pltpu.VMEM((count, VD), F32),
            pltpu.VMEM((count, VD), F32),
            pltpu.VMEM((VD, 2 * TILE), F32),
        ],
        compiler_params=params(),
        cost_estimate=pl.CostEstimate(
            flops=20 * count * count * VD * HEADS, bytes_accessed=count * QW * 24, transcendentals=count * count * HEADS
        ),
        name="attend_back",
    )(low, lam, q, k, v, start, gain, maps, log_mass, da, cosine, sine, cosine, sine)


def middle_kernel(
    x_ref, gain_ref, a_ref, w_ref, a_hbm, attn_hbm, n_ref, own_ref, a_in, w_in, total, s_a, s_ay, s_ar, s_w
):
    i = pl.program_id(0)
    me = lax.axis_index("batch")
    y, core = me // 2, me % 2
    to_core = {"batch": y * 2 + 1 - core}
    to_y = {"batch": (1 - y) * 2 + core}
    blocks = a_in.shape[1]
    mine = attn_hbm.at[:, pl.ds(3 * QW, QW)]

    def a_copies(b):
        source = a_hbm.at[pl.ds(b * TILE, TILE)]
        return (
            lambda: remote(source, a_in.at[0, b], s_a, b, to_core),
            lambda: remote(source, a_in.at[1, b], s_ay, b, to_y),
            lambda: remote(a_in.at[1, b], a_in.at[2, b], s_ar, b, to_core),
        )

    w_copies = (
        lambda: remote(mine, w_in.at[0], s_w, 0, to_core),
        lambda: remote(mine, w_in.at[1], s_w, 1, to_y),
        lambda: remote(w_in.at[1], w_in.at[2], s_w, 2, to_core),
    )

    @pl.when(i == 0)
    def begin():
        greet((to_core, to_y))
        w_copies[1]().start()
        for b in range(blocks):
            a_copies(b)[1]().start()
        w_copies[0]().start()
        for b in range(blocks):
            a_copies(b)[0]().start()
        w_copies[1]().wait_recv()
        w_copies[2]().start()

    @pl.when(i < blocks)
    def relay():
        a_copies(i)[1]().wait_recv()
        a_copies(i)[2]().start()

    @pl.when(i == 1)
    def weights():
        w_copies[0]().wait_recv()
        w_copies[2]().wait_recv()

    @pl.when(i >= 1)
    def compute():
        b = i - 1
        a_copies(b)[0]().wait_recv()
        a_copies(b)[2]().wait_recv()
        x1 = x_ref[...].astype(F32) + dot_last(a_ref[...], w_ref[...])
        for other in range(3):
            x1 += dot_last(a_in[other, b], w_in[other])
        total[...] = x1
        r = lax.rsqrt(jnp.mean(x1 * x1, axis=-1, keepdims=True) + norm_epsilon)
        n_ref[...] = (x1 * r * gain_ref[...]).astype(BF)
        part = TILE // 4
        own_ref[0] = total[pl.ds(pl.multiple_of(me * part, part), part), :]

    @pl.when(i == blocks)
    def finish():
        for copy in w_copies:
            copy().wait_send()
        for b in range(blocks):
            for copy in a_copies(b):
                copy().wait_send()


def middle(a, x, attn, gain):
    count = x.shape[0]
    blocks = count // TILE
    late = lambda i: (jnp.maximum(i - 1, 0), 0)
    hbm = pl.BlockSpec(memory_space=pl.ANY)
    sems = lambda n: pltpu.SemaphoreType.DMA((2, n))
    return pl.pallas_call(
        middle_kernel,
        grid=(blocks + 1,),
        in_specs=[
            pl.BlockSpec((TILE, D), late),
            pl.BlockSpec((1, D), lambda i: (0, 0)),
            pl.BlockSpec((TILE, QW), late),
            pl.BlockSpec((D, QW), lambda i: (0, 3), pipeline_mode=pl.Buffered(1)),
            hbm,
            hbm,
        ],
        out_specs=[
            pl.BlockSpec((TILE, D), late),
            pl.BlockSpec((1, TILE // 4, D), lambda i: (jnp.maximum(i - 1, 0), 0, 0)),
        ],
        out_shape=[
            jax.ShapeDtypeStruct((count, D), BF),
            jax.ShapeDtypeStruct((blocks, TILE // 4, D), F32),
        ],
        scratch_shapes=[
            pltpu.VMEM((3, blocks, TILE, QW), BF),
            pltpu.VMEM((3, D, QW), BF),
            pltpu.VMEM((TILE, D), F32),
            sems(blocks),
            sems(blocks),
            sems(blocks),
            sems(3),
        ],
        compiler_params=params(collective_id=5, has_side_effects=True),
        cost_estimate=pl.CostEstimate(
            flops=2 * count * D * D, bytes_accessed=count * D * 7 + 2 * D * D, transcendentals=0
        ),
        name="middle",
    )(x, gain, a, attn, a, attn)


def feed_kernel(
    n_ref, dy_ref, w_ref, wd_ref, x1_ref, dyo_ref, wo_ref, gain_ref, act_ref, out_ref, dx_ref, low_ref, da_ref, dgain_ref,
    part, near_in, near, far_in, gathered, s_near, s_far, s_y, s_core, s_relay,
):
    i = pl.program_id(0)
    me = lax.axis_index("batch")
    y, core = me // 2, me % 2
    to_core = {"batch": y * 2 + 1 - core}
    to_y = {"batch": (1 - y) * 2 + core}
    blocks = part.shape[0]

    def near_copy(b):
        return remote(part.at[b, :, 1 - core], near_in.at[b], s_near, b, to_core)

    def far_copy(b):
        return remote(near.at[b], far_in.at[b], s_far, b, to_y)

    def own_copy(b, sems, device):
        return remote(gathered.at[b, me], gathered.at[b, me], sems, b, device)

    def relay_copy(b):
        slab = (1 - y) * 2 + core
        return remote(gathered.at[b, slab], gathered.at[b, slab], s_relay, b, to_core)

    @pl.when(i == 0)
    def begin():
        greet((to_core, to_y))
        dgain_ref[...] = jnp.zeros_like(dgain_ref)

    @pl.when((i >= 1) & (i < blocks + 1))
    def send_far():
        b = i - 1
        near_copy(b).wait_recv()
        both = part[b, 1 - y, core].astype(F32) + near_in[b, 1 - y].astype(F32)
        near[b] = both.astype(BF)
        far_copy(b).start()

    @pl.when((i >= 2) & (i < blocks + 2))
    def send_own():
        b = i - 2
        far_copy(b).wait_recv()
        dn = part[b, y, core].astype(F32) + near_in[b, y].astype(F32) + far_in[b].astype(F32)
        x1 = x1_ref[0]
        r = lax.rsqrt(jnp.mean(x1 * x1, axis=-1, keepdims=True) + norm_epsilon)
        t = x1 * r
        e = dn * gain_ref[...]
        dx = dyo_ref[0].astype(F32) + r * (e - t * jnp.mean(e * t, axis=-1, keepdims=True))
        dgain_ref[...] += jnp.sum(dn * t, axis=0, keepdims=True)
        dx_ref[0] = dx
        gathered[b, me] = dx.astype(BF)
        own_copy(b, s_y, to_y).start()
        own_copy(b, s_core, to_core).start()

    @pl.when((i >= 3) & (i < blocks + 3))
    def send_relay():
        b = i - 3
        own_copy(b, s_y, to_y).wait_recv()
        relay_copy(b).start()

    @pl.when(i >= 4)
    def use():
        b = i - 4
        own_copy(b, s_core, to_core).wait_recv()
        relay_copy(b).wait_recv()
        whole = jnp.concatenate([gathered[b, other] for other in range(4)], axis=0)
        low_ref[...] = whole
        da_ref[...] = dot_plain(whole, wo_ref[...])

    @pl.when(i < blocks)
    def compute():
        n, dy = n_ref[...], dy_ref[...]
        wg, wu, wd = w_ref[:, :FQ], w_ref[:, FQ:], wd_ref[...]
        gate = dot_plain(n, wg)
        up = dot_plain(n, wu)
        dhidden = dot_plain(dy, wd)
        share = 1.0 / (1.0 + jnp.exp(-gate))
        silu = gate * share
        hidden = (silu * up).astype(BF)
        dup = (dhidden * silu).astype(BF)
        dgate = (dhidden * up * (share * (1.0 + gate * (1.0 - share)))).astype(BF)
        act_ref[:, :FQ] = dgate
        act_ref[:, FQ : 2 * FQ] = dup
        act_ref[:, 2 * FQ :] = hidden
        dn = (dot_last(dgate, wg) + dot_last(dup, wu)).astype(BF)
        size = dn.shape[0] // 4
        for other in range(4):
            part[i, other // 2, other % 2] = dn[other * size : (other + 1) * size]
        near_copy(i).start()
        out_ref[...] = dot_last(hidden, wd).astype(BF)

    @pl.when(i == blocks + 3)
    def finish():
        for b in range(blocks):
            near_copy(b).wait_send()
            far_copy(b).wait_send()
            own_copy(b, s_y, to_y).wait_send()
            own_copy(b, s_core, to_core).wait_send()
            relay_copy(b).wait_send()


def feed(n, dy, weights, down, x1, dy_own, attn, gain):
    count = n.shape[0]
    blocks = count // TILE
    size = TILE // 4
    late = lambda lag: lambda i: (jnp.clip(i - lag, 0, blocks - 1), 0)
    late3 = lambda lag: lambda i: (jnp.clip(i - lag, 0, blocks - 1), 0, 0)
    rows = lambda w, lag: pl.BlockSpec((TILE, w), late(lag))
    own = pl.BlockSpec((1, size, D), late3(2))
    shape = lambda w, kind=BF: jax.ShapeDtypeStruct((count, w), kind)
    sems = pltpu.SemaphoreType.DMA((2, blocks))
    return pl.pallas_call(
        feed_kernel,
        grid=(blocks + 4,),
        in_specs=[
            rows(D, 0),
            rows(D, 0),
            pl.BlockSpec((D, 2 * FQ), lambda i: (0, 0), pipeline_mode=pl.Buffered(1)),
            pl.BlockSpec((D, FQ), lambda i: (0, 0), pipeline_mode=pl.Buffered(1)),
            own,
            own,
            pl.BlockSpec((D, QW), lambda i: (0, 3), pipeline_mode=pl.Buffered(1)),
            pl.BlockSpec((1, D), lambda i: (0, 0)),
        ],
        out_specs=[
            rows(3 * FQ, 0),
            rows(D, 0),
            own,
            rows(D, 4),
            rows(QW, 4),
            pl.BlockSpec((1, D), lambda i: (0, 0)),
        ],
        out_shape=[
            shape(3 * FQ),
            shape(D),
            jax.ShapeDtypeStruct((blocks, size, D), F32),
            shape(D),
            shape(QW, F32),
            jax.ShapeDtypeStruct((1, D), F32),
        ],
        scratch_shapes=[
            pltpu.VMEM((blocks, 2, 2, size, D), BF),
            pltpu.VMEM((blocks, 2, size, D), BF),
            pltpu.VMEM((blocks, size, D), BF),
            pltpu.VMEM((blocks, size, D), BF),
            pltpu.VMEM((blocks, 4, size, D), BF),
            sems,
            sems,
            sems,
            sems,
            sems,
        ],
        compiler_params=params(collective_id=1, has_side_effects=True),
        cost_estimate=pl.CostEstimate(
            flops=12 * count * D * FQ, bytes_accessed=count * (8 * D + 6 * FQ) + 6 * D * FQ, transcendentals=count * FQ
        ),
        name="feed",
    )(n, dy, weights, down, x1, dy_own, attn, gain)


def return_rows_copies(source, target, sems, me, blk):
    size = source.shape[1]

    def copies(act_local, act_remote):
        for k in range(8):
            here = (me == blk // 2) & (blk == k)
            piece = target.at[blk % 2, pl.ds(pl.multiple_of(me * size, size), size)]

            @pl.when(here)
            def stay():
                act_local(pltpu.make_async_copy(source.at[k], piece, sems.at[0, k]))

            @pl.when(jnp.logical_not(here))
            def go():
                act_remote(
                    pltpu.make_async_remote_copy(
                        src_ref=source.at[k],
                        dst_ref=piece,
                        send_sem=sems.at[0, k],
                        recv_sem=sems.at[1, (blk % 2) * 4 + me],
                        device_id=(blk // 2, k),
                        device_id_type=MESH,
                    )
                )

    def start():
        copies(lambda copy: copy.start(), lambda copy: copy.start())

    def finish():
        copies(lambda copy: copy.wait(), lambda copy: copy.wait_send())
        for i in range(2):
            for other in range(4):

                @pl.when((me != other) | (blk != 2 * me + i))
                def arrived():
                    pltpu.make_async_remote_copy(
                        src_ref=source.at[0],
                        dst_ref=target.at[i, pl.ds(other * size, size)],
                        send_sem=sems.at[0, 0],
                        recv_sem=sems.at[1, 4 * i + other],
                        device_id=(me, blk),
                        device_id_type=MESH,
                    ).wait_recv()

    return start, finish


def ring_kernel(exchanged, sent_back, *refs):
    refs = list(refs)
    grad = refs.pop(0)
    extras = [refs.pop(0) for _ in range(exchanged)]
    rows_ref = refs.pop(0) if sent_back else None
    sums_ref = refs.pop(0)
    extra_outs = [refs.pop(0) for _ in range(exchanged)]
    back_ref = refs.pop(0) if sent_back else None
    up_in, down_in, total, s_up, s_down, s_out, s_extra, s_back, s_local = refs
    me, blk = lax.axis_index("batch"), lax.axis_index("blk")
    y, core = me // 2, me % 2
    to_core = {"batch": y * 2 + 1 - core}
    to_y = {"batch": (1 - y) * 2 + core}
    place = ring_place(blk)
    after_me, before_me = {"blk": ring_owner(place + 1)}, {"blk": ring_owner(place - 1)}
    part = grad.shape[0] // 8
    half = part // 2
    parts = up_in.shape[1]
    width = grad.shape[1] // parts

    def own(t, up, p):
        owner = ring_owner(place - 1 - t) if up else ring_owner(place + 1 + t)
        begin = pl.multiple_of(owner * part + (0 if up else half), half)
        return grad.at[pl.ds(begin, half), pl.ds(p * width, width)]

    def ring(t, up, p):
        here = up_in if up else down_in
        source = own(0, up, p) if t == 0 else here.at[t - 1, p]
        return remote(source, here.at[t, p], s_up if up else s_down, parts * t + p, after_me if up else before_me)

    def exchange(source, out, sems, n):
        return (
            lambda: remote(source, out.at[1], sems, 3 * n, to_core),
            lambda: remote(source, out.at[2], sems, 3 * n + 1, to_y),
            lambda: remote(out.at[2], out.at[3], sems, 3 * n + 2, to_core),
        )

    extra_sets = [exchange(extras[n], extra_outs[n], s_extra, n) for n in range(exchanged)]
    extra_locals = [pltpu.make_async_copy(extras[n], extra_outs[n].at[0], s_local.at[1 + n]) for n in range(exchanged)]
    greet_all()
    for p in range(parts):
        ring(0, True, p).start()
        ring(0, False, p).start()
    for n in range(exchanged):
        extra_sets[n][1]().start()
        extra_sets[n][0]().start()
        extra_locals[n].start()
    if sent_back:
        back_start, back_finish = return_rows_copies(rows_ref, back_ref, s_back, me, blk)
        back_start()
    for t in range(1, 8):
        for p in range(parts):
            for up in (True, False):
                here = up_in if up else down_in
                ring(t - 1, up, p).wait_recv()
                value = (here[t - 1, p].astype(F32) + own(t, up, p)[...].astype(F32)).astype(BF)
                if t < 7:
                    here[t - 1, p] = value
                    ring(t, up, p).start()
                else:
                    total[0 if up else half : half if up else part, p * width : (p + 1) * width] = value
        if t == 5:
            for n in range(exchanged):
                extra_sets[n][1]().wait_recv()
                extra_sets[n][2]().start()
    if exchanged:
        near, far, relay = exchange(total, sums_ref, s_out, 0)
        local = pltpu.make_async_copy(total, sums_ref.at[0], s_local.at[0])
        far().start()
        near().start()
        local.start()
        far().wait_recv()
        relay().start()
        near().wait()
        far().wait_send()
        relay().wait()
        local.wait()
    else:
        local = pltpu.make_async_copy(total, sums_ref, s_local.at[0])
        local.start()
        local.wait()
    for n in range(exchanged):
        near, far, relay = extra_sets[n]
        near().wait()
        far().wait_send()
        relay().wait()
        extra_locals[n].wait()
    if sent_back:
        back_finish()
    for t in range(7):
        for p in range(parts):
            ring(t, True, p).wait_send()
            ring(t, False, p).wait_send()


def ring_sums(grad, extras, rows, collective_id):
    height, width = grad.shape
    part = height // 8
    parts = 2
    hbm = pl.BlockSpec(memory_space=pl.ANY)
    sems = lambda n: pltpu.SemaphoreType.DMA((2, n))
    four = lambda array: jax.ShapeDtypeStruct((4,) + array, BF)
    out_shape = [four((part, width)) if extras else jax.ShapeDtypeStruct((part, width), BF)]
    out_shape += [four(extra.shape) for extra in extras]
    operands = [grad, *extras]
    if rows is not None:
        out_shape.append(jax.ShapeDtypeStruct((2, 4 * rows.shape[1], rows.shape[2]), BF))
        operands.append(rows)
    buffers = pltpu.VMEM((7, parts, part // 2, width // parts), BF)
    return pl.pallas_call(
        functools.partial(ring_kernel, len(extras), rows is not None),
        in_specs=[pl.BlockSpec(memory_space=pltpu.VMEM)] + [hbm] * (len(operands) - 1),
        out_specs=[hbm] * len(out_shape),
        out_shape=out_shape,
        scratch_shapes=[
            buffers,
            buffers,
            pltpu.VMEM((part, width), BF),
            sems(7 * parts),
            sems(7 * parts),
            sems(3),
            sems(3 * max(1, len(extras))),
            sems(8),
            pltpu.SemaphoreType.DMA((1 + len(extras),)),
        ],
        compiler_params=params(collective_id=collective_id, has_side_effects=True),
        cost_estimate=pl.CostEstimate(flops=6 * 10**10, bytes_accessed=3 * height * width, transcendentals=0),
        name=f"ring_sums_{collective_id}",
    )(*operands)


def rotate_kernel(
    g_ref, base_ref, other_ref, first_ref, second_ref, master_ref, rows_ref, scale_ref, new_first_ref, new_second_ref,
    new_master_ref, rows_out_ref, g, base, other, firsts, seconds, masters, g_in, part, x_in, near, z_in, far, p_in, step, steps,
    back, back_in, steps_own, load, store, s_g, s_x, s_z, s_p, s_step, s_back, s_up, s_side, s_rows,
):
    blk = lax.axis_index("blk")
    zh, zl, xx = blk // 4, (blk // 2) % 2, blk % 2
    to_x = {"blk": blk + 1 - 2 * xx}
    to_z = {"blk": blk + 4 - 8 * zh}
    to_pair = {"blk": blk + 2 - 4 * zl}
    count = g.shape[0]
    half = UW // 2
    own = pl.ds(pl.multiple_of(zl * half, half), half)
    away = pl.ds(pl.multiple_of((1 - zl) * half, half), half)
    block = 4 * zh + xx
    loads = [
        (g_ref, g), (base_ref, base), (other_ref, other), (first_ref, firsts), (second_ref, seconds), (master_ref, masters),
    ]
    stores = [(firsts, new_first_ref), (seconds, new_second_ref), (masters, new_master_ref)]

    def loading(i, s):
        return pltpu.make_async_copy(loads[i][0].at[s], loads[i][1].at[s], load.at[i, s])

    def storing(i, s):
        return pltpu.make_async_copy(stores[i][0].at[s], stores[i][1].at[s], store.at[i, s])

    def send_g(s):
        return remote(g.at[s, :, away], g_in.at[s], s_g, s, to_pair)

    def send_x(s):
        return remote(part.at[s % 3, :, 1 - xx], x_in.at[s], s_x, s, to_x)

    def send_z(s):
        return remote(near.at[s % 3, 1 - zh], z_in.at[s], s_z, s, to_z)

    def send_p(s):
        return remote(far.at[s % 3], p_in.at[s], s_p, s, to_pair)

    def step_pair(s):
        return remote(step.at[s, :, away], steps.at[s, block + 2 * zl], s_step, s, to_pair)

    def step_z(s, a):
        return remote(steps.at[s, block + 2 * a], steps.at[s, block + 2 * a], s_up, 2 * s + a, to_z)

    def step_x(s, a):
        at = 2 * a + xx
        return remote(steps.at[s, at], steps.at[s, at], s_side, 4 * s + a, to_x)

    def send_back(s):
        return remote(back.at[s % 3], back_in.at[s], s_back, s, to_pair)

    for i in range(len(loads)):
        for s in range(count):
            loading(i, s).start()
    rows_start, rows_finish = return_rows_copies(rows_ref, rows_out_ref, s_rows, lax.axis_index("batch"), blk)
    greet_all()
    for s in range(count):
        loading(0, s).wait()
        send_g(s).start()
    rows_start()

    rows = base.shape[1]

    def tick(t, carry):
        def stage(lag, act):
            @pl.when((t >= lag) & (t < count + lag))
            def run():
                act(t - lag)

        def finish(s):
            send_back(s).wait_recv()
            loading(5, s).wait()
            for at, update in ((own, steps_own[s % 2]), (away, back_in[s].astype(F32))):
                value = masters[s, :, at]
                masters[s, :, at] = value - scale_ref[0] * (update + weight_decay * value)
            storing(2, s).start()

        def update(s):
            for a in range(4):
                step_x(s, a).wait_recv()
            whole = jnp.concatenate([steps[s, b] for b in range(8)], axis=0)
            steps_own[s % 2] = dot_plain(base[s], whole)

            @pl.when(s >= 3)
            def reuse():
                send_back(s - 3).wait_send()

            back[s % 3] = dot_plain(other[s], whole).astype(BF)
            send_back(s).start()

        def relay_x(s):
            for a in range(2):
                step_z(s, a).wait_recv()
            for a in range(4):
                step_x(s, a).start()

        def relay_z(s):
            step_pair(s).wait_recv()
            for a in range(2):
                step_z(s, a).start()

        def adam(s):
            send_p(s).wait_recv()
            loading(3, s).wait()
            loading(4, s).wait()
            mine = near[s % 3, zh, zl].astype(F32) + z_in[s, zl].astype(F32)
            for at, turned in ((own, mine), (away, p_in[s].astype(F32))):
                new_first = beta_one * firsts[s, :, at] + (1.0 - beta_one) * turned
                new_second = beta_two * seconds[s, :, at] + (1.0 - beta_two) * turned * turned
                firsts[s, :, at] = new_first
                seconds[s, :, at] = new_second
                moved = new_first / scale_ref[1] / (jnp.sqrt(new_second / scale_ref[2]) + adam_epsilon)
                step[s, :, at] = moved.astype(BF)
            storing(0, s).start()
            storing(1, s).start()
            steps[s, block + 2 * zl] = step[s, :, own]
            step_pair(s).start()

        def send_far(s):
            send_z(s).wait_recv()

            @pl.when(s >= 3)
            def reuse():
                send_p(s - 3).wait_send()

            far[s % 3] = (near[s % 3, zh, 1 - zl].astype(F32) + z_in[s, 1 - zl].astype(F32)).astype(BF)
            send_p(s).start()

        def send_near(s):
            send_x(s).wait_recv()

            @pl.when(s >= 3)
            def reuse():
                send_z(s - 3).wait_send()

            for a in range(2):
                for b in range(2):
                    at = 2 * a + b
                    total = part[s % 3, at, xx].astype(F32) + x_in[s, at].astype(F32)
                    near[s % 3, a, b] = total.astype(BF)
            send_z(s).start()

        def turn_slot(s):
            loading(1, s).wait()
            loading(2, s).wait()
            send_g(s).wait_recv()

            @pl.when(s >= 3)
            def reuse():
                send_x(s - 3).wait_send()

            turned = dot_first(base[s], g[s, :, own]) + dot_first(other[s], g_in[s])
            for b in range(8):
                part[s % 3, b // 2, b % 2] = turned[b * rows : (b + 1) * rows].astype(BF)
            send_x(s).start()

        stage(7, finish)
        stage(6, update)
        stage(5, relay_x)
        stage(4, relay_z)
        stage(3, adam)
        stage(2, send_far)
        stage(1, send_near)
        stage(0, turn_slot)
        return carry

    lax.fori_loop(0, count + 7, tick, 0)
    rows_finish()
    for s in range(count):
        send_g(s).wait_send()
        step_pair(s).wait_send()
        for a in range(2):
            step_z(s, a).wait_send()
        for a in range(4):
            step_x(s, a).wait_send()
        for i in range(3):
            storing(i, s).wait()
    for s in range(count - 3, count):
        send_x(s).wait_send()
        send_z(s).wait_send()
        send_p(s).wait_send()
        send_back(s).wait_send()


def rotate_slots(grads, base, other, first, second, master, tokens, scales):
    count, rows, width = grads.shape
    half = width // 2
    hbm = pl.BlockSpec(memory_space=pl.ANY)
    shape = jax.ShapeDtypeStruct(master.shape, F32)
    sems = lambda n: pltpu.SemaphoreType.DMA((2, n))
    return pl.pallas_call(
        rotate_kernel,
        in_specs=[hbm] * 7 + [pl.BlockSpec(memory_space=pltpu.SMEM)],
        out_specs=[hbm] * 4,
        out_shape=[shape] * 3 + [jax.ShapeDtypeStruct((2, 4 * tokens.shape[1], D), BF)],
        scratch_shapes=[
            pltpu.VMEM((count, rows, width), BF),
            pltpu.VMEM((count, rows, D), BF),
            pltpu.VMEM((count, rows, D), BF),
            pltpu.VMEM((count, rows, width), F32),
            pltpu.VMEM((count, rows, width), F32),
            pltpu.VMEM((count, rows, width), F32),
            pltpu.VMEM((count, rows, half), BF),
            pltpu.VMEM((3, 4, 2, rows, half), BF),
            pltpu.VMEM((count, 4, rows, half), BF),
            pltpu.VMEM((3, 2, 2, rows, half), BF),
            pltpu.VMEM((count, 2, rows, half), BF),
            pltpu.VMEM((3, rows, half), BF),
            pltpu.VMEM((count, rows, half), BF),
            pltpu.VMEM((count, rows, width), BF),
            pltpu.VMEM((count, 8, rows, half), BF),
            pltpu.VMEM((3, rows, half), BF),
            pltpu.VMEM((count, rows, half), BF),
            pltpu.VMEM((2, rows, half), F32),
            pltpu.SemaphoreType.DMA((6, count)),
            pltpu.SemaphoreType.DMA((3, count)),
            sems(count),
            sems(count),
            sems(count),
            sems(count),
            sems(count),
            sems(count),
            sems(2 * count),
            sems(4 * count),
            sems(8),
        ],
        compiler_params=params(collective_id=2, has_side_effects=True),
        name="rotate_slots",
    )(grads, base, other, first, second, master, tokens, scales)


def row_tables(lengths, row, count):
    everyone = jnp.stack(batch_pieces(lengths))
    holder = (row // 2) ^ lax.axis_index("batch")
    mine = jnp.sum(jnp.where(jnp.arange(4)[:, None, None] == holder, everyone, 0), axis=0)
    mine = jnp.where(row % 2 == 0, mine[:1], mine[1:])
    ends = doc_ends(mine)[0]
    places = jnp.arange(count, dtype=jnp.int32)
    begin = jnp.sum(jnp.where(places[:, None] >= ends[None, :], mine, 0), axis=1)
    start = jnp.where(places >= ends[NDOC - 2], places, begin)
    low = start.reshape(-1, TILE)[:, 0] // TILE
    cosine, sine = turn_tables(places - begin)
    cosine = jnp.tile(cosine, (1, 4))
    sine = jnp.tile(jnp.concatenate([-sine, sine], axis=1), (1, 2))
    return start, low, cosine, sine


def row_groups(
    tokens,
    cotangent,
    lengths,
    unit_owner,
    step_count,
    master,
    first,
    second,
    bases,
    small,
    small_first,
    small_second,
):
    me, blk = lax.axis_index("batch"), lax.axis_index("blk")
    count = tokens.shape[1] * 8
    learn_rate = 2.0 / D**0.5
    slots = lambda array: jnp.transpose(array, (1, 0, 2))
    master_slots = slots(master)

    groups = (8, 4, count // 32, D)

    place = ((unit_owner // 9) ^ me) * 9 + unit_owner % 9
    master_low = master_slots.astype(BF)
    pieces, x_own = begin(master_low, tokens)
    start, low, cosine, sine = row_tables(lengths, blk, count)
    start = start.reshape(1, count)
    attn_shard, gate_up_shard, down_shard = pick_units(place, me, master_low, pieces)
    attn, down, x, dy_own, dy = gather(attn_shard, down_shard, x_own, cotangent)
    down = down.reshape(D, FQ)
    gate_up = lax.all_gather(after(gate_up_shard, attn), "blk", axis=0, tiled=True)
    attn, x, dy = attn.reshape(D, 4 * QW), x.reshape(count, D), dy.reshape(count, D)
    base = slots(bases).astype(BF)

    gain_one = small[:D].reshape(1, D)
    gain_two = small[D : 2 * D].reshape(1, D)
    head_gain = small[2 * D : 2 * D + VD].reshape(VD, 1)
    mixer, mixer_back = jax.vjp(mix_value, small[2 * D + VD :].reshape(4, HD))
    lam = mixer.reshape(1)

    n1, q, k, v = project(x, attn, gain_one, cosine, sine)
    a_own, maps, log_mass = attend(low, lam, q, k, v, start, head_gain)
    n2, x1 = middle(a_own, x, attn, gain_two)
    base_other = swap_blk(after(base, gate_up), 2)
    acts, out_part, dx1, dx1_low, da, gain_two_grad = feed(
        n2, dy, gate_up, down, x1, dy_own, attn, gain_two
    )
    gain_two_grad = gain_two_grad.reshape(D)

    near_out = near_sum(out_part.reshape(groups), me)
    down_sums = lax.psum_scatter(
        dot_first(dy, acts[:, 2 * FQ :]).astype(BF), "blk", scatter_dimension=0, tiled=True
    )
    gate_up_grad = dot_first(n2, acts[:, : 2 * FQ]).astype(BF)
    out_grad = dot_first(dx1_low, a_own).astype(BF)
    da = after(da, (near_out, gate_up_grad, out_grad, base_other))
    dq, dk, dv, head_gain_sums, mixer_sums = attend_back(
        low, lam, q, k, v, start, head_gain, maps, log_mass, da, cosine, sine
    )
    dqkv = jnp.concatenate([dq, dk, dv], axis=1)
    attn_grad = jnp.concatenate([dot_first(n1, dqkv).astype(BF), out_grad], axis=1)
    near_dn1 = near_sum(dot_last(dqkv, attn[:, : 3 * QW]).astype(BF).reshape(groups), me)
    out_rows = (x1 + far_sum(near_out, me)).astype(BF)
    gate_up_grad = after(gate_up_grad, (near_dn1, attn_grad))
    gate_up_sums, block_out = ring_sums(gate_up_grad, [], out_rows, 6)
    attn_pieces, gate_up_pieces, down_pieces = ring_sums(attn_grad, [gate_up_sums, down_sums], None, 7)

    dn1 = far_sum(near_dn1, me)
    x_f = x_own.astype(F32)
    r1 = lax.rsqrt(jnp.mean(x_f * x_f, axis=-1, keepdims=True) + norm_epsilon)
    t1 = x_f * r1
    e1 = dn1 * gain_one
    dx = dx1 + r1 * (e1 - t1 * jnp.mean(e1 * t1, axis=-1, keepdims=True))
    gain_one_grad = jnp.sum(dn1 * t1, axis=(0, 1))

    (mixers_grad,) = mixer_back(jnp.sum(mixer_sums))
    small_local = jnp.concatenate(
        [gain_one_grad, gain_two_grad, jnp.sum(head_gain_sums, axis=(0, 2)), mixers_grad.reshape(-1)]
    )
    small_grads = sum_everywhere(small_local)

    unit_of = inverse_order(unit_owner)
    units = lax.dynamic_slice_in_dim(unit_of, me * 9, 9)
    grads = place_units(units, me, attn_pieces, gate_up_pieces, down_pieces)

    steps_done = step_count[0].astype(F32)
    scales = jnp.stack([jnp.float32(learn_rate), 1.0 - beta_one**steps_done, 1.0 - beta_two**steps_done])
    new_first, new_second, new_master, input_grad = rotate_slots(
        grads, base, base_other, slots(first), slots(second), master_slots, dx.astype(BF), scales
    )
    new_small_first = beta_one * small_first + (1.0 - beta_one) * small_grads
    new_small_second = beta_two * small_second + (1.0 - beta_two) * small_grads * small_grads
    new_small = small - small_rate * adam_step(new_small_first, new_small_second, steps_done)
    return (
        block_out,
        input_grad,
        slots(new_master),
        slots(new_first),
        slots(new_second),
        small_grads,
        new_small,
        new_small_first,
        new_small_second,
    )


def solution(mesh):
    in_specs = (
        P("batch", "blk", None),
        P("batch", "blk", None),
        P("batch", None),
        P(),
        P(),
        P("blk", "batch", None),
        P("blk", "batch", None),
        P("blk", "batch", None),
        P("blk", "batch", None),
        P(),
        P(),
        P(),
    )
    out_specs = (
        P("batch", "blk", None),
        P("batch", "blk", None),
        P("blk", "batch", None),
        P("blk", "batch", None),
        P("blk", "batch", None),
        P(),
        P(),
        P(),
        P(),
    )
    by_rows = mesh.shape["blk"] == 8 and mesh.shape["batch"] == 4
    body = row_groups if by_rows else any_mesh
    return jax.shard_map(body, mesh=mesh, in_specs=in_specs, out_specs=out_specs, check_vma=False)
```

```python
import functools

import jax
import jax.numpy as jnp
from jax import lax
from jax.experimental import pallas as pl
from jax.experimental.pallas import tpu as pltpu
from jax.sharding import PartitionSpec as P

D = 1536
H = 12
HD = 64
VD = 128
FF = 4096
UW = 512
NDOC = 6
UNITS = 36


norm_epsilon = 1e-05
lambda_start = 0.2
rope_base = 10000.0
masked_fill = -1000000000.0
beta_one = 0.9
beta_two = 0.95
adam_epsilon = 1e-08
weight_decay = 0.01
small_rate = 1.0


def from_behind(shard, axis, by):
    count = lax.axis_size(axis)
    return lax.ppermute(shard, axis, [(i, (i + by) % count) for i in range(count)])


def root_norm(values, gain):
    return (
        values * lax.rsqrt(jnp.mean(values * values, axis=-1, keepdims=True) + norm_epsilon) * gain
    )


def mix_value(mixers):
    return (
        jnp.exp(jnp.sum(mixers[0] * mixers[1]))
        - jnp.exp(jnp.sum(mixers[2] * mixers[3]))
        + lambda_start
    )


def head_mix(maps_out, head_gain, mixer):
    combined = maps_out[:, :, 0] - mixer * maps_out[:, :, 1]
    normed = (
        combined
        * lax.rsqrt(jnp.mean(combined * combined, axis=-1, keepdims=True) + norm_epsilon)
        * head_gain
        * (1.0 - lambda_start)
    )
    rows_count, heads, positions, width = normed.shape
    return jnp.transpose(normed, (0, 2, 1, 3)).reshape(rows_count, positions, heads * width)


def gated_unit(gate, up):
    return jax.nn.silu(gate) * up


def doc_ends(lengths):
    count = lengths.shape[1]
    ends = [lengths[:, 0]]
    for j in range(1, count):
        ends.append(ends[-1] + lengths[:, j])
    return jnp.stack(ends, axis=1)


def document_places(lengths, places):
    ends = doc_ends(lengths)
    starts = ends - lengths
    segment = jnp.sum((places[None, :, None] >= ends[:, None, :]).astype(jnp.int32), axis=2)
    chosen = segment[:, :, None] == jnp.arange(lengths.shape[1], dtype=jnp.int32)[None, None, :]
    offset = jnp.sum(jnp.where(chosen, starts[:, None, :], 0), axis=2)
    return (segment, places[None, :] - offset)


def allowed(seg_query, place_query, seg_key, place_key, last):
    same = seg_query[:, :, None] == seg_key[:, None, :]
    causal = place_key[None, None, :] <= place_query[None, :, None]
    itself = place_key[None, None, :] == place_query[None, :, None]
    return same & causal & ((seg_query[:, :, None] < last) | itself)


def turn_tables(position):
    rates = rope_base ** (-2.0 * jnp.arange(HD // 2, dtype=jnp.float32) / HD)
    angle = position.astype(jnp.float32)[..., None] * rates
    return (jnp.cos(angle), jnp.sin(angle))


def rotate(values, cosine, sine):
    half = values.shape[-1] // 2
    front = values[..., :half]
    back = values[..., half:]
    return jnp.concatenate([front * cosine - back * sine, back * cosine + front * sine], axis=-1)


def adam_step(first_new, second_new, steps_done):
    return (
        first_new
        / (1.0 - beta_one**steps_done)
        / (jnp.sqrt(second_new / (1.0 - beta_two**steps_done)) + adam_epsilon)
    )


def take_units(stacked, order):
    parts = [lax.dynamic_slice_in_dim(stacked, order[i], 1, axis=1) for i in range(UNITS)]
    return jnp.concatenate(parts, axis=1)


def inverse_order(owner):
    numbers = jnp.arange(UNITS, dtype=jnp.int32)
    return jnp.sum(jnp.where(owner[None, :] == numbers[:, None], numbers[None, :], 0), axis=1)


def contract_rows(left, right):
    return lax.dot_general(
        left, right, (((1,), (1,)), ((), ())), preferred_element_type=jnp.float32
    )


def any_mesh(
    tokens,
    cotangent,
    lengths,
    unit_owner,
    step_count,
    master,
    first,
    second,
    bases,
    small,
    small_first,
    small_second,
):
    rows_count, seq_part, width = tokens.shape
    token_count = rows_count * seq_part
    axis_count = lax.axis_size("blk")
    axis_place = lax.axis_index("blk")
    rows_part = master.shape[0]
    scale = HD ** (-0.5)
    highest = lax.Precision.HIGHEST
    learn_rate = 2.0 / D**0.5
    every_slot = lax.all_gather(master.astype(jnp.bfloat16), "batch", axis=1, tiled=True)
    by_unit = take_units(every_slot, unit_owner).reshape(rows_part, UNITS * UW)
    attention_whole = lax.all_gather(by_unit[:, : 4 * D], "blk", axis=0, tiled=True)
    gate_whole = lax.all_gather(by_unit[:, 4 * D : 4 * D + 2 * FF], "blk", axis=0, tiled=True)
    down_whole = lax.all_gather(by_unit[:, 4 * D + 2 * FF :], "blk", axis=0, tiled=True)
    places = axis_place * seq_part + jnp.arange(seq_part, dtype=jnp.int32)
    segment, position = document_places(lengths, places)
    cosine, sine = turn_tables(position)
    cosine = cosine[:, :, None, None, :]
    sine = sine[:, :, None, None, :]
    residual = tokens.astype(jnp.float32)
    gain_one = small[:D]
    gain_two = small[D : 2 * D]
    head_gain = small[2 * D : 2 * D + VD]
    mixer, mixer_back = jax.vjp(mix_value, small[2 * D + VD :].reshape(4, HD))
    normed_exact, norm_one_back = jax.vjp(root_norm, residual, gain_one)
    normed_one = normed_exact.astype(jnp.bfloat16).reshape(token_count, D)
    projected = jnp.dot(normed_one, attention_whole[:, : 3 * D], preferred_element_type=jnp.float32)
    query = rotate(projected[:, :D].reshape(rows_count, seq_part, H, 2, HD), cosine, sine).astype(
        jnp.bfloat16
    )
    key_own = (
        rotate(projected[:, D : 2 * D].reshape(rows_count, seq_part, H, 2, HD), cosine, sine)
        .astype(jnp.bfloat16)
        .reshape(rows_count, seq_part, D)
    )
    value_own = projected[:, 2 * D :].astype(jnp.bfloat16).reshape(rows_count, seq_part, D)
    best = jnp.full((rows_count, H, 2, seq_part), masked_fill, jnp.float32)
    key_piece = lax.all_gather(key_own, "blk", axis=1, tiled=True)
    value_piece = lax.all_gather(value_own, "blk", axis=1, tiled=True)
    count = key_piece.shape[1]
    key_places = jnp.arange(count, dtype=jnp.int32)
    key_segment, unused = document_places(lengths, key_places)
    mask = allowed(segment, places, key_segment, key_places, NDOC - 1)[:, None, None]
    keys = key_piece.reshape(rows_count, count, H, 2, HD)
    values = value_piece.reshape(rows_count, count, H, VD)
    scores = (
        jnp.einsum("rqhcd,rkhcd->rhcqk", query, keys, preferred_element_type=jnp.float32) * scale
    )
    scores = jnp.where(mask, scores, masked_fill)
    top = jnp.maximum(best, jnp.max(scores, axis=-1))
    shares = jnp.where(mask, jnp.exp(scores - top[..., None]), 0.0)
    mass = jnp.sum(shares, axis=-1)
    summed = jnp.einsum(
        "rhcqk,rkhe->rhcqe", shares.astype(jnp.bfloat16), values, preferred_element_type=jnp.float32
    )
    best, mass, summed = (top, mass, summed)
    maps_out = summed / mass[..., None]
    log_mass = best + jnp.log(mass)
    mixed_exact, mix_back = jax.vjp(head_mix, maps_out, head_gain, mixer)
    mixed = mixed_exact.astype(jnp.bfloat16).reshape(token_count, D)
    middle = residual.reshape(token_count, D) + contract_rows(mixed, attention_whole[:, 3 * D :])
    normed_two_exact, norm_two_back = jax.vjp(root_norm, middle, gain_two)
    normed_two = normed_two_exact.astype(jnp.bfloat16)
    gate_up = jnp.dot(normed_two, gate_whole, preferred_element_type=jnp.float32)
    hidden_exact, gated_back = jax.vjp(gated_unit, gate_up[:, :FF], gate_up[:, FF:])
    hidden = hidden_exact.astype(jnp.bfloat16)
    result = middle + contract_rows(hidden, down_whole)
    block_out = result.astype(jnp.bfloat16).reshape(rows_count, seq_part, D)
    output_grad = cotangent.reshape(token_count, D)
    hidden_grad = jnp.dot(output_grad, down_whole, preferred_element_type=jnp.float32)
    gate_grad, up_grad = gated_back(hidden_grad)
    gate_up_grad = jnp.concatenate([gate_grad, up_grad], axis=1).astype(jnp.bfloat16)
    normed_two_grad = contract_rows(gate_up_grad, gate_whole)
    middle_part, gain_two_grad = norm_two_back(normed_two_grad)
    middle_grad = output_grad.astype(jnp.float32) + middle_part
    middle_low = middle_grad.astype(jnp.bfloat16)
    mixed_grad = jnp.dot(
        middle_low, attention_whole[:, 3 * D :], preferred_element_type=jnp.float32
    )
    maps_grad, head_gain_grad, mixer_grad = mix_back(mixed_grad.reshape(rows_count, seq_part, D))
    maps_low = maps_grad.astype(jnp.bfloat16)
    offset_term = jnp.sum(maps_low.astype(jnp.float32) * maps_out, axis=-1)

    def circle(turn_index, carry):
        moving, moving_grad, query_grad = carry
        source = (axis_place - turn_index) % axis_count
        key_places = source * seq_part + jnp.arange(seq_part, dtype=jnp.int32)
        key_segment, unused = document_places(lengths, key_places)
        mask = allowed(segment, places, key_segment, key_places, NDOC - 1)[:, None, None]
        keys = moving[0].astype(jnp.bfloat16).reshape(rows_count, seq_part, H, 2, HD)
        values = moving[1].astype(jnp.bfloat16).reshape(rows_count, seq_part, H, VD)
        scores = (
            jnp.einsum("rqhcd,rkhcd->rhcqk", query, keys, preferred_element_type=jnp.float32)
            * scale
        )
        shares = jnp.where(mask, jnp.exp(scores - log_mass[..., None]), 0.0)
        value_term = jnp.einsum(
            "rhcqk,rhcqe->rkhe",
            shares.astype(jnp.bfloat16),
            maps_low,
            preferred_element_type=jnp.float32,
        )
        share_grad = jnp.einsum(
            "rhcqe,rkhe->rhcqk", maps_low, values, preferred_element_type=jnp.float32
        )
        score_low = (shares * (share_grad - offset_term[..., None])).astype(jnp.bfloat16)
        query_grad = query_grad + jnp.einsum(
            "rhcqk,rkhcd->rqhcd", score_low, keys, preferred_element_type=jnp.float32
        )
        key_term = jnp.einsum(
            "rhcqk,rqhcd->rkhcd", score_low, query, preferred_element_type=jnp.float32
        )
        update = jnp.stack(
            [key_term.reshape(rows_count, seq_part, D), value_term.reshape(rows_count, seq_part, D)]
        )
        moving_grad = moving_grad + update
        moving, moving_grad = (
            from_behind(moving.astype(jnp.bfloat16), "blk", 1).astype(moving.dtype),
            from_behind(moving_grad.astype(jnp.bfloat16), "blk", 1).astype(moving_grad.dtype),
        )
        return (moving, moving_grad, query_grad)

    circle_start = (
        jnp.stack([key_own, value_own]).astype(jnp.float32),
        jnp.zeros((2, rows_count, seq_part, D), jnp.float32),
        jnp.zeros((rows_count, seq_part, H, 2, HD), jnp.float32),
    )
    moving, moving_grad, query_grad = lax.fori_loop(0, axis_count, circle, circle_start)
    key_grad = moving_grad[0].reshape(rows_count, seq_part, H, 2, HD) * scale
    query_pre = rotate(query_grad * scale, cosine, -sine).reshape(token_count, D)
    key_pre = rotate(key_grad, cosine, -sine).reshape(token_count, D)
    projected_grad = jnp.concatenate(
        [query_pre, key_pre, moving_grad[1].reshape(token_count, D)], axis=1
    ).astype(jnp.bfloat16)
    normed_one_grad = contract_rows(projected_grad, attention_whole[:, : 3 * D])
    residual_part, gain_one_grad = norm_one_back(normed_one_grad.reshape(rows_count, seq_part, D))
    input_grad = (middle_grad.reshape(rows_count, seq_part, D) + residual_part).astype(jnp.bfloat16)
    (mixers_grad,) = mixer_back(mixer_grad)
    small_local = jnp.concatenate(
        [gain_one_grad, gain_two_grad, head_gain_grad, mixers_grad.reshape(-1)]
    )
    small_grads = lax.psum(small_local, ("batch", "blk"))
    right_side = jnp.concatenate([projected_grad, mixed, gate_up_grad, hidden], axis=1)
    left_sides = (normed_one, middle_low, normed_two, output_grad)
    bounds = (0, 3 * D, 4 * D, 4 * D + 2 * FF, 4 * D + 3 * FF)
    slot_order = inverse_order(unit_owner)
    parts = []
    for group in range(4):
        left_rows = left_sides[group]
        parts.append(
            lax.dot_general(
                left_rows,
                right_side[:, bounds[group] : bounds[group + 1]],
                (((0,), (0,)), ((), ())),
                preferred_element_type=jnp.float32,
            )
        )
    row_sums = lax.psum_scatter(
        jnp.concatenate(parts, axis=1).astype(jnp.bfloat16), "blk", scatter_dimension=0, tiled=True
    ).astype(jnp.float32)
    placed = take_units(row_sums.reshape(rows_part, UNITS, UW), slot_order)
    grad_slots = lax.psum_scatter(
        placed.astype(jnp.bfloat16), "batch", scatter_dimension=1, tiled=True
    ).astype(jnp.float32)
    columns = bases
    turned = lax.psum_scatter(
        jnp.einsum("ksa,ksn->asn", columns, grad_slots, precision=highest).astype(jnp.bfloat16),
        "blk",
        scatter_dimension=0,
        tiled=True,
    ).astype(jnp.float32)
    steps_done = step_count[0].astype(jnp.float32)
    new_first = beta_one * first + (1.0 - beta_one) * turned
    new_second = beta_two * second + (1.0 - beta_two) * turned * turned
    normalized = adam_step(new_first, new_second, steps_done)
    columns = bases
    update = jnp.zeros_like(master) + jnp.einsum(
        "ksa,asn->ksn",
        columns,
        lax.all_gather(normalized.astype(jnp.bfloat16), "blk", axis=0, tiled=True).astype(
            jnp.float32
        ),
        precision=highest,
    )
    new_master = master - learn_rate * (update + weight_decay * master)
    new_small_first = beta_one * small_first + (1.0 - beta_one) * small_grads
    new_small_second = beta_two * small_second + (1.0 - beta_two) * small_grads * small_grads
    new_small = small - small_rate * adam_step(new_small_first, new_small_second, steps_done)
    return (
        block_out,
        input_grad,
        new_master,
        new_first,
        new_second,
        small_grads,
        new_small,
        new_small_first,
        new_small_second,
    )


BF = jnp.bfloat16
F32 = jnp.float32
TILE = 256
HEADS = 3
QW = HEADS * VD
FQ = FF // 4
VMEM_LIMIT = 56 * 2**20


def params(limit=VMEM_LIMIT, **more):
    return pltpu.CompilerParams(vmem_limit_bytes=limit, **more)


def dot_last(left, right):
    return lax.dot_general(left, right, (((1,), (1,)), ((), ())), preferred_element_type=F32)


def dot_first(left, right):
    return lax.dot_general(left, right, (((0,), (0,)), ((), ())), preferred_element_type=F32)


def dot_plain(left, right):
    return jnp.dot(left, right, preferred_element_type=F32)


def swap_core(piece):
    return lax.ppermute(piece, "batch", [(i, i ^ 1) for i in range(4)])


def swap_y(piece):
    return lax.ppermute(piece, "batch", [(i, i ^ 2) for i in range(4)])


def sum_everywhere(values):
    values = values + swap_core(values)
    values = values + swap_y(values)
    for bit in (1, 2, 4):
        values = values + lax.ppermute(values, "blk", [(i, i ^ bit) for i in range(8)])
    return values


def after(values, earlier):
    return lax.optimization_barrier((values, earlier))[0]


def ring_place(blk):
    side = blk % 2
    return (1 - side) * (blk // 2) + side * (7 - blk // 2)


def ring_owner(place):
    place = (place + 16) % 8
    side = place // 4
    return 2 * ((1 - side) * place + side * (7 - place)) + side


def batch_pieces(piece):
    far = swap_y(piece)
    return (piece, swap_core(piece), far, swap_core(far))


def swap_blk(piece, bit):
    return lax.ppermute(piece, "blk", [(i, i ^ bit) for i in range(8)])


MESH = pl.DeviceIdType.MESH


def greet(devices):
    barrier = pltpu.get_barrier_semaphore()
    for device in devices:
        pl.semaphore_signal(barrier, inc=1, device_id=device, device_id_type=MESH)
    pl.semaphore_wait(barrier, len(devices))


def greet_all():
    barrier = pltpu.get_barrier_semaphore()
    me, blk = lax.axis_index("batch"), lax.axis_index("blk")

    def signal(n, carry):
        at = (me * 8 + blk + n) % 32
        pl.semaphore_signal(barrier, inc=1, device_id=(at // 8, at % 8), device_id_type=MESH)
        return carry

    lax.fori_loop(1, 32, signal, 0)
    pl.semaphore_wait(barrier, 31)


def remote(source, target, sems, at, device):
    return pltpu.make_async_remote_copy(
        src_ref=source,
        dst_ref=target,
        send_sem=sems.at[0, at],
        recv_sem=sems.at[1, at],
        device_id=device,
        device_id_type=MESH,
    )


def to_group_copies(source, between, target, s_batch, s_blk, me, blk):
    size = target.shape[1]

    def over_group(n):
        other = (me + n) % 4
        return pltpu.make_async_remote_copy(
            src_ref=source.at[:, pl.ds(pl.multiple_of(other * size, size), size)],
            dst_ref=between.at[pl.ds(2 * me, 2)],
            send_sem=s_batch.at[0, n],
            recv_sem=s_batch.at[1, 4 - n],
            device_id={"batch": other},
            device_id_type=MESH,
        )

    def group_arrival(n):
        other = (me + n) % 4
        return pltpu.make_async_remote_copy(
            src_ref=source.at[:, pl.ds(0, size)],
            dst_ref=between.at[pl.ds(2 * other, 2)],
            send_sem=s_batch.at[0, n],
            recv_sem=s_batch.at[1, n],
            device_id={"batch": other},
            device_id_type=MESH,
        )

    def over_blk(n, i, local, remote_act):
        other = (me + n) % 4
        row = 2 * other + i
        if n == 0:
            piece = source.at[i, pl.ds(pl.multiple_of(me * size, size), size)]
        else:
            piece = between.at[row]

        @pl.when(row == blk)
        def stay():
            local(pltpu.make_async_copy(piece, target.at[blk], s_blk.at[0, 2 * n + i]))

        @pl.when(row != blk)
        def go():
            remote_act(
                pltpu.make_async_remote_copy(
                    src_ref=piece,
                    dst_ref=target.at[blk],
                    send_sem=s_blk.at[0, 2 * n + i],
                    recv_sem=s_blk.at[1, blk],
                    device_id={"blk": row},
                    device_id_type=MESH,
                )
            )

    def start_group():
        for n in (2, 3, 1):
            over_group(n).start()

    def start_blk(n):
        if n:
            group_arrival(n).wait_recv()
        for i in range(2):
            over_blk(n, i, lambda copy: copy.start(), lambda copy: copy.start())

    def finish():
        for n in (1, 2, 3):
            over_group(n).wait_send()
        for n in range(4):
            for i in range(2):
                over_blk(n, i, lambda copy: copy.wait(), lambda copy: copy.wait_send())
        for k in range(8):

            @pl.when(blk != k)
            def arrived():
                pltpu.make_async_remote_copy(
                    src_ref=between.at[0],
                    dst_ref=target.at[k],
                    send_sem=s_blk.at[0, 0],
                    recv_sem=s_blk.at[1, k],
                    device_id={"blk": k},
                    device_id_type=MESH,
                ).wait_recv()

    return start_group, start_blk, finish


def begin_kernel(
    master_ref, tokens_ref, grad_ref, bases_ref, pieces_ref, x_ref, dy_ref, base_ref, wide, narrow, x_between,
    dy_between, s_core, s_y, s_relay, s_x, s_x2, s_dy, s_dy2, s_load, s_store,
):
    me, blk = lax.axis_index("batch"), lax.axis_index("blk")
    y, core = me // 2, me % 2
    to_core = {"batch": y * 2 + 1 - core}
    to_y = {"batch": (1 - y) * 2 + core}
    x_group, x_blk, x_finish = to_group_copies(tokens_ref, x_between, x_ref, s_x, s_x2, me, blk)
    dy_group, dy_blk, dy_finish = to_group_copies(grad_ref, dy_between, dy_ref, s_dy, s_dy2, me, blk)
    slots = bases_ref.shape[0]

    def load(n):
        return pltpu.make_async_copy(bases_ref.at[n], wide.at[n % 2], s_load.at[n])

    def store(n):
        return pltpu.make_async_copy(narrow.at[n % 2], base_ref.at[n], s_store.at[n])

    def cast(n):
        load(n).wait()
        if n >= 2:
            store(n - 2).wait()
        narrow[n % 2] = wide[n % 2].astype(BF)
        store(n).start()
        if n + 2 < slots:
            load(n + 2).start()

    def copies(c):
        at = pl.ds(3 * c, 3)
        return (
            lambda: remote(master_ref.at[at], pieces_ref.at[0, at], s_core, c, to_core),
            lambda: remote(master_ref.at[at], pieces_ref.at[1, at], s_y, c, to_y),
            lambda: remote(pieces_ref.at[1, at], pieces_ref.at[2, at], s_relay, c, to_core),
        )

    greet([{"batch": (me + n) % 4} for n in (1, 2, 3)] + [{"blk": (blk + n) % 8} for n in range(1, 8)])
    x_group()
    load(0).start()
    load(1).start()
    x_blk(0)
    cast(0)
    cast(1)
    for c in range(3):
        copies(c)[1]().start()
    dy_group()
    for c in range(3):
        copies(c)[0]().start()
    for n in (1, 2, 3):
        x_blk(n)
    for n in range(2, slots):
        cast(n)
    store(slots - 2).wait()
    store(slots - 1).wait()
    for n in range(4):
        dy_blk(n)
    for c in range(3):
        copies(c)[1]().wait_recv()
        copies(c)[2]().start()
    for c in range(3):
        near, far, relay = copies(c)
        near().wait()
        far().wait_send()
        relay().wait()
    x_finish()
    dy_finish()


def begin(master, tokens, cotangent, bases):
    hbm = pl.BlockSpec(memory_space=pl.ANY)
    size = tokens.shape[1] // 4
    sems = lambda n: pltpu.SemaphoreType.DMA((2, n))
    return pl.pallas_call(
        begin_kernel,
        in_specs=[hbm] * 4,
        out_specs=[hbm] * 4,
        out_shape=[
            jax.ShapeDtypeStruct((3,) + master.shape, BF),
            jax.ShapeDtypeStruct((8, size, D), BF),
            jax.ShapeDtypeStruct((8, size, D), BF),
            jax.ShapeDtypeStruct(bases.shape, BF),
        ],
        scratch_shapes=[
            pltpu.VMEM((2,) + bases.shape[1:], F32),
            pltpu.VMEM((2,) + bases.shape[1:], BF),
            pltpu.VMEM((8, size, D), BF),
            pltpu.VMEM((8, size, D), BF),
            sems(3),
            sems(3),
            sems(3),
            sems(4),
            sems(8),
            sems(4),
            sems(8),
            pltpu.SemaphoreType.DMA((bases.shape[0],)),
            pltpu.SemaphoreType.DMA((bases.shape[0],)),
        ],
        compiler_params=params(collective_id=3, has_side_effects=True),
        name="begin",
    )(master, tokens, cotangent, bases)


def gather_kernel(
    shard_ref, down_ref, x_ref, dy_ref, attn_ref, downs_ref, xs_ref, dys_ref, outs_ref, s_local, s_up, s_down, s_up2,
    s_down2, s_x, s_dys, s_out,
):
    me, blk = lax.axis_index("batch"), lax.axis_index("blk")
    y, core = me // 2, me % 2
    to_core = {"batch": y * 2 + 1 - core}
    to_y = {"batch": (1 - y) * 2 + core}
    place = ring_place(blk)
    after_me, before_me = {"blk": ring_owner(place + 1)}, {"blk": ring_owner(place - 1)}
    half = shard_ref.shape[0] // 2
    sub = half // 2
    far_slab = (1 - y) * 2 + core

    def ring(t, up, part, second=False):
        owner = ring_owner(place - t) if up else ring_owner(place + t)
        at = pl.ds((0 if up else half) + part * sub, sub)
        target = (downs_ref if second else attn_ref).at[owner, at]
        source = (down_ref if second else shard_ref).at[at] if t == 0 else target
        sems = (s_up2 if up else s_down2) if second else (s_up if up else s_down)
        return remote(source, target, sems, 2 * t + part, after_me if up else before_me)

    def spread(source, whole, sems, c):
        at = pl.ds(4 * c, 4)
        return (
            lambda: remote(source.at[at], whole.at[at, me], sems, c, to_core),
            lambda: remote(source.at[at], whole.at[at, me], sems, 2 + c, to_y),
            lambda: remote(whole.at[at, far_slab], whole.at[at, far_slab], sems, 4 + c, to_core),
        )

    mine = attn_ref.at[:, :, pl.ds(3 * QW, QW)]
    out = (
        lambda: remote(mine, outs_ref.at[0], s_out, 0, to_core),
        lambda: remote(mine, outs_ref.at[1], s_out, 1, to_y),
        lambda: remote(outs_ref.at[1], outs_ref.at[2], s_out, 2, to_core),
    )
    locals_ = [
        pltpu.make_async_copy(shard_ref, attn_ref.at[blk], s_local.at[0]),
        pltpu.make_async_copy(x_ref, xs_ref.at[:, me], s_local.at[1]),
        pltpu.make_async_copy(dy_ref, dys_ref.at[:, me], s_local.at[2]),
        pltpu.make_async_copy(down_ref, downs_ref.at[blk], s_local.at[3]),
    ]
    both = ((x_ref, xs_ref, s_x), (dy_ref, dys_ref, s_dys))
    greet((to_core, to_y, after_me, before_me))
    for part in range(2):
        ring(0, True, part).start()
        ring(0, False, part).start()
    for source, whole, sems in both:
        for c in range(2):
            spread(source, whole, sems, c)[1]().start()
    for source, whole, sems in both:
        for c in range(2):
            spread(source, whole, sems, c)[0]().start()
    for copy in locals_:
        copy.start()

    def relay(n):
        source, whole, sems = both[n // 2]
        copies = spread(source, whole, sems, n % 2)
        copies[1]().wait_recv()
        copies[2]().start()

    for t in range(1, 7):
        for part in range(2):
            for up in (True, False):
                ring(t - 1, up, part).wait_recv()
                ring(t, up, part).start()
    for part in range(2):
        for up in (True, False):
            ring(0, up, part, True).start()
            ring(6, up, part).wait_recv()
    locals_[0].wait()
    out[1]().start()
    out[0]().start()
    for t in range(1, 7):
        for part in range(2):
            for up in (True, False):
                ring(t - 1, up, part, True).wait_recv()
                ring(t, up, part, True).start()
        if t in (3, 4):
            relay(t - 3)
    for part in range(2):
        for up in (True, False):
            ring(6, up, part, True).wait_recv()
    relay(2)
    relay(3)
    out[1]().wait_recv()
    out[2]().start()
    for t in range(7):
        for part in range(2):
            for up in (True, False):
                ring(t, up, part).wait_send()
                ring(t, up, part, True).wait_send()
    for source, whole, sems in both:
        for c in range(2):
            near, far, again = spread(source, whole, sems, c)
            near().wait()
            far().wait_send()
            again().wait()
    out[0]().wait()
    out[1]().wait_send()
    out[2]().wait()
    for copy in locals_[1:]:
        copy.wait()


def gather(shard, down, x, dy):
    hbm = pl.BlockSpec(memory_space=pl.ANY)
    size = x.shape[1]
    sems = lambda n: pltpu.SemaphoreType.DMA((2, n))
    whole = jax.ShapeDtypeStruct((8, 4, size, D), BF)
    return pl.pallas_call(
        gather_kernel,
        in_specs=[pl.BlockSpec(memory_space=pltpu.VMEM)] * 4,
        out_specs=[hbm] * 5,
        out_shape=[
            jax.ShapeDtypeStruct((8,) + shard.shape, BF),
            jax.ShapeDtypeStruct((8,) + down.shape, BF),
            whole,
            whole,
            jax.ShapeDtypeStruct((3, 8, shard.shape[0], QW), BF),
        ],
        scratch_shapes=[pltpu.SemaphoreType.DMA((4,))] + [sems(14)] * 4 + [sems(6), sems(6), sems(3)],
        compiler_params=params(collective_id=4, has_side_effects=True),
        name="gather",
    )(shard, down, x, dy)


def attention_pieces(me):
    pieces = []
    for matrix in range(4):
        for j in range(HEADS):
            block = HEADS * me + j
            pieces.append((3 * matrix + block // 4, block % 4, HEADS * matrix + j))
    return pieces


def pick_kernel(place_ref, me_ref, own, pieces, attn_ref, ffn_ref, down_ref, sems):
    me = me_ref[0]
    waits = []

    def begin(unit, source, target, sem):
        at = place_ref[unit]
        for other, ref in enumerate((own, pieces.at[0], pieces.at[1], pieces.at[2])):

            @pl.when(at // 9 == other)
            def start():
                pltpu.make_async_copy(source(ref.at[at % 9]), target, sem).start()

        waits.append(pltpu.make_async_copy(source(own.at[0]), target, sem))

    for i, (unit, block, packed) in enumerate(attention_pieces(me)):
        column = pl.multiple_of(block * 128, 128)
        begin(unit, lambda r, c=column: r.at[:, pl.ds(c, 128)], attn_ref.at[:, pl.ds(packed * 128, 128)], sems.at[i])
    for i in range(6):
        unit = 12 + 8 * (i // 2) + 2 * me + i % 2
        target = ffn_ref.at[:, pl.ds(i * UW, UW)] if i < 4 else down_ref.at[:, pl.ds((i - 4) * UW, UW)]
        begin(unit, lambda r: r, target, sems.at[12 + i])
    for wait in waits:
        wait.wait()


def pick_units(place, me, own, pieces):
    rows = own.shape[1]
    hbm = pl.BlockSpec(memory_space=pl.ANY)
    smem = pl.BlockSpec(memory_space=pltpu.SMEM)
    vmem = pl.BlockSpec(memory_space=pltpu.VMEM)
    return pl.pallas_call(
        pick_kernel,
        in_specs=[smem, smem, hbm, hbm],
        out_specs=[vmem, vmem, vmem],
        out_shape=[
            jax.ShapeDtypeStruct((rows, 4 * QW), BF),
            jax.ShapeDtypeStruct((rows, 4 * UW), BF),
            jax.ShapeDtypeStruct((rows, 2 * UW), BF),
        ],
        scratch_shapes=[pltpu.SemaphoreType.DMA((18,))],
        compiler_params=params(),
        name="pick_units",
    )(place, me.reshape(1), own, pieces)


def place_kernel(unit_ref, me_ref, attn, gate_up, down, out_ref, sems):
    me = me_ref[0]
    waits = []
    for i in range(9):
        unit = unit_ref[i]
        f = jnp.maximum(unit - 12, 0)
        for q in range(4):
            block = (unit % 3) * 4 + q
            low = f % 16
            choices = (
                (unit < 12, attn, block // HEADS, (unit // 3) * QW + (block % HEADS) * 128),
                ((unit >= 12) & (unit < 28), gate_up, (low % 8) // 2, (low // 8) * FQ + (low % 2) * UW + q * 128),
                (unit >= 28, down, (f % 8) // 2, (f % 2) * UW + q * 128),
            )
            target, sem = out_ref.at[i, :, pl.ds(q * 128, 128)], sems.at[i, q]
            for chosen, pieces, holder, column in choices:

                @pl.when(chosen)
                def start(pieces=pieces, holder=holder, column=column, target=target, sem=sem):
                    source = pieces.at[holder ^ me, :, pl.ds(pl.multiple_of(column, 128), 128)]
                    pltpu.make_async_copy(source, target, sem).start()

            waits.append(pltpu.make_async_copy(attn.at[0, :, pl.ds(0, 128)], target, sem))
    for wait in waits:
        wait.wait()


def place_units(units, me, attn_pieces, gate_up_pieces, down_pieces):
    rows = attn_pieces.shape[1]
    hbm = pl.BlockSpec(memory_space=pl.ANY)
    smem = pl.BlockSpec(memory_space=pltpu.SMEM)
    return pl.pallas_call(
        place_kernel,
        in_specs=[smem, smem] + [hbm] * 3,
        out_specs=pl.BlockSpec(memory_space=pltpu.VMEM),
        out_shape=jax.ShapeDtypeStruct((9, rows, UW), BF),
        scratch_shapes=[pltpu.SemaphoreType.DMA((9, 4))],
        compiler_params=params(),
        name="place_units",
    )(units, me.reshape(1), attn_pieces, gate_up_pieces, down_pieces)


def turn(values, cosine, sine, lane):
    partner = jnp.where(lane % HD < HD // 2, pltpu.roll(values, 96, 1), pltpu.roll(values, 32, 1))
    return values * cosine + partner * sine


def project_kernel(x_ref, w_ref, gain_ref, cos_ref, sin_ref, n_ref, q_ref, k_ref, v_ref):
    x = x_ref[...].astype(F32)
    r = lax.rsqrt(jnp.mean(x * x, axis=-1, keepdims=True) + norm_epsilon)
    n = (x * r * gain_ref[...]).astype(BF)
    n_ref[...] = n
    lane = lax.broadcasted_iota(jnp.int32, (x.shape[0], VD), 1)
    cosine, sine = cos_ref[...], sin_ref[...]
    out = dot_plain(n, w_ref[...])
    for h in range(HEADS):
        at = slice(h * VD, (h + 1) * VD)
        q = turn(out[:, h * VD : (h + 1) * VD], cosine, sine, lane)
        q_ref[:, at] = (q.astype(BF).astype(F32) * HD**-0.5).astype(BF)
        k = turn(out[:, QW + h * VD : QW + (h + 1) * VD], cosine, sine, lane)
        k_ref[:, at] = k.astype(BF)
    v_ref[...] = out[:, 2 * QW :].astype(BF)


def project(x, weights, gain, cosine, sine):
    count = x.shape[0]
    rows = lambda w: pl.BlockSpec((TILE, w), lambda i: (i, 0))
    fixed = lambda h, w: pl.BlockSpec((h, w), lambda i: (0, 0), pipeline_mode=pl.Buffered(1))
    narrow = jax.ShapeDtypeStruct((count, QW), BF)
    return pl.pallas_call(
        project_kernel,
        grid=(count // TILE,),
        in_specs=[rows(D), fixed(D, 3 * QW), fixed(1, D), rows(VD), rows(VD)],
        out_specs=[rows(D), rows(QW), rows(QW), rows(QW)],
        out_shape=[jax.ShapeDtypeStruct((count, D), BF), narrow, narrow, narrow],
        compiler_params=params(),
        cost_estimate=pl.CostEstimate(
            flops=2 * count * D * 3 * QW, bytes_accessed=count * D * 6 + 6 * D * QW, transcendentals=0
        ),
        name="project",
    )(x, weights, gain, cosine, sine)


def split_halves(q):
    lane = lax.broadcasted_iota(jnp.int32, q.shape, 1)
    zero = jnp.zeros_like(q)
    return jnp.concatenate([jnp.where(lane < HD, q, zero), jnp.where(lane >= HD, q, zero)], axis=0)


def block_mask(j, i, start):
    key = j * TILE + lax.broadcasted_iota(jnp.int32, (TILE, 2 * TILE), 0)
    query = i * TILE + lax.broadcasted_iota(jnp.int32, (TILE, TILE), 1)
    query = jnp.concatenate([query, query], axis=1)
    return (key >= start) & (key <= query)


def attend_kernel(low_ref, lam_ref, q_ref, k_ref, v_ref, start_ref, gain_ref, a_ref, maps_ref, log_ref, vt_ref):
    i = pl.program_id(1)

    @pl.when(i == 0)
    def turn_values():
        for j in range(vt_ref.shape[0]):
            vt_ref[j] = v_ref[j * TILE : (j + 1) * TILE, :].astype(F32).T.astype(BF)

    q = split_halves(q_ref[...])
    start = jnp.concatenate([start_ref[...], start_ref[...]], axis=1)

    def step(j, carry):
        top, mass, total = carry
        keys = k_ref[pl.ds(pl.multiple_of(j * TILE, TILE), TILE), :]
        scores = jnp.where(block_mask(j, i, start), dot_last(keys, q), masked_fill)
        new = jnp.maximum(top, jnp.max(scores, axis=0, keepdims=True))
        shares = jnp.exp(scores - new)
        keep = jnp.exp(top - new)
        mass = mass * keep + jnp.sum(shares, axis=0, keepdims=True)
        total = total * keep + dot_plain(vt_ref[j], shares.astype(BF))
        return new, mass, total

    first = (
        jnp.full((1, 2 * TILE), masked_fill, F32),
        jnp.zeros((1, 2 * TILE), F32),
        jnp.zeros((VD, 2 * TILE), F32),
    )
    top, mass, total = lax.fori_loop(low_ref[i], i + 1, step, first)
    maps = total / mass
    one, two = maps[:, :TILE], maps[:, TILE:]
    maps_ref[0, 0] = one
    maps_ref[0, 1] = two
    log_ref[0, 0] = top + jnp.log(mass)
    mixed = one - lam_ref[0] * two
    r = lax.rsqrt(jnp.mean(mixed * mixed, axis=0, keepdims=True) + norm_epsilon)
    a_ref[...] = (mixed * r * gain_ref[...] * (1.0 - lambda_start)).T.astype(BF)


def attend(low, lam, q, k, v, start, gain):
    count = q.shape[0]
    blocks = count // TILE
    smem = pl.BlockSpec(memory_space=pltpu.SMEM)
    return pl.pallas_call(
        attend_kernel,
        grid=(HEADS, blocks),
        in_specs=[
            smem,
            smem,
            pl.BlockSpec((TILE, VD), lambda h, i: (i, h)),
            pl.BlockSpec((count, VD), lambda h, i: (0, h)),
            pl.BlockSpec((count, VD), lambda h, i: (0, h)),
            pl.BlockSpec((1, TILE), lambda h, i: (0, i)),
            pl.BlockSpec((VD, 1), lambda h, i: (0, 0)),
        ],
        out_specs=[
            pl.BlockSpec((TILE, VD), lambda h, i: (i, h)),
            pl.BlockSpec((1, 2, VD, TILE), lambda h, i: (h, 0, 0, i)),
            pl.BlockSpec((1, 1, 1, 2 * TILE), lambda h, i: (h, i, 0, 0)),
        ],
        out_shape=[
            jax.ShapeDtypeStruct((count, QW), BF),
            jax.ShapeDtypeStruct((HEADS, 2, VD, count), F32),
            jax.ShapeDtypeStruct((HEADS, blocks, 1, 2 * TILE), F32),
        ],
        scratch_shapes=[pltpu.VMEM((blocks, VD, TILE), BF)],
        compiler_params=params(),
        cost_estimate=pl.CostEstimate(
            flops=8 * count * count * VD * HEADS, bytes_accessed=count * QW * 16, transcendentals=count * count * HEADS
        ),
        name="attend",
    )(low, lam, q, k, v, start, gain)


def attend_back_kernel(
    low_ref, lam_ref, q_ref, k_ref, v_ref, start_ref, gain_ref, maps_ref, log_ref, da_ref, cosq_ref, sinq_ref,
    cosk_ref, sink_ref, dq_ref, dk_ref, dv_ref, dgain_ref, dlam_ref, kt_ref, dk_sum, dv_sum, dq_sum,
):
    i = pl.program_id(1)
    blocks = kt_ref.shape[0]

    @pl.when(i == 0)
    def begin():
        for j in range(blocks):
            kt_ref[j] = k_ref[j * TILE : (j + 1) * TILE, :].astype(F32).T.astype(BF)
        dk_sum[...] = jnp.zeros_like(dk_sum)
        dv_sum[...] = jnp.zeros_like(dv_sum)
        dgain_ref[...] = jnp.zeros_like(dgain_ref)
        dlam_ref[...] = jnp.zeros_like(dlam_ref)

    lam = lam_ref[0]
    q = split_halves(q_ref[...])
    start = jnp.concatenate([start_ref[...], start_ref[...]], axis=1)
    log_mass = log_ref[0, 0]
    one, two = maps_ref[0, 0], maps_ref[0, 1]
    mixed = one - lam * two
    r = lax.rsqrt(jnp.mean(mixed * mixed, axis=0, keepdims=True) + norm_epsilon)
    t = mixed * r
    da = da_ref[...].T * (1.0 - lambda_start)
    dgain_ref[0] += da * t
    e = da * gain_ref[...]
    dmixed = r * (e - t * jnp.mean(e * t, axis=0, keepdims=True))
    dlam_ref[0] -= jnp.sum(dmixed * two, axis=0, keepdims=True)
    dmaps = jnp.concatenate([dmixed, -lam * dmixed], axis=1).astype(BF)
    maps = jnp.concatenate([one, two], axis=1)
    offset = jnp.sum(dmaps.astype(F32) * maps, axis=0, keepdims=True)
    dq_sum[...] = jnp.zeros_like(dq_sum)

    def step(j, carry):
        at = pl.ds(pl.multiple_of(j * TILE, TILE), TILE)
        keys, values = k_ref[at, :], v_ref[at, :]
        scores = dot_last(keys, q)
        shares = jnp.where(block_mask(j, i, start), jnp.exp(scores - log_mass), 0.0)
        dshares = dot_plain(values, dmaps)
        dscores = (shares * (dshares - offset)).astype(BF)
        dv_sum[at, :] += dot_last(shares.astype(BF), dmaps)
        dk_sum[at, :] += dot_plain(dscores, q)
        dq_sum[...] += dot_plain(kt_ref[j], dscores)
        return carry

    lax.fori_loop(low_ref[i], i + 1, step, 0)
    lane = lax.broadcasted_iota(jnp.int32, (TILE, VD), 1)
    dq = jnp.concatenate([dq_sum[:HD, :TILE], dq_sum[HD:, TILE:]], axis=0).T * HD**-0.5
    dq_ref[...] = turn(dq, cosq_ref[...], -sinq_ref[...], lane).astype(BF)

    @pl.when(i == blocks - 1)
    def finish():
        for j in range(blocks):
            at = slice(j * TILE, (j + 1) * TILE)
            dk_ref[at, :] = turn(dk_sum[at, :], cosk_ref[at, :], -sink_ref[at, :], lane).astype(BF)
        dv_ref[...] = dv_sum[...].astype(BF)


def attend_back(low, lam, q, k, v, start, gain, maps, log_mass, da, cosine, sine):
    count = q.shape[0]
    blocks = count // TILE
    smem = pl.BlockSpec(memory_space=pltpu.SMEM)
    tile = pl.BlockSpec((TILE, VD), lambda h, i: (i, h))
    whole = pl.BlockSpec((count, VD), lambda h, i: (0, h))
    table = pl.BlockSpec((TILE, VD), lambda h, i: (i, 0))
    full_table = pl.BlockSpec((count, VD), lambda h, i: (0, 0), pipeline_mode=pl.Buffered(1))
    narrow = jax.ShapeDtypeStruct((count, QW), BF)
    return pl.pallas_call(
        attend_back_kernel,
        grid=(HEADS, blocks),
        in_specs=[
            smem,
            smem,
            tile,
            whole,
            whole,
            pl.BlockSpec((1, TILE), lambda h, i: (0, i)),
            pl.BlockSpec((VD, 1), lambda h, i: (0, 0)),
            pl.BlockSpec((1, 2, VD, TILE), lambda h, i: (h, 0, 0, i)),
            pl.BlockSpec((1, 1, 1, 2 * TILE), lambda h, i: (h, i, 0, 0)),
            tile,
            table,
            table,
            full_table,
            full_table,
        ],
        out_specs=[
            tile,
            whole,
            whole,
            pl.BlockSpec((1, VD, TILE), lambda h, i: (h, 0, 0)),
            pl.BlockSpec((1, 1, TILE), lambda h, i: (h, 0, 0)),
        ],
        out_shape=[
            narrow,
            narrow,
            narrow,
            jax.ShapeDtypeStruct((HEADS, VD, TILE), F32),
            jax.ShapeDtypeStruct((HEADS, 1, TILE), F32),
        ],
        scratch_shapes=[
            pltpu.VMEM((blocks, VD, TILE), BF),
            pltpu.VMEM((count, VD), F32),
            pltpu.VMEM((count, VD), F32),
            pltpu.VMEM((VD, 2 * TILE), F32),
        ],
        compiler_params=params(),
        cost_estimate=pl.CostEstimate(
            flops=20 * count * count * VD * HEADS, bytes_accessed=count * QW * 24, transcendentals=count * count * HEADS
        ),
        name="attend_back",
    )(low, lam, q, k, v, start, gain, maps, log_mass, da, cosine, sine, cosine, sine)


def middle_kernel(
    x_ref, gain_ref, a_ref, w_ref, w_in, a_hbm, n_ref, own_ref, a_in, total, s_a, s_ay, s_ar
):
    i = pl.program_id(0)
    me = lax.axis_index("batch")
    y, core = me // 2, me % 2
    to_core = {"batch": y * 2 + 1 - core}
    to_y = {"batch": (1 - y) * 2 + core}
    blocks = a_in.shape[1]

    def a_copies(b):
        source = a_hbm.at[pl.ds(b * TILE, TILE)]
        return (
            lambda: remote(source, a_in.at[0, b], s_a, b, to_core),
            lambda: remote(source, a_in.at[1, b], s_ay, b, to_y),
            lambda: remote(a_in.at[1, b], a_in.at[2, b], s_ar, b, to_core),
        )

    @pl.when(i == 0)
    def begin():
        greet((to_core, to_y))
        for b in range(blocks):
            a_copies(b)[1]().start()
        for b in range(blocks):
            a_copies(b)[0]().start()

    @pl.when(i < blocks)
    def relay():
        a_copies(i)[1]().wait_recv()
        a_copies(i)[2]().start()

    @pl.when(i >= 1)
    def compute():
        b = i - 1
        a_copies(b)[0]().wait_recv()
        a_copies(b)[2]().wait_recv()
        x1 = x_ref[...].astype(F32) + dot_last(a_ref[...], w_ref[...])
        for other in range(3):
            x1 += dot_last(a_in[other, b], w_in[other])
        total[...] = x1
        r = lax.rsqrt(jnp.mean(x1 * x1, axis=-1, keepdims=True) + norm_epsilon)
        n_ref[...] = (x1 * r * gain_ref[...]).astype(BF)
        part = TILE // 4
        own_ref[0] = total[pl.ds(pl.multiple_of(me * part, part), part), :]

    @pl.when(i == blocks)
    def finish():
        for b in range(blocks):
            for copy in a_copies(b):
                copy().wait_send()


def middle(a, x, attn, others, gain):
    count = x.shape[0]
    blocks = count // TILE
    late = lambda i: (jnp.maximum(i - 1, 0), 0)
    hbm = pl.BlockSpec(memory_space=pl.ANY)
    sems = lambda n: pltpu.SemaphoreType.DMA((2, n))
    return pl.pallas_call(
        middle_kernel,
        grid=(blocks + 1,),
        in_specs=[
            pl.BlockSpec((TILE, D), late),
            pl.BlockSpec((1, D), lambda i: (0, 0)),
            pl.BlockSpec((TILE, QW), late),
            pl.BlockSpec((D, QW), lambda i: (0, 3), pipeline_mode=pl.Buffered(1)),
            pl.BlockSpec((3, D, QW), lambda i: (0, 0, 0), pipeline_mode=pl.Buffered(1)),
            hbm,
        ],
        out_specs=[
            pl.BlockSpec((TILE, D), late),
            pl.BlockSpec((1, TILE // 4, D), lambda i: (jnp.maximum(i - 1, 0), 0, 0)),
        ],
        out_shape=[
            jax.ShapeDtypeStruct((count, D), BF),
            jax.ShapeDtypeStruct((blocks, TILE // 4, D), F32),
        ],
        scratch_shapes=[
            pltpu.VMEM((3, blocks, TILE, QW), BF),
            pltpu.VMEM((TILE, D), F32),
            sems(blocks),
            sems(blocks),
            sems(blocks),
        ],
        compiler_params=params(collective_id=5, has_side_effects=True),
        cost_estimate=pl.CostEstimate(
            flops=2 * count * D * D, bytes_accessed=count * D * 7 + 2 * D * D, transcendentals=0
        ),
        name="middle",
    )(x, gain, a, attn, others, a)


def feed_kernel(
    n_ref, dy_ref, w_ref, wd_ref, x1_ref, dyo_ref, wo_ref, gain_ref, dup_ref, out_ref, dx_ref, low_ref, da_ref, dgain_ref,
    gate_grad_ref, down_grad_ref, part, near_in, near, far_in, gathered, gate_sum, down_sum, staged, s_near, s_far, s_y,
    s_core, s_relay, s_grad, s_low,
):
    i = pl.program_id(0)
    me = lax.axis_index("batch")
    y, core = me // 2, me % 2
    to_core = {"batch": y * 2 + 1 - core}
    to_y = {"batch": (1 - y) * 2 + core}
    blocks = near_in.shape[0]

    def near_copy(b):
        return remote(part.at[b % 3, :, 1 - core], near_in.at[b], s_near, b, to_core)

    def low_copy(b):
        return pltpu.make_async_copy(gathered.at[b], low_ref.at[b], s_low.at[b])

    grads = ((gate_sum, gate_grad_ref), (down_sum, down_grad_ref))
    strip = gate_sum.shape[0] // 4

    def grad_copy(n, which):
        at = pl.ds(pl.multiple_of(n * strip, strip), strip)
        return pltpu.make_async_copy(staged.at[which], grads[which][1].at[at], s_grad.at[which, n])

    def far_copy(b):
        return remote(near.at[b], far_in.at[b], s_far, b, to_y)

    def own_copy(b, sems, device):
        return remote(gathered.at[b, me], gathered.at[b, me], sems, b, device)

    def relay_copy(b):
        slab = (1 - y) * 2 + core
        return remote(gathered.at[b, slab], gathered.at[b, slab], s_relay, b, to_core)

    @pl.when(i == 0)
    def begin():
        greet((to_core, to_y))
        dgain_ref[...] = jnp.zeros_like(dgain_ref)
        gate_sum[...] = jnp.zeros_like(gate_sum)
        down_sum[...] = jnp.zeros_like(down_sum)

    @pl.when((i >= 1) & (i < blocks + 1))
    def send_far():
        b = i - 1
        near_copy(b).wait_recv()
        both = part[b % 3, 1 - y, core].astype(F32) + near_in[b, 1 - y].astype(F32)
        near[b] = both.astype(BF)
        far_copy(b).start()

    @pl.when((i >= 2) & (i < blocks + 2))
    def send_own():
        b = i - 2
        far_copy(b).wait_recv()
        dn = part[b % 3, y, core].astype(F32) + near_in[b, y].astype(F32) + far_in[b].astype(F32)
        x1 = x1_ref[0]
        r = lax.rsqrt(jnp.mean(x1 * x1, axis=-1, keepdims=True) + norm_epsilon)
        t = x1 * r
        e = dn * gain_ref[...]
        dx = dyo_ref[0].astype(F32) + r * (e - t * jnp.mean(e * t, axis=-1, keepdims=True))
        dgain_ref[...] += jnp.sum(dn * t, axis=0, keepdims=True)
        dx_ref[0] = dx
        gathered[b, me] = dx.astype(BF)
        own_copy(b, s_y, to_y).start()
        own_copy(b, s_core, to_core).start()

    @pl.when((i >= 3) & (i < blocks + 3))
    def send_relay():
        b = i - 3
        own_copy(b, s_y, to_y).wait_recv()
        relay_copy(b).start()

    @pl.when(i >= 4)
    def use():
        b = i - 4
        own_copy(b, s_core, to_core).wait_recv()
        relay_copy(b).wait_recv()
        whole = jnp.concatenate([gathered[b, other] for other in range(4)], axis=0)
        low_copy(b).start()
        da_ref[...] = dot_plain(whole, wo_ref[...])

    @pl.when(i < blocks)
    def compute():
        n, dy = n_ref[...], dy_ref[...]
        wg, wu, wd = w_ref[:, :FQ], w_ref[:, FQ:], wd_ref[...]
        gate = dot_plain(n, wg)
        up = dot_plain(n, wu)
        dhidden = dot_plain(dy, wd)
        share = 1.0 / (1.0 + jnp.exp(-gate))
        silu = gate * share
        hidden = (silu * up).astype(BF)
        dup = (dhidden * silu).astype(BF)
        dgate = (dhidden * up * (share * (1.0 + gate * (1.0 - share)))).astype(BF)
        dup_ref[...] = dup
        dn = (dot_last(dgate, wg) + dot_last(dup, wu)).astype(BF)
        size = dn.shape[0] // 4

        @pl.when(i >= 3)
        def reuse():
            near_copy(i - 3).wait_send()

        for other in range(4):
            part[i % 3, other // 2, other % 2] = dn[other * size : (other + 1) * size]
        near_copy(i).start()
        out_ref[...] = dot_last(hidden, wd).astype(BF)
        for c in range(0, n.shape[1], TILE):
            gate_sum[c : c + TILE, :] += dot_first(n[:, c : c + TILE], dgate)
            down_sum[c : c + TILE, :] += dot_first(dy[:, c : c + TILE], hidden)

    @pl.when(i >= blocks)
    def keep():
        n = i - blocks
        for which in range(2):

            @pl.when(n >= 1)
            def reuse(which=which):
                grad_copy(n - 1, which).wait()

            at = pl.ds(pl.multiple_of(n * strip, strip), strip)
            staged[which] = grads[which][0][at, :].astype(BF)
            grad_copy(n, which).start()

    @pl.when(i == blocks + 3)
    def finish():
        for which in range(2):
            grad_copy(3, which).wait()
        for b in range(blocks - 3, blocks):
            near_copy(b).wait_send()
        for b in range(blocks):
            far_copy(b).wait_send()
            own_copy(b, s_y, to_y).wait_send()
            own_copy(b, s_core, to_core).wait_send()
            relay_copy(b).wait_send()
            low_copy(b).wait()


def feed(n, dy, weights, down, x1, dy_own, attn, gain):
    count = n.shape[0]
    blocks = count // TILE
    size = TILE // 4
    late = lambda lag: lambda i: (jnp.clip(i - lag, 0, blocks - 1), 0)
    late3 = lambda lag: lambda i: (jnp.clip(i - lag, 0, blocks - 1), 0, 0)
    rows = lambda w, lag: pl.BlockSpec((TILE, w), late(lag))
    own = pl.BlockSpec((1, size, D), late3(2))
    shape = lambda w, kind=BF: jax.ShapeDtypeStruct((count, w), kind)
    sems = pltpu.SemaphoreType.DMA((2, blocks))
    return pl.pallas_call(
        feed_kernel,
        grid=(blocks + 4,),
        in_specs=[
            rows(D, 0),
            rows(D, 0),
            pl.BlockSpec((D, 2 * FQ), lambda i: (0, 0), pipeline_mode=pl.Buffered(1)),
            pl.BlockSpec((D, FQ), lambda i: (0, 0), pipeline_mode=pl.Buffered(1)),
            own,
            own,
            pl.BlockSpec((D, QW), lambda i: (0, 3), pipeline_mode=pl.Buffered(1)),
            pl.BlockSpec((1, D), lambda i: (0, 0)),
        ],
        out_specs=[
            rows(FQ, 0),
            rows(D, 0),
            own,
            pl.BlockSpec(memory_space=pl.ANY),
            rows(QW, 4),
            pl.BlockSpec((1, D), lambda i: (0, 0)),
            pl.BlockSpec(memory_space=pl.ANY),
            pl.BlockSpec(memory_space=pl.ANY),
        ],
        out_shape=[
            shape(FQ),
            shape(D),
            jax.ShapeDtypeStruct((blocks, size, D), F32),
            jax.ShapeDtypeStruct((blocks, 4, size, D), BF),
            shape(QW, F32),
            jax.ShapeDtypeStruct((1, D), F32),
            jax.ShapeDtypeStruct((D, FQ), BF),
            jax.ShapeDtypeStruct((D, FQ), BF),
        ],
        scratch_shapes=[
            pltpu.VMEM((3, 2, 2, size, D), BF),
            pltpu.VMEM((blocks, 2, size, D), BF),
            pltpu.VMEM((blocks, size, D), BF),
            pltpu.VMEM((blocks, size, D), BF),
            pltpu.VMEM((blocks, 4, size, D), BF),
            pltpu.VMEM((D, FQ), F32),
            pltpu.VMEM((D, FQ), F32),
            pltpu.VMEM((2, D // 4, FQ), BF),
            sems,
            sems,
            sems,
            sems,
            sems,
            pltpu.SemaphoreType.DMA((2, 4)),
            pltpu.SemaphoreType.DMA((blocks,)),
        ],
        compiler_params=params(63 * 2**20, collective_id=1, has_side_effects=True),
        cost_estimate=pl.CostEstimate(
            flops=12 * count * D * FQ, bytes_accessed=count * (8 * D + 6 * FQ) + 6 * D * FQ, transcendentals=count * FQ
        ),
        name="feed",
    )(n, dy, weights, down, x1, dy_own, attn, gain)


def return_rows_copies(source, target, sems, me, blk):
    size = source.shape[1]

    def copies(act_local, act_remote):
        for k in range(8):
            here = (me == blk // 2) & (blk == k)
            piece = target.at[blk % 2, pl.ds(pl.multiple_of(me * size, size), size)]

            @pl.when(here)
            def stay():
                act_local(pltpu.make_async_copy(source.at[k], piece, sems.at[0, k]))

            @pl.when(jnp.logical_not(here))
            def go():
                act_remote(
                    pltpu.make_async_remote_copy(
                        src_ref=source.at[k],
                        dst_ref=piece,
                        send_sem=sems.at[0, k],
                        recv_sem=sems.at[1, (blk % 2) * 4 + me],
                        device_id=(blk // 2, k),
                        device_id_type=MESH,
                    )
                )

    def start():
        copies(lambda copy: copy.start(), lambda copy: copy.start())

    def finish():
        copies(lambda copy: copy.wait(), lambda copy: copy.wait_send())
        for i in range(2):
            for other in range(4):

                @pl.when((me != other) | (blk != 2 * me + i))
                def arrived():
                    pltpu.make_async_remote_copy(
                        src_ref=source.at[0],
                        dst_ref=target.at[i, pl.ds(other * size, size)],
                        send_sem=sems.at[0, 0],
                        recv_sem=sems.at[1, 4 * i + other],
                        device_id=(me, blk),
                        device_id_type=MESH,
                    ).wait_recv()

    return start, finish


def collect_kernel(
    gate, up, qkv, out, down_ref, out_part_ref, dn1_part_ref, x1_ref, dx1_ref, x_ref, gain_ref, attn_ref, gate_up_ref,
    downs_ref, dx_ref, back_ref, dgain_ref, first_in, second_in, first_sum, second_sum, own, near_in, near, far_in,
    out_rows, s_up, s_down, s_up2, s_down2, s_near, s_own, s_far, s_pieces, s_local, s_back,
):
    me, blk = lax.axis_index("batch"), lax.axis_index("blk")
    y, core = me // 2, me % 2
    to_core = {"batch": y * 2 + 1 - core}
    to_y = {"batch": (1 - y) * 2 + core}
    place = ring_place(blk)
    after_me, before_me = {"blk": ring_owner(place + 1)}, {"blk": ring_owner(place - 1)}
    part = first_sum.shape[0]
    half = part // 2
    blocks = dx1_ref.shape[0]

    wide = QW + 256
    plans = (
        ((gate, 0, FQ, 0), (up, 0, FQ, FQ)),
        ((qkv, 0, wide, 0), (qkv, wide, 3 * QW - wide, wide), (out, 0, QW, 3 * QW)),
    )
    buffers, totals = (first_in, second_in), (first_sum, second_sum)
    ring_sems = ((s_up, s_down), (s_up2, s_down2))

    def mine(r, t, up_way, p):
        grad, column, width, _ = plans[r][p]
        owner = ring_owner(place - 1 - t) if up_way else ring_owner(place + 1 + t)
        begin = pl.multiple_of(owner * part + (0 if up_way else half), half)
        return grad.at[pl.ds(begin, half), pl.ds(column, width)]

    def landing(r, t, up_way, p):
        _, _, width, to = plans[r][p]
        return buffers[r].at[0 if up_way else 1, t, :, pl.ds(to, width)]

    def ring(r, t, up_way, p):
        source = mine(r, 0, up_way, p) if t == 0 else landing(r, t - 1, up_way, p)
        sems = ring_sems[r][0 if up_way else 1]
        at = len(plans[r]) * t + p
        return remote(source, landing(r, t, up_way, p), sems, at, after_me if up_way else before_me)

    def ring_start(r):
        for p in range(len(plans[r])):
            ring(r, 0, True, p).start()
            ring(r, 0, False, p).start()

    def ring_step(r, t, p):
        _, _, width, to = plans[r][p]
        for up_way in (True, False):
            ring(r, t - 1, up_way, p).wait_recv()
            here = landing(r, t - 1, up_way, p)
            value = (here[...].astype(F32) + mine(r, t, up_way, p)[...].astype(F32)).astype(BF)
            if t < 7:
                here[...] = value
                ring(r, t, up_way, p).start()
            else:
                totals[r][0 if up_way else half : half if up_way else part, to : to + width] = value

    def exchange(source, target, n):
        return (
            lambda: remote(source, target.at[1], s_pieces, 3 * n, to_core),
            lambda: remote(source, target.at[2], s_pieces, 3 * n + 1, to_y),
            lambda: remote(target.at[2], target.at[3], s_pieces, 3 * n + 2, to_core),
            lambda: pltpu.make_async_copy(source, target.at[0], s_local.at[n]),
        )

    exchanges = (exchange(down_ref, downs_ref, 0), exchange(first_sum, gate_up_ref, 1), exchange(second_sum, attn_ref, 2))

    def spread(n):
        for way in (1, 0, 3):
            exchanges[n][way]().start()

    def relay(n):
        exchanges[n][1]().wait_recv()
        exchanges[n][2]().start()

    parts = (out_part_ref, dn1_part_ref)

    def near_copy(j):
        return remote(parts[j // blocks].at[j % blocks, :, 1 - core], near_in.at[j], s_near, j, to_core)

    def own_copy(j):
        return pltpu.make_async_copy(parts[j // blocks].at[j % blocks, :, core], own.at[j], s_own.at[j])

    def far_copy(j):
        return remote(near.at[j], far_in.at[j], s_far, j, to_y)

    def near_step(j):
        near_copy(j).wait_recv()
        own_copy(j).wait()
        near[j] = (own[j, 1 - y].astype(F32) + near_in[j, 1 - y].astype(F32)).astype(BF)
        far_copy(j).start()

    def far_step(j):
        far_copy(j).wait_recv()
        total = own[j, y].astype(F32) + near_in[j, y].astype(F32) + far_in[j].astype(F32)
        b = j % blocks
        if j < blocks:
            out_rows[b] = (x1_ref[b] + total).astype(BF)
            return
        x = x_ref[b].astype(F32)
        r = lax.rsqrt(jnp.mean(x * x, axis=-1, keepdims=True) + norm_epsilon)
        t = x * r
        e = total * gain_ref[...]
        dx = dx1_ref[b] + r * (e - t * jnp.mean(e * t, axis=-1, keepdims=True))
        dx_ref[b] = dx.astype(BF)
        dgain_ref[...] += jnp.sum(total * t, axis=0, keepdims=True)

    back_start, back_finish = return_rows_copies(out_rows, back_ref, s_back, me, blk)
    dgain_ref[...] = jnp.zeros_like(dgain_ref)
    greet_all()
    ring_start(0)
    for j in range(2 * blocks):
        own_copy(j).start()
        near_copy(j).start()
    spread(0)
    groups = [(r, t, p) for r in range(2) for t in range(1, 8) for p in range(len(plans[r]))]
    for g, (r, t, p) in enumerate(groups):
        ring_step(r, t, p)
        if g < 2 * blocks:
            near_step(g)
        if 3 <= g < 2 * blocks + 3:
            far_step(g - 3)
        if (r, t, p) == (0, 6, 1):
            ring_start(1)
            relay(0)
        if (r, t, p) == (0, 7, 1):
            spread(1)
            back_start()
        if (r, t, p) == (1, 5, 0):
            relay(1)
    spread(2)
    relay(2)
    back_finish()
    for n in range(3):
        near_piece, far_piece, relay_piece, local = exchanges[n]
        near_piece().wait()
        far_piece().wait_send()
        relay_piece().wait()
        local().wait()
    for j in range(2 * blocks):
        near_copy(j).wait_send()
        far_copy(j).wait_send()
    for r in range(2):
        for t in range(7):
            for p in range(len(plans[r])):
                ring(r, t, True, p).wait_send()
                ring(r, t, False, p).wait_send()


def collect(gate, up, qkv, out, down, out_part, dn1_part, x1, dx1, x, gain):
    part = D // 8
    size = x.shape[1]
    items = 2 * x.shape[0]
    hbm = pl.BlockSpec(memory_space=pl.ANY)
    vmem = pl.BlockSpec(memory_space=pltpu.VMEM)
    sems = lambda n: pltpu.SemaphoreType.DMA((2, n))
    four = lambda width: jax.ShapeDtypeStruct((4, part, width), BF)
    return pl.pallas_call(
        collect_kernel,
        in_specs=[vmem] * 4 + [hbm] * 3 + [vmem] * 4,
        out_specs=[hbm] * 3 + [vmem, hbm, vmem],
        out_shape=[
            four(4 * QW),
            four(2 * FQ),
            four(FQ),
            jax.ShapeDtypeStruct(x.shape, BF),
            jax.ShapeDtypeStruct((2, 4 * size, D), BF),
            jax.ShapeDtypeStruct((1, D), F32),
        ],
        scratch_shapes=[
            pltpu.VMEM((2, 7, part // 2, 2 * FQ), BF),
            pltpu.VMEM((2, 7, part // 2, 4 * QW), BF),
            pltpu.VMEM((part, 2 * FQ), BF),
            pltpu.VMEM((part, 4 * QW), BF),
            pltpu.VMEM((items, 2, size, D), BF),
            pltpu.VMEM((items, 2, size, D), BF),
            pltpu.VMEM((items, size, D), BF),
            pltpu.VMEM((items, size, D), BF),
            pltpu.VMEM(x.shape, BF),
            sems(14),
            sems(14),
            sems(21),
            sems(21),
            sems(items),
            pltpu.SemaphoreType.DMA((items,)),
            sems(items),
            sems(9),
            pltpu.SemaphoreType.DMA((3,)),
            sems(8),
        ],
        compiler_params=params(collective_id=6, has_side_effects=True),
        cost_estimate=pl.CostEstimate(flops=10**11, bytes_accessed=2**25, transcendentals=0),
        name="collect",
    )(gate, up, qkv, out, down, out_part, dn1_part, x1, dx1, x, gain)


def rotate_kernel(
    g_ref, base_ref, other_ref, first_ref, second_ref, master_ref, rows_ref, scale_ref, new_first_ref, new_second_ref,
    new_master_ref, rows_out_ref, g, base, other, firsts, seconds, masters, g_in, part, x_in, near, z_in, far, p_in, step, steps,
    back, back_in, steps_own, load, store, s_g, s_x, s_z, s_p, s_step, s_back, s_up, s_side, s_rows,
):
    blk = lax.axis_index("blk")
    zh, zl, xx = blk // 4, (blk // 2) % 2, blk % 2
    to_x = {"blk": blk + 1 - 2 * xx}
    to_z = {"blk": blk + 4 - 8 * zh}
    to_pair = {"blk": blk + 2 - 4 * zl}
    count = g.shape[0]
    half = UW // 2
    own = pl.ds(pl.multiple_of(zl * half, half), half)
    away = pl.ds(pl.multiple_of((1 - zl) * half, half), half)
    block = 4 * zh + xx
    loads = [
        (g_ref, g), (base_ref, base), (other_ref, other), (first_ref, firsts), (second_ref, seconds), (master_ref, masters),
    ]
    stores = [(firsts, new_first_ref), (seconds, new_second_ref), (masters, new_master_ref)]

    def loading(i, s):
        return pltpu.make_async_copy(loads[i][0].at[s], loads[i][1].at[s], load.at[i, s])

    def storing(i, s):
        return pltpu.make_async_copy(stores[i][0].at[s], stores[i][1].at[s], store.at[i, s])

    def send_g(s):
        return remote(g.at[s, :, away], g_in.at[s], s_g, s, to_pair)

    def send_x(s):
        return remote(part.at[s % 3, :, 1 - xx], x_in.at[s], s_x, s, to_x)

    def send_z(s):
        return remote(near.at[s % 3, 1 - zh], z_in.at[s], s_z, s, to_z)

    def send_p(s):
        return remote(far.at[s % 3], p_in.at[s], s_p, s, to_pair)

    def step_pair(s):
        return remote(step.at[s, :, away], steps.at[s, block + 2 * zl], s_step, s, to_pair)

    def step_z(s, a):
        return remote(steps.at[s, block + 2 * a], steps.at[s, block + 2 * a], s_up, 2 * s + a, to_z)

    def step_x(s, a):
        at = 2 * a + xx
        return remote(steps.at[s, at], steps.at[s, at], s_side, 4 * s + a, to_x)

    def send_back(s):
        return remote(back.at[s % 3], back_in.at[s], s_back, s, to_pair)

    for i in range(len(loads)):
        for s in range(count):
            loading(i, s).start()
    rows_start, rows_finish = return_rows_copies(rows_ref, rows_out_ref, s_rows, lax.axis_index("batch"), blk)
    greet_all()
    for s in range(count):
        loading(0, s).wait()
        send_g(s).start()
    rows_start()

    rows = base.shape[1]

    def tick(t, carry):
        def stage(lag, act):
            @pl.when((t >= lag) & (t < count + lag))
            def run():
                act(t - lag)

        def finish(s):
            send_back(s).wait_recv()
            loading(5, s).wait()
            for at, update in ((own, steps_own[s % 2]), (away, back_in[s].astype(F32))):
                value = masters[s, :, at]
                masters[s, :, at] = value - scale_ref[0] * (update + weight_decay * value)
            storing(2, s).start()

        def update(s):
            for a in range(4):
                step_x(s, a).wait_recv()
            whole = jnp.concatenate([steps[s, b] for b in range(8)], axis=0)
            steps_own[s % 2] = dot_plain(base[s], whole)

            @pl.when(s >= 3)
            def reuse():
                send_back(s - 3).wait_send()

            back[s % 3] = dot_plain(other[s], whole).astype(BF)
            send_back(s).start()

        def relay_x(s):
            for a in range(2):
                step_z(s, a).wait_recv()
            for a in range(4):
                step_x(s, a).start()

        def relay_z(s):
            step_pair(s).wait_recv()
            for a in range(2):
                step_z(s, a).start()

        def adam(s):
            send_p(s).wait_recv()
            loading(3, s).wait()
            loading(4, s).wait()
            mine = near[s % 3, zh, zl].astype(F32) + z_in[s, zl].astype(F32)
            for at, turned in ((own, mine), (away, p_in[s].astype(F32))):
                new_first = beta_one * firsts[s, :, at] + (1.0 - beta_one) * turned
                new_second = beta_two * seconds[s, :, at] + (1.0 - beta_two) * turned * turned
                firsts[s, :, at] = new_first
                seconds[s, :, at] = new_second
                moved = new_first / scale_ref[1] / (jnp.sqrt(new_second / scale_ref[2]) + adam_epsilon)
                step[s, :, at] = moved.astype(BF)
            storing(0, s).start()
            storing(1, s).start()
            steps[s, block + 2 * zl] = step[s, :, own]
            step_pair(s).start()

        def send_far(s):
            send_z(s).wait_recv()

            @pl.when(s >= 3)
            def reuse():
                send_p(s - 3).wait_send()

            far[s % 3] = (near[s % 3, zh, 1 - zl].astype(F32) + z_in[s, 1 - zl].astype(F32)).astype(BF)
            send_p(s).start()

        def send_near(s):
            send_x(s).wait_recv()

            @pl.when(s >= 3)
            def reuse():
                send_z(s - 3).wait_send()

            for a in range(2):
                for b in range(2):
                    at = 2 * a + b
                    total = part[s % 3, at, xx].astype(F32) + x_in[s, at].astype(F32)
                    near[s % 3, a, b] = total.astype(BF)
            send_z(s).start()

        def turn_slot(s):
            loading(1, s).wait()
            loading(2, s).wait()
            send_g(s).wait_recv()

            @pl.when(s >= 3)
            def reuse():
                send_x(s - 3).wait_send()

            turned = dot_first(base[s], g[s, :, own]) + dot_first(other[s], g_in[s])
            for b in range(8):
                part[s % 3, b // 2, b % 2] = turned[b * rows : (b + 1) * rows].astype(BF)
            send_x(s).start()

        stage(7, finish)
        stage(6, update)
        stage(5, relay_x)
        stage(4, relay_z)
        stage(3, adam)
        stage(2, send_far)
        stage(1, send_near)
        stage(0, turn_slot)
        return carry

    lax.fori_loop(0, count + 7, tick, 0)
    rows_finish()
    for s in range(count):
        send_g(s).wait_send()
        step_pair(s).wait_send()
        for a in range(2):
            step_z(s, a).wait_send()
        for a in range(4):
            step_x(s, a).wait_send()
        for i in range(3):
            storing(i, s).wait()
    for s in range(count - 3, count):
        send_x(s).wait_send()
        send_z(s).wait_send()
        send_p(s).wait_send()
        send_back(s).wait_send()


def rotate_slots(grads, base, other, first, second, master, tokens, scales):
    count, rows, width = grads.shape
    half = width // 2
    hbm = pl.BlockSpec(memory_space=pl.ANY)
    shape = jax.ShapeDtypeStruct(master.shape, F32)
    sems = lambda n: pltpu.SemaphoreType.DMA((2, n))
    return pl.pallas_call(
        rotate_kernel,
        in_specs=[hbm] * 7 + [pl.BlockSpec(memory_space=pltpu.SMEM)],
        out_specs=[hbm] * 4,
        out_shape=[shape] * 3 + [jax.ShapeDtypeStruct((2, 4 * tokens.shape[1], D), BF)],
        scratch_shapes=[
            pltpu.VMEM((count, rows, width), BF),
            pltpu.VMEM((count, rows, D), BF),
            pltpu.VMEM((count, rows, D), BF),
            pltpu.VMEM((count, rows, width), F32),
            pltpu.VMEM((count, rows, width), F32),
            pltpu.VMEM((count, rows, width), F32),
            pltpu.VMEM((count, rows, half), BF),
            pltpu.VMEM((3, 4, 2, rows, half), BF),
            pltpu.VMEM((count, 4, rows, half), BF),
            pltpu.VMEM((3, 2, 2, rows, half), BF),
            pltpu.VMEM((count, 2, rows, half), BF),
            pltpu.VMEM((3, rows, half), BF),
            pltpu.VMEM((count, rows, half), BF),
            pltpu.VMEM((count, rows, width), BF),
            pltpu.VMEM((count, 8, rows, half), BF),
            pltpu.VMEM((3, rows, half), BF),
            pltpu.VMEM((count, rows, half), BF),
            pltpu.VMEM((2, rows, half), F32),
            pltpu.SemaphoreType.DMA((6, count)),
            pltpu.SemaphoreType.DMA((3, count)),
            sems(count),
            sems(count),
            sems(count),
            sems(count),
            sems(count),
            sems(count),
            sems(2 * count),
            sems(4 * count),
            sems(8),
        ],
        compiler_params=params(collective_id=2, has_side_effects=True),
        name="rotate_slots",
    )(grads, base, other, first, second, master, tokens, scales)


def row_tables(lengths, row, count):
    everyone = jnp.stack(batch_pieces(lengths))
    holder = (row // 2) ^ lax.axis_index("batch")
    mine = jnp.sum(jnp.where(jnp.arange(4)[:, None, None] == holder, everyone, 0), axis=0)
    mine = jnp.where(row % 2 == 0, mine[:1], mine[1:])
    ends = doc_ends(mine)[0]
    places = jnp.arange(count, dtype=jnp.int32)
    begin = jnp.sum(jnp.where(places[:, None] >= ends[None, :], mine, 0), axis=1)
    start = jnp.where(places >= ends[NDOC - 2], places, begin)
    low = start.reshape(-1, TILE)[:, 0] // TILE
    cosine, sine = turn_tables(places - begin)
    cosine = jnp.tile(cosine, (1, 4))
    sine = jnp.tile(jnp.concatenate([-sine, sine], axis=1), (1, 2))
    return start, low, cosine, sine


def row_groups(
    tokens,
    cotangent,
    lengths,
    unit_owner,
    step_count,
    master,
    first,
    second,
    bases,
    small,
    small_first,
    small_second,
):
    me, blk = lax.axis_index("batch"), lax.axis_index("blk")
    count = tokens.shape[1] * 8
    learn_rate = 2.0 / D**0.5
    slots = lambda array: jnp.transpose(array, (1, 0, 2))
    master_slots = slots(master)

    place = ((unit_owner // 9) ^ me) * 9 + unit_owner % 9
    master_low = master_slots.astype(BF)
    pieces, x_own, dy_own, base = begin(master_low, tokens, cotangent, slots(bases))
    start, low, cosine, sine = row_tables(lengths, blk, count)
    start = start.reshape(1, count)
    attn_shard, gate_up_shard, down_shard = pick_units(place, me, master_low, pieces)
    attn, down, x, dy, other_out = gather(attn_shard, down_shard, x_own, dy_own)
    down = down.reshape(D, FQ)
    gate_up = lax.all_gather(after(gate_up_shard, attn), "blk", axis=0, tiled=True)
    attn, x, dy = attn.reshape(D, 4 * QW), x.reshape(count, D), dy.reshape(count, D)

    gain_one = small[:D].reshape(1, D)
    gain_two = small[D : 2 * D].reshape(1, D)
    head_gain = small[2 * D : 2 * D + VD].reshape(VD, 1)
    mixer, mixer_back = jax.vjp(mix_value, small[2 * D + VD :].reshape(4, HD))
    lam = mixer.reshape(1)

    n1, q, k, v = project(x, attn, gain_one, cosine, sine)
    a_own, maps, log_mass = attend(low, lam, q, k, v, start, head_gain)
    n2, x1 = middle(a_own, x, attn, other_out.reshape(3, D, QW), gain_two)
    base_other = swap_blk(after(base, gate_up), 2)
    dup, out_part, dx1, dx1_low, da, gain_two_grad, gate_grad, down_grad = feed(
        n2, dy, gate_up, down, x1, dy_own, attn, gain_two
    )

    down_sums = lax.psum_scatter(down_grad, "blk", scatter_dimension=0, tiled=True)
    up_grad = dot_first(n2, dup).astype(BF)
    dx1_low = dx1_low.reshape(count, D)
    out_grad = dot_first(dx1_low, a_own).astype(BF)
    da = after(da, (up_grad, out_grad, base_other))
    dq, dk, dv, head_gain_sums, mixer_sums = attend_back(
        low, lam, q, k, v, start, head_gain, maps, log_mass, da, cosine, sine
    )
    dqkv = jnp.concatenate([dq, dk, dv], axis=1)
    qkv_grad = dot_first(n1, dqkv).astype(BF)
    dn1_part = dot_last(dqkv, attn[:, : 3 * QW]).astype(BF)
    groups = (8, 2, 2, count // 32, D)
    attn_pieces, gate_up_pieces, down_pieces, dx, block_out, gain_one_grad = collect(
        gate_grad, up_grad, qkv_grad, out_grad, down_sums, out_part.reshape(groups), dn1_part.reshape(groups),
        x1, dx1, x_own, gain_one,
    )

    (mixers_grad,) = mixer_back(jnp.sum(mixer_sums))
    small_local = jnp.concatenate(
        [gain_one_grad.reshape(D), gain_two_grad.reshape(D), jnp.sum(head_gain_sums, axis=(0, 2)), mixers_grad.reshape(-1)]
    )
    small_grads = sum_everywhere(small_local)

    unit_of = inverse_order(unit_owner)
    units = lax.dynamic_slice_in_dim(unit_of, me * 9, 9)
    grads = place_units(units, me, attn_pieces, gate_up_pieces, down_pieces)

    steps_done = step_count[0].astype(F32)
    scales = jnp.stack([jnp.float32(learn_rate), 1.0 - beta_one**steps_done, 1.0 - beta_two**steps_done])
    new_first, new_second, new_master, input_grad = rotate_slots(
        grads, base, base_other, slots(first), slots(second), master_slots, dx, scales
    )
    new_small_first = beta_one * small_first + (1.0 - beta_one) * small_grads
    new_small_second = beta_two * small_second + (1.0 - beta_two) * small_grads * small_grads
    new_small = small - small_rate * adam_step(new_small_first, new_small_second, steps_done)
    return (
        block_out,
        input_grad,
        slots(new_master),
        slots(new_first),
        slots(new_second),
        small_grads,
        new_small,
        new_small_first,
        new_small_second,
    )


def solution(mesh):
    in_specs = (
        P("batch", "blk", None),
        P("batch", "blk", None),
        P("batch", None),
        P(),
        P(),
        P("blk", "batch", None),
        P("blk", "batch", None),
        P("blk", "batch", None),
        P("blk", "batch", None),
        P(),
        P(),
        P(),
    )
    out_specs = (
        P("batch", "blk", None),
        P("batch", "blk", None),
        P("blk", "batch", None),
        P("blk", "batch", None),
        P("blk", "batch", None),
        P(),
        P(),
        P(),
        P(),
    )
    by_rows = mesh.shape["blk"] == 8 and mesh.shape["batch"] == 4
    body = row_groups if by_rows else any_mesh
    return jax.shard_map(body, mesh=mesh, in_specs=in_specs, out_specs=out_specs, check_vma=False)
```

```python
import functools

import jax
import jax.numpy as jnp
from jax import lax
from jax.experimental import pallas as pl
from jax.experimental.pallas import tpu as pltpu
from jax.sharding import PartitionSpec as P

D = 1536
H = 12
HD = 64
VD = 128
FF = 4096
UW = 512
NDOC = 6
UNITS = 36


norm_epsilon = 1e-05
lambda_start = 0.2
rope_base = 10000.0
masked_fill = -1000000000.0
beta_one = 0.9
beta_two = 0.95
adam_epsilon = 1e-08
weight_decay = 0.01
small_rate = 1.0


def from_behind(shard, axis, by):
    count = lax.axis_size(axis)
    return lax.ppermute(shard, axis, [(i, (i + by) % count) for i in range(count)])


def root_norm(values, gain):
    return (
        values * lax.rsqrt(jnp.mean(values * values, axis=-1, keepdims=True) + norm_epsilon) * gain
    )


def mix_value(mixers):
    return (
        jnp.exp(jnp.sum(mixers[0] * mixers[1]))
        - jnp.exp(jnp.sum(mixers[2] * mixers[3]))
        + lambda_start
    )


def head_mix(maps_out, head_gain, mixer):
    combined = maps_out[:, :, 0] - mixer * maps_out[:, :, 1]
    normed = (
        combined
        * lax.rsqrt(jnp.mean(combined * combined, axis=-1, keepdims=True) + norm_epsilon)
        * head_gain
        * (1.0 - lambda_start)
    )
    rows_count, heads, positions, width = normed.shape
    return jnp.transpose(normed, (0, 2, 1, 3)).reshape(rows_count, positions, heads * width)


def gated_unit(gate, up):
    return jax.nn.silu(gate) * up


def doc_ends(lengths):
    count = lengths.shape[1]
    ends = [lengths[:, 0]]
    for j in range(1, count):
        ends.append(ends[-1] + lengths[:, j])
    return jnp.stack(ends, axis=1)


def document_places(lengths, places):
    ends = doc_ends(lengths)
    starts = ends - lengths
    segment = jnp.sum((places[None, :, None] >= ends[:, None, :]).astype(jnp.int32), axis=2)
    chosen = segment[:, :, None] == jnp.arange(lengths.shape[1], dtype=jnp.int32)[None, None, :]
    offset = jnp.sum(jnp.where(chosen, starts[:, None, :], 0), axis=2)
    return (segment, places[None, :] - offset)


def allowed(seg_query, place_query, seg_key, place_key, last):
    same = seg_query[:, :, None] == seg_key[:, None, :]
    causal = place_key[None, None, :] <= place_query[None, :, None]
    itself = place_key[None, None, :] == place_query[None, :, None]
    return same & causal & ((seg_query[:, :, None] < last) | itself)


def turn_tables(position):
    rates = rope_base ** (-2.0 * jnp.arange(HD // 2, dtype=jnp.float32) / HD)
    angle = position.astype(jnp.float32)[..., None] * rates
    return (jnp.cos(angle), jnp.sin(angle))


def rotate(values, cosine, sine):
    half = values.shape[-1] // 2
    front = values[..., :half]
    back = values[..., half:]
    return jnp.concatenate([front * cosine - back * sine, back * cosine + front * sine], axis=-1)


def adam_step(first_new, second_new, steps_done):
    return (
        first_new
        / (1.0 - beta_one**steps_done)
        / (jnp.sqrt(second_new / (1.0 - beta_two**steps_done)) + adam_epsilon)
    )


def take_units(stacked, order):
    parts = [lax.dynamic_slice_in_dim(stacked, order[i], 1, axis=1) for i in range(UNITS)]
    return jnp.concatenate(parts, axis=1)


def inverse_order(owner):
    numbers = jnp.arange(UNITS, dtype=jnp.int32)
    return jnp.sum(jnp.where(owner[None, :] == numbers[:, None], numbers[None, :], 0), axis=1)


def contract_rows(left, right):
    return lax.dot_general(
        left, right, (((1,), (1,)), ((), ())), preferred_element_type=jnp.float32
    )


def any_mesh(
    tokens,
    cotangent,
    lengths,
    unit_owner,
    step_count,
    master,
    first,
    second,
    bases,
    small,
    small_first,
    small_second,
):
    rows_count, seq_part, width = tokens.shape
    token_count = rows_count * seq_part
    axis_count = lax.axis_size("blk")
    axis_place = lax.axis_index("blk")
    rows_part = master.shape[0]
    scale = HD ** (-0.5)
    highest = lax.Precision.HIGHEST
    learn_rate = 2.0 / D**0.5
    every_slot = lax.all_gather(master.astype(jnp.bfloat16), "batch", axis=1, tiled=True)
    by_unit = take_units(every_slot, unit_owner).reshape(rows_part, UNITS * UW)
    attention_whole = lax.all_gather(by_unit[:, : 4 * D], "blk", axis=0, tiled=True)
    gate_whole = lax.all_gather(by_unit[:, 4 * D : 4 * D + 2 * FF], "blk", axis=0, tiled=True)
    down_whole = lax.all_gather(by_unit[:, 4 * D + 2 * FF :], "blk", axis=0, tiled=True)
    places = axis_place * seq_part + jnp.arange(seq_part, dtype=jnp.int32)
    segment, position = document_places(lengths, places)
    cosine, sine = turn_tables(position)
    cosine = cosine[:, :, None, None, :]
    sine = sine[:, :, None, None, :]
    residual = tokens.astype(jnp.float32)
    gain_one = small[:D]
    gain_two = small[D : 2 * D]
    head_gain = small[2 * D : 2 * D + VD]
    mixer, mixer_back = jax.vjp(mix_value, small[2 * D + VD :].reshape(4, HD))
    normed_exact, norm_one_back = jax.vjp(root_norm, residual, gain_one)
    normed_one = normed_exact.astype(jnp.bfloat16).reshape(token_count, D)
    projected = jnp.dot(normed_one, attention_whole[:, : 3 * D], preferred_element_type=jnp.float32)
    query = rotate(projected[:, :D].reshape(rows_count, seq_part, H, 2, HD), cosine, sine).astype(
        jnp.bfloat16
    )
    key_own = (
        rotate(projected[:, D : 2 * D].reshape(rows_count, seq_part, H, 2, HD), cosine, sine)
        .astype(jnp.bfloat16)
        .reshape(rows_count, seq_part, D)
    )
    value_own = projected[:, 2 * D :].astype(jnp.bfloat16).reshape(rows_count, seq_part, D)
    best = jnp.full((rows_count, H, 2, seq_part), masked_fill, jnp.float32)
    key_piece = lax.all_gather(key_own, "blk", axis=1, tiled=True)
    value_piece = lax.all_gather(value_own, "blk", axis=1, tiled=True)
    count = key_piece.shape[1]
    key_places = jnp.arange(count, dtype=jnp.int32)
    key_segment, unused = document_places(lengths, key_places)
    mask = allowed(segment, places, key_segment, key_places, NDOC - 1)[:, None, None]
    keys = key_piece.reshape(rows_count, count, H, 2, HD)
    values = value_piece.reshape(rows_count, count, H, VD)
    scores = (
        jnp.einsum("rqhcd,rkhcd->rhcqk", query, keys, preferred_element_type=jnp.float32) * scale
    )
    scores = jnp.where(mask, scores, masked_fill)
    top = jnp.maximum(best, jnp.max(scores, axis=-1))
    shares = jnp.where(mask, jnp.exp(scores - top[..., None]), 0.0)
    mass = jnp.sum(shares, axis=-1)
    summed = jnp.einsum(
        "rhcqk,rkhe->rhcqe", shares.astype(jnp.bfloat16), values, preferred_element_type=jnp.float32
    )
    best, mass, summed = (top, mass, summed)
    maps_out = summed / mass[..., None]
    log_mass = best + jnp.log(mass)
    mixed_exact, mix_back = jax.vjp(head_mix, maps_out, head_gain, mixer)
    mixed = mixed_exact.astype(jnp.bfloat16).reshape(token_count, D)
    middle = residual.reshape(token_count, D) + contract_rows(mixed, attention_whole[:, 3 * D :])
    normed_two_exact, norm_two_back = jax.vjp(root_norm, middle, gain_two)
    normed_two = normed_two_exact.astype(jnp.bfloat16)
    gate_up = jnp.dot(normed_two, gate_whole, preferred_element_type=jnp.float32)
    hidden_exact, gated_back = jax.vjp(gated_unit, gate_up[:, :FF], gate_up[:, FF:])
    hidden = hidden_exact.astype(jnp.bfloat16)
    result = middle + contract_rows(hidden, down_whole)
    block_out = result.astype(jnp.bfloat16).reshape(rows_count, seq_part, D)
    output_grad = cotangent.reshape(token_count, D)
    hidden_grad = jnp.dot(output_grad, down_whole, preferred_element_type=jnp.float32)
    gate_grad, up_grad = gated_back(hidden_grad)
    gate_up_grad = jnp.concatenate([gate_grad, up_grad], axis=1).astype(jnp.bfloat16)
    normed_two_grad = contract_rows(gate_up_grad, gate_whole)
    middle_part, gain_two_grad = norm_two_back(normed_two_grad)
    middle_grad = output_grad.astype(jnp.float32) + middle_part
    middle_low = middle_grad.astype(jnp.bfloat16)
    mixed_grad = jnp.dot(
        middle_low, attention_whole[:, 3 * D :], preferred_element_type=jnp.float32
    )
    maps_grad, head_gain_grad, mixer_grad = mix_back(mixed_grad.reshape(rows_count, seq_part, D))
    maps_low = maps_grad.astype(jnp.bfloat16)
    offset_term = jnp.sum(maps_low.astype(jnp.float32) * maps_out, axis=-1)

    def circle(turn_index, carry):
        moving, moving_grad, query_grad = carry
        source = (axis_place - turn_index) % axis_count
        key_places = source * seq_part + jnp.arange(seq_part, dtype=jnp.int32)
        key_segment, unused = document_places(lengths, key_places)
        mask = allowed(segment, places, key_segment, key_places, NDOC - 1)[:, None, None]
        keys = moving[0].astype(jnp.bfloat16).reshape(rows_count, seq_part, H, 2, HD)
        values = moving[1].astype(jnp.bfloat16).reshape(rows_count, seq_part, H, VD)
        scores = (
            jnp.einsum("rqhcd,rkhcd->rhcqk", query, keys, preferred_element_type=jnp.float32)
            * scale
        )
        shares = jnp.where(mask, jnp.exp(scores - log_mass[..., None]), 0.0)
        value_term = jnp.einsum(
            "rhcqk,rhcqe->rkhe",
            shares.astype(jnp.bfloat16),
            maps_low,
            preferred_element_type=jnp.float32,
        )
        share_grad = jnp.einsum(
            "rhcqe,rkhe->rhcqk", maps_low, values, preferred_element_type=jnp.float32
        )
        score_low = (shares * (share_grad - offset_term[..., None])).astype(jnp.bfloat16)
        query_grad = query_grad + jnp.einsum(
            "rhcqk,rkhcd->rqhcd", score_low, keys, preferred_element_type=jnp.float32
        )
        key_term = jnp.einsum(
            "rhcqk,rqhcd->rkhcd", score_low, query, preferred_element_type=jnp.float32
        )
        update = jnp.stack(
            [key_term.reshape(rows_count, seq_part, D), value_term.reshape(rows_count, seq_part, D)]
        )
        moving_grad = moving_grad + update
        moving, moving_grad = (
            from_behind(moving.astype(jnp.bfloat16), "blk", 1).astype(moving.dtype),
            from_behind(moving_grad.astype(jnp.bfloat16), "blk", 1).astype(moving_grad.dtype),
        )
        return (moving, moving_grad, query_grad)

    circle_start = (
        jnp.stack([key_own, value_own]).astype(jnp.float32),
        jnp.zeros((2, rows_count, seq_part, D), jnp.float32),
        jnp.zeros((rows_count, seq_part, H, 2, HD), jnp.float32),
    )
    moving, moving_grad, query_grad = lax.fori_loop(0, axis_count, circle, circle_start)
    key_grad = moving_grad[0].reshape(rows_count, seq_part, H, 2, HD) * scale
    query_pre = rotate(query_grad * scale, cosine, -sine).reshape(token_count, D)
    key_pre = rotate(key_grad, cosine, -sine).reshape(token_count, D)
    projected_grad = jnp.concatenate(
        [query_pre, key_pre, moving_grad[1].reshape(token_count, D)], axis=1
    ).astype(jnp.bfloat16)
    normed_one_grad = contract_rows(projected_grad, attention_whole[:, : 3 * D])
    residual_part, gain_one_grad = norm_one_back(normed_one_grad.reshape(rows_count, seq_part, D))
    input_grad = (middle_grad.reshape(rows_count, seq_part, D) + residual_part).astype(jnp.bfloat16)
    (mixers_grad,) = mixer_back(mixer_grad)
    small_local = jnp.concatenate(
        [gain_one_grad, gain_two_grad, head_gain_grad, mixers_grad.reshape(-1)]
    )
    small_grads = lax.psum(small_local, ("batch", "blk"))
    right_side = jnp.concatenate([projected_grad, mixed, gate_up_grad, hidden], axis=1)
    left_sides = (normed_one, middle_low, normed_two, output_grad)
    bounds = (0, 3 * D, 4 * D, 4 * D + 2 * FF, 4 * D + 3 * FF)
    slot_order = inverse_order(unit_owner)
    parts = []
    for group in range(4):
        left_rows = left_sides[group]
        parts.append(
            lax.dot_general(
                left_rows,
                right_side[:, bounds[group] : bounds[group + 1]],
                (((0,), (0,)), ((), ())),
                preferred_element_type=jnp.float32,
            )
        )
    row_sums = lax.psum_scatter(
        jnp.concatenate(parts, axis=1).astype(jnp.bfloat16), "blk", scatter_dimension=0, tiled=True
    ).astype(jnp.float32)
    placed = take_units(row_sums.reshape(rows_part, UNITS, UW), slot_order)
    grad_slots = lax.psum_scatter(
        placed.astype(jnp.bfloat16), "batch", scatter_dimension=1, tiled=True
    ).astype(jnp.float32)
    columns = bases
    turned = lax.psum_scatter(
        jnp.einsum("ksa,ksn->asn", columns, grad_slots, precision=highest).astype(jnp.bfloat16),
        "blk",
        scatter_dimension=0,
        tiled=True,
    ).astype(jnp.float32)
    steps_done = step_count[0].astype(jnp.float32)
    new_first = beta_one * first + (1.0 - beta_one) * turned
    new_second = beta_two * second + (1.0 - beta_two) * turned * turned
    normalized = adam_step(new_first, new_second, steps_done)
    columns = bases
    update = jnp.zeros_like(master) + jnp.einsum(
        "ksa,asn->ksn",
        columns,
        lax.all_gather(normalized.astype(jnp.bfloat16), "blk", axis=0, tiled=True).astype(
            jnp.float32
        ),
        precision=highest,
    )
    new_master = master - learn_rate * (update + weight_decay * master)
    new_small_first = beta_one * small_first + (1.0 - beta_one) * small_grads
    new_small_second = beta_two * small_second + (1.0 - beta_two) * small_grads * small_grads
    new_small = small - small_rate * adam_step(new_small_first, new_small_second, steps_done)
    return (
        block_out,
        input_grad,
        new_master,
        new_first,
        new_second,
        small_grads,
        new_small,
        new_small_first,
        new_small_second,
    )


BF = jnp.bfloat16
F32 = jnp.float32
TILE = 256
HEADS = 3
QW = HEADS * VD
FQ = FF // 4
EARLY = 2
VMEM_LIMIT = 56 * 2**20


def params(limit=VMEM_LIMIT, **more):
    return pltpu.CompilerParams(vmem_limit_bytes=limit, **more)


def dot_last(left, right):
    return lax.dot_general(left, right, (((1,), (1,)), ((), ())), preferred_element_type=F32)


def dot_first(left, right):
    return lax.dot_general(left, right, (((0,), (0,)), ((), ())), preferred_element_type=F32)


def dot_plain(left, right):
    return jnp.dot(left, right, preferred_element_type=F32)


def swap_core(piece):
    return lax.ppermute(piece, "batch", [(i, i ^ 1) for i in range(4)])


def swap_y(piece):
    return lax.ppermute(piece, "batch", [(i, i ^ 2) for i in range(4)])


def after(values, earlier):
    return lax.optimization_barrier((values, earlier))[0]


def ring_place(blk):
    side = blk % 2
    return (1 - side) * (blk // 2) + side * (7 - blk // 2)


def ring_owner(place):
    place = (place + 16) % 8
    side = place // 4
    return 2 * ((1 - side) * place + side * (7 - place)) + side


MESH = pl.DeviceIdType.MESH


def greet(devices):
    barrier = pltpu.get_barrier_semaphore()
    for device in devices:
        pl.semaphore_signal(barrier, inc=1, device_id=device, device_id_type=MESH)
    pl.semaphore_wait(barrier, len(devices))


def greet_all():
    barrier = pltpu.get_barrier_semaphore()
    me, blk = lax.axis_index("batch"), lax.axis_index("blk")

    def signal(n, carry):
        at = (me * 8 + blk + n) % 32
        pl.semaphore_signal(barrier, inc=1, device_id=(at // 8, at % 8), device_id_type=MESH)
        return carry

    lax.fori_loop(1, 32, signal, 0)
    pl.semaphore_wait(barrier, 31)


def remote(source, target, sems, at, device):
    return pltpu.make_async_remote_copy(
        src_ref=source,
        dst_ref=target,
        send_sem=sems.at[0, at],
        recv_sem=sems.at[1, at],
        device_id=device,
        device_id_type=MESH,
    )


def to_group_copies(source, between, target, s_batch, s_blk, me, blk):
    size = target.shape[1]

    def over_group(n):
        other = (me + n) % 4
        return pltpu.make_async_remote_copy(
            src_ref=source.at[:, pl.ds(pl.multiple_of(other * size, size), size)],
            dst_ref=between.at[pl.ds(2 * me, 2)],
            send_sem=s_batch.at[0, n],
            recv_sem=s_batch.at[1, 4 - n],
            device_id={"batch": other},
            device_id_type=MESH,
        )

    def group_arrival(n):
        other = (me + n) % 4
        return pltpu.make_async_remote_copy(
            src_ref=source.at[:, pl.ds(0, size)],
            dst_ref=between.at[pl.ds(2 * other, 2)],
            send_sem=s_batch.at[0, n],
            recv_sem=s_batch.at[1, n],
            device_id={"batch": other},
            device_id_type=MESH,
        )

    def over_blk(n, i, local, remote_act):
        other = (me + n) % 4
        row = 2 * other + i
        if n == 0:
            piece = source.at[i, pl.ds(pl.multiple_of(me * size, size), size)]
        else:
            piece = between.at[row]

        @pl.when(row == blk)
        def stay():
            local(pltpu.make_async_copy(piece, target.at[blk], s_blk.at[0, 2 * n + i]))

        @pl.when(row != blk)
        def go():
            remote_act(
                pltpu.make_async_remote_copy(
                    src_ref=piece,
                    dst_ref=target.at[blk],
                    send_sem=s_blk.at[0, 2 * n + i],
                    recv_sem=s_blk.at[1, blk],
                    device_id={"blk": row},
                    device_id_type=MESH,
                )
            )

    def start_group():
        for n in (2, 3, 1):
            over_group(n).start()

    def start_blk(n):
        if n:
            group_arrival(n).wait_recv()
        for i in range(2):
            over_blk(n, i, lambda copy: copy.start(), lambda copy: copy.start())

    def finish():
        for n in (1, 2, 3):
            over_group(n).wait_send()
        for n in range(4):
            for i in range(2):
                over_blk(n, i, lambda copy: copy.wait(), lambda copy: copy.wait_send())
        for k in range(8):

            @pl.when(blk != k)
            def arrived():
                pltpu.make_async_remote_copy(
                    src_ref=between.at[0],
                    dst_ref=target.at[k],
                    send_sem=s_blk.at[0, 0],
                    recv_sem=s_blk.at[1, k],
                    device_id={"blk": k},
                    device_id_type=MESH,
                ).wait_recv()

    return start_group, start_blk, finish


def begin_kernel(
    master_ref, tokens_ref, grad_ref, bases_ref, lengths_ref, pieces_ref, x_ref, dy_ref, base_ref, other_ref, lens_ref, wide, narrow, x_between,
    dy_between, s_core, s_y, s_relay, s_x, s_x2, s_dy, s_dy2, s_load, s_store, s_len, s_other,
):
    me, blk = lax.axis_index("batch"), lax.axis_index("blk")
    y, core = me // 2, me % 2
    to_core = {"batch": y * 2 + 1 - core}
    to_y = {"batch": (1 - y) * 2 + core}
    x_group, x_blk, x_finish = to_group_copies(tokens_ref, x_between, x_ref, s_x, s_x2, me, blk)
    dy_group, dy_blk, dy_finish = to_group_copies(grad_ref, dy_between, dy_ref, s_dy, s_dy2, me, blk)
    slots = bases_ref.shape[0]

    def load(n):
        return pltpu.make_async_copy(bases_ref.at[n], wide.at[n % 2], s_load.at[n])

    def store(n):
        return pltpu.make_async_copy(narrow.at[n % 2], base_ref.at[n], s_store.at[n])

    def lengths_copy(n, at):
        return pltpu.make_async_remote_copy(
            src_ref=lengths_ref,
            dst_ref=lens_ref.at[at],
            send_sem=s_len.at[0, n],
            recv_sem=s_len.at[1, 4 - n if at is me else n],
            device_id={"batch": (me + n) % 4},
            device_id_type=MESH,
        )

    zl = (blk // 2) % 2

    def share(n):
        return remote(base_ref.at[n], other_ref.at[n], s_other, n, {"blk": blk + 2 - 4 * zl})

    def cast(n):
        load(n).wait()
        if n >= 2:
            store(n - 2).wait()
            if n - 2 < EARLY:
                share(n - 2).start()
        narrow[n % 2] = wide[n % 2].astype(BF)
        store(n).start()
        if n + 2 < slots:
            load(n + 2).start()

    def copies(c):
        at = pl.ds(3 * c, 3)
        return (
            lambda: remote(master_ref.at[at], pieces_ref.at[0, at], s_core, c, to_core),
            lambda: remote(master_ref.at[at], pieces_ref.at[1, at], s_y, c, to_y),
            lambda: remote(pieces_ref.at[1, at], pieces_ref.at[2, at], s_relay, c, to_core),
        )

    greet([{"batch": (me + n) % 4} for n in (1, 2, 3)] + [{"blk": (blk + n) % 8} for n in range(1, 8)])
    x_group()
    own_lengths = pltpu.make_async_copy(lengths_ref, lens_ref.at[me], s_len.at[0, 0])
    own_lengths.start()
    for n in (1, 2, 3):
        lengths_copy(n, me).start()
    load(0).start()
    load(1).start()
    x_blk(0)
    cast(0)
    cast(1)
    for c in range(3):
        copies(c)[1]().start()
    dy_group()
    for c in range(3):
        copies(c)[0]().start()
    for n in (1, 2, 3):
        x_blk(n)
    for n in range(2, slots):
        cast(n)
    store(slots - 2).wait()
    store(slots - 1).wait()
    for n in range(4):
        dy_blk(n)
    for c in range(3):
        copies(c)[1]().wait_recv()
        copies(c)[2]().start()
    for c in range(3):
        near, far, relay = copies(c)
        near().wait()
        far().wait_send()
        relay().wait()
    for n in range(EARLY):
        share(n).wait()
    own_lengths.wait()
    for n in (1, 2, 3):
        lengths_copy(n, me).wait_send()
        lengths_copy(n, (me + n) % 4).wait_recv()
    x_finish()
    dy_finish()


def begin(master, tokens, cotangent, bases, lengths):
    hbm = pl.BlockSpec(memory_space=pl.ANY)
    size = tokens.shape[1] // 4
    sems = lambda n: pltpu.SemaphoreType.DMA((2, n))
    return pl.pallas_call(
        begin_kernel,
        in_specs=[hbm] * 4 + [pl.BlockSpec(memory_space=pltpu.VMEM)],
        out_specs=[hbm] * 6,
        out_shape=[
            jax.ShapeDtypeStruct((3,) + master.shape, BF),
            jax.ShapeDtypeStruct((8, size, D), BF),
            jax.ShapeDtypeStruct((8, size, D), BF),
            jax.ShapeDtypeStruct(bases.shape, BF),
            jax.ShapeDtypeStruct((EARLY,) + bases.shape[1:], BF),
            jax.ShapeDtypeStruct((4,) + lengths.shape, jnp.int32),
        ],
        scratch_shapes=[
            pltpu.VMEM((2,) + bases.shape[1:], F32),
            pltpu.VMEM((2,) + bases.shape[1:], BF),
            pltpu.VMEM((8, size, D), BF),
            pltpu.VMEM((8, size, D), BF),
            sems(3),
            sems(3),
            sems(3),
            sems(4),
            sems(8),
            sems(4),
            sems(8),
            pltpu.SemaphoreType.DMA((bases.shape[0],)),
            pltpu.SemaphoreType.DMA((bases.shape[0],)),
            sems(4),
            sems(EARLY),
        ],
        compiler_params=params(collective_id=3, has_side_effects=True),
        name="begin",
    )(master, tokens, cotangent, bases, lengths)


def gather_kernel(
    shard_ref, down_ref, x_ref, rate_ref, lens_ref, attn_ref, downs_ref, xs_ref, outs_ref, cos_ref, sin_ref, start_ref,
    s_local, s_up, s_down, s_up2, s_down2, s_x, s_out,
):
    me, blk = lax.axis_index("batch"), lax.axis_index("blk")
    y, core = me // 2, me % 2
    to_core = {"batch": y * 2 + 1 - core}
    to_y = {"batch": (1 - y) * 2 + core}
    place = ring_place(blk)
    after_me, before_me = {"blk": ring_owner(place + 1)}, {"blk": ring_owner(place - 1)}
    half = shard_ref.shape[0] // 2
    sub = half // 2
    far_slab = (1 - y) * 2 + core

    def ring(t, up, part, second=False):
        owner = ring_owner(place - t) if up else ring_owner(place + t)
        at = pl.ds((0 if up else half) + part * sub, sub)
        target = (downs_ref if second else attn_ref).at[owner, at]
        source = (down_ref if second else shard_ref).at[at] if t == 0 else target
        sems = (s_up2 if up else s_down2) if second else (s_up if up else s_down)
        return remote(source, target, sems, 2 * t + part, after_me if up else before_me)

    def spread(source, whole, sems, c):
        at = pl.ds(4 * c, 4)
        return (
            lambda: remote(source.at[at], whole.at[at, me], sems, c, to_core),
            lambda: remote(source.at[at], whole.at[at, me], sems, 2 + c, to_y),
            lambda: remote(whole.at[at, far_slab], whole.at[at, far_slab], sems, 4 + c, to_core),
        )

    mine = attn_ref.at[:, :, pl.ds(3 * QW, QW)]
    out = (
        lambda: remote(mine, outs_ref.at[0], s_out, 0, to_core),
        lambda: remote(mine, outs_ref.at[1], s_out, 1, to_y),
        lambda: remote(outs_ref.at[1], outs_ref.at[2], s_out, 2, to_core),
    )
    locals_ = [
        pltpu.make_async_copy(shard_ref, attn_ref.at[blk], s_local.at[0]),
        pltpu.make_async_copy(x_ref, xs_ref.at[:, me], s_local.at[1]),
        pltpu.make_async_copy(down_ref, downs_ref.at[blk], s_local.at[2]),
    ]

    def tables():
        lens = [lens_ref[blk // 2, blk % 2, j] for j in range(NDOC)]
        ends = [lens[0]]
        for j in range(1, NDOC):
            ends.append(ends[-1] + lens[j])

        def first_of(places):
            first = jnp.zeros_like(places)
            for j in range(NDOC):
                first += jnp.where(places >= ends[j], lens[j], 0)
            return first

        places = lax.broadcasted_iota(jnp.int32, start_ref.shape, 1)
        start_ref[...] = jnp.where(places >= ends[NDOC - 2], places, first_of(places))
        lane = lax.broadcasted_iota(jnp.int32, (TILE, VD), 1)
        for b in range(cos_ref.shape[0] // TILE):
            places = b * TILE + lax.broadcasted_iota(jnp.int32, (TILE, VD), 0)
            angle = (places - first_of(places)).astype(F32) * rate_ref[...]
            sine = jnp.sin(angle)
            at = slice(b * TILE, (b + 1) * TILE)
            cos_ref[at, :] = jnp.cos(angle)
            sin_ref[at, :] = jnp.where(lane % HD < HD // 2, -sine, sine)

    greet((to_core, to_y, after_me, before_me))
    for part in range(2):
        ring(0, True, part).start()
        ring(0, False, part).start()
    for way in (1, 0):
        for c in range(2):
            spread(x_ref, xs_ref, s_x, c)[way]().start()
    for copy in locals_:
        copy.start()

    def relay(c):
        copies = spread(x_ref, xs_ref, s_x, c)
        copies[1]().wait_recv()
        copies[2]().start()

    tables()
    for t in range(1, 7):
        for part in range(2):
            for up in (True, False):
                ring(t - 1, up, part).wait_recv()
                ring(t, up, part).start()
    for part in range(2):
        for up in (True, False):
            ring(0, up, part, True).start()
            ring(6, up, part).wait_recv()
    locals_[0].wait()
    out[1]().start()
    out[0]().start()
    for t in range(1, 7):
        for part in range(2):
            for up in (True, False):
                ring(t - 1, up, part, True).wait_recv()
                ring(t, up, part, True).start()
        if t in (3, 4):
            relay(t - 3)
    for part in range(2):
        for up in (True, False):
            ring(6, up, part, True).wait_recv()
    out[1]().wait_recv()
    out[2]().start()
    for t in range(7):
        for part in range(2):
            for up in (True, False):
                ring(t, up, part).wait_send()
                ring(t, up, part, True).wait_send()
    for c in range(2):
        near, far, again = spread(x_ref, xs_ref, s_x, c)
        near().wait()
        far().wait_send()
        again().wait()
    out[0]().wait()
    out[1]().wait_send()
    out[2]().wait()
    for copy in locals_[1:]:
        copy.wait()


def gather(shard, down, x, lens):
    hbm = pl.BlockSpec(memory_space=pl.ANY)
    size = x.shape[1]
    sems = lambda n: pltpu.SemaphoreType.DMA((2, n))
    count = 32 * size
    vmem = pl.BlockSpec(memory_space=pltpu.VMEM)
    rates = jnp.tile(rope_base ** (-2.0 * jnp.arange(HD // 2, dtype=F32) / HD), 4).reshape(1, VD)
    return pl.pallas_call(
        gather_kernel,
        in_specs=[vmem] * 4 + [pl.BlockSpec(memory_space=pltpu.SMEM)],
        out_specs=[hbm] * 4 + [vmem] * 3,
        out_shape=[
            jax.ShapeDtypeStruct((8,) + shard.shape, BF),
            jax.ShapeDtypeStruct((8,) + down.shape, BF),
            jax.ShapeDtypeStruct((8, 4, size, D), BF),
            jax.ShapeDtypeStruct((3, 8, shard.shape[0], QW), BF),
            jax.ShapeDtypeStruct((count, VD), F32),
            jax.ShapeDtypeStruct((count, VD), F32),
            jax.ShapeDtypeStruct((1, count), jnp.int32),
        ],
        scratch_shapes=[pltpu.SemaphoreType.DMA((3,))] + [sems(14)] * 4 + [sems(6), sems(3)],
        compiler_params=params(collective_id=4, has_side_effects=True),
        name="gather",
    )(shard, down, x, rates, lens)


def attention_pieces(me):
    pieces = []
    for matrix in range(4):
        for j in range(HEADS):
            block = HEADS * me + j
            pieces.append((3 * matrix + block // 4, block % 4, HEADS * matrix + j))
    return pieces


def pick_kernel(place_ref, me_ref, own, pieces, attn_ref, ffn_ref, down_ref, sems):
    me = me_ref[0]
    waits = []

    def begin(unit, source, target, sem):
        at = place_ref[unit]
        for other, ref in enumerate((own, pieces.at[0], pieces.at[1], pieces.at[2])):

            @pl.when(at // 9 == other)
            def start():
                pltpu.make_async_copy(source(ref.at[at % 9]), target, sem).start()

        waits.append(pltpu.make_async_copy(source(own.at[0]), target, sem))

    for i, (unit, block, packed) in enumerate(attention_pieces(me)):
        column = pl.multiple_of(block * 128, 128)
        begin(unit, lambda r, c=column: r.at[:, pl.ds(c, 128)], attn_ref.at[:, pl.ds(packed * 128, 128)], sems.at[i])
    for i in range(6):
        unit = 12 + 8 * (i // 2) + 2 * me + i % 2
        target = ffn_ref.at[:, pl.ds(i * UW, UW)] if i < 4 else down_ref.at[:, pl.ds((i - 4) * UW, UW)]
        begin(unit, lambda r: r, target, sems.at[12 + i])
    for wait in waits:
        wait.wait()


def pick_units(place, me, own, pieces):
    rows = own.shape[1]
    hbm = pl.BlockSpec(memory_space=pl.ANY)
    smem = pl.BlockSpec(memory_space=pltpu.SMEM)
    vmem = pl.BlockSpec(memory_space=pltpu.VMEM)
    return pl.pallas_call(
        pick_kernel,
        in_specs=[smem, smem, hbm, hbm],
        out_specs=[vmem, vmem, vmem],
        out_shape=[
            jax.ShapeDtypeStruct((rows, 4 * QW), BF),
            jax.ShapeDtypeStruct((rows, 4 * UW), BF),
            jax.ShapeDtypeStruct((rows, 2 * UW), BF),
        ],
        scratch_shapes=[pltpu.SemaphoreType.DMA((18,))],
        compiler_params=params(),
        name="pick_units",
    )(place, me.reshape(1), own, pieces)


def place_kernel(unit_ref, me_ref, attn, gate_up, down, out_ref, sems):
    me = me_ref[0]
    waits = []
    for i in range(9):
        unit = unit_ref[i]
        f = jnp.maximum(unit - 12, 0)
        for q in range(4):
            block = (unit % 3) * 4 + q
            low = f % 16
            choices = (
                (unit < 12, attn, block // HEADS, (unit // 3) * QW + (block % HEADS) * 128),
                ((unit >= 12) & (unit < 28), gate_up, (low % 8) // 2, (low // 8) * FQ + (low % 2) * UW + q * 128),
                (unit >= 28, down, (f % 8) // 2, (f % 2) * UW + q * 128),
            )
            target, sem = out_ref.at[i, :, pl.ds(q * 128, 128)], sems.at[i, q]
            for chosen, pieces, holder, column in choices:

                @pl.when(chosen)
                def start(pieces=pieces, holder=holder, column=column, target=target, sem=sem):
                    source = pieces.at[holder ^ me, :, pl.ds(pl.multiple_of(column, 128), 128)]
                    pltpu.make_async_copy(source, target, sem).start()

            waits.append(pltpu.make_async_copy(attn.at[0, :, pl.ds(0, 128)], target, sem))
    for wait in waits:
        wait.wait()


def place_units(units, me, attn_pieces, gate_up_pieces, down_pieces):
    rows = attn_pieces.shape[1]
    hbm = pl.BlockSpec(memory_space=pl.ANY)
    smem = pl.BlockSpec(memory_space=pltpu.SMEM)
    return pl.pallas_call(
        place_kernel,
        in_specs=[smem, smem] + [hbm] * 3,
        out_specs=pl.BlockSpec(memory_space=pltpu.VMEM),
        out_shape=jax.ShapeDtypeStruct((9, rows, UW), BF),
        scratch_shapes=[pltpu.SemaphoreType.DMA((9, 4))],
        compiler_params=params(),
        name="place_units",
    )(units, me.reshape(1), attn_pieces, gate_up_pieces, down_pieces)


def turn(values, cosine, sine, lane):
    partner = jnp.where(lane % HD < HD // 2, pltpu.roll(values, 96, 1), pltpu.roll(values, 32, 1))
    return values * cosine + partner * sine


def project_kernel(x_ref, w_ref, gain_ref, cos_ref, sin_ref, n_ref, q_ref, k_ref, v_ref):
    x = x_ref[...].astype(F32)
    r = lax.rsqrt(jnp.mean(x * x, axis=-1, keepdims=True) + norm_epsilon)
    n = (x * r * gain_ref[...]).astype(BF)
    n_ref[...] = n
    lane = lax.broadcasted_iota(jnp.int32, (x.shape[0], VD), 1)
    cosine, sine = cos_ref[...], sin_ref[...]
    out = dot_plain(n, w_ref[...])
    for h in range(HEADS):
        at = slice(h * VD, (h + 1) * VD)
        q = turn(out[:, h * VD : (h + 1) * VD], cosine, sine, lane)
        q_ref[:, at] = (q.astype(BF).astype(F32) * HD**-0.5).astype(BF)
        k = turn(out[:, QW + h * VD : QW + (h + 1) * VD], cosine, sine, lane)
        k_ref[:, at] = k.astype(BF)
    v_ref[...] = out[:, 2 * QW :].astype(BF)


def project(x, weights, gain, cosine, sine):
    count = x.shape[0]
    rows = lambda w: pl.BlockSpec((TILE, w), lambda i: (i, 0))
    fixed = lambda h, w: pl.BlockSpec((h, w), lambda i: (0, 0), pipeline_mode=pl.Buffered(1))
    narrow = jax.ShapeDtypeStruct((count, QW), BF)
    return pl.pallas_call(
        project_kernel,
        grid=(count // TILE,),
        in_specs=[rows(D), fixed(D, 3 * QW), fixed(1, D), rows(VD), rows(VD)],
        out_specs=[rows(D), rows(QW), rows(QW), rows(QW)],
        out_shape=[jax.ShapeDtypeStruct((count, D), BF), narrow, narrow, narrow],
        compiler_params=params(),
        cost_estimate=pl.CostEstimate(
            flops=2 * count * D * 3 * QW, bytes_accessed=count * D * 6 + 6 * D * QW, transcendentals=0
        ),
        name="project",
    )(x, weights, gain, cosine, sine)


def split_halves(q):
    lane = lax.broadcasted_iota(jnp.int32, q.shape, 1)
    zero = jnp.zeros_like(q)
    return jnp.concatenate([jnp.where(lane < HD, q, zero), jnp.where(lane >= HD, q, zero)], axis=0)


def block_mask(j, i, start):
    key = j * TILE + lax.broadcasted_iota(jnp.int32, (TILE, 2 * TILE), 0)
    query = i * TILE + lax.broadcasted_iota(jnp.int32, (TILE, TILE), 1)
    query = jnp.concatenate([query, query], axis=1)
    return (key >= start) & (key <= query)


def attend_kernel(low_ref, lam_ref, q_ref, k_ref, v_ref, start_ref, gain_ref, a_ref, maps_ref, log_ref, vt_ref):
    i = pl.program_id(1)

    @pl.when(i == 0)
    def turn_values():
        for j in range(vt_ref.shape[0]):
            vt_ref[j] = v_ref[j * TILE : (j + 1) * TILE, :].astype(F32).T.astype(BF)

    q = split_halves(q_ref[...])
    start = jnp.concatenate([start_ref[...], start_ref[...]], axis=1)

    def step(j, carry):
        top, mass, total = carry
        keys = k_ref[pl.ds(pl.multiple_of(j * TILE, TILE), TILE), :]
        scores = jnp.where(block_mask(j, i, start), dot_last(keys, q), masked_fill)
        new = jnp.maximum(top, jnp.max(scores, axis=0, keepdims=True))
        shares = jnp.exp(scores - new)
        keep = jnp.exp(top - new)
        mass = mass * keep + jnp.sum(shares, axis=0, keepdims=True)
        total = total * keep + dot_plain(vt_ref[j], shares.astype(BF))
        return new, mass, total

    first = (
        jnp.full((1, 2 * TILE), masked_fill, F32),
        jnp.zeros((1, 2 * TILE), F32),
        jnp.zeros((VD, 2 * TILE), F32),
    )
    top, mass, total = lax.fori_loop(low_ref[i], i + 1, step, first)
    maps = total / mass
    one, two = maps[:, :TILE], maps[:, TILE:]
    maps_ref[0, 0] = one
    maps_ref[0, 1] = two
    log_ref[0, 0] = top + jnp.log(mass)
    mixed = one - lam_ref[0] * two
    r = lax.rsqrt(jnp.mean(mixed * mixed, axis=0, keepdims=True) + norm_epsilon)
    a_ref[...] = (mixed * r * gain_ref[...] * (1.0 - lambda_start)).T.astype(BF)


def attend(low, lam, q, k, v, start, gain):
    count = q.shape[0]
    blocks = count // TILE
    smem = pl.BlockSpec(memory_space=pltpu.SMEM)
    return pl.pallas_call(
        attend_kernel,
        grid=(HEADS, blocks),
        in_specs=[
            smem,
            smem,
            pl.BlockSpec((TILE, VD), lambda h, i: (i, h)),
            pl.BlockSpec((count, VD), lambda h, i: (0, h)),
            pl.BlockSpec((count, VD), lambda h, i: (0, h)),
            pl.BlockSpec((1, TILE), lambda h, i: (0, i)),
            pl.BlockSpec((VD, 1), lambda h, i: (0, 0)),
        ],
        out_specs=[
            pl.BlockSpec((TILE, VD), lambda h, i: (i, h)),
            pl.BlockSpec((1, 2, VD, TILE), lambda h, i: (h, 0, 0, i)),
            pl.BlockSpec((1, 1, 1, 2 * TILE), lambda h, i: (h, i, 0, 0)),
        ],
        out_shape=[
            jax.ShapeDtypeStruct((count, QW), BF),
            jax.ShapeDtypeStruct((HEADS, 2, VD, count), F32),
            jax.ShapeDtypeStruct((HEADS, blocks, 1, 2 * TILE), F32),
        ],
        scratch_shapes=[pltpu.VMEM((blocks, VD, TILE), BF)],
        compiler_params=params(),
        cost_estimate=pl.CostEstimate(
            flops=8 * count * count * VD * HEADS, bytes_accessed=count * QW * 16, transcendentals=count * count * HEADS
        ),
        name="attend",
    )(low, lam, q, k, v, start, gain)


def attend_back_kernel(
    low_ref, lam_ref, q_ref, k_ref, v_ref, start_ref, gain_ref, maps_ref, log_ref, da_ref, cosq_ref, sinq_ref,
    cosk_ref, sink_ref, dq_ref, dk_ref, dv_ref, dgain_ref, dlam_ref, kt_ref, dk_sum, dv_sum, dq_sum,
):
    i = pl.program_id(1)
    blocks = kt_ref.shape[0]

    @pl.when(i == 0)
    def begin():
        for j in range(blocks):
            kt_ref[j] = k_ref[j * TILE : (j + 1) * TILE, :].astype(F32).T.astype(BF)
        dk_sum[...] = jnp.zeros_like(dk_sum)
        dv_sum[...] = jnp.zeros_like(dv_sum)
        dgain_ref[...] = jnp.zeros_like(dgain_ref)
        dlam_ref[...] = jnp.zeros_like(dlam_ref)

    lam = lam_ref[0]
    q = split_halves(q_ref[...])
    start = jnp.concatenate([start_ref[...], start_ref[...]], axis=1)
    log_mass = log_ref[0, 0]
    one, two = maps_ref[0, 0], maps_ref[0, 1]
    mixed = one - lam * two
    r = lax.rsqrt(jnp.mean(mixed * mixed, axis=0, keepdims=True) + norm_epsilon)
    t = mixed * r
    da = da_ref[...].T * (1.0 - lambda_start)
    dgain_ref[0] += da * t
    e = da * gain_ref[...]
    dmixed = r * (e - t * jnp.mean(e * t, axis=0, keepdims=True))
    dlam_ref[0] -= jnp.sum(dmixed * two, axis=0, keepdims=True)
    dmaps = jnp.concatenate([dmixed, -lam * dmixed], axis=1).astype(BF)
    maps = jnp.concatenate([one, two], axis=1)
    offset = jnp.sum(dmaps.astype(F32) * maps, axis=0, keepdims=True)
    dq_sum[...] = jnp.zeros_like(dq_sum)

    def step(j, carry):
        at = pl.ds(pl.multiple_of(j * TILE, TILE), TILE)
        keys, values = k_ref[at, :], v_ref[at, :]
        scores = dot_last(keys, q)
        shares = jnp.where(block_mask(j, i, start), jnp.exp(scores - log_mass), 0.0)
        dshares = dot_plain(values, dmaps)
        dscores = (shares * (dshares - offset)).astype(BF)
        dv_sum[at, :] += dot_last(shares.astype(BF), dmaps)
        dk_sum[at, :] += dot_plain(dscores, q)
        dq_sum[...] += dot_plain(kt_ref[j], dscores)
        return carry

    lax.fori_loop(low_ref[i], i + 1, step, 0)
    lane = lax.broadcasted_iota(jnp.int32, (TILE, VD), 1)
    dq = jnp.concatenate([dq_sum[:HD, :TILE], dq_sum[HD:, TILE:]], axis=0).T * HD**-0.5
    dq_ref[...] = turn(dq, cosq_ref[...], -sinq_ref[...], lane).astype(BF)

    @pl.when(i == blocks - 1)
    def finish():
        for j in range(blocks):
            at = slice(j * TILE, (j + 1) * TILE)
            dk_ref[at, :] = turn(dk_sum[at, :], cosk_ref[at, :], -sink_ref[at, :], lane).astype(BF)
        dv_ref[...] = dv_sum[...].astype(BF)


def attend_back(low, lam, q, k, v, start, gain, maps, log_mass, da, cosine, sine):
    count = q.shape[0]
    blocks = count // TILE
    smem = pl.BlockSpec(memory_space=pltpu.SMEM)
    tile = pl.BlockSpec((TILE, VD), lambda h, i: (i, h))
    whole = pl.BlockSpec((count, VD), lambda h, i: (0, h))
    table = pl.BlockSpec((TILE, VD), lambda h, i: (i, 0))
    full_table = pl.BlockSpec((count, VD), lambda h, i: (0, 0), pipeline_mode=pl.Buffered(1))
    narrow = jax.ShapeDtypeStruct((count, QW), BF)
    return pl.pallas_call(
        attend_back_kernel,
        grid=(HEADS, blocks),
        in_specs=[
            smem,
            smem,
            tile,
            whole,
            whole,
            pl.BlockSpec((1, TILE), lambda h, i: (0, i)),
            pl.BlockSpec((VD, 1), lambda h, i: (0, 0)),
            pl.BlockSpec((1, 2, VD, TILE), lambda h, i: (h, 0, 0, i)),
            pl.BlockSpec((1, 1, 1, 2 * TILE), lambda h, i: (h, i, 0, 0)),
            tile,
            table,
            table,
            full_table,
            full_table,
        ],
        out_specs=[
            tile,
            whole,
            whole,
            pl.BlockSpec((1, VD, TILE), lambda h, i: (h, 0, 0)),
            pl.BlockSpec((1, 1, TILE), lambda h, i: (h, 0, 0)),
        ],
        out_shape=[
            narrow,
            narrow,
            narrow,
            jax.ShapeDtypeStruct((HEADS, VD, TILE), F32),
            jax.ShapeDtypeStruct((HEADS, 1, TILE), F32),
        ],
        scratch_shapes=[
            pltpu.VMEM((blocks, VD, TILE), BF),
            pltpu.VMEM((count, VD), F32),
            pltpu.VMEM((count, VD), F32),
            pltpu.VMEM((VD, 2 * TILE), F32),
        ],
        compiler_params=params(),
        cost_estimate=pl.CostEstimate(
            flops=20 * count * count * VD * HEADS, bytes_accessed=count * QW * 24, transcendentals=count * count * HEADS
        ),
        name="attend_back",
    )(low, lam, q, k, v, start, gain, maps, log_mass, da, cosine, sine, cosine, sine)


def middle_kernel(
    x_ref, gain_ref, a_ref, w_ref, w_in, a_hbm, n_ref, own_ref, a_in, total, s_a, s_ay, s_ar
):
    i = pl.program_id(0)
    me = lax.axis_index("batch")
    y, core = me // 2, me % 2
    to_core = {"batch": y * 2 + 1 - core}
    to_y = {"batch": (1 - y) * 2 + core}
    blocks = a_in.shape[1]

    def a_copies(b):
        source = a_hbm.at[pl.ds(b * TILE, TILE)]
        return (
            lambda: remote(source, a_in.at[0, b], s_a, b, to_core),
            lambda: remote(source, a_in.at[1, b], s_ay, b, to_y),
            lambda: remote(a_in.at[1, b], a_in.at[2, b], s_ar, b, to_core),
        )

    @pl.when(i == 0)
    def begin():
        greet((to_core, to_y))
        for b in range(blocks):
            a_copies(b)[1]().start()
        for b in range(blocks):
            a_copies(b)[0]().start()

    @pl.when(i < blocks)
    def relay():
        a_copies(i)[1]().wait_recv()
        a_copies(i)[2]().start()

    @pl.when(i >= 1)
    def compute():
        b = i - 1
        a_copies(b)[0]().wait_recv()
        a_copies(b)[2]().wait_recv()
        x1 = x_ref[...].astype(F32) + dot_last(a_ref[...], w_ref[...])
        for other in range(3):
            x1 += dot_last(a_in[other, b], w_in[other])
        total[...] = x1
        r = lax.rsqrt(jnp.mean(x1 * x1, axis=-1, keepdims=True) + norm_epsilon)
        n_ref[...] = (x1 * r * gain_ref[...]).astype(BF)
        part = TILE // 4
        own_ref[0] = total[pl.ds(pl.multiple_of(me * part, part), part), :]

    @pl.when(i == blocks)
    def finish():
        for b in range(blocks):
            for copy in a_copies(b):
                copy().wait_send()


def middle(a, x, attn, others, gain):
    count = x.shape[0]
    blocks = count // TILE
    late = lambda i: (jnp.maximum(i - 1, 0), 0)
    hbm = pl.BlockSpec(memory_space=pl.ANY)
    sems = lambda n: pltpu.SemaphoreType.DMA((2, n))
    return pl.pallas_call(
        middle_kernel,
        grid=(blocks + 1,),
        in_specs=[
            pl.BlockSpec((TILE, D), late),
            pl.BlockSpec((1, D), lambda i: (0, 0)),
            pl.BlockSpec((TILE, QW), late),
            pl.BlockSpec((D, QW), lambda i: (0, 3), pipeline_mode=pl.Buffered(1)),
            pl.BlockSpec((3, D, QW), lambda i: (0, 0, 0), pipeline_mode=pl.Buffered(1)),
            hbm,
        ],
        out_specs=[
            pl.BlockSpec((TILE, D), late),
            pl.BlockSpec((1, TILE // 4, D), lambda i: (jnp.maximum(i - 1, 0), 0, 0)),
        ],
        out_shape=[
            jax.ShapeDtypeStruct((count, D), BF),
            jax.ShapeDtypeStruct((blocks, TILE // 4, D), F32),
        ],
        scratch_shapes=[
            pltpu.VMEM((3, blocks, TILE, QW), BF),
            pltpu.VMEM((TILE, D), F32),
            sems(blocks),
            sems(blocks),
            sems(blocks),
        ],
        compiler_params=params(collective_id=5, has_side_effects=True),
        cost_estimate=pl.CostEstimate(
            flops=2 * count * D * D, bytes_accessed=count * D * 7 + 2 * D * D, transcendentals=0
        ),
        name="middle",
    )(x, gain, a, attn, others, a)


def feed_kernel(
    n_ref, dy0_ref, dy1_ref, dy2_ref, dy3_ref, w_ref, wd_ref, x1_ref, dyo_ref, wo_ref, gain_ref, base_ref, dup_ref, out_ref, dx_ref, low_ref, da_ref, dgain_ref,
    gate_grad_ref, down_grad_ref, other_ref, dy_ref, part, near_in, near, far_in, gathered, gate_sum, down_sum, staged, s_near, s_far, s_y,
    s_core, s_relay, s_grad, s_low, s_other,
):
    i = pl.program_id(0)
    me = lax.axis_index("batch")
    y, core = me // 2, me % 2
    to_core = {"batch": y * 2 + 1 - core}
    to_y = {"batch": (1 - y) * 2 + core}
    blocks = near_in.shape[0]

    def near_copy(b):
        return remote(part.at[b % 3, :, 1 - core], near_in.at[b], s_near, b, to_core)

    blk = lax.axis_index("blk")
    to_pair = {"blk": blk + 2 - 4 * ((blk // 2) % 2)}

    def share(n):
        return remote(base_ref.at[EARLY + n], other_ref.at[n], s_other, n, to_pair)

    def low_copy(b):
        return pltpu.make_async_copy(gathered.at[b], low_ref.at[b], s_low.at[b])

    grads = ((gate_sum, gate_grad_ref), (down_sum, down_grad_ref))
    strip = gate_sum.shape[0] // 4

    def grad_copy(n, which):
        at = pl.ds(pl.multiple_of(n * strip, strip), strip)
        return pltpu.make_async_copy(staged.at[which], grads[which][1].at[at], s_grad.at[which, n])

    def far_copy(b):
        return remote(near.at[b], far_in.at[b], s_far, b, to_y)

    def own_copy(b, sems, device):
        return remote(gathered.at[b, me], gathered.at[b, me], sems, b, device)

    def relay_copy(b):
        slab = (1 - y) * 2 + core
        return remote(gathered.at[b, slab], gathered.at[b, slab], s_relay, b, to_core)

    @pl.when(i == 0)
    def begin():
        greet((to_core, to_y, to_pair))
        for n in range(other_ref.shape[0]):
            share(n).start()
        dgain_ref[...] = jnp.zeros_like(dgain_ref)
        gate_sum[...] = jnp.zeros_like(gate_sum)
        down_sum[...] = jnp.zeros_like(down_sum)

    @pl.when((i >= 1) & (i < blocks + 1))
    def send_far():
        b = i - 1
        near_copy(b).wait_recv()
        both = part[b % 3, 1 - y, core].astype(F32) + near_in[b, 1 - y].astype(F32)
        near[b] = both.astype(BF)
        far_copy(b).start()

    @pl.when((i >= 2) & (i < blocks + 2))
    def send_own():
        b = i - 2
        far_copy(b).wait_recv()
        dn = part[b % 3, y, core].astype(F32) + near_in[b, y].astype(F32) + far_in[b].astype(F32)
        x1 = x1_ref[0]
        r = lax.rsqrt(jnp.mean(x1 * x1, axis=-1, keepdims=True) + norm_epsilon)
        t = x1 * r
        e = dn * gain_ref[...]
        dx = dyo_ref[0].astype(F32) + r * (e - t * jnp.mean(e * t, axis=-1, keepdims=True))
        dgain_ref[...] += jnp.sum(dn * t, axis=0, keepdims=True)
        dx_ref[0] = dx
        gathered[b, me] = dx.astype(BF)
        own_copy(b, s_y, to_y).start()
        own_copy(b, s_core, to_core).start()

    @pl.when((i >= 3) & (i < blocks + 3))
    def send_relay():
        b = i - 3
        own_copy(b, s_y, to_y).wait_recv()
        relay_copy(b).start()

    @pl.when(i >= 4)
    def use():
        b = i - 4
        own_copy(b, s_core, to_core).wait_recv()
        relay_copy(b).wait_recv()
        whole = jnp.concatenate([gathered[b, other] for other in range(4)], axis=0)
        low_copy(b).start()
        da_ref[...] = dot_plain(whole, wo_ref[...])

    @pl.when(i < blocks)
    def compute():
        size = dy0_ref.shape[1]
        slabs = (me, 2 * y + 1 - core, 2 * (1 - y) + core, 2 * (1 - y) + 1 - core)
        for slab, piece in zip(slabs, (dy0_ref, dy1_ref, dy2_ref, dy3_ref)):
            dy_ref[pl.ds(pl.multiple_of(slab * size, size), size), :] = piece[0]
        n, dy = n_ref[...], dy_ref[...]
        wg, wu, wd = w_ref[:, :FQ], w_ref[:, FQ:], wd_ref[...]
        gate = dot_plain(n, wg)
        up = dot_plain(n, wu)
        dhidden = dot_plain(dy, wd)
        share = 1.0 / (1.0 + jnp.exp(-gate))
        silu = gate * share
        hidden = (silu * up).astype(BF)
        dup = (dhidden * silu).astype(BF)
        dgate = (dhidden * up * (share * (1.0 + gate * (1.0 - share)))).astype(BF)
        dup_ref[...] = dup
        dn = (dot_last(dgate, wg) + dot_last(dup, wu)).astype(BF)

        @pl.when(i >= 3)
        def reuse():
            near_copy(i - 3).wait_send()

        for other in range(4):
            part[i % 3, other // 2, other % 2] = dn[other * size : (other + 1) * size]
        near_copy(i).start()
        out_ref[...] = dot_last(hidden, wd).astype(BF)
        for c in range(0, n.shape[1], TILE):
            gate_sum[c : c + TILE, :] += dot_first(n[:, c : c + TILE], dgate)
            down_sum[c : c + TILE, :] += dot_first(dy[:, c : c + TILE], hidden)

    @pl.when(i >= blocks)
    def keep():
        n = i - blocks
        for which in range(2):

            @pl.when(n >= 1)
            def reuse(which=which):
                grad_copy(n - 1, which).wait()

            at = pl.ds(pl.multiple_of(n * strip, strip), strip)
            staged[which] = grads[which][0][at, :].astype(BF)
            grad_copy(n, which).start()

    @pl.when(i == blocks + 3)
    def finish():
        for which in range(2):
            grad_copy(3, which).wait()
        for b in range(blocks - 3, blocks):
            near_copy(b).wait_send()
        for b in range(blocks):
            far_copy(b).wait_send()
            own_copy(b, s_y, to_y).wait_send()
            own_copy(b, s_core, to_core).wait_send()
            relay_copy(b).wait_send()
            low_copy(b).wait()
        for n in range(other_ref.shape[0]):
            share(n).wait()


def feed(n, dy, weights, down, x1, dy_own, attn, gain, base):
    count = n.shape[0]
    blocks = count // TILE
    size = TILE // 4
    late = lambda lag: lambda i: (jnp.clip(i - lag, 0, blocks - 1), 0)
    late3 = lambda lag: lambda i: (jnp.clip(i - lag, 0, blocks - 1), 0, 0)
    rows = lambda w, lag: pl.BlockSpec((TILE, w), late(lag))
    own = pl.BlockSpec((1, size, D), late3(2))
    shape = lambda w, kind=BF: jax.ShapeDtypeStruct((count, w), kind)
    sems = pltpu.SemaphoreType.DMA((2, blocks))
    return pl.pallas_call(
        feed_kernel,
        grid=(blocks + 4,),
        in_specs=[
            rows(D, 0),
            pl.BlockSpec((1, size, D), late3(0)),
            pl.BlockSpec((1, size, D), late3(0)),
            pl.BlockSpec((1, size, D), late3(0)),
            pl.BlockSpec((1, size, D), late3(0)),
            pl.BlockSpec((D, 2 * FQ), lambda i: (0, 0), pipeline_mode=pl.Buffered(1)),
            pl.BlockSpec((D, FQ), lambda i: (0, 0), pipeline_mode=pl.Buffered(1)),
            own,
            own,
            pl.BlockSpec((D, QW), lambda i: (0, 3), pipeline_mode=pl.Buffered(1)),
            pl.BlockSpec((1, D), lambda i: (0, 0)),
            pl.BlockSpec(memory_space=pl.ANY),
        ],
        out_specs=[
            rows(FQ, 0),
            rows(D, 0),
            own,
            pl.BlockSpec(memory_space=pl.ANY),
            rows(QW, 4),
            pl.BlockSpec((1, D), lambda i: (0, 0)),
            pl.BlockSpec(memory_space=pl.ANY),
            pl.BlockSpec(memory_space=pl.ANY),
            pl.BlockSpec(memory_space=pl.ANY),
        ],
        out_shape=[
            shape(FQ),
            shape(D),
            jax.ShapeDtypeStruct((blocks, size, D), F32),
            jax.ShapeDtypeStruct((blocks, 4, size, D), BF),
            shape(QW, F32),
            jax.ShapeDtypeStruct((1, D), F32),
            jax.ShapeDtypeStruct((D, FQ), BF),
            jax.ShapeDtypeStruct((D, FQ), BF),
            jax.ShapeDtypeStruct((base.shape[0] - EARLY,) + base.shape[1:], BF),
        ],
        scratch_shapes=[
            pltpu.VMEM((TILE, D), BF),
            pltpu.VMEM((3, 2, 2, size, D), BF),
            pltpu.VMEM((blocks, 2, size, D), BF),
            pltpu.VMEM((blocks, size, D), BF),
            pltpu.VMEM((blocks, size, D), BF),
            pltpu.VMEM((blocks, 4, size, D), BF),
            pltpu.VMEM((D, FQ), F32),
            pltpu.VMEM((D, FQ), F32),
            pltpu.VMEM((2, D // 4, FQ), BF),
            sems,
            sems,
            sems,
            sems,
            sems,
            pltpu.SemaphoreType.DMA((2, 4)),
            pltpu.SemaphoreType.DMA((blocks,)),
            pltpu.SemaphoreType.DMA((2, base.shape[0] - EARLY)),
        ],
        compiler_params=params(63 * 2**20, collective_id=1, has_side_effects=True),
        cost_estimate=pl.CostEstimate(
            flops=12 * count * D * FQ, bytes_accessed=count * (8 * D + 6 * FQ) + 6 * D * FQ, transcendentals=count * FQ
        ),
        name="feed",
    )(n, *dy, weights, down, x1, dy_own, attn, gain, base)


def return_rows_copies(source, target, sems, me, blk):
    size = source.shape[1]

    def copies(act_local, act_remote):
        for k in range(8):
            here = (me == blk // 2) & (blk == k)
            piece = target.at[blk % 2, pl.ds(pl.multiple_of(me * size, size), size)]

            @pl.when(here)
            def stay():
                act_local(pltpu.make_async_copy(source.at[k], piece, sems.at[0, k]))

            @pl.when(jnp.logical_not(here))
            def go():
                act_remote(
                    pltpu.make_async_remote_copy(
                        src_ref=source.at[k],
                        dst_ref=piece,
                        send_sem=sems.at[0, k],
                        recv_sem=sems.at[1, (blk % 2) * 4 + me],
                        device_id=(blk // 2, k),
                        device_id_type=MESH,
                    )
                )

    def start():
        copies(lambda copy: copy.start(), lambda copy: copy.start())

    def finish():
        copies(lambda copy: copy.wait(), lambda copy: copy.wait_send())
        for i in range(2):
            for other in range(4):

                @pl.when((me != other) | (blk != 2 * me + i))
                def arrived():
                    pltpu.make_async_remote_copy(
                        src_ref=source.at[0],
                        dst_ref=target.at[i, pl.ds(other * size, size)],
                        send_sem=sems.at[0, 0],
                        recv_sem=sems.at[1, 4 * i + other],
                        device_id=(me, blk),
                        device_id_type=MESH,
                    ).wait_recv()

    return start, finish


def collect_kernel(
    gate, up, dqkv, a_own, n1_ref, low_ref, down_ref, out_part_ref, dn1_part_ref, x1_ref, dx1_ref, x_ref, gain_ref, attn_ref, gate_up_ref,
    downs_ref, dx_ref, back_ref, dgain_ref, qkv, out, strips, first_in, second_in, first_sum, second_sum, own, near_in, near, far_in,
    out_rows, s_up, s_down, s_up2, s_down2, s_near, s_own, s_far, s_pieces, s_local, s_back,
    s_strip,
):
    me, blk = lax.axis_index("batch"), lax.axis_index("blk")
    y, core = me // 2, me % 2
    to_core = {"batch": y * 2 + 1 - core}
    to_y = {"batch": (1 - y) * 2 + core}
    place = ring_place(blk)
    after_me, before_me = {"blk": ring_owner(place + 1)}, {"blk": ring_owner(place - 1)}
    part = first_sum.shape[0]
    half = part // 2
    blocks = dx1_ref.shape[0]

    wide = QW + 256
    plans = (
        ((gate, 0, FQ, 0), (up, 0, FQ, FQ)),
        ((qkv, 0, wide, 0), (qkv, wide, 3 * QW - wide, wide), (out, 0, QW, 3 * QW)),
    )
    buffers, totals = (first_in, second_in), (first_sum, second_sum)
    ring_sems = ((s_up, s_down), (s_up2, s_down2))

    def mine(r, t, up_way, p):
        grad, column, width, _ = plans[r][p]
        owner = ring_owner(place - 1 - t) if up_way else ring_owner(place + 1 + t)
        begin = pl.multiple_of(owner * part + (0 if up_way else half), half)
        return grad.at[pl.ds(begin, half), pl.ds(column, width)]

    def landing(r, t, up_way, p):
        _, _, width, to = plans[r][p]
        return buffers[r].at[0 if up_way else 1, t, :, pl.ds(to, width)]

    def ring(r, t, up_way, p):
        source = mine(r, 0, up_way, p) if t == 0 else landing(r, t - 1, up_way, p)
        sems = ring_sems[r][0 if up_way else 1]
        at = len(plans[r]) * t + p
        return remote(source, landing(r, t, up_way, p), sems, at, after_me if up_way else before_me)

    def ring_start(r):
        for p in range(len(plans[r])):
            ring(r, 0, True, p).start()
            ring(r, 0, False, p).start()

    def ring_step(r, t, p):
        _, _, width, to = plans[r][p]
        for up_way in (True, False):
            ring(r, t - 1, up_way, p).wait_recv()
            here = landing(r, t - 1, up_way, p)
            value = (here[...].astype(F32) + mine(r, t, up_way, p)[...].astype(F32)).astype(BF)
            if t < 7:
                here[...] = value
                ring(r, t, up_way, p).start()
            else:
                totals[r][0 if up_way else half : half if up_way else part, to : to + width] = value

    def exchange(source, target, n):
        return (
            lambda: remote(source, target.at[1], s_pieces, 3 * n, to_core),
            lambda: remote(source, target.at[2], s_pieces, 3 * n + 1, to_y),
            lambda: remote(target.at[2], target.at[3], s_pieces, 3 * n + 2, to_core),
            lambda: pltpu.make_async_copy(source, target.at[0], s_local.at[n]),
        )

    exchanges = [exchange(down_ref, downs_ref, 0), exchange(first_sum, gate_up_ref, 1)]
    for p, (_, _, width, to) in enumerate(plans[1]):
        at = pl.ds(to, width)
        exchanges.append(exchange(second_sum.at[:, at], attn_ref.at[:, :, at], 2 + p))

    strip = strips.shape[2]
    count = D // strip
    lefts, rights, results = (n1_ref, low_ref), (dqkv, a_own), (qkv, out)

    def strip_copy(n):
        source = lefts[n // count].at[:, pl.ds((n % count) * strip, strip)]
        return pltpu.make_async_copy(source, strips.at[n % 2], s_strip.at[n])

    def strip_product(n):
        strip_copy(n).wait()
        at = pl.ds((n % count) * strip, strip)
        results[n // count][at, :] = dot_first(strips[n % 2], rights[n // count][...]).astype(BF)
        if n + 2 < 2 * count:
            strip_copy(n + 2).start()

    def spread(n):
        for way in (1, 0, 3):
            exchanges[n][way]().start()

    def relay(n):
        exchanges[n][1]().wait_recv()
        exchanges[n][2]().start()

    parts = (out_part_ref, dn1_part_ref)

    def near_copy(j):
        return remote(parts[j // blocks].at[j % blocks, :, 1 - core], near_in.at[j], s_near, j, to_core)

    def own_copy(j):
        return pltpu.make_async_copy(parts[j // blocks].at[j % blocks, :, core], own.at[j], s_own.at[j])

    def far_copy(j):
        return remote(near.at[j], far_in.at[j], s_far, j, to_y)

    def near_step(j):
        near_copy(j).wait_recv()
        own_copy(j).wait()
        near[j] = (own[j, 1 - y].astype(F32) + near_in[j, 1 - y].astype(F32)).astype(BF)
        far_copy(j).start()

    def far_step(j):
        far_copy(j).wait_recv()
        total = own[j, y].astype(F32) + near_in[j, y].astype(F32) + far_in[j].astype(F32)
        b = j % blocks
        if j < blocks:
            out_rows[b] = (x1_ref[b] + total).astype(BF)
            return
        x = x_ref[b].astype(F32)
        r = lax.rsqrt(jnp.mean(x * x, axis=-1, keepdims=True) + norm_epsilon)
        t = x * r
        e = total * gain_ref[...]
        dx = dx1_ref[b] + r * (e - t * jnp.mean(e * t, axis=-1, keepdims=True))
        dx_ref[b] = dx.astype(BF)
        dgain_ref[...] += jnp.sum(total * t, axis=0, keepdims=True)

    back_start, back_finish = return_rows_copies(out_rows, back_ref, s_back, me, blk)
    dgain_ref[...] = jnp.zeros_like(dgain_ref)
    greet_all()
    ring_start(0)
    for j in range(2 * blocks):
        own_copy(j).start()
        near_copy(j).start()
    spread(0)
    strip_copy(0).start()
    strip_copy(1).start()
    groups = [(r, t, p) for r in range(2) for t in range(1, 8) for p in range(len(plans[r]))]
    for g, (r, t, p) in enumerate(groups):
        ring_step(r, t, p)
        if g < 2 * count:
            strip_product(g)
        if g < 2 * blocks:
            near_step(g)
        if 3 <= g < 2 * blocks + 3:
            far_step(g - 3)
        if (r, t, p) == (0, 6, 1):
            ring_start(1)
            relay(0)
        if (r, t, p) == (0, 7, 1):
            spread(1)
            back_start()
        if (r, t, p) == (1, 5, 0):
            relay(1)
        if (r, t) == (1, 7):
            spread(2 + p)
    for p in range(3):
        relay(2 + p)
    back_finish()
    for n in range(5):
        near_piece, far_piece, relay_piece, local = exchanges[n]
        near_piece().wait()
        far_piece().wait_send()
        relay_piece().wait()
        local().wait()
    for j in range(2 * blocks):
        near_copy(j).wait_send()
        far_copy(j).wait_send()
    for r in range(2):
        for t in range(7):
            for p in range(len(plans[r])):
                ring(r, t, True, p).wait_send()
                ring(r, t, False, p).wait_send()


def collect(gate, up, n1, dqkv, low, a_own, down, out_part, dn1_part, x1, dx1, x, gain):
    part = D // 8
    size = x.shape[1]
    items = 2 * x.shape[0]
    hbm = pl.BlockSpec(memory_space=pl.ANY)
    vmem = pl.BlockSpec(memory_space=pltpu.VMEM)
    sems = lambda n: pltpu.SemaphoreType.DMA((2, n))
    four = lambda width: jax.ShapeDtypeStruct((4, part, width), BF)
    return pl.pallas_call(
        collect_kernel,
        in_specs=[vmem] * 4 + [hbm] * 5 + [vmem] * 4,
        out_specs=[hbm] * 3 + [vmem, hbm, vmem],
        out_shape=[
            four(4 * QW),
            four(2 * FQ),
            four(FQ),
            jax.ShapeDtypeStruct(x.shape, BF),
            jax.ShapeDtypeStruct((2, 4 * size, D), BF),
            jax.ShapeDtypeStruct((1, D), F32),
        ],
        scratch_shapes=[
            pltpu.VMEM((D, 3 * QW), BF),
            pltpu.VMEM((D, QW), BF),
            pltpu.VMEM((2, n1.shape[0], TILE), BF),
            pltpu.VMEM((2, 7, part // 2, 2 * FQ), BF),
            pltpu.VMEM((2, 7, part // 2, 4 * QW), BF),
            pltpu.VMEM((part, 2 * FQ), BF),
            pltpu.VMEM((part, 4 * QW), BF),
            pltpu.VMEM((items, 2, size, D), BF),
            pltpu.VMEM((items, 2, size, D), BF),
            pltpu.VMEM((items, size, D), BF),
            pltpu.VMEM((items, size, D), BF),
            pltpu.VMEM(x.shape, BF),
            sems(14),
            sems(14),
            sems(21),
            sems(21),
            sems(items),
            pltpu.SemaphoreType.DMA((items,)),
            sems(items),
            sems(15),
            pltpu.SemaphoreType.DMA((5,)),
            sems(8),
            pltpu.SemaphoreType.DMA((2 * D // TILE,)),
        ],
        compiler_params=params(63 * 2**20, collective_id=6, has_side_effects=True),
        cost_estimate=pl.CostEstimate(flops=10**11, bytes_accessed=2**25, transcendentals=0),
        name="collect",
    )(gate, up, dqkv, a_own, n1, low, down, out_part, dn1_part, x1, dx1, x, gain)


def rotate_kernel(
    g_ref, base_ref, early_ref, other_ref, first_ref, second_ref, master_ref, rows_ref, small_ref, scale_ref, new_first_ref,
    new_second_ref, new_master_ref, rows_out_ref, small_out_ref, group_small, blk_small, g, base, other, firsts, seconds, masters, g_in, part, x_in, near, z_in, far, p_in, step, steps,
    back, back_in, steps_own, load, store, s_g, s_x, s_z, s_p, s_step, s_back, s_up, s_side, s_rows,
    s_small, s_small2,
):
    blk = lax.axis_index("blk")
    zh, zl, xx = blk // 4, (blk // 2) % 2, blk % 2
    to_x = {"blk": blk + 1 - 2 * xx}
    to_z = {"blk": blk + 4 - 8 * zh}
    to_pair = {"blk": blk + 2 - 4 * zl}
    count = g.shape[0]
    half = UW // 2
    own = pl.ds(pl.multiple_of(zl * half, half), half)
    away = pl.ds(pl.multiple_of((1 - zl) * half, half), half)
    block = 4 * zh + xx
    loads = [
        (g_ref, g), (base_ref, base), (other_ref, other), (first_ref, firsts), (second_ref, seconds), (master_ref, masters),
    ]
    stores = [(firsts, new_first_ref), (seconds, new_second_ref), (masters, new_master_ref)]

    def loading(i, s):
        if i == 2:
            early = isinstance(s, int) and s < EARLY
            source = early_ref.at[s] if early else other_ref.at[jnp.maximum(s - EARLY, 0)]
            return pltpu.make_async_copy(source, other.at[s], load.at[i, s])
        return pltpu.make_async_copy(loads[i][0].at[s], loads[i][1].at[s], load.at[i, s])

    def storing(i, s):
        return pltpu.make_async_copy(stores[i][0].at[s], stores[i][1].at[s], store.at[i, s])

    def send_g(s):
        return remote(g.at[s, :, away], g_in.at[s], s_g, s, to_pair)

    def send_x(s):
        return remote(part.at[s % 3, :, 1 - xx], x_in.at[s], s_x, s, to_x)

    def send_z(s):
        return remote(near.at[s % 3, 1 - zh], z_in.at[s], s_z, s, to_z)

    def send_p(s):
        return remote(far.at[s % 3], p_in.at[s], s_p, s, to_pair)

    def step_pair(s):
        return remote(step.at[s, :, away], steps.at[s, block + 2 * zl], s_step, s, to_pair)

    def step_z(s, a):
        return remote(steps.at[s, block + 2 * a], steps.at[s, block + 2 * a], s_up, 2 * s + a, to_z)

    def step_x(s, a):
        at = 2 * a + xx
        return remote(steps.at[s, at], steps.at[s, at], s_side, 4 * s + a, to_x)

    def send_back(s):
        return remote(back.at[s % 3], back_in.at[s], s_back, s, to_pair)

    for i in range(len(loads)):
        for s in range(count):
            loading(i, s).start()
    rows_start, rows_finish = return_rows_copies(rows_ref, rows_out_ref, s_rows, lax.axis_index("batch"), blk)
    greet_all()
    for s in range(count):
        loading(0, s).wait()
        send_g(s).start()
    rows_start()
    me = lax.axis_index("batch")
    group_small[me] = small_ref[...]

    def small_over(buffer, at, n, size, axis, sems):
        return pltpu.make_async_remote_copy(
            src_ref=buffer.at[at],
            dst_ref=buffer.at[at],
            send_sem=sems.at[0, n],
            recv_sem=sems.at[1, size - n],
            device_id={axis: (at + n) % size},
            device_id_type=MESH,
        )

    def small_from(buffer, at, n, size, axis, sems):
        other = (at + n) % size
        return pltpu.make_async_remote_copy(
            src_ref=buffer.at[other],
            dst_ref=buffer.at[other],
            send_sem=sems.at[0, n],
            recv_sem=sems.at[1, n],
            device_id={axis: other},
            device_id_type=MESH,
        )

    over_group = (group_small, me, 4, "batch", s_small)
    over_blk = (blk_small, blk, 8, "blk", s_small2)

    def small_each(which, act, begin):
        buffer, at, size, axis, sems = which
        for n in range(1, size):
            act(begin(buffer, at, n, size, axis, sems))

    rows = base.shape[1]

    def tick(t, carry):
        def stage(lag, act):
            @pl.when((t >= lag) & (t < count + lag))
            def run():
                act(t - lag)

        def finish(s):
            send_back(s).wait_recv()
            loading(5, s).wait()
            for at, update in ((own, steps_own[s % 2]), (away, back_in[s].astype(F32))):
                value = masters[s, :, at]
                masters[s, :, at] = value - scale_ref[0] * (update + weight_decay * value)
            storing(2, s).start()

        def update(s):
            for a in range(4):
                step_x(s, a).wait_recv()
            whole = jnp.concatenate([steps[s, b] for b in range(8)], axis=0)
            steps_own[s % 2] = dot_plain(base[s], whole)

            @pl.when(s >= 3)
            def reuse():
                send_back(s - 3).wait_send()

            back[s % 3] = dot_plain(other[s], whole).astype(BF)
            send_back(s).start()

        def relay_x(s):
            for a in range(2):
                step_z(s, a).wait_recv()
            for a in range(4):
                step_x(s, a).start()

        def relay_z(s):
            step_pair(s).wait_recv()
            for a in range(2):
                step_z(s, a).start()

        def adam(s):
            send_p(s).wait_recv()
            loading(3, s).wait()
            loading(4, s).wait()
            mine = near[s % 3, zh, zl].astype(F32) + z_in[s, zl].astype(F32)
            for at, turned in ((own, mine), (away, p_in[s].astype(F32))):
                new_first = beta_one * firsts[s, :, at] + (1.0 - beta_one) * turned
                new_second = beta_two * seconds[s, :, at] + (1.0 - beta_two) * turned * turned
                firsts[s, :, at] = new_first
                seconds[s, :, at] = new_second
                moved = new_first / scale_ref[1] / (jnp.sqrt(new_second / scale_ref[2]) + adam_epsilon)
                step[s, :, at] = moved.astype(BF)
            storing(0, s).start()
            storing(1, s).start()
            steps[s, block + 2 * zl] = step[s, :, own]
            step_pair(s).start()

        def send_far(s):
            send_z(s).wait_recv()

            @pl.when(s >= 3)
            def reuse():
                send_p(s - 3).wait_send()

            far[s % 3] = (near[s % 3, zh, 1 - zl].astype(F32) + z_in[s, 1 - zl].astype(F32)).astype(BF)
            send_p(s).start()

        def send_near(s):
            send_x(s).wait_recv()

            @pl.when(s >= 3)
            def reuse():
                send_z(s - 3).wait_send()

            for a in range(2):
                for b in range(2):
                    at = 2 * a + b
                    total = part[s % 3, at, xx].astype(F32) + x_in[s, at].astype(F32)
                    near[s % 3, a, b] = total.astype(BF)
            send_z(s).start()

        def turn_slot(s):
            loading(1, s).wait()
            loading(2, s).wait()
            send_g(s).wait_recv()

            @pl.when(s >= 3)
            def reuse():
                send_x(s - 3).wait_send()

            turned = dot_first(base[s], g[s, :, own]) + dot_first(other[s], g_in[s])
            for b in range(8):
                part[s % 3, b // 2, b % 2] = turned[b * rows : (b + 1) * rows].astype(BF)
            send_x(s).start()

        @pl.when(t == 2)
        def small_start():
            small_each(over_group, lambda copy: copy.start(), small_over)

        @pl.when(t == 8)
        def small_middle():
            small_each(over_group, lambda copy: copy.wait_recv(), small_from)
            total = group_small[0]
            for n in range(1, 4):
                total += group_small[n]
            blk_small[blk] = total
            small_each(over_blk, lambda copy: copy.start(), small_over)

        stage(7, finish)
        stage(6, update)
        stage(5, relay_x)
        stage(4, relay_z)
        stage(3, adam)
        stage(2, send_far)
        stage(1, send_near)
        stage(0, turn_slot)
        return carry

    lax.fori_loop(0, count + 7, tick, 0)
    small_each(over_blk, lambda copy: copy.wait_recv(), small_from)
    small = blk_small[0]
    for n in range(1, 8):
        small += blk_small[n]
    small_each(over_group, lambda copy: copy.wait_send(), small_over)
    small_each(over_blk, lambda copy: copy.wait_send(), small_over)
    small_out_ref[...] = small
    rows_finish()
    for s in range(count):
        send_g(s).wait_send()
        step_pair(s).wait_send()
        for a in range(2):
            step_z(s, a).wait_send()
        for a in range(4):
            step_x(s, a).wait_send()
        for i in range(3):
            storing(i, s).wait()
    for s in range(count - 3, count):
        send_x(s).wait_send()
        send_z(s).wait_send()
        send_p(s).wait_send()
        send_back(s).wait_send()


def rotate_slots(grads, base, early, other, first, second, master, tokens, small, scales):
    count, rows, width = grads.shape
    half = width // 2
    hbm = pl.BlockSpec(memory_space=pl.ANY)
    shape = jax.ShapeDtypeStruct(master.shape, F32)
    sems = lambda n: pltpu.SemaphoreType.DMA((2, n))
    return pl.pallas_call(
        rotate_kernel,
        in_specs=[hbm] * 8 + [pl.BlockSpec(memory_space=pltpu.VMEM), pl.BlockSpec(memory_space=pltpu.SMEM)],
        out_specs=[hbm] * 4 + [pl.BlockSpec(memory_space=pltpu.VMEM)],
        out_shape=[shape] * 3
        + [jax.ShapeDtypeStruct((2, 4 * tokens.shape[1], D), BF), jax.ShapeDtypeStruct(small.shape, F32)],
        scratch_shapes=[
            pltpu.VMEM((4,) + small.shape, F32),
            pltpu.VMEM((8,) + small.shape, F32),
            pltpu.VMEM((count, rows, width), BF),
            pltpu.VMEM((count, rows, D), BF),
            pltpu.VMEM((count, rows, D), BF),
            pltpu.VMEM((count, rows, width), F32),
            pltpu.VMEM((count, rows, width), F32),
            pltpu.VMEM((count, rows, width), F32),
            pltpu.VMEM((count, rows, half), BF),
            pltpu.VMEM((3, 4, 2, rows, half), BF),
            pltpu.VMEM((count, 4, rows, half), BF),
            pltpu.VMEM((3, 2, 2, rows, half), BF),
            pltpu.VMEM((count, 2, rows, half), BF),
            pltpu.VMEM((3, rows, half), BF),
            pltpu.VMEM((count, rows, half), BF),
            pltpu.VMEM((count, rows, width), BF),
            pltpu.VMEM((count, 8, rows, half), BF),
            pltpu.VMEM((3, rows, half), BF),
            pltpu.VMEM((count, rows, half), BF),
            pltpu.VMEM((2, rows, half), F32),
            pltpu.SemaphoreType.DMA((6, count)),
            pltpu.SemaphoreType.DMA((3, count)),
            sems(count),
            sems(count),
            sems(count),
            sems(count),
            sems(count),
            sems(count),
            sems(2 * count),
            sems(4 * count),
            sems(8),
            sems(4),
            sems(8),
        ],
        compiler_params=params(collective_id=2, has_side_effects=True),
        name="rotate_slots",
    )(grads, base, early, other, first, second, master, tokens, small, scales)


def row_groups(
    tokens,
    cotangent,
    lengths,
    unit_owner,
    step_count,
    master,
    first,
    second,
    bases,
    small,
    small_first,
    small_second,
):
    me, blk = lax.axis_index("batch"), lax.axis_index("blk")
    count = tokens.shape[1] * 8
    learn_rate = 2.0 / D**0.5
    slots = lambda array: jnp.transpose(array, (1, 0, 2))
    master_slots = slots(master)

    place = ((unit_owner // 9) ^ me) * 9 + unit_owner % 9
    master_low = master_slots.astype(BF)
    lengths_tile = jnp.pad(lengths, ((0, 8 - lengths.shape[0]), (0, 128 - NDOC)))
    pieces, x_own, dy_own, base, base_early, lens = begin(master_low, tokens, cotangent, slots(bases), lengths_tile)
    attn_shard, gate_up_shard, down_shard = pick_units(place, me, master_low, pieces)
    attn, down, x, other_out, cosine, sine, start = gather(attn_shard, down_shard, x_own, lens)
    low = start.reshape(-1, TILE)[:, 0] // TILE
    down = down.reshape(D, FQ)
    gate_up = lax.all_gather(after(gate_up_shard, attn), "blk", axis=0, tiled=True)
    attn, x = attn.reshape(D, 4 * QW), x.reshape(count, D)
    dy_near, dy_far = swap_core(after(dy_own, attn)), swap_y(after(dy_own, attn))

    gain_one = small[:D].reshape(1, D)
    gain_two = small[D : 2 * D].reshape(1, D)
    head_gain = small[2 * D : 2 * D + VD].reshape(VD, 1)
    mixer, mixer_back = jax.vjp(mix_value, small[2 * D + VD :].reshape(4, HD))
    lam = mixer.reshape(1)

    n1, q, k, v = project(x, attn, gain_one, cosine, sine)
    a_own, maps, log_mass = attend(low, lam, q, k, v, start, head_gain)
    dy = (dy_own, dy_near, dy_far, swap_core(after(dy_far, a_own)))
    n2, x1 = middle(a_own, x, attn, other_out.reshape(3, D, QW), gain_two)
    dup, out_part, dx1, dx1_low, da, gain_two_grad, gate_grad, down_grad, base_other = feed(
        n2, dy, gate_up, down, x1, dy_own, attn, gain_two, base
    )

    down_sums = lax.psum_scatter(down_grad, "blk", scatter_dimension=0, tiled=True)
    up_grad = dot_first(n2, dup).astype(BF)
    dx1_low = dx1_low.reshape(count, D)
    da = after(da, up_grad)
    dq, dk, dv, head_gain_sums, mixer_sums = attend_back(
        low, lam, q, k, v, start, head_gain, maps, log_mass, da, cosine, sine
    )
    dqkv = jnp.concatenate([dq, dk, dv], axis=1)
    dn1_part = dot_last(dqkv, attn[:, : 3 * QW]).astype(BF)
    groups = (8, 2, 2, count // 32, D)
    attn_pieces, gate_up_pieces, down_pieces, dx, block_out, gain_one_grad = collect(
        gate_grad, up_grad, n1, dqkv, dx1_low, a_own, down_sums, out_part.reshape(groups), dn1_part.reshape(groups),
        x1, dx1, x_own, gain_one,
    )

    (mixers_grad,) = mixer_back(jnp.sum(mixer_sums))
    small_local = jnp.concatenate(
        [gain_one_grad.reshape(D), gain_two_grad.reshape(D), jnp.sum(head_gain_sums, axis=(0, 2)), mixers_grad.reshape(-1)]
    )
    small_rows = jnp.pad(small_local, (0, 32 * 128 - small_local.shape[0])).reshape(32, 128)

    unit_of = inverse_order(unit_owner)
    units = lax.dynamic_slice_in_dim(unit_of, me * 9, 9)
    grads = place_units(units, me, attn_pieces, gate_up_pieces, down_pieces)

    steps_done = step_count[0].astype(F32)
    scales = jnp.stack([jnp.float32(learn_rate), 1.0 - beta_one**steps_done, 1.0 - beta_two**steps_done])
    new_first, new_second, new_master, input_grad, small_sums = rotate_slots(
        grads, base, base_early, base_other, slots(first), slots(second), master_slots, dx, small_rows, scales
    )
    small_grads = small_sums.reshape(-1)[: small_local.shape[0]]
    new_small_first = beta_one * small_first + (1.0 - beta_one) * small_grads
    new_small_second = beta_two * small_second + (1.0 - beta_two) * small_grads * small_grads
    new_small = small - small_rate * adam_step(new_small_first, new_small_second, steps_done)
    return (
        block_out,
        input_grad,
        slots(new_master),
        slots(new_first),
        slots(new_second),
        small_grads,
        new_small,
        new_small_first,
        new_small_second,
    )


def solution(mesh):
    in_specs = (
        P("batch", "blk", None),
        P("batch", "blk", None),
        P("batch", None),
        P(),
        P(),
        P("blk", "batch", None),
        P("blk", "batch", None),
        P("blk", "batch", None),
        P("blk", "batch", None),
        P(),
        P(),
        P(),
    )
    out_specs = (
        P("batch", "blk", None),
        P("batch", "blk", None),
        P("blk", "batch", None),
        P("blk", "batch", None),
        P("blk", "batch", None),
        P(),
        P(),
        P(),
        P(),
    )
    by_rows = mesh.shape["blk"] == 8 and mesh.shape["batch"] == 4
    body = row_groups if by_rows else any_mesh
    return jax.shard_map(body, mesh=mesh, in_specs=in_specs, out_specs=out_specs, check_vma=False)
```

```python
import functools

import jax
import jax.numpy as jnp
from jax import lax
from jax.experimental import pallas as pl
from jax.experimental.pallas import tpu as pltpu
from jax.sharding import PartitionSpec as P

D = 1536
H = 12
HD = 64
VD = 128
FF = 4096
UW = 512
NDOC = 6
UNITS = 36


norm_epsilon = 1e-05
lambda_start = 0.2
rope_base = 10000.0
masked_fill = -1000000000.0
beta_one = 0.9
beta_two = 0.95
adam_epsilon = 1e-08
weight_decay = 0.01
small_rate = 1.0


def from_behind(shard, axis, by):
    count = lax.axis_size(axis)
    return lax.ppermute(shard, axis, [(i, (i + by) % count) for i in range(count)])


def root_norm(values, gain):
    return (
        values * lax.rsqrt(jnp.mean(values * values, axis=-1, keepdims=True) + norm_epsilon) * gain
    )


def mix_value(mixers):
    return (
        jnp.exp(jnp.sum(mixers[0] * mixers[1]))
        - jnp.exp(jnp.sum(mixers[2] * mixers[3]))
        + lambda_start
    )


def head_mix(maps_out, head_gain, mixer):
    combined = maps_out[:, :, 0] - mixer * maps_out[:, :, 1]
    normed = (
        combined
        * lax.rsqrt(jnp.mean(combined * combined, axis=-1, keepdims=True) + norm_epsilon)
        * head_gain
        * (1.0 - lambda_start)
    )
    rows_count, heads, positions, width = normed.shape
    return jnp.transpose(normed, (0, 2, 1, 3)).reshape(rows_count, positions, heads * width)


def gated_unit(gate, up):
    return jax.nn.silu(gate) * up


def doc_ends(lengths):
    count = lengths.shape[1]
    ends = [lengths[:, 0]]
    for j in range(1, count):
        ends.append(ends[-1] + lengths[:, j])
    return jnp.stack(ends, axis=1)


def document_places(lengths, places):
    ends = doc_ends(lengths)
    starts = ends - lengths
    segment = jnp.sum((places[None, :, None] >= ends[:, None, :]).astype(jnp.int32), axis=2)
    chosen = segment[:, :, None] == jnp.arange(lengths.shape[1], dtype=jnp.int32)[None, None, :]
    offset = jnp.sum(jnp.where(chosen, starts[:, None, :], 0), axis=2)
    return (segment, places[None, :] - offset)


def allowed(seg_query, place_query, seg_key, place_key, last):
    same = seg_query[:, :, None] == seg_key[:, None, :]
    causal = place_key[None, None, :] <= place_query[None, :, None]
    itself = place_key[None, None, :] == place_query[None, :, None]
    return same & causal & ((seg_query[:, :, None] < last) | itself)


def turn_tables(position):
    rates = rope_base ** (-2.0 * jnp.arange(HD // 2, dtype=jnp.float32) / HD)
    angle = position.astype(jnp.float32)[..., None] * rates
    return (jnp.cos(angle), jnp.sin(angle))


def rotate(values, cosine, sine):
    half = values.shape[-1] // 2
    front = values[..., :half]
    back = values[..., half:]
    return jnp.concatenate([front * cosine - back * sine, back * cosine + front * sine], axis=-1)


def adam_step(first_new, second_new, steps_done):
    return (
        first_new
        / (1.0 - beta_one**steps_done)
        / (jnp.sqrt(second_new / (1.0 - beta_two**steps_done)) + adam_epsilon)
    )


def take_units(stacked, order):
    parts = [lax.dynamic_slice_in_dim(stacked, order[i], 1, axis=1) for i in range(UNITS)]
    return jnp.concatenate(parts, axis=1)


def inverse_order(owner):
    numbers = jnp.arange(UNITS, dtype=jnp.int32)
    return jnp.sum(jnp.where(owner[None, :] == numbers[:, None], numbers[None, :], 0), axis=1)


def contract_rows(left, right):
    return lax.dot_general(
        left, right, (((1,), (1,)), ((), ())), preferred_element_type=jnp.float32
    )


def any_mesh(
    tokens,
    cotangent,
    lengths,
    unit_owner,
    step_count,
    master,
    first,
    second,
    bases,
    small,
    small_first,
    small_second,
):
    rows_count, seq_part, width = tokens.shape
    token_count = rows_count * seq_part
    axis_count = lax.axis_size("blk")
    axis_place = lax.axis_index("blk")
    rows_part = master.shape[0]
    scale = HD ** (-0.5)
    highest = lax.Precision.HIGHEST
    learn_rate = 2.0 / D**0.5
    every_slot = lax.all_gather(master.astype(jnp.bfloat16), "batch", axis=1, tiled=True)
    by_unit = take_units(every_slot, unit_owner).reshape(rows_part, UNITS * UW)
    attention_whole = lax.all_gather(by_unit[:, : 4 * D], "blk", axis=0, tiled=True)
    gate_whole = lax.all_gather(by_unit[:, 4 * D : 4 * D + 2 * FF], "blk", axis=0, tiled=True)
    down_whole = lax.all_gather(by_unit[:, 4 * D + 2 * FF :], "blk", axis=0, tiled=True)
    places = axis_place * seq_part + jnp.arange(seq_part, dtype=jnp.int32)
    segment, position = document_places(lengths, places)
    cosine, sine = turn_tables(position)
    cosine = cosine[:, :, None, None, :]
    sine = sine[:, :, None, None, :]
    residual = tokens.astype(jnp.float32)
    gain_one = small[:D]
    gain_two = small[D : 2 * D]
    head_gain = small[2 * D : 2 * D + VD]
    mixer, mixer_back = jax.vjp(mix_value, small[2 * D + VD :].reshape(4, HD))
    normed_exact, norm_one_back = jax.vjp(root_norm, residual, gain_one)
    normed_one = normed_exact.astype(jnp.bfloat16).reshape(token_count, D)
    projected = jnp.dot(normed_one, attention_whole[:, : 3 * D], preferred_element_type=jnp.float32)
    query = rotate(projected[:, :D].reshape(rows_count, seq_part, H, 2, HD), cosine, sine).astype(
        jnp.bfloat16
    )
    key_own = (
        rotate(projected[:, D : 2 * D].reshape(rows_count, seq_part, H, 2, HD), cosine, sine)
        .astype(jnp.bfloat16)
        .reshape(rows_count, seq_part, D)
    )
    value_own = projected[:, 2 * D :].astype(jnp.bfloat16).reshape(rows_count, seq_part, D)
    best = jnp.full((rows_count, H, 2, seq_part), masked_fill, jnp.float32)
    key_piece = lax.all_gather(key_own, "blk", axis=1, tiled=True)
    value_piece = lax.all_gather(value_own, "blk", axis=1, tiled=True)
    count = key_piece.shape[1]
    key_places = jnp.arange(count, dtype=jnp.int32)
    key_segment, unused = document_places(lengths, key_places)
    mask = allowed(segment, places, key_segment, key_places, NDOC - 1)[:, None, None]
    keys = key_piece.reshape(rows_count, count, H, 2, HD)
    values = value_piece.reshape(rows_count, count, H, VD)
    scores = (
        jnp.einsum("rqhcd,rkhcd->rhcqk", query, keys, preferred_element_type=jnp.float32) * scale
    )
    scores = jnp.where(mask, scores, masked_fill)
    top = jnp.maximum(best, jnp.max(scores, axis=-1))
    shares = jnp.where(mask, jnp.exp(scores - top[..., None]), 0.0)
    mass = jnp.sum(shares, axis=-1)
    summed = jnp.einsum(
        "rhcqk,rkhe->rhcqe", shares.astype(jnp.bfloat16), values, preferred_element_type=jnp.float32
    )
    best, mass, summed = (top, mass, summed)
    maps_out = summed / mass[..., None]
    log_mass = best + jnp.log(mass)
    mixed_exact, mix_back = jax.vjp(head_mix, maps_out, head_gain, mixer)
    mixed = mixed_exact.astype(jnp.bfloat16).reshape(token_count, D)
    middle = residual.reshape(token_count, D) + contract_rows(mixed, attention_whole[:, 3 * D :])
    normed_two_exact, norm_two_back = jax.vjp(root_norm, middle, gain_two)
    normed_two = normed_two_exact.astype(jnp.bfloat16)
    gate_up = jnp.dot(normed_two, gate_whole, preferred_element_type=jnp.float32)
    hidden_exact, gated_back = jax.vjp(gated_unit, gate_up[:, :FF], gate_up[:, FF:])
    hidden = hidden_exact.astype(jnp.bfloat16)
    result = middle + contract_rows(hidden, down_whole)
    block_out = result.astype(jnp.bfloat16).reshape(rows_count, seq_part, D)
    output_grad = cotangent.reshape(token_count, D)
    hidden_grad = jnp.dot(output_grad, down_whole, preferred_element_type=jnp.float32)
    gate_grad, up_grad = gated_back(hidden_grad)
    gate_up_grad = jnp.concatenate([gate_grad, up_grad], axis=1).astype(jnp.bfloat16)
    normed_two_grad = contract_rows(gate_up_grad, gate_whole)
    middle_part, gain_two_grad = norm_two_back(normed_two_grad)
    middle_grad = output_grad.astype(jnp.float32) + middle_part
    middle_low = middle_grad.astype(jnp.bfloat16)
    mixed_grad = jnp.dot(
        middle_low, attention_whole[:, 3 * D :], preferred_element_type=jnp.float32
    )
    maps_grad, head_gain_grad, mixer_grad = mix_back(mixed_grad.reshape(rows_count, seq_part, D))
    maps_low = maps_grad.astype(jnp.bfloat16)
    offset_term = jnp.sum(maps_low.astype(jnp.float32) * maps_out, axis=-1)

    def circle(turn_index, carry):
        moving, moving_grad, query_grad = carry
        source = (axis_place - turn_index) % axis_count
        key_places = source * seq_part + jnp.arange(seq_part, dtype=jnp.int32)
        key_segment, unused = document_places(lengths, key_places)
        mask = allowed(segment, places, key_segment, key_places, NDOC - 1)[:, None, None]
        keys = moving[0].astype(jnp.bfloat16).reshape(rows_count, seq_part, H, 2, HD)
        values = moving[1].astype(jnp.bfloat16).reshape(rows_count, seq_part, H, VD)
        scores = (
            jnp.einsum("rqhcd,rkhcd->rhcqk", query, keys, preferred_element_type=jnp.float32)
            * scale
        )
        shares = jnp.where(mask, jnp.exp(scores - log_mass[..., None]), 0.0)
        value_term = jnp.einsum(
            "rhcqk,rhcqe->rkhe",
            shares.astype(jnp.bfloat16),
            maps_low,
            preferred_element_type=jnp.float32,
        )
        share_grad = jnp.einsum(
            "rhcqe,rkhe->rhcqk", maps_low, values, preferred_element_type=jnp.float32
        )
        score_low = (shares * (share_grad - offset_term[..., None])).astype(jnp.bfloat16)
        query_grad = query_grad + jnp.einsum(
            "rhcqk,rkhcd->rqhcd", score_low, keys, preferred_element_type=jnp.float32
        )
        key_term = jnp.einsum(
            "rhcqk,rqhcd->rkhcd", score_low, query, preferred_element_type=jnp.float32
        )
        update = jnp.stack(
            [key_term.reshape(rows_count, seq_part, D), value_term.reshape(rows_count, seq_part, D)]
        )
        moving_grad = moving_grad + update
        moving, moving_grad = (
            from_behind(moving.astype(jnp.bfloat16), "blk", 1).astype(moving.dtype),
            from_behind(moving_grad.astype(jnp.bfloat16), "blk", 1).astype(moving_grad.dtype),
        )
        return (moving, moving_grad, query_grad)

    circle_start = (
        jnp.stack([key_own, value_own]).astype(jnp.float32),
        jnp.zeros((2, rows_count, seq_part, D), jnp.float32),
        jnp.zeros((rows_count, seq_part, H, 2, HD), jnp.float32),
    )
    moving, moving_grad, query_grad = lax.fori_loop(0, axis_count, circle, circle_start)
    key_grad = moving_grad[0].reshape(rows_count, seq_part, H, 2, HD) * scale
    query_pre = rotate(query_grad * scale, cosine, -sine).reshape(token_count, D)
    key_pre = rotate(key_grad, cosine, -sine).reshape(token_count, D)
    projected_grad = jnp.concatenate(
        [query_pre, key_pre, moving_grad[1].reshape(token_count, D)], axis=1
    ).astype(jnp.bfloat16)
    normed_one_grad = contract_rows(projected_grad, attention_whole[:, : 3 * D])
    residual_part, gain_one_grad = norm_one_back(normed_one_grad.reshape(rows_count, seq_part, D))
    input_grad = (middle_grad.reshape(rows_count, seq_part, D) + residual_part).astype(jnp.bfloat16)
    (mixers_grad,) = mixer_back(mixer_grad)
    small_local = jnp.concatenate(
        [gain_one_grad, gain_two_grad, head_gain_grad, mixers_grad.reshape(-1)]
    )
    small_grads = lax.psum(small_local, ("batch", "blk"))
    right_side = jnp.concatenate([projected_grad, mixed, gate_up_grad, hidden], axis=1)
    left_sides = (normed_one, middle_low, normed_two, output_grad)
    bounds = (0, 3 * D, 4 * D, 4 * D + 2 * FF, 4 * D + 3 * FF)
    slot_order = inverse_order(unit_owner)
    parts = []
    for group in range(4):
        left_rows = left_sides[group]
        parts.append(
            lax.dot_general(
                left_rows,
                right_side[:, bounds[group] : bounds[group + 1]],
                (((0,), (0,)), ((), ())),
                preferred_element_type=jnp.float32,
            )
        )
    row_sums = lax.psum_scatter(
        jnp.concatenate(parts, axis=1).astype(jnp.bfloat16), "blk", scatter_dimension=0, tiled=True
    ).astype(jnp.float32)
    placed = take_units(row_sums.reshape(rows_part, UNITS, UW), slot_order)
    grad_slots = lax.psum_scatter(
        placed.astype(jnp.bfloat16), "batch", scatter_dimension=1, tiled=True
    ).astype(jnp.float32)
    columns = bases
    turned = lax.psum_scatter(
        jnp.einsum("ksa,ksn->asn", columns, grad_slots, precision=highest).astype(jnp.bfloat16),
        "blk",
        scatter_dimension=0,
        tiled=True,
    ).astype(jnp.float32)
    steps_done = step_count[0].astype(jnp.float32)
    new_first = beta_one * first + (1.0 - beta_one) * turned
    new_second = beta_two * second + (1.0 - beta_two) * turned * turned
    normalized = adam_step(new_first, new_second, steps_done)
    columns = bases
    update = jnp.zeros_like(master) + jnp.einsum(
        "ksa,asn->ksn",
        columns,
        lax.all_gather(normalized.astype(jnp.bfloat16), "blk", axis=0, tiled=True).astype(
            jnp.float32
        ),
        precision=highest,
    )
    new_master = master - learn_rate * (update + weight_decay * master)
    new_small_first = beta_one * small_first + (1.0 - beta_one) * small_grads
    new_small_second = beta_two * small_second + (1.0 - beta_two) * small_grads * small_grads
    new_small = small - small_rate * adam_step(new_small_first, new_small_second, steps_done)
    return (
        block_out,
        input_grad,
        new_master,
        new_first,
        new_second,
        small_grads,
        new_small,
        new_small_first,
        new_small_second,
    )


BF = jnp.bfloat16
F32 = jnp.float32
TILE = 256
HEADS = 3
QW = HEADS * VD
FQ = FF // 4
EARLY = 2
VMEM_LIMIT = 56 * 2**20


def params(limit=VMEM_LIMIT, **more):
    return pltpu.CompilerParams(vmem_limit_bytes=limit, **more)


def dot_last(left, right):
    return lax.dot_general(left, right, (((1,), (1,)), ((), ())), preferred_element_type=F32)


def dot_first(left, right):
    return lax.dot_general(left, right, (((0,), (0,)), ((), ())), preferred_element_type=F32)


def dot_plain(left, right):
    return jnp.dot(left, right, preferred_element_type=F32)


def swap_core(piece):
    return lax.ppermute(piece, "batch", [(i, i ^ 1) for i in range(4)])


def swap_y(piece):
    return lax.ppermute(piece, "batch", [(i, i ^ 2) for i in range(4)])


def after(values, earlier):
    return lax.optimization_barrier((values, earlier))[0]


def ring_place(blk):
    side = blk % 2
    return (1 - side) * (blk // 2) + side * (7 - blk // 2)


def ring_owner(place):
    place = (place + 16) % 8
    side = place // 4
    return 2 * ((1 - side) * place + side * (7 - place)) + side


MESH = pl.DeviceIdType.MESH


def greet(devices):
    barrier = pltpu.get_barrier_semaphore()
    for device in devices:
        pl.semaphore_signal(barrier, inc=1, device_id=device, device_id_type=MESH)
    pl.semaphore_wait(barrier, len(devices))


def greet_all():
    barrier = pltpu.get_barrier_semaphore()
    me, blk = lax.axis_index("batch"), lax.axis_index("blk")

    def signal(n, carry):
        at = (me * 8 + blk + n) % 32
        pl.semaphore_signal(barrier, inc=1, device_id=(at // 8, at % 8), device_id_type=MESH)
        return carry

    lax.fori_loop(1, 32, signal, 0)
    pl.semaphore_wait(barrier, 31)


def remote(source, target, sems, at, device):
    return pltpu.make_async_remote_copy(
        src_ref=source,
        dst_ref=target,
        send_sem=sems.at[0, at],
        recv_sem=sems.at[1, at],
        device_id=device,
        device_id_type=MESH,
    )


def to_group_copies(source, between, target, s_batch, s_blk, me, blk):
    size = target.shape[1]

    def over_group(n):
        other = (me + n) % 4
        return pltpu.make_async_remote_copy(
            src_ref=source.at[:, pl.ds(pl.multiple_of(other * size, size), size)],
            dst_ref=between.at[pl.ds(2 * me, 2)],
            send_sem=s_batch.at[0, n],
            recv_sem=s_batch.at[1, 4 - n],
            device_id={"batch": other},
            device_id_type=MESH,
        )

    def group_arrival(n):
        other = (me + n) % 4
        return pltpu.make_async_remote_copy(
            src_ref=source.at[:, pl.ds(0, size)],
            dst_ref=between.at[pl.ds(2 * other, 2)],
            send_sem=s_batch.at[0, n],
            recv_sem=s_batch.at[1, n],
            device_id={"batch": other},
            device_id_type=MESH,
        )

    def over_blk(n, i, local, remote_act):
        other = (me + n) % 4
        row = 2 * other + i
        if n == 0:
            piece = source.at[i, pl.ds(pl.multiple_of(me * size, size), size)]
        else:
            piece = between.at[row]

        @pl.when(row == blk)
        def stay():
            local(pltpu.make_async_copy(piece, target.at[blk], s_blk.at[0, 2 * n + i]))

        @pl.when(row != blk)
        def go():
            remote_act(
                pltpu.make_async_remote_copy(
                    src_ref=piece,
                    dst_ref=target.at[blk],
                    send_sem=s_blk.at[0, 2 * n + i],
                    recv_sem=s_blk.at[1, blk],
                    device_id={"blk": row},
                    device_id_type=MESH,
                )
            )

    def start_group():
        for n in (2, 3, 1):
            over_group(n).start()

    def start_blk(n):
        if n:
            group_arrival(n).wait_recv()
        for i in range(2):
            over_blk(n, i, lambda copy: copy.start(), lambda copy: copy.start())

    def finish():
        for n in (1, 2, 3):
            over_group(n).wait_send()
        for n in range(4):
            for i in range(2):
                over_blk(n, i, lambda copy: copy.wait(), lambda copy: copy.wait_send())
        for k in range(8):

            @pl.when(blk != k)
            def arrived():
                pltpu.make_async_remote_copy(
                    src_ref=between.at[0],
                    dst_ref=target.at[k],
                    send_sem=s_blk.at[0, 0],
                    recv_sem=s_blk.at[1, k],
                    device_id={"blk": k},
                    device_id_type=MESH,
                ).wait_recv()

    return start_group, start_blk, finish


def begin_kernel(
    master_ref, tokens_ref, grad_ref, bases_ref, lengths_ref, pieces_ref, x_ref, dy_ref, base_ref, other_ref, lens_ref, wide, narrow, x_between,
    dy_between, s_core, s_y, s_relay, s_x, s_x2, s_dy, s_dy2, s_load, s_store, s_len, s_other,
):
    me, blk = lax.axis_index("batch"), lax.axis_index("blk")
    y, core = me // 2, me % 2
    to_core = {"batch": y * 2 + 1 - core}
    to_y = {"batch": (1 - y) * 2 + core}
    x_group, x_blk, x_finish = to_group_copies(tokens_ref, x_between, x_ref, s_x, s_x2, me, blk)
    dy_group, dy_blk, dy_finish = to_group_copies(grad_ref, dy_between, dy_ref, s_dy, s_dy2, me, blk)
    slots = bases_ref.shape[0]

    def load(n):
        return pltpu.make_async_copy(bases_ref.at[n], wide.at[n % 2], s_load.at[n])

    def store(n):
        return pltpu.make_async_copy(narrow.at[n % 2], base_ref.at[n], s_store.at[n])

    def lengths_copy(n, at):
        return pltpu.make_async_remote_copy(
            src_ref=lengths_ref,
            dst_ref=lens_ref.at[at],
            send_sem=s_len.at[0, n],
            recv_sem=s_len.at[1, 4 - n if at is me else n],
            device_id={"batch": (me + n) % 4},
            device_id_type=MESH,
        )

    zl = (blk // 2) % 2

    def share(n):
        return remote(base_ref.at[n], other_ref.at[n], s_other, n, {"blk": blk + 2 - 4 * zl})

    def cast(n):
        load(n).wait()
        if n >= 2:
            store(n - 2).wait()
            if n - 2 < EARLY:
                share(n - 2).start()
        narrow[n % 2] = wide[n % 2].astype(BF)
        store(n).start()
        if n + 2 < slots:
            load(n + 2).start()

    def copies(c):
        at = pl.ds(3 * c, 3)
        return (
            lambda: remote(master_ref.at[at], pieces_ref.at[0, at], s_core, c, to_core),
            lambda: remote(master_ref.at[at], pieces_ref.at[1, at], s_y, c, to_y),
            lambda: remote(pieces_ref.at[1, at], pieces_ref.at[2, at], s_relay, c, to_core),
        )

    greet([{"batch": (me + n) % 4} for n in (1, 2, 3)] + [{"blk": (blk + n) % 8} for n in range(1, 8)])
    x_group()
    own_lengths = pltpu.make_async_copy(lengths_ref, lens_ref.at[me], s_len.at[0, 0])
    own_lengths.start()
    for n in (1, 2, 3):
        lengths_copy(n, me).start()
    load(0).start()
    load(1).start()
    x_blk(0)
    cast(0)
    cast(1)
    for c in range(3):
        copies(c)[1]().start()
    dy_group()
    for c in range(3):
        copies(c)[0]().start()
    for n in (1, 2, 3):
        x_blk(n)
    for n in range(2, slots):
        cast(n)
    store(slots - 2).wait()
    store(slots - 1).wait()
    for n in range(4):
        dy_blk(n)
    for c in range(3):
        copies(c)[1]().wait_recv()
        copies(c)[2]().start()
    for c in range(3):
        near, far, relay = copies(c)
        near().wait()
        far().wait_send()
        relay().wait()
    for n in range(EARLY):
        share(n).wait()
    own_lengths.wait()
    for n in (1, 2, 3):
        lengths_copy(n, me).wait_send()
        lengths_copy(n, (me + n) % 4).wait_recv()
    x_finish()
    dy_finish()


def begin(master, tokens, cotangent, bases, lengths):
    hbm = pl.BlockSpec(memory_space=pl.ANY)
    size = tokens.shape[1] // 4
    sems = lambda n: pltpu.SemaphoreType.DMA((2, n))
    return pl.pallas_call(
        begin_kernel,
        in_specs=[hbm] * 4 + [pl.BlockSpec(memory_space=pltpu.VMEM)],
        out_specs=[hbm] * 6,
        out_shape=[
            jax.ShapeDtypeStruct((3,) + master.shape, BF),
            jax.ShapeDtypeStruct((8, size, D), BF),
            jax.ShapeDtypeStruct((8, size, D), BF),
            jax.ShapeDtypeStruct(bases.shape, BF),
            jax.ShapeDtypeStruct((EARLY,) + bases.shape[1:], BF),
            jax.ShapeDtypeStruct((4,) + lengths.shape, jnp.int32),
        ],
        scratch_shapes=[
            pltpu.VMEM((2,) + bases.shape[1:], F32),
            pltpu.VMEM((2,) + bases.shape[1:], BF),
            pltpu.VMEM((8, size, D), BF),
            pltpu.VMEM((8, size, D), BF),
            sems(3),
            sems(3),
            sems(3),
            sems(4),
            sems(8),
            sems(4),
            sems(8),
            pltpu.SemaphoreType.DMA((bases.shape[0],)),
            pltpu.SemaphoreType.DMA((bases.shape[0],)),
            sems(4),
            sems(EARLY),
        ],
        compiler_params=params(collective_id=3, has_side_effects=True),
        name="begin",
    )(master, tokens, cotangent, bases, lengths)


def gather_kernel(
    shard_ref, down_ref, x_ref, rate_ref, lens_ref, attn_ref, downs_ref, xs_ref, outs_ref, cos_ref, sin_ref, start_ref,
    s_local, s_up, s_down, s_up2, s_down2, s_x, s_out,
):
    me, blk = lax.axis_index("batch"), lax.axis_index("blk")
    y, core = me // 2, me % 2
    to_core = {"batch": y * 2 + 1 - core}
    to_y = {"batch": (1 - y) * 2 + core}
    place = ring_place(blk)
    after_me, before_me = {"blk": ring_owner(place + 1)}, {"blk": ring_owner(place - 1)}
    half = shard_ref.shape[0] // 2
    sub = half // 2
    far_slab = (1 - y) * 2 + core

    def ring(t, up, part, second=False):
        owner = ring_owner(place - t) if up else ring_owner(place + t)
        at = pl.ds((0 if up else half) + part * sub, sub)
        target = (downs_ref if second else attn_ref).at[owner, at]
        source = (down_ref if second else shard_ref).at[at] if t == 0 else target
        sems = (s_up2 if up else s_down2) if second else (s_up if up else s_down)
        return remote(source, target, sems, 2 * t + part, after_me if up else before_me)

    def spread(source, whole, sems, c):
        at = pl.ds(4 * c, 4)
        return (
            lambda: remote(source.at[at], whole.at[at, me], sems, c, to_core),
            lambda: remote(source.at[at], whole.at[at, me], sems, 2 + c, to_y),
            lambda: remote(whole.at[at, far_slab], whole.at[at, far_slab], sems, 4 + c, to_core),
        )

    mine = attn_ref.at[:, :, pl.ds(3 * QW, QW)]
    out = (
        lambda: remote(mine, outs_ref.at[0], s_out, 0, to_core),
        lambda: remote(mine, outs_ref.at[1], s_out, 1, to_y),
        lambda: remote(outs_ref.at[1], outs_ref.at[2], s_out, 2, to_core),
    )
    locals_ = [
        pltpu.make_async_copy(shard_ref, attn_ref.at[blk], s_local.at[0]),
        pltpu.make_async_copy(x_ref, xs_ref.at[:, me], s_local.at[1]),
        pltpu.make_async_copy(down_ref, downs_ref.at[blk], s_local.at[2]),
    ]

    lens = [lens_ref[blk // 2, blk % 2, j] for j in range(NDOC)]
    ends = [lens[0]]
    for j in range(1, NDOC):
        ends.append(ends[-1] + lens[j])

    def first_of(places):
        first = jnp.zeros_like(places)
        for j in range(NDOC):
            first += jnp.where(places >= ends[j], lens[j], 0)
        return first

    def starts():
        places = lax.broadcasted_iota(jnp.int32, start_ref.shape, 1)
        start_ref[...] = jnp.where(places >= ends[NDOC - 2], places, first_of(places))

    def table(b):
        lane = lax.broadcasted_iota(jnp.int32, (TILE, VD), 1)
        places = b * TILE + lax.broadcasted_iota(jnp.int32, (TILE, VD), 0)
        angle = (places - first_of(places)).astype(F32) * rate_ref[...]
        sine = jnp.sin(angle)
        at = slice(b * TILE, (b + 1) * TILE)
        cos_ref[at, :] = jnp.cos(angle)
        sin_ref[at, :] = jnp.where(lane % HD < HD // 2, -sine, sine)

    greet((to_core, to_y, after_me, before_me))
    for part in range(2):
        ring(0, True, part).start()
        ring(0, False, part).start()
    for way in (1, 0):
        for c in range(2):
            spread(x_ref, xs_ref, s_x, c)[way]().start()
    for copy in locals_:
        copy.start()

    def relay(c):
        copies = spread(x_ref, xs_ref, s_x, c)
        copies[1]().wait_recv()
        copies[2]().start()

    starts()
    for t in range(1, 7):
        for part in range(2):
            for up in (True, False):
                ring(t - 1, up, part).wait_recv()
                ring(t, up, part).start()
        table(t - 1)
    for part in range(2):
        for up in (True, False):
            ring(0, up, part, True).start()
            ring(6, up, part).wait_recv()
    locals_[0].wait()
    out[1]().start()
    out[0]().start()
    for t in range(1, 7):
        for part in range(2):
            for up in (True, False):
                ring(t - 1, up, part, True).wait_recv()
                ring(t, up, part, True).start()
        if t in (3, 4):
            relay(t - 3)
        if t in (1, 2):
            table(t + 5)
    for part in range(2):
        for up in (True, False):
            ring(6, up, part, True).wait_recv()
    out[1]().wait_recv()
    out[2]().start()
    for t in range(7):
        for part in range(2):
            for up in (True, False):
                ring(t, up, part).wait_send()
                ring(t, up, part, True).wait_send()
    for c in range(2):
        near, far, again = spread(x_ref, xs_ref, s_x, c)
        near().wait()
        far().wait_send()
        again().wait()
    out[0]().wait()
    out[1]().wait_send()
    out[2]().wait()
    for copy in locals_[1:]:
        copy.wait()


def gather(shard, down, x, lens):
    hbm = pl.BlockSpec(memory_space=pl.ANY)
    size = x.shape[1]
    sems = lambda n: pltpu.SemaphoreType.DMA((2, n))
    count = 32 * size
    vmem = pl.BlockSpec(memory_space=pltpu.VMEM)
    rates = jnp.tile(rope_base ** (-2.0 * jnp.arange(HD // 2, dtype=F32) / HD), 4).reshape(1, VD)
    return pl.pallas_call(
        gather_kernel,
        in_specs=[vmem] * 4 + [pl.BlockSpec(memory_space=pltpu.SMEM)],
        out_specs=[hbm] * 4 + [vmem] * 3,
        out_shape=[
            jax.ShapeDtypeStruct((8,) + shard.shape, BF),
            jax.ShapeDtypeStruct((8,) + down.shape, BF),
            jax.ShapeDtypeStruct((8, 4, size, D), BF),
            jax.ShapeDtypeStruct((3, 8, shard.shape[0], QW), BF),
            jax.ShapeDtypeStruct((count, VD), F32),
            jax.ShapeDtypeStruct((count, VD), F32),
            jax.ShapeDtypeStruct((1, count), jnp.int32),
        ],
        scratch_shapes=[pltpu.SemaphoreType.DMA((3,))] + [sems(14)] * 4 + [sems(6), sems(3)],
        compiler_params=params(collective_id=4, has_side_effects=True),
        name="gather",
    )(shard, down, x, rates, lens)


def attention_pieces(me):
    pieces = []
    for matrix in range(4):
        for j in range(HEADS):
            block = HEADS * me + j
            pieces.append((3 * matrix + block // 4, block % 4, HEADS * matrix + j))
    return pieces


def pick_kernel(place_ref, me_ref, own, pieces, attn_ref, ffn_ref, down_ref, sems):
    me = me_ref[0]
    waits = []

    def begin(unit, source, target, sem):
        at = place_ref[unit]
        for other, ref in enumerate((own, pieces.at[0], pieces.at[1], pieces.at[2])):

            @pl.when(at // 9 == other)
            def start():
                pltpu.make_async_copy(source(ref.at[at % 9]), target, sem).start()

        waits.append(pltpu.make_async_copy(source(own.at[0]), target, sem))

    for i, (unit, block, packed) in enumerate(attention_pieces(me)):
        column = pl.multiple_of(block * 128, 128)
        begin(unit, lambda r, c=column: r.at[:, pl.ds(c, 128)], attn_ref.at[:, pl.ds(packed * 128, 128)], sems.at[i])
    for i in range(6):
        unit = 12 + 8 * (i // 2) + 2 * me + i % 2
        target = ffn_ref.at[:, pl.ds(i * UW, UW)] if i < 4 else down_ref.at[:, pl.ds((i - 4) * UW, UW)]
        begin(unit, lambda r: r, target, sems.at[12 + i])
    for wait in waits:
        wait.wait()


def pick_units(place, me, own, pieces):
    rows = own.shape[1]
    hbm = pl.BlockSpec(memory_space=pl.ANY)
    smem = pl.BlockSpec(memory_space=pltpu.SMEM)
    vmem = pl.BlockSpec(memory_space=pltpu.VMEM)
    return pl.pallas_call(
        pick_kernel,
        in_specs=[smem, smem, hbm, hbm],
        out_specs=[vmem, vmem, vmem],
        out_shape=[
            jax.ShapeDtypeStruct((rows, 4 * QW), BF),
            jax.ShapeDtypeStruct((rows, 4 * UW), BF),
            jax.ShapeDtypeStruct((rows, 2 * UW), BF),
        ],
        scratch_shapes=[pltpu.SemaphoreType.DMA((18,))],
        compiler_params=params(),
        name="pick_units",
    )(place, me.reshape(1), own, pieces)


def place_kernel(unit_ref, me_ref, attn, gate_up, down, out_ref, sems):
    me = me_ref[0]
    waits = []
    for i in range(9):
        unit = unit_ref[i]
        f = jnp.maximum(unit - 12, 0)
        for q in range(4):
            block = (unit % 3) * 4 + q
            low = f % 16
            choices = (
                (unit < 12, attn, block // HEADS, (unit // 3) * QW + (block % HEADS) * 128),
                ((unit >= 12) & (unit < 28), gate_up, (low % 8) // 2, (low // 8) * FQ + (low % 2) * UW + q * 128),
                (unit >= 28, down, (f % 8) // 2, (f % 2) * UW + q * 128),
            )
            target, sem = out_ref.at[i, :, pl.ds(q * 128, 128)], sems.at[i, q]
            for chosen, pieces, holder, column in choices:

                @pl.when(chosen)
                def start(pieces=pieces, holder=holder, column=column, target=target, sem=sem):
                    source = pieces.at[holder ^ me, :, pl.ds(pl.multiple_of(column, 128), 128)]
                    pltpu.make_async_copy(source, target, sem).start()

            waits.append(pltpu.make_async_copy(attn.at[0, :, pl.ds(0, 128)], target, sem))
    for wait in waits:
        wait.wait()


def place_units(units, me, attn_pieces, gate_up_pieces, down_pieces):
    rows = attn_pieces.shape[1]
    hbm = pl.BlockSpec(memory_space=pl.ANY)
    smem = pl.BlockSpec(memory_space=pltpu.SMEM)
    return pl.pallas_call(
        place_kernel,
        in_specs=[smem, smem] + [hbm] * 3,
        out_specs=pl.BlockSpec(memory_space=pltpu.VMEM),
        out_shape=jax.ShapeDtypeStruct((9, rows, UW), BF),
        scratch_shapes=[pltpu.SemaphoreType.DMA((9, 4))],
        compiler_params=params(),
        name="place_units",
    )(units, me.reshape(1), attn_pieces, gate_up_pieces, down_pieces)


def turn(values, cosine, sine, lane):
    partner = jnp.where(lane % HD < HD // 2, pltpu.roll(values, 96, 1), pltpu.roll(values, 32, 1))
    return values * cosine + partner * sine


def project_kernel(x_ref, w_ref, gain_ref, cos_ref, sin_ref, n_ref, q_ref, k_ref, v_ref):
    x = x_ref[...].astype(F32)
    r = lax.rsqrt(jnp.mean(x * x, axis=-1, keepdims=True) + norm_epsilon)
    n = (x * r * gain_ref[...]).astype(BF)
    n_ref[...] = n
    lane = lax.broadcasted_iota(jnp.int32, (x.shape[0], VD), 1)
    cosine, sine = cos_ref[...], sin_ref[...]
    out = dot_plain(n, w_ref[...])
    for h in range(HEADS):
        at = slice(h * VD, (h + 1) * VD)
        q = turn(out[:, h * VD : (h + 1) * VD], cosine, sine, lane)
        q_ref[:, at] = (q.astype(BF).astype(F32) * HD**-0.5).astype(BF)
        k = turn(out[:, QW + h * VD : QW + (h + 1) * VD], cosine, sine, lane)
        k_ref[:, at] = k.astype(BF)
    v_ref[...] = out[:, 2 * QW :].astype(BF)


def project(x, weights, gain, cosine, sine):
    count = x.shape[0]
    rows = lambda w: pl.BlockSpec((TILE, w), lambda i: (i, 0))
    fixed = lambda h, w: pl.BlockSpec((h, w), lambda i: (0, 0), pipeline_mode=pl.Buffered(1))
    narrow = jax.ShapeDtypeStruct((count, QW), BF)
    return pl.pallas_call(
        project_kernel,
        grid=(count // TILE,),
        in_specs=[rows(D), fixed(D, 3 * QW), fixed(1, D), rows(VD), rows(VD)],
        out_specs=[rows(D), rows(QW), rows(QW), rows(QW)],
        out_shape=[jax.ShapeDtypeStruct((count, D), BF), narrow, narrow, narrow],
        compiler_params=params(),
        cost_estimate=pl.CostEstimate(
            flops=2 * count * D * 3 * QW, bytes_accessed=count * D * 6 + 6 * D * QW, transcendentals=0
        ),
        name="project",
    )(x, weights, gain, cosine, sine)


def split_halves(q):
    lane = lax.broadcasted_iota(jnp.int32, q.shape, 1)
    zero = jnp.zeros_like(q)
    return jnp.concatenate([jnp.where(lane < HD, q, zero), jnp.where(lane >= HD, q, zero)], axis=0)


def block_mask(j, n, i, start):
    key = j * TILE + lax.broadcasted_iota(jnp.int32, (n * TILE, 2 * TILE), 0)
    query = i * TILE + lax.broadcasted_iota(jnp.int32, (n * TILE, TILE), 1)
    query = jnp.concatenate([query, query], axis=1)
    return (key >= start) & (key <= query)


def over_blocks(low, high, step, carry):
    odd = (high - low) % 2
    carry = lax.fori_loop(low, low + odd, lambda j, c: step(j, 1, c), carry)
    pairs = (high - low) // 2
    return lax.fori_loop(0, pairs, lambda p, c: step(low + odd + 2 * p, 2, c), carry)


def attend_kernel(low_ref, lam_ref, q_ref, k_ref, v_ref, start_ref, gain_ref, a_ref, maps_ref, log_ref, vt_ref):
    i = pl.program_id(1)

    @pl.when(i == 0)
    def turn_values():
        for j in range(vt_ref.shape[0]):
            vt_ref[j] = v_ref[j * TILE : (j + 1) * TILE, :].astype(F32).T.astype(BF)

    q = split_halves(q_ref[...])
    start = jnp.concatenate([start_ref[...], start_ref[...]], axis=1)

    def step(j, n, carry):
        top, mass, total = carry
        keys = k_ref[pl.ds(pl.multiple_of(j * TILE, TILE), n * TILE), :]
        scores = jnp.where(block_mask(j, n, i, start), dot_last(keys, q), masked_fill)
        new = jnp.maximum(top, jnp.max(scores, axis=0, keepdims=True))
        shares = jnp.exp(scores - new)
        keep = jnp.exp(top - new)
        mass = mass * keep + jnp.sum(shares, axis=0, keepdims=True)
        low_shares = shares.astype(BF)
        total = total * keep
        for b in range(n):
            total += dot_plain(vt_ref[j + b], low_shares[b * TILE : (b + 1) * TILE])
        return new, mass, total

    first = (
        jnp.full((1, 2 * TILE), masked_fill, F32),
        jnp.zeros((1, 2 * TILE), F32),
        jnp.zeros((VD, 2 * TILE), F32),
    )
    top, mass, total = over_blocks(low_ref[i], i + 1, step, first)
    maps = total / mass
    one, two = maps[:, :TILE], maps[:, TILE:]
    maps_ref[0, 0] = one
    maps_ref[0, 1] = two
    log_ref[0, 0] = top + jnp.log(mass)
    mixed = one - lam_ref[0] * two
    r = lax.rsqrt(jnp.mean(mixed * mixed, axis=0, keepdims=True) + norm_epsilon)
    a_ref[...] = (mixed * r * gain_ref[...] * (1.0 - lambda_start)).T.astype(BF)


def attend(low, lam, q, k, v, start, gain):
    count = q.shape[0]
    blocks = count // TILE
    smem = pl.BlockSpec(memory_space=pltpu.SMEM)
    return pl.pallas_call(
        attend_kernel,
        grid=(HEADS, blocks),
        in_specs=[
            smem,
            smem,
            pl.BlockSpec((TILE, VD), lambda h, i: (i, h)),
            pl.BlockSpec((count, VD), lambda h, i: (0, h)),
            pl.BlockSpec((count, VD), lambda h, i: (0, h)),
            pl.BlockSpec((1, TILE), lambda h, i: (0, i)),
            pl.BlockSpec((VD, 1), lambda h, i: (0, 0)),
        ],
        out_specs=[
            pl.BlockSpec((TILE, VD), lambda h, i: (i, h)),
            pl.BlockSpec((1, 2, VD, TILE), lambda h, i: (h, 0, 0, i)),
            pl.BlockSpec((1, 1, 1, 2 * TILE), lambda h, i: (h, i, 0, 0)),
        ],
        out_shape=[
            jax.ShapeDtypeStruct((count, QW), BF),
            jax.ShapeDtypeStruct((HEADS, 2, VD, count), F32),
            jax.ShapeDtypeStruct((HEADS, blocks, 1, 2 * TILE), F32),
        ],
        scratch_shapes=[pltpu.VMEM((blocks, VD, TILE), BF)],
        compiler_params=params(),
        cost_estimate=pl.CostEstimate(
            flops=8 * count * count * VD * HEADS, bytes_accessed=count * QW * 16, transcendentals=count * count * HEADS
        ),
        name="attend",
    )(low, lam, q, k, v, start, gain)


def attend_back_kernel(
    low_ref, lam_ref, q_ref, k_ref, v_ref, start_ref, gain_ref, maps_ref, log_ref, da_ref, cosq_ref, sinq_ref,
    cosk_ref, sink_ref, dq_ref, dk_ref, dv_ref, dgain_ref, dlam_ref, kt_ref, dk_sum, dv_sum, dq_sum,
):
    i = pl.program_id(1)
    blocks = kt_ref.shape[0]

    @pl.when(i == 0)
    def begin():
        for j in range(blocks):
            kt_ref[j] = k_ref[j * TILE : (j + 1) * TILE, :].astype(F32).T.astype(BF)
        dk_sum[...] = jnp.zeros_like(dk_sum)
        dv_sum[...] = jnp.zeros_like(dv_sum)
        dgain_ref[...] = jnp.zeros_like(dgain_ref)
        dlam_ref[...] = jnp.zeros_like(dlam_ref)

    lam = lam_ref[0]
    q = split_halves(q_ref[...])
    start = jnp.concatenate([start_ref[...], start_ref[...]], axis=1)
    log_mass = log_ref[0, 0]
    one, two = maps_ref[0, 0], maps_ref[0, 1]
    mixed = one - lam * two
    r = lax.rsqrt(jnp.mean(mixed * mixed, axis=0, keepdims=True) + norm_epsilon)
    t = mixed * r
    da = da_ref[...].T * (1.0 - lambda_start)
    dgain_ref[0] += da * t
    e = da * gain_ref[...]
    dmixed = r * (e - t * jnp.mean(e * t, axis=0, keepdims=True))
    dlam_ref[0] -= jnp.sum(dmixed * two, axis=0, keepdims=True)
    dmaps = jnp.concatenate([dmixed, -lam * dmixed], axis=1).astype(BF)
    maps = jnp.concatenate([one, two], axis=1)
    offset = jnp.sum(dmaps.astype(F32) * maps, axis=0, keepdims=True)
    dq_sum[...] = jnp.zeros_like(dq_sum)

    def step(j, n, carry):
        at = pl.ds(pl.multiple_of(j * TILE, TILE), n * TILE)
        keys, values = k_ref[at, :], v_ref[at, :]
        scores = dot_last(keys, q)
        shares = jnp.where(block_mask(j, n, i, start), jnp.exp(scores - log_mass), 0.0)
        dshares = dot_plain(values, dmaps)
        dscores = (shares * (dshares - offset)).astype(BF)
        dv_sum[at, :] += dot_last(shares.astype(BF), dmaps)
        dk_sum[at, :] += dot_plain(dscores, q)
        dq = dot_plain(kt_ref[j], dscores[:TILE])
        for b in range(1, n):
            dq += dot_plain(kt_ref[j + b], dscores[b * TILE : (b + 1) * TILE])
        dq_sum[...] += dq
        return carry

    over_blocks(low_ref[i], i + 1, step, 0)
    lane = lax.broadcasted_iota(jnp.int32, (TILE, VD), 1)
    dq = jnp.concatenate([dq_sum[:HD, :TILE], dq_sum[HD:, TILE:]], axis=0).T * HD**-0.5
    dq_ref[...] = turn(dq, cosq_ref[...], -sinq_ref[...], lane).astype(BF)

    @pl.when(i == blocks - 1)
    def finish():
        for j in range(blocks):
            at = slice(j * TILE, (j + 1) * TILE)
            dk_ref[at, :] = turn(dk_sum[at, :], cosk_ref[at, :], -sink_ref[at, :], lane).astype(BF)
        dv_ref[...] = dv_sum[...].astype(BF)


def attend_back(low, lam, q, k, v, start, gain, maps, log_mass, da, cosine, sine):
    count = q.shape[0]
    blocks = count // TILE
    smem = pl.BlockSpec(memory_space=pltpu.SMEM)
    tile = pl.BlockSpec((TILE, VD), lambda h, i: (i, h))
    whole = pl.BlockSpec((count, VD), lambda h, i: (0, h))
    table = pl.BlockSpec((TILE, VD), lambda h, i: (i, 0))
    full_table = pl.BlockSpec((count, VD), lambda h, i: (0, 0), pipeline_mode=pl.Buffered(1))
    narrow = jax.ShapeDtypeStruct((count, QW), BF)
    return pl.pallas_call(
        attend_back_kernel,
        grid=(HEADS, blocks),
        in_specs=[
            smem,
            smem,
            tile,
            whole,
            whole,
            pl.BlockSpec((1, TILE), lambda h, i: (0, i)),
            pl.BlockSpec((VD, 1), lambda h, i: (0, 0)),
            pl.BlockSpec((1, 2, VD, TILE), lambda h, i: (h, 0, 0, i)),
            pl.BlockSpec((1, 1, 1, 2 * TILE), lambda h, i: (h, i, 0, 0)),
            tile,
            table,
            table,
            full_table,
            full_table,
        ],
        out_specs=[
            tile,
            whole,
            whole,
            pl.BlockSpec((1, VD, TILE), lambda h, i: (h, 0, 0)),
            pl.BlockSpec((1, 1, TILE), lambda h, i: (h, 0, 0)),
        ],
        out_shape=[
            narrow,
            narrow,
            narrow,
            jax.ShapeDtypeStruct((HEADS, VD, TILE), F32),
            jax.ShapeDtypeStruct((HEADS, 1, TILE), F32),
        ],
        scratch_shapes=[
            pltpu.VMEM((blocks, VD, TILE), BF),
            pltpu.VMEM((count, VD), F32),
            pltpu.VMEM((count, VD), F32),
            pltpu.VMEM((VD, 2 * TILE), F32),
        ],
        compiler_params=params(),
        cost_estimate=pl.CostEstimate(
            flops=20 * count * count * VD * HEADS, bytes_accessed=count * QW * 24, transcendentals=count * count * HEADS
        ),
        name="attend_back",
    )(low, lam, q, k, v, start, gain, maps, log_mass, da, cosine, sine, cosine, sine)


def middle_kernel(
    x_ref, gain_ref, a_ref, w_ref, w_in, a_hbm, n_ref, own_ref, a_in, total, s_a, s_ay, s_ar
):
    i = pl.program_id(0)
    me = lax.axis_index("batch")
    y, core = me // 2, me % 2
    to_core = {"batch": y * 2 + 1 - core}
    to_y = {"batch": (1 - y) * 2 + core}
    blocks = a_in.shape[1]

    def a_copies(b):
        source = a_hbm.at[pl.ds(b * TILE, TILE)]
        return (
            lambda: remote(source, a_in.at[0, b], s_a, b, to_core),
            lambda: remote(source, a_in.at[1, b], s_ay, b, to_y),
            lambda: remote(a_in.at[1, b], a_in.at[2, b], s_ar, b, to_core),
        )

    @pl.when(i == 0)
    def begin():
        greet((to_core, to_y))
        for b in range(blocks):
            a_copies(b)[1]().start()
        for b in range(blocks):
            a_copies(b)[0]().start()

    @pl.when(i < blocks)
    def relay():
        a_copies(i)[1]().wait_recv()
        a_copies(i)[2]().start()

    @pl.when(i >= 1)
    def compute():
        b = i - 1
        a_copies(b)[0]().wait_recv()
        a_copies(b)[2]().wait_recv()
        x1 = x_ref[...].astype(F32) + dot_last(a_ref[...], w_ref[...])
        for other in range(3):
            x1 += dot_last(a_in[other, b], w_in[other])
        total[...] = x1
        r = lax.rsqrt(jnp.mean(x1 * x1, axis=-1, keepdims=True) + norm_epsilon)
        n_ref[...] = (x1 * r * gain_ref[...]).astype(BF)
        part = TILE // 4
        own_ref[0] = total[pl.ds(pl.multiple_of(me * part, part), part), :]

    @pl.when(i == blocks)
    def finish():
        for b in range(blocks):
            for copy in a_copies(b):
                copy().wait_send()


def middle(a, x, attn, others, gain):
    count = x.shape[0]
    blocks = count // TILE
    late = lambda i: (jnp.maximum(i - 1, 0), 0)
    hbm = pl.BlockSpec(memory_space=pl.ANY)
    sems = lambda n: pltpu.SemaphoreType.DMA((2, n))
    return pl.pallas_call(
        middle_kernel,
        grid=(blocks + 1,),
        in_specs=[
            pl.BlockSpec((TILE, D), late),
            pl.BlockSpec((1, D), lambda i: (0, 0)),
            pl.BlockSpec((TILE, QW), late),
            pl.BlockSpec((D, QW), lambda i: (0, 3), pipeline_mode=pl.Buffered(1)),
            pl.BlockSpec((3, D, QW), lambda i: (0, 0, 0), pipeline_mode=pl.Buffered(1)),
            hbm,
        ],
        out_specs=[
            pl.BlockSpec((TILE, D), late),
            pl.BlockSpec((1, TILE // 4, D), lambda i: (jnp.maximum(i - 1, 0), 0, 0)),
        ],
        out_shape=[
            jax.ShapeDtypeStruct((count, D), BF),
            jax.ShapeDtypeStruct((blocks, TILE // 4, D), F32),
        ],
        scratch_shapes=[
            pltpu.VMEM((3, blocks, TILE, QW), BF),
            pltpu.VMEM((TILE, D), F32),
            sems(blocks),
            sems(blocks),
            sems(blocks),
        ],
        compiler_params=params(collective_id=5, has_side_effects=True),
        cost_estimate=pl.CostEstimate(
            flops=2 * count * D * D, bytes_accessed=count * D * 7 + 2 * D * D, transcendentals=0
        ),
        name="middle",
    )(x, gain, a, attn, others, a)


def feed_kernel(
    n_ref, dy0_ref, dy1_ref, dy2_ref, dy3_ref, w_ref, wd_ref, x1_ref, dyo_ref, wo_ref, gain_ref, base_ref, dup_ref, out_ref, dx_ref, low_ref, da_ref, dgain_ref,
    gate_grad_ref, down_grad_ref, other_ref, dy_ref, part, near_in, near, far_in, gathered, gate_sum, down_sum, staged, s_near, s_far, s_y,
    s_core, s_relay, s_grad, s_low, s_other,
):
    i = pl.program_id(0)
    me = lax.axis_index("batch")
    y, core = me // 2, me % 2
    to_core = {"batch": y * 2 + 1 - core}
    to_y = {"batch": (1 - y) * 2 + core}
    blocks = near_in.shape[0]

    def near_copy(b):
        return remote(part.at[b % 3, :, 1 - core], near_in.at[b], s_near, b, to_core)

    blk = lax.axis_index("blk")
    to_pair = {"blk": blk + 2 - 4 * ((blk // 2) % 2)}

    def share(n):
        return remote(base_ref.at[EARLY + n], other_ref.at[n], s_other, n, to_pair)

    def low_copy(b):
        return pltpu.make_async_copy(gathered.at[b], low_ref.at[b], s_low.at[b])

    grads = ((gate_sum, gate_grad_ref), (down_sum, down_grad_ref))
    strip = gate_sum.shape[0] // 4

    def grad_copy(n, which):
        at = pl.ds(pl.multiple_of(n * strip, strip), strip)
        return pltpu.make_async_copy(staged.at[which], grads[which][1].at[at], s_grad.at[which, n])

    def far_copy(b):
        return remote(near.at[b], far_in.at[b], s_far, b, to_y)

    def own_copy(b, sems, device):
        return remote(gathered.at[b, me], gathered.at[b, me], sems, b, device)

    def relay_copy(b):
        slab = (1 - y) * 2 + core
        return remote(gathered.at[b, slab], gathered.at[b, slab], s_relay, b, to_core)

    @pl.when(i == 0)
    def begin():
        greet((to_core, to_y, to_pair))
        for n in range(other_ref.shape[0]):
            share(n).start()
        dgain_ref[...] = jnp.zeros_like(dgain_ref)
        gate_sum[...] = jnp.zeros_like(gate_sum)
        down_sum[...] = jnp.zeros_like(down_sum)

    @pl.when((i >= 1) & (i < blocks + 1))
    def send_far():
        b = i - 1
        near_copy(b).wait_recv()
        both = part[b % 3, 1 - y, core].astype(F32) + near_in[b, 1 - y].astype(F32)
        near[b] = both.astype(BF)
        far_copy(b).start()

    @pl.when((i >= 2) & (i < blocks + 2))
    def send_own():
        b = i - 2
        far_copy(b).wait_recv()
        dn = part[b % 3, y, core].astype(F32) + near_in[b, y].astype(F32) + far_in[b].astype(F32)
        x1 = x1_ref[0]
        r = lax.rsqrt(jnp.mean(x1 * x1, axis=-1, keepdims=True) + norm_epsilon)
        t = x1 * r
        e = dn * gain_ref[...]
        dx = dyo_ref[0].astype(F32) + r * (e - t * jnp.mean(e * t, axis=-1, keepdims=True))
        dgain_ref[...] += jnp.sum(dn * t, axis=0, keepdims=True)
        dx_ref[0] = dx
        gathered[b, me] = dx.astype(BF)
        own_copy(b, s_y, to_y).start()
        own_copy(b, s_core, to_core).start()

    @pl.when((i >= 3) & (i < blocks + 3))
    def send_relay():
        b = i - 3
        own_copy(b, s_y, to_y).wait_recv()
        relay_copy(b).start()

    @pl.when(i >= 4)
    def use():
        b = i - 4
        own_copy(b, s_core, to_core).wait_recv()
        relay_copy(b).wait_recv()
        whole = jnp.concatenate([gathered[b, other] for other in range(4)], axis=0)
        low_copy(b).start()
        da_ref[...] = dot_plain(whole, wo_ref[...])

    @pl.when(i < blocks)
    def compute():
        size = dy0_ref.shape[1]
        slabs = (me, 2 * y + 1 - core, 2 * (1 - y) + core, 2 * (1 - y) + 1 - core)
        for slab, piece in zip(slabs, (dy0_ref, dy1_ref, dy2_ref, dy3_ref)):
            dy_ref[pl.ds(pl.multiple_of(slab * size, size), size), :] = piece[0]
        n, dy = n_ref[...], dy_ref[...]
        wg, wu, wd = w_ref[:, :FQ], w_ref[:, FQ:], wd_ref[...]
        gate = dot_plain(n, wg)
        up = dot_plain(n, wu)
        dhidden = dot_plain(dy, wd)
        share = 1.0 / (1.0 + jnp.exp(-gate))
        silu = gate * share
        hidden = (silu * up).astype(BF)
        dup = (dhidden * silu).astype(BF)
        dgate = (dhidden * up * (share * (1.0 + gate * (1.0 - share)))).astype(BF)
        dup_ref[...] = dup
        dn = (dot_last(dgate, wg) + dot_last(dup, wu)).astype(BF)

        @pl.when(i >= 3)
        def reuse():
            near_copy(i - 3).wait_send()

        for other in range(4):
            part[i % 3, other // 2, other % 2] = dn[other * size : (other + 1) * size]
        near_copy(i).start()
        out_ref[...] = dot_last(hidden, wd).astype(BF)
        for c in range(0, n.shape[1], TILE):
            gate_sum[c : c + TILE, :] += dot_first(n[:, c : c + TILE], dgate)
            down_sum[c : c + TILE, :] += dot_first(dy[:, c : c + TILE], hidden)

    @pl.when(i >= blocks)
    def keep():
        n = i - blocks
        for which in range(2):

            @pl.when(n >= 1)
            def reuse(which=which):
                grad_copy(n - 1, which).wait()

            at = pl.ds(pl.multiple_of(n * strip, strip), strip)
            staged[which] = grads[which][0][at, :].astype(BF)
            grad_copy(n, which).start()

    @pl.when(i == blocks + 3)
    def finish():
        for which in range(2):
            grad_copy(3, which).wait()
        for b in range(blocks - 3, blocks):
            near_copy(b).wait_send()
        for b in range(blocks):
            far_copy(b).wait_send()
            own_copy(b, s_y, to_y).wait_send()
            own_copy(b, s_core, to_core).wait_send()
            relay_copy(b).wait_send()
            low_copy(b).wait()
        for n in range(other_ref.shape[0]):
            share(n).wait()


def feed(n, dy, weights, down, x1, dy_own, attn, gain, base):
    count = n.shape[0]
    blocks = count // TILE
    size = TILE // 4
    late = lambda lag: lambda i: (jnp.clip(i - lag, 0, blocks - 1), 0)
    late3 = lambda lag: lambda i: (jnp.clip(i - lag, 0, blocks - 1), 0, 0)
    rows = lambda w, lag: pl.BlockSpec((TILE, w), late(lag))
    own = pl.BlockSpec((1, size, D), late3(2))
    shape = lambda w, kind=BF: jax.ShapeDtypeStruct((count, w), kind)
    sems = pltpu.SemaphoreType.DMA((2, blocks))
    return pl.pallas_call(
        feed_kernel,
        grid=(blocks + 4,),
        in_specs=[
            rows(D, 0),
            pl.BlockSpec((1, size, D), late3(0)),
            pl.BlockSpec((1, size, D), late3(0)),
            pl.BlockSpec((1, size, D), late3(0)),
            pl.BlockSpec((1, size, D), late3(0)),
            pl.BlockSpec((D, 2 * FQ), lambda i: (0, 0), pipeline_mode=pl.Buffered(1)),
            pl.BlockSpec((D, FQ), lambda i: (0, 0), pipeline_mode=pl.Buffered(1)),
            own,
            own,
            pl.BlockSpec((D, QW), lambda i: (0, 3), pipeline_mode=pl.Buffered(1)),
            pl.BlockSpec((1, D), lambda i: (0, 0)),
            pl.BlockSpec(memory_space=pl.ANY),
        ],
        out_specs=[
            rows(FQ, 0),
            rows(D, 0),
            own,
            pl.BlockSpec(memory_space=pl.ANY),
            rows(QW, 4),
            pl.BlockSpec((1, D), lambda i: (0, 0)),
            pl.BlockSpec(memory_space=pl.ANY),
            pl.BlockSpec(memory_space=pl.ANY),
            pl.BlockSpec(memory_space=pl.ANY),
        ],
        out_shape=[
            shape(FQ),
            shape(D),
            jax.ShapeDtypeStruct((blocks, size, D), F32),
            jax.ShapeDtypeStruct((blocks, 4, size, D), BF),
            shape(QW, F32),
            jax.ShapeDtypeStruct((1, D), F32),
            jax.ShapeDtypeStruct((D, FQ), BF),
            jax.ShapeDtypeStruct((D, FQ), BF),
            jax.ShapeDtypeStruct((base.shape[0] - EARLY,) + base.shape[1:], BF),
        ],
        scratch_shapes=[
            pltpu.VMEM((TILE, D), BF),
            pltpu.VMEM((3, 2, 2, size, D), BF),
            pltpu.VMEM((blocks, 2, size, D), BF),
            pltpu.VMEM((blocks, size, D), BF),
            pltpu.VMEM((blocks, size, D), BF),
            pltpu.VMEM((blocks, 4, size, D), BF),
            pltpu.VMEM((D, FQ), F32),
            pltpu.VMEM((D, FQ), F32),
            pltpu.VMEM((2, D // 4, FQ), BF),
            sems,
            sems,
            sems,
            sems,
            sems,
            pltpu.SemaphoreType.DMA((2, 4)),
            pltpu.SemaphoreType.DMA((blocks,)),
            pltpu.SemaphoreType.DMA((2, base.shape[0] - EARLY)),
        ],
        compiler_params=params(63 * 2**20, collective_id=1, has_side_effects=True),
        cost_estimate=pl.CostEstimate(
            flops=12 * count * D * FQ, bytes_accessed=count * (8 * D + 6 * FQ) + 6 * D * FQ, transcendentals=count * FQ
        ),
        name="feed",
    )(n, *dy, weights, down, x1, dy_own, attn, gain, base)


def return_rows_copies(source, target, sems, me, blk):
    size = source.shape[1]

    def copies(act_local, act_remote):
        for k in range(8):
            here = (me == blk // 2) & (blk == k)
            piece = target.at[blk % 2, pl.ds(pl.multiple_of(me * size, size), size)]

            @pl.when(here)
            def stay():
                act_local(pltpu.make_async_copy(source.at[k], piece, sems.at[0, k]))

            @pl.when(jnp.logical_not(here))
            def go():
                act_remote(
                    pltpu.make_async_remote_copy(
                        src_ref=source.at[k],
                        dst_ref=piece,
                        send_sem=sems.at[0, k],
                        recv_sem=sems.at[1, (blk % 2) * 4 + me],
                        device_id=(blk // 2, k),
                        device_id_type=MESH,
                    )
                )

    def start():
        copies(lambda copy: copy.start(), lambda copy: copy.start())

    def finish():
        copies(lambda copy: copy.wait(), lambda copy: copy.wait_send())
        for i in range(2):
            for other in range(4):

                @pl.when((me != other) | (blk != 2 * me + i))
                def arrived():
                    pltpu.make_async_remote_copy(
                        src_ref=source.at[0],
                        dst_ref=target.at[i, pl.ds(other * size, size)],
                        send_sem=sems.at[0, 0],
                        recv_sem=sems.at[1, 4 * i + other],
                        device_id=(me, blk),
                        device_id_type=MESH,
                    ).wait_recv()

    return start, finish


def collect_kernel(
    gate, up, dqkv, a_own, n1_ref, low_ref, down_ref, out_part_ref, dn1_part_ref, x1_ref, dx1_ref, x_ref, gain_ref, attn_ref, gate_up_ref,
    downs_ref, dx_ref, back_ref, dgain_ref, qkv, out, strips, first_in, second_in, first_sum, second_sum, own, near_in, near, far_in,
    out_rows, s_up, s_down, s_up2, s_down2, s_near, s_own, s_far, s_pieces, s_local, s_back,
    s_strip,
):
    me, blk = lax.axis_index("batch"), lax.axis_index("blk")
    y, core = me // 2, me % 2
    to_core = {"batch": y * 2 + 1 - core}
    to_y = {"batch": (1 - y) * 2 + core}
    place = ring_place(blk)
    after_me, before_me = {"blk": ring_owner(place + 1)}, {"blk": ring_owner(place - 1)}
    part = first_sum.shape[0]
    half = part // 2
    blocks = dx1_ref.shape[0]

    wide = QW + 256
    plans = (
        ((gate, 0, FQ, 0), (up, 0, FQ, FQ)),
        ((qkv, 0, wide, 0), (qkv, wide, 3 * QW - wide, wide), (out, 0, QW, 3 * QW)),
    )
    buffers, totals = (first_in, second_in), (first_sum, second_sum)
    ring_sems = ((s_up, s_down), (s_up2, s_down2))

    def mine(r, t, up_way, p):
        grad, column, width, _ = plans[r][p]
        owner = ring_owner(place - 1 - t) if up_way else ring_owner(place + 1 + t)
        begin = pl.multiple_of(owner * part + (0 if up_way else half), half)
        return grad.at[pl.ds(begin, half), pl.ds(column, width)]

    def landing(r, t, up_way, p):
        _, _, width, to = plans[r][p]
        return buffers[r].at[0 if up_way else 1, t, :, pl.ds(to, width)]

    def ring(r, t, up_way, p):
        source = mine(r, 0, up_way, p) if t == 0 else landing(r, t - 1, up_way, p)
        sems = ring_sems[r][0 if up_way else 1]
        at = len(plans[r]) * t + p
        return remote(source, landing(r, t, up_way, p), sems, at, after_me if up_way else before_me)

    def ring_start(r):
        for p in range(len(plans[r])):
            ring(r, 0, True, p).start()
            ring(r, 0, False, p).start()

    def ring_step(r, t, p):
        _, _, width, to = plans[r][p]
        for up_way in (True, False):
            ring(r, t - 1, up_way, p).wait_recv()
            here = landing(r, t - 1, up_way, p)
            value = (here[...].astype(F32) + mine(r, t, up_way, p)[...].astype(F32)).astype(BF)
            if t < 7:
                here[...] = value
                ring(r, t, up_way, p).start()
            else:
                totals[r][0 if up_way else half : half if up_way else part, to : to + width] = value

    def exchange(source, target, n):
        return (
            lambda: remote(source, target.at[1], s_pieces, 3 * n, to_core),
            lambda: remote(source, target.at[2], s_pieces, 3 * n + 1, to_y),
            lambda: remote(target.at[2], target.at[3], s_pieces, 3 * n + 2, to_core),
            lambda: pltpu.make_async_copy(source, target.at[0], s_local.at[n]),
        )

    exchanges = [exchange(down_ref, downs_ref, 0), exchange(first_sum, gate_up_ref, 1)]
    for p, (_, _, width, to) in enumerate(plans[1]):
        at = pl.ds(to, width)
        exchanges.append(exchange(second_sum.at[:, at], attn_ref.at[:, :, at], 2 + p))

    strip = strips.shape[2]
    count = D // strip
    lefts, rights, results = (n1_ref, low_ref), (dqkv, a_own), (qkv, out)

    def strip_copy(n):
        source = lefts[n // count].at[:, pl.ds((n % count) * strip, strip)]
        return pltpu.make_async_copy(source, strips.at[n % 2], s_strip.at[n])

    def strip_product(n):
        strip_copy(n).wait()
        at = pl.ds((n % count) * strip, strip)
        results[n // count][at, :] = dot_first(strips[n % 2], rights[n // count][...]).astype(BF)
        if n + 2 < 2 * count:
            strip_copy(n + 2).start()

    def spread(n):
        for way in (1, 0, 3):
            exchanges[n][way]().start()

    def relay(n):
        exchanges[n][1]().wait_recv()
        exchanges[n][2]().start()

    parts = (out_part_ref, dn1_part_ref)

    def near_copy(j):
        return remote(parts[j // blocks].at[j % blocks, :, 1 - core], near_in.at[j], s_near, j, to_core)

    def own_copy(j):
        return pltpu.make_async_copy(parts[j // blocks].at[j % blocks, :, core], own.at[j], s_own.at[j])

    def far_copy(j):
        return remote(near.at[j], far_in.at[j], s_far, j, to_y)

    def near_step(j):
        near_copy(j).wait_recv()
        own_copy(j).wait()
        near[j] = (own[j, 1 - y].astype(F32) + near_in[j, 1 - y].astype(F32)).astype(BF)
        far_copy(j).start()

    def far_step(j):
        far_copy(j).wait_recv()
        total = own[j, y].astype(F32) + near_in[j, y].astype(F32) + far_in[j].astype(F32)
        b = j % blocks
        if j < blocks:
            out_rows[b] = (x1_ref[b] + total).astype(BF)
            return
        x = x_ref[b].astype(F32)
        r = lax.rsqrt(jnp.mean(x * x, axis=-1, keepdims=True) + norm_epsilon)
        t = x * r
        e = total * gain_ref[...]
        dx = dx1_ref[b] + r * (e - t * jnp.mean(e * t, axis=-1, keepdims=True))
        dx_ref[b] = dx.astype(BF)
        dgain_ref[...] += jnp.sum(total * t, axis=0, keepdims=True)

    back_start, back_finish = return_rows_copies(out_rows, back_ref, s_back, me, blk)
    dgain_ref[...] = jnp.zeros_like(dgain_ref)
    greet_all()
    ring_start(0)
    for j in range(2 * blocks):
        own_copy(j).start()
        near_copy(j).start()
    spread(0)
    strip_copy(0).start()
    strip_copy(1).start()
    groups = [(r, t, p) for r in range(2) for t in range(1, 8) for p in range(len(plans[r]))]
    for g, (r, t, p) in enumerate(groups):
        ring_step(r, t, p)
        if g < 2 * count:
            strip_product(g)
        if g < 2 * blocks:
            near_step(g)
        if 3 <= g < 2 * blocks + 3:
            far_step(g - 3)
        if (r, t, p) == (0, 6, 1):
            ring_start(1)
            relay(0)
        if (r, t, p) == (0, 7, 1):
            spread(1)
            back_start()
        if (r, t, p) == (1, 5, 0):
            relay(1)
        if (r, t) == (1, 7):
            spread(2 + p)
    for p in range(3):
        relay(2 + p)
    back_finish()
    for n in range(5):
        near_piece, far_piece, relay_piece, local = exchanges[n]
        near_piece().wait()
        far_piece().wait_send()
        relay_piece().wait()
        local().wait()
    for j in range(2 * blocks):
        near_copy(j).wait_send()
        far_copy(j).wait_send()
    for r in range(2):
        for t in range(7):
            for p in range(len(plans[r])):
                ring(r, t, True, p).wait_send()
                ring(r, t, False, p).wait_send()


def collect(gate, up, n1, dqkv, low, a_own, down, out_part, dn1_part, x1, dx1, x, gain):
    part = D // 8
    size = x.shape[1]
    items = 2 * x.shape[0]
    hbm = pl.BlockSpec(memory_space=pl.ANY)
    vmem = pl.BlockSpec(memory_space=pltpu.VMEM)
    sems = lambda n: pltpu.SemaphoreType.DMA((2, n))
    four = lambda width: jax.ShapeDtypeStruct((4, part, width), BF)
    return pl.pallas_call(
        collect_kernel,
        in_specs=[vmem] * 4 + [hbm] * 5 + [vmem] * 4,
        out_specs=[hbm] * 3 + [vmem, hbm, vmem],
        out_shape=[
            four(4 * QW),
            four(2 * FQ),
            four(FQ),
            jax.ShapeDtypeStruct(x.shape, BF),
            jax.ShapeDtypeStruct((2, 4 * size, D), BF),
            jax.ShapeDtypeStruct((1, D), F32),
        ],
        scratch_shapes=[
            pltpu.VMEM((D, 3 * QW), BF),
            pltpu.VMEM((D, QW), BF),
            pltpu.VMEM((2, n1.shape[0], TILE), BF),
            pltpu.VMEM((2, 7, part // 2, 2 * FQ), BF),
            pltpu.VMEM((2, 7, part // 2, 4 * QW), BF),
            pltpu.VMEM((part, 2 * FQ), BF),
            pltpu.VMEM((part, 4 * QW), BF),
            pltpu.VMEM((items, 2, size, D), BF),
            pltpu.VMEM((items, 2, size, D), BF),
            pltpu.VMEM((items, size, D), BF),
            pltpu.VMEM((items, size, D), BF),
            pltpu.VMEM(x.shape, BF),
            sems(14),
            sems(14),
            sems(21),
            sems(21),
            sems(items),
            pltpu.SemaphoreType.DMA((items,)),
            sems(items),
            sems(15),
            pltpu.SemaphoreType.DMA((5,)),
            sems(8),
            pltpu.SemaphoreType.DMA((2 * D // TILE,)),
        ],
        compiler_params=params(63 * 2**20, collective_id=6, has_side_effects=True),
        cost_estimate=pl.CostEstimate(flops=10**11, bytes_accessed=2**25, transcendentals=0),
        name="collect",
    )(gate, up, dqkv, a_own, n1, low, down, out_part, dn1_part, x1, dx1, x, gain)


def rotate_kernel(
    g_ref, base_ref, early_ref, other_ref, first_ref, second_ref, master_ref, rows_ref, small_ref, scale_ref, new_first_ref,
    new_second_ref, new_master_ref, rows_out_ref, small_out_ref, group_small, blk_small, g, base, other, firsts, seconds, masters, g_in, part, x_in, near, z_in, far, p_in, step, steps,
    back, back_in, steps_own, load, store, s_g, s_x, s_z, s_p, s_step, s_back, s_up, s_side, s_rows,
    s_small, s_small2,
):
    blk = lax.axis_index("blk")
    zh, zl, xx = blk // 4, (blk // 2) % 2, blk % 2
    to_x = {"blk": blk + 1 - 2 * xx}
    to_z = {"blk": blk + 4 - 8 * zh}
    to_pair = {"blk": blk + 2 - 4 * zl}
    count = g.shape[0]
    half = UW // 2
    own = pl.ds(pl.multiple_of(zl * half, half), half)
    away = pl.ds(pl.multiple_of((1 - zl) * half, half), half)
    block = 4 * zh + xx
    loads = [
        (g_ref, g), (base_ref, base), (other_ref, other), (first_ref, firsts), (second_ref, seconds), (master_ref, masters),
    ]
    stores = [(firsts, new_first_ref), (seconds, new_second_ref), (masters, new_master_ref)]

    def loading(i, s):
        if i == 2:
            early = isinstance(s, int) and s < EARLY
            source = early_ref.at[s] if early else other_ref.at[jnp.maximum(s - EARLY, 0)]
            return pltpu.make_async_copy(source, other.at[s], load.at[i, s])
        return pltpu.make_async_copy(loads[i][0].at[s], loads[i][1].at[s], load.at[i, s])

    def storing(i, s):
        return pltpu.make_async_copy(stores[i][0].at[s], stores[i][1].at[s], store.at[i, s])

    def send_g(s):
        return remote(g.at[s, :, away], g_in.at[s], s_g, s, to_pair)

    def send_x(s):
        return remote(part.at[s % 3, :, 1 - xx], x_in.at[s], s_x, s, to_x)

    def send_z(s):
        return remote(near.at[s % 3, 1 - zh], z_in.at[s], s_z, s, to_z)

    def send_p(s):
        return remote(far.at[s % 3], p_in.at[s], s_p, s, to_pair)

    def step_pair(s):
        return remote(step.at[s, :, away], steps.at[s, block + 2 * zl], s_step, s, to_pair)

    def step_z(s, a):
        return remote(steps.at[s, block + 2 * a], steps.at[s, block + 2 * a], s_up, 2 * s + a, to_z)

    def step_x(s, a):
        at = 2 * a + xx
        return remote(steps.at[s, at], steps.at[s, at], s_side, 4 * s + a, to_x)

    def send_back(s):
        return remote(back.at[s % 3], back_in.at[s], s_back, s, to_pair)

    for i in range(len(loads)):
        for s in range(count):
            loading(i, s).start()
    rows_start, rows_finish = return_rows_copies(rows_ref, rows_out_ref, s_rows, lax.axis_index("batch"), blk)
    greet_all()
    rows_start()
    for s in range(count):
        loading(0, s).wait()
        send_g(s).start()
    me = lax.axis_index("batch")
    group_small[me] = small_ref[...]

    def small_over(buffer, at, n, size, axis, sems):
        return pltpu.make_async_remote_copy(
            src_ref=buffer.at[at],
            dst_ref=buffer.at[at],
            send_sem=sems.at[0, n],
            recv_sem=sems.at[1, size - n],
            device_id={axis: (at + n) % size},
            device_id_type=MESH,
        )

    def small_from(buffer, at, n, size, axis, sems):
        other = (at + n) % size
        return pltpu.make_async_remote_copy(
            src_ref=buffer.at[other],
            dst_ref=buffer.at[other],
            send_sem=sems.at[0, n],
            recv_sem=sems.at[1, n],
            device_id={axis: other},
            device_id_type=MESH,
        )

    over_group = (group_small, me, 4, "batch", s_small)
    over_blk = (blk_small, blk, 8, "blk", s_small2)

    def small_each(which, act, begin):
        buffer, at, size, axis, sems = which
        for n in range(1, size):
            act(begin(buffer, at, n, size, axis, sems))

    rows = base.shape[1]

    def tick(t, carry):
        def stage(lag, act):
            @pl.when((t >= lag) & (t < count + lag))
            def run():
                act(t - lag)

        def finish(s):
            send_back(s).wait_recv()
            loading(5, s).wait()
            for at, update in ((own, steps_own[s % 2]), (away, back_in[s].astype(F32))):
                value = masters[s, :, at]
                masters[s, :, at] = value - scale_ref[0] * (update + weight_decay * value)
            storing(2, s).start()

        def update(s):
            for a in range(4):
                step_x(s, a).wait_recv()
            whole = jnp.concatenate([steps[s, b] for b in range(8)], axis=0)
            steps_own[s % 2] = dot_plain(base[s], whole)

            @pl.when(s >= 3)
            def reuse():
                send_back(s - 3).wait_send()

            back[s % 3] = dot_plain(other[s], whole).astype(BF)
            send_back(s).start()

        def relay_x(s):
            for a in range(2):
                step_z(s, a).wait_recv()
            for a in range(4):
                step_x(s, a).start()

        def relay_z(s):
            step_pair(s).wait_recv()
            for a in range(2):
                step_z(s, a).start()

        def adam(s):
            send_p(s).wait_recv()
            loading(3, s).wait()
            loading(4, s).wait()
            mine = near[s % 3, zh, zl].astype(F32) + z_in[s, zl].astype(F32)
            for at, turned in ((own, mine), (away, p_in[s].astype(F32))):
                new_first = beta_one * firsts[s, :, at] + (1.0 - beta_one) * turned
                new_second = beta_two * seconds[s, :, at] + (1.0 - beta_two) * turned * turned
                firsts[s, :, at] = new_first
                seconds[s, :, at] = new_second
                moved = new_first / scale_ref[1] / (jnp.sqrt(new_second / scale_ref[2]) + adam_epsilon)
                step[s, :, at] = moved.astype(BF)
            storing(0, s).start()
            storing(1, s).start()
            steps[s, block + 2 * zl] = step[s, :, own]
            step_pair(s).start()

        def send_far(s):
            send_z(s).wait_recv()

            @pl.when(s >= 3)
            def reuse():
                send_p(s - 3).wait_send()

            far[s % 3] = (near[s % 3, zh, 1 - zl].astype(F32) + z_in[s, 1 - zl].astype(F32)).astype(BF)
            send_p(s).start()

        def send_near(s):
            send_x(s).wait_recv()

            @pl.when(s >= 3)
            def reuse():
                send_z(s - 3).wait_send()

            for a in range(2):
                for b in range(2):
                    at = 2 * a + b
                    total = part[s % 3, at, xx].astype(F32) + x_in[s, at].astype(F32)
                    near[s % 3, a, b] = total.astype(BF)
            send_z(s).start()

        def turn_slot(s):
            loading(1, s).wait()
            loading(2, s).wait()
            send_g(s).wait_recv()

            @pl.when(s >= 3)
            def reuse():
                send_x(s - 3).wait_send()

            turned = dot_first(base[s], g[s, :, own]) + dot_first(other[s], g_in[s])
            for b in range(8):
                part[s % 3, b // 2, b % 2] = turned[b * rows : (b + 1) * rows].astype(BF)
            send_x(s).start()

        @pl.when(t == 2)
        def small_start():
            small_each(over_group, lambda copy: copy.start(), small_over)

        @pl.when(t == 8)
        def small_middle():
            small_each(over_group, lambda copy: copy.wait_recv(), small_from)
            total = group_small[0]
            for n in range(1, 4):
                total += group_small[n]
            blk_small[blk] = total
            small_each(over_blk, lambda copy: copy.start(), small_over)

        stage(7, finish)
        stage(6, update)
        stage(5, relay_x)
        stage(4, relay_z)
        stage(3, adam)
        stage(2, send_far)
        stage(1, send_near)
        stage(0, turn_slot)
        return carry

    lax.fori_loop(0, count + 7, tick, 0)
    small_each(over_blk, lambda copy: copy.wait_recv(), small_from)
    small = blk_small[0]
    for n in range(1, 8):
        small += blk_small[n]
    small_each(over_group, lambda copy: copy.wait_send(), small_over)
    small_each(over_blk, lambda copy: copy.wait_send(), small_over)
    small_out_ref[...] = small
    rows_finish()
    for s in range(count):
        send_g(s).wait_send()
        step_pair(s).wait_send()
        for a in range(2):
            step_z(s, a).wait_send()
        for a in range(4):
            step_x(s, a).wait_send()
        for i in range(3):
            storing(i, s).wait()
    for s in range(count - 3, count):
        send_x(s).wait_send()
        send_z(s).wait_send()
        send_p(s).wait_send()
        send_back(s).wait_send()


def rotate_slots(grads, base, early, other, first, second, master, tokens, small, scales):
    count, rows, width = grads.shape
    half = width // 2
    hbm = pl.BlockSpec(memory_space=pl.ANY)
    shape = jax.ShapeDtypeStruct(master.shape, F32)
    sems = lambda n: pltpu.SemaphoreType.DMA((2, n))
    return pl.pallas_call(
        rotate_kernel,
        in_specs=[hbm] * 8 + [pl.BlockSpec(memory_space=pltpu.VMEM), pl.BlockSpec(memory_space=pltpu.SMEM)],
        out_specs=[hbm] * 4 + [pl.BlockSpec(memory_space=pltpu.VMEM)],
        out_shape=[shape] * 3
        + [jax.ShapeDtypeStruct((2, 4 * tokens.shape[1], D), BF), jax.ShapeDtypeStruct(small.shape, F32)],
        scratch_shapes=[
            pltpu.VMEM((4,) + small.shape, F32),
            pltpu.VMEM((8,) + small.shape, F32),
            pltpu.VMEM((count, rows, width), BF),
            pltpu.VMEM((count, rows, D), BF),
            pltpu.VMEM((count, rows, D), BF),
            pltpu.VMEM((count, rows, width), F32),
            pltpu.VMEM((count, rows, width), F32),
            pltpu.VMEM((count, rows, width), F32),
            pltpu.VMEM((count, rows, half), BF),
            pltpu.VMEM((3, 4, 2, rows, half), BF),
            pltpu.VMEM((count, 4, rows, half), BF),
            pltpu.VMEM((3, 2, 2, rows, half), BF),
            pltpu.VMEM((count, 2, rows, half), BF),
            pltpu.VMEM((3, rows, half), BF),
            pltpu.VMEM((count, rows, half), BF),
            pltpu.VMEM((count, rows, width), BF),
            pltpu.VMEM((count, 8, rows, half), BF),
            pltpu.VMEM((3, rows, half), BF),
            pltpu.VMEM((count, rows, half), BF),
            pltpu.VMEM((2, rows, half), F32),
            pltpu.SemaphoreType.DMA((6, count)),
            pltpu.SemaphoreType.DMA((3, count)),
            sems(count),
            sems(count),
            sems(count),
            sems(count),
            sems(count),
            sems(count),
            sems(2 * count),
            sems(4 * count),
            sems(8),
            sems(4),
            sems(8),
        ],
        compiler_params=params(collective_id=2, has_side_effects=True),
        name="rotate_slots",
    )(grads, base, early, other, first, second, master, tokens, small, scales)


def row_groups(
    tokens,
    cotangent,
    lengths,
    unit_owner,
    step_count,
    master,
    first,
    second,
    bases,
    small,
    small_first,
    small_second,
):
    me, blk = lax.axis_index("batch"), lax.axis_index("blk")
    count = tokens.shape[1] * 8
    learn_rate = 2.0 / D**0.5
    slots = lambda array: jnp.transpose(array, (1, 0, 2))
    master_slots = slots(master)

    place = ((unit_owner // 9) ^ me) * 9 + unit_owner % 9
    master_low = master_slots.astype(BF)
    lengths_tile = jnp.pad(lengths, ((0, 8 - lengths.shape[0]), (0, 128 - NDOC)))
    pieces, x_own, dy_own, base, base_early, lens = begin(master_low, tokens, cotangent, slots(bases), lengths_tile)
    attn_shard, gate_up_shard, down_shard = pick_units(place, me, master_low, pieces)
    attn, down, x, other_out, cosine, sine, start = gather(attn_shard, down_shard, x_own, lens)
    low = start.reshape(-1, TILE)[:, 0] // TILE
    down = down.reshape(D, FQ)
    gate_up = lax.all_gather(after(gate_up_shard, attn), "blk", axis=0, tiled=True)
    attn, x = attn.reshape(D, 4 * QW), x.reshape(count, D)
    dy_near, dy_far = swap_core(after(dy_own, attn)), swap_y(after(dy_own, attn))

    gain_one = small[:D].reshape(1, D)
    gain_two = small[D : 2 * D].reshape(1, D)
    head_gain = small[2 * D : 2 * D + VD].reshape(VD, 1)
    mixer, mixer_back = jax.vjp(mix_value, small[2 * D + VD :].reshape(4, HD))
    lam = mixer.reshape(1)

    n1, q, k, v = project(x, attn, gain_one, cosine, sine)
    a_own, maps, log_mass = attend(low, lam, q, k, v, start, head_gain)
    dy = (dy_own, dy_near, dy_far, swap_core(after(dy_far, a_own)))
    n2, x1 = middle(a_own, x, attn, other_out.reshape(3, D, QW), gain_two)
    dup, out_part, dx1, dx1_low, da, gain_two_grad, gate_grad, down_grad, base_other = feed(
        n2, dy, gate_up, down, x1, dy_own, attn, gain_two, base
    )

    down_sums = lax.psum_scatter(down_grad, "blk", scatter_dimension=0, tiled=True)
    dx1_low = dx1_low.reshape(count, D)
    dq, dk, dv, head_gain_sums, mixer_sums = attend_back(
        low, lam, q, k, v, start, head_gain, maps, log_mass, da, cosine, sine
    )
    up_grad = dot_first(n2, after(dup, dq)).astype(BF)
    dqkv = jnp.concatenate([dq, dk, dv], axis=1)
    dn1_part = dot_last(dqkv, attn[:, : 3 * QW]).astype(BF)
    groups = (8, 2, 2, count // 32, D)
    attn_pieces, gate_up_pieces, down_pieces, dx, block_out, gain_one_grad = collect(
        gate_grad, up_grad, n1, dqkv, dx1_low, a_own, down_sums, out_part.reshape(groups), dn1_part.reshape(groups),
        x1, dx1, x_own, gain_one,
    )

    (mixers_grad,) = mixer_back(jnp.sum(mixer_sums))
    small_local = jnp.concatenate(
        [gain_one_grad.reshape(D), gain_two_grad.reshape(D), jnp.sum(head_gain_sums, axis=(0, 2)), mixers_grad.reshape(-1)]
    )
    small_rows = jnp.pad(small_local, (0, 32 * 128 - small_local.shape[0])).reshape(32, 128)

    unit_of = inverse_order(unit_owner)
    units = lax.dynamic_slice_in_dim(unit_of, me * 9, 9)
    grads = place_units(units, me, attn_pieces, gate_up_pieces, down_pieces)

    steps_done = step_count[0].astype(F32)
    scales = jnp.stack([jnp.float32(learn_rate), 1.0 - beta_one**steps_done, 1.0 - beta_two**steps_done])
    new_first, new_second, new_master, input_grad, small_sums = rotate_slots(
        grads, base, base_early, base_other, slots(first), slots(second), master_slots, dx, small_rows, scales
    )
    small_grads = small_sums.reshape(-1)[: small_local.shape[0]]
    new_small_first = beta_one * small_first + (1.0 - beta_one) * small_grads
    new_small_second = beta_two * small_second + (1.0 - beta_two) * small_grads * small_grads
    new_small = small - small_rate * adam_step(new_small_first, new_small_second, steps_done)
    return (
        block_out,
        input_grad,
        slots(new_master),
        slots(new_first),
        slots(new_second),
        small_grads,
        new_small,
        new_small_first,
        new_small_second,
    )


def solution(mesh):
    in_specs = (
        P("batch", "blk", None),
        P("batch", "blk", None),
        P("batch", None),
        P(),
        P(),
        P("blk", "batch", None),
        P("blk", "batch", None),
        P("blk", "batch", None),
        P("blk", "batch", None),
        P(),
        P(),
        P(),
    )
    out_specs = (
        P("batch", "blk", None),
        P("batch", "blk", None),
        P("blk", "batch", None),
        P("blk", "batch", None),
        P("blk", "batch", None),
        P(),
        P(),
        P(),
        P(),
    )
    by_rows = mesh.shape["blk"] == 8 and mesh.shape["batch"] == 4
    body = row_groups if by_rows else any_mesh
    return jax.shard_map(body, mesh=mesh, in_specs=in_specs, out_specs=out_specs, check_vma=False)
```

```python
import functools

import jax
import jax.numpy as jnp
from jax import lax
from jax.experimental import pallas as pl
from jax.experimental.pallas import tpu as pltpu
from jax.sharding import PartitionSpec as P

D = 1536
H = 12
HD = 64
VD = 128
FF = 4096
UW = 512
NDOC = 6
UNITS = 36


norm_epsilon = 1e-05
lambda_start = 0.2
rope_base = 10000.0
masked_fill = -1000000000.0
beta_one = 0.9
beta_two = 0.95
adam_epsilon = 1e-08
weight_decay = 0.01
small_rate = 1.0


def from_behind(shard, axis, by):
    count = lax.axis_size(axis)
    return lax.ppermute(shard, axis, [(i, (i + by) % count) for i in range(count)])


def root_norm(values, gain):
    return (
        values * lax.rsqrt(jnp.mean(values * values, axis=-1, keepdims=True) + norm_epsilon) * gain
    )


def mix_value(mixers):
    return (
        jnp.exp(jnp.sum(mixers[0] * mixers[1]))
        - jnp.exp(jnp.sum(mixers[2] * mixers[3]))
        + lambda_start
    )


def head_mix(maps_out, head_gain, mixer):
    combined = maps_out[:, :, 0] - mixer * maps_out[:, :, 1]
    normed = (
        combined
        * lax.rsqrt(jnp.mean(combined * combined, axis=-1, keepdims=True) + norm_epsilon)
        * head_gain
        * (1.0 - lambda_start)
    )
    rows_count, heads, positions, width = normed.shape
    return jnp.transpose(normed, (0, 2, 1, 3)).reshape(rows_count, positions, heads * width)


def gated_unit(gate, up):
    return jax.nn.silu(gate) * up


def doc_ends(lengths):
    count = lengths.shape[1]
    ends = [lengths[:, 0]]
    for j in range(1, count):
        ends.append(ends[-1] + lengths[:, j])
    return jnp.stack(ends, axis=1)


def document_places(lengths, places):
    ends = doc_ends(lengths)
    starts = ends - lengths
    segment = jnp.sum((places[None, :, None] >= ends[:, None, :]).astype(jnp.int32), axis=2)
    chosen = segment[:, :, None] == jnp.arange(lengths.shape[1], dtype=jnp.int32)[None, None, :]
    offset = jnp.sum(jnp.where(chosen, starts[:, None, :], 0), axis=2)
    return (segment, places[None, :] - offset)


def allowed(seg_query, place_query, seg_key, place_key, last):
    same = seg_query[:, :, None] == seg_key[:, None, :]
    causal = place_key[None, None, :] <= place_query[None, :, None]
    itself = place_key[None, None, :] == place_query[None, :, None]
    return same & causal & ((seg_query[:, :, None] < last) | itself)


def turn_tables(position):
    rates = rope_base ** (-2.0 * jnp.arange(HD // 2, dtype=jnp.float32) / HD)
    angle = position.astype(jnp.float32)[..., None] * rates
    return (jnp.cos(angle), jnp.sin(angle))


def rotate(values, cosine, sine):
    half = values.shape[-1] // 2
    front = values[..., :half]
    back = values[..., half:]
    return jnp.concatenate([front * cosine - back * sine, back * cosine + front * sine], axis=-1)


def adam_step(first_new, second_new, steps_done):
    return (
        first_new
        / (1.0 - beta_one**steps_done)
        / (jnp.sqrt(second_new / (1.0 - beta_two**steps_done)) + adam_epsilon)
    )


def take_units(stacked, order):
    parts = [lax.dynamic_slice_in_dim(stacked, order[i], 1, axis=1) for i in range(UNITS)]
    return jnp.concatenate(parts, axis=1)


def inverse_order(owner):
    numbers = jnp.arange(UNITS, dtype=jnp.int32)
    return jnp.sum(jnp.where(owner[None, :] == numbers[:, None], numbers[None, :], 0), axis=1)


def contract_rows(left, right):
    return lax.dot_general(
        left, right, (((1,), (1,)), ((), ())), preferred_element_type=jnp.float32
    )


def any_mesh(
    tokens,
    cotangent,
    lengths,
    unit_owner,
    step_count,
    master,
    first,
    second,
    bases,
    small,
    small_first,
    small_second,
):
    rows_count, seq_part, width = tokens.shape
    token_count = rows_count * seq_part
    axis_count = lax.axis_size("blk")
    axis_place = lax.axis_index("blk")
    rows_part = master.shape[0]
    scale = HD ** (-0.5)
    highest = lax.Precision.HIGHEST
    learn_rate = 2.0 / D**0.5
    every_slot = lax.all_gather(master.astype(jnp.bfloat16), "batch", axis=1, tiled=True)
    by_unit = take_units(every_slot, unit_owner).reshape(rows_part, UNITS * UW)
    attention_whole = lax.all_gather(by_unit[:, : 4 * D], "blk", axis=0, tiled=True)
    gate_whole = lax.all_gather(by_unit[:, 4 * D : 4 * D + 2 * FF], "blk", axis=0, tiled=True)
    down_whole = lax.all_gather(by_unit[:, 4 * D + 2 * FF :], "blk", axis=0, tiled=True)
    places = axis_place * seq_part + jnp.arange(seq_part, dtype=jnp.int32)
    segment, position = document_places(lengths, places)
    cosine, sine = turn_tables(position)
    cosine = cosine[:, :, None, None, :]
    sine = sine[:, :, None, None, :]
    residual = tokens.astype(jnp.float32)
    gain_one = small[:D]
    gain_two = small[D : 2 * D]
    head_gain = small[2 * D : 2 * D + VD]
    mixer, mixer_back = jax.vjp(mix_value, small[2 * D + VD :].reshape(4, HD))
    normed_exact, norm_one_back = jax.vjp(root_norm, residual, gain_one)
    normed_one = normed_exact.astype(jnp.bfloat16).reshape(token_count, D)
    projected = jnp.dot(normed_one, attention_whole[:, : 3 * D], preferred_element_type=jnp.float32)
    query = rotate(projected[:, :D].reshape(rows_count, seq_part, H, 2, HD), cosine, sine).astype(
        jnp.bfloat16
    )
    key_own = (
        rotate(projected[:, D : 2 * D].reshape(rows_count, seq_part, H, 2, HD), cosine, sine)
        .astype(jnp.bfloat16)
        .reshape(rows_count, seq_part, D)
    )
    value_own = projected[:, 2 * D :].astype(jnp.bfloat16).reshape(rows_count, seq_part, D)
    best = jnp.full((rows_count, H, 2, seq_part), masked_fill, jnp.float32)
    key_piece = lax.all_gather(key_own, "blk", axis=1, tiled=True)
    value_piece = lax.all_gather(value_own, "blk", axis=1, tiled=True)
    count = key_piece.shape[1]
    key_places = jnp.arange(count, dtype=jnp.int32)
    key_segment, unused = document_places(lengths, key_places)
    mask = allowed(segment, places, key_segment, key_places, NDOC - 1)[:, None, None]
    keys = key_piece.reshape(rows_count, count, H, 2, HD)
    values = value_piece.reshape(rows_count, count, H, VD)
    scores = (
        jnp.einsum("rqhcd,rkhcd->rhcqk", query, keys, preferred_element_type=jnp.float32) * scale
    )
    scores = jnp.where(mask, scores, masked_fill)
    top = jnp.maximum(best, jnp.max(scores, axis=-1))
    shares = jnp.where(mask, jnp.exp(scores - top[..., None]), 0.0)
    mass = jnp.sum(shares, axis=-1)
    summed = jnp.einsum(
        "rhcqk,rkhe->rhcqe", shares.astype(jnp.bfloat16), values, preferred_element_type=jnp.float32
    )
    best, mass, summed = (top, mass, summed)
    maps_out = summed / mass[..., None]
    log_mass = best + jnp.log(mass)
    mixed_exact, mix_back = jax.vjp(head_mix, maps_out, head_gain, mixer)
    mixed = mixed_exact.astype(jnp.bfloat16).reshape(token_count, D)
    middle = residual.reshape(token_count, D) + contract_rows(mixed, attention_whole[:, 3 * D :])
    normed_two_exact, norm_two_back = jax.vjp(root_norm, middle, gain_two)
    normed_two = normed_two_exact.astype(jnp.bfloat16)
    gate_up = jnp.dot(normed_two, gate_whole, preferred_element_type=jnp.float32)
    hidden_exact, gated_back = jax.vjp(gated_unit, gate_up[:, :FF], gate_up[:, FF:])
    hidden = hidden_exact.astype(jnp.bfloat16)
    result = middle + contract_rows(hidden, down_whole)
    block_out = result.astype(jnp.bfloat16).reshape(rows_count, seq_part, D)
    output_grad = cotangent.reshape(token_count, D)
    hidden_grad = jnp.dot(output_grad, down_whole, preferred_element_type=jnp.float32)
    gate_grad, up_grad = gated_back(hidden_grad)
    gate_up_grad = jnp.concatenate([gate_grad, up_grad], axis=1).astype(jnp.bfloat16)
    normed_two_grad = contract_rows(gate_up_grad, gate_whole)
    middle_part, gain_two_grad = norm_two_back(normed_two_grad)
    middle_grad = output_grad.astype(jnp.float32) + middle_part
    middle_low = middle_grad.astype(jnp.bfloat16)
    mixed_grad = jnp.dot(
        middle_low, attention_whole[:, 3 * D :], preferred_element_type=jnp.float32
    )
    maps_grad, head_gain_grad, mixer_grad = mix_back(mixed_grad.reshape(rows_count, seq_part, D))
    maps_low = maps_grad.astype(jnp.bfloat16)
    offset_term = jnp.sum(maps_low.astype(jnp.float32) * maps_out, axis=-1)

    def circle(turn_index, carry):
        moving, moving_grad, query_grad = carry
        source = (axis_place - turn_index) % axis_count
        key_places = source * seq_part + jnp.arange(seq_part, dtype=jnp.int32)
        key_segment, unused = document_places(lengths, key_places)
        mask = allowed(segment, places, key_segment, key_places, NDOC - 1)[:, None, None]
        keys = moving[0].astype(jnp.bfloat16).reshape(rows_count, seq_part, H, 2, HD)
        values = moving[1].astype(jnp.bfloat16).reshape(rows_count, seq_part, H, VD)
        scores = (
            jnp.einsum("rqhcd,rkhcd->rhcqk", query, keys, preferred_element_type=jnp.float32)
            * scale
        )
        shares = jnp.where(mask, jnp.exp(scores - log_mass[..., None]), 0.0)
        value_term = jnp.einsum(
            "rhcqk,rhcqe->rkhe",
            shares.astype(jnp.bfloat16),
            maps_low,
            preferred_element_type=jnp.float32,
        )
        share_grad = jnp.einsum(
            "rhcqe,rkhe->rhcqk", maps_low, values, preferred_element_type=jnp.float32
        )
        score_low = (shares * (share_grad - offset_term[..., None])).astype(jnp.bfloat16)
        query_grad = query_grad + jnp.einsum(
            "rhcqk,rkhcd->rqhcd", score_low, keys, preferred_element_type=jnp.float32
        )
        key_term = jnp.einsum(
            "rhcqk,rqhcd->rkhcd", score_low, query, preferred_element_type=jnp.float32
        )
        update = jnp.stack(
            [key_term.reshape(rows_count, seq_part, D), value_term.reshape(rows_count, seq_part, D)]
        )
        moving_grad = moving_grad + update
        moving, moving_grad = (
            from_behind(moving.astype(jnp.bfloat16), "blk", 1).astype(moving.dtype),
            from_behind(moving_grad.astype(jnp.bfloat16), "blk", 1).astype(moving_grad.dtype),
        )
        return (moving, moving_grad, query_grad)

    circle_start = (
        jnp.stack([key_own, value_own]).astype(jnp.float32),
        jnp.zeros((2, rows_count, seq_part, D), jnp.float32),
        jnp.zeros((rows_count, seq_part, H, 2, HD), jnp.float32),
    )
    moving, moving_grad, query_grad = lax.fori_loop(0, axis_count, circle, circle_start)
    key_grad = moving_grad[0].reshape(rows_count, seq_part, H, 2, HD) * scale
    query_pre = rotate(query_grad * scale, cosine, -sine).reshape(token_count, D)
    key_pre = rotate(key_grad, cosine, -sine).reshape(token_count, D)
    projected_grad = jnp.concatenate(
        [query_pre, key_pre, moving_grad[1].reshape(token_count, D)], axis=1
    ).astype(jnp.bfloat16)
    normed_one_grad = contract_rows(projected_grad, attention_whole[:, : 3 * D])
    residual_part, gain_one_grad = norm_one_back(normed_one_grad.reshape(rows_count, seq_part, D))
    input_grad = (middle_grad.reshape(rows_count, seq_part, D) + residual_part).astype(jnp.bfloat16)
    (mixers_grad,) = mixer_back(mixer_grad)
    small_local = jnp.concatenate(
        [gain_one_grad, gain_two_grad, head_gain_grad, mixers_grad.reshape(-1)]
    )
    small_grads = lax.psum(small_local, ("batch", "blk"))
    right_side = jnp.concatenate([projected_grad, mixed, gate_up_grad, hidden], axis=1)
    left_sides = (normed_one, middle_low, normed_two, output_grad)
    bounds = (0, 3 * D, 4 * D, 4 * D + 2 * FF, 4 * D + 3 * FF)
    slot_order = inverse_order(unit_owner)
    parts = []
    for group in range(4):
        left_rows = left_sides[group]
        parts.append(
            lax.dot_general(
                left_rows,
                right_side[:, bounds[group] : bounds[group + 1]],
                (((0,), (0,)), ((), ())),
                preferred_element_type=jnp.float32,
            )
        )
    row_sums = lax.psum_scatter(
        jnp.concatenate(parts, axis=1).astype(jnp.bfloat16), "blk", scatter_dimension=0, tiled=True
    ).astype(jnp.float32)
    placed = take_units(row_sums.reshape(rows_part, UNITS, UW), slot_order)
    grad_slots = lax.psum_scatter(
        placed.astype(jnp.bfloat16), "batch", scatter_dimension=1, tiled=True
    ).astype(jnp.float32)
    columns = bases
    turned = lax.psum_scatter(
        jnp.einsum("ksa,ksn->asn", columns, grad_slots, precision=highest).astype(jnp.bfloat16),
        "blk",
        scatter_dimension=0,
        tiled=True,
    ).astype(jnp.float32)
    steps_done = step_count[0].astype(jnp.float32)
    new_first = beta_one * first + (1.0 - beta_one) * turned
    new_second = beta_two * second + (1.0 - beta_two) * turned * turned
    normalized = adam_step(new_first, new_second, steps_done)
    columns = bases
    update = jnp.zeros_like(master) + jnp.einsum(
        "ksa,asn->ksn",
        columns,
        lax.all_gather(normalized.astype(jnp.bfloat16), "blk", axis=0, tiled=True).astype(
            jnp.float32
        ),
        precision=highest,
    )
    new_master = master - learn_rate * (update + weight_decay * master)
    new_small_first = beta_one * small_first + (1.0 - beta_one) * small_grads
    new_small_second = beta_two * small_second + (1.0 - beta_two) * small_grads * small_grads
    new_small = small - small_rate * adam_step(new_small_first, new_small_second, steps_done)
    return (
        block_out,
        input_grad,
        new_master,
        new_first,
        new_second,
        small_grads,
        new_small,
        new_small_first,
        new_small_second,
    )


BF = jnp.bfloat16
F32 = jnp.float32
TILE = 256
HEADS = 3
QW = HEADS * VD
FQ = FF // 4
EARLY = 3
VMEM_LIMIT = 56 * 2**20


def params(limit=VMEM_LIMIT, **more):
    return pltpu.CompilerParams(vmem_limit_bytes=limit, **more)


def dot_last(left, right):
    return lax.dot_general(left, right, (((1,), (1,)), ((), ())), preferred_element_type=F32)


def dot_first(left, right):
    return lax.dot_general(left, right, (((0,), (0,)), ((), ())), preferred_element_type=F32)


def dot_plain(left, right):
    return jnp.dot(left, right, preferred_element_type=F32)


def swap_core(piece):
    return lax.ppermute(piece, "batch", [(i, i ^ 1) for i in range(4)])


def swap_y(piece):
    return lax.ppermute(piece, "batch", [(i, i ^ 2) for i in range(4)])


def after(values, earlier):
    return lax.optimization_barrier((values, earlier))[0]


def ring_place(blk):
    side = blk % 2
    return (1 - side) * (blk // 2) + side * (7 - blk // 2)


def ring_owner(place):
    place = (place + 16) % 8
    side = place // 4
    return 2 * ((1 - side) * place + side * (7 - place)) + side


MESH = pl.DeviceIdType.MESH


def greet(devices):
    barrier = pltpu.get_barrier_semaphore()
    for device in devices:
        pl.semaphore_signal(barrier, inc=1, device_id=device, device_id_type=MESH)
    pl.semaphore_wait(barrier, len(devices))


def greet_all():
    barrier = pltpu.get_barrier_semaphore()
    me, blk = lax.axis_index("batch"), lax.axis_index("blk")

    def signal(n, carry):
        at = (me * 8 + blk + n) % 32
        pl.semaphore_signal(barrier, inc=1, device_id=(at // 8, at % 8), device_id_type=MESH)
        return carry

    lax.fori_loop(1, 32, signal, 0)
    pl.semaphore_wait(barrier, 31)


def remote(source, target, sems, at, device):
    return pltpu.make_async_remote_copy(
        src_ref=source,
        dst_ref=target,
        send_sem=sems.at[0, at],
        recv_sem=sems.at[1, at],
        device_id=device,
        device_id_type=MESH,
    )


def to_group_copies(source, between, target, s_batch, s_blk, me, blk):
    size = target.shape[1]

    def over_group(n):
        other = (me + n) % 4
        return pltpu.make_async_remote_copy(
            src_ref=source.at[:, pl.ds(pl.multiple_of(other * size, size), size)],
            dst_ref=between.at[pl.ds(2 * me, 2)],
            send_sem=s_batch.at[0, n],
            recv_sem=s_batch.at[1, 4 - n],
            device_id={"batch": other},
            device_id_type=MESH,
        )

    def group_arrival(n):
        other = (me + n) % 4
        return pltpu.make_async_remote_copy(
            src_ref=source.at[:, pl.ds(0, size)],
            dst_ref=between.at[pl.ds(2 * other, 2)],
            send_sem=s_batch.at[0, n],
            recv_sem=s_batch.at[1, n],
            device_id={"batch": other},
            device_id_type=MESH,
        )

    def over_blk(n, i, local, remote_act):
        other = (me + n) % 4
        row = 2 * other + i
        if n == 0:
            piece = source.at[i, pl.ds(pl.multiple_of(me * size, size), size)]
        else:
            piece = between.at[row]

        @pl.when(row == blk)
        def stay():
            local(pltpu.make_async_copy(piece, target.at[blk], s_blk.at[0, 2 * n + i]))

        @pl.when(row != blk)
        def go():
            remote_act(
                pltpu.make_async_remote_copy(
                    src_ref=piece,
                    dst_ref=target.at[blk],
                    send_sem=s_blk.at[0, 2 * n + i],
                    recv_sem=s_blk.at[1, blk],
                    device_id={"blk": row},
                    device_id_type=MESH,
                )
            )

    def start_group():
        for n in (2, 3, 1):
            over_group(n).start()

    def start_blk(n):
        if n:
            group_arrival(n).wait_recv()
        for i in range(2):
            over_blk(n, i, lambda copy: copy.start(), lambda copy: copy.start())

    def finish():
        for n in (1, 2, 3):
            over_group(n).wait_send()
        for n in range(4):
            for i in range(2):
                over_blk(n, i, lambda copy: copy.wait(), lambda copy: copy.wait_send())
        for k in range(8):

            @pl.when(blk != k)
            def arrived():
                pltpu.make_async_remote_copy(
                    src_ref=between.at[0],
                    dst_ref=target.at[k],
                    send_sem=s_blk.at[0, 0],
                    recv_sem=s_blk.at[1, k],
                    device_id={"blk": k},
                    device_id_type=MESH,
                ).wait_recv()

    return start_group, start_blk, finish


def begin_kernel(
    master_ref, tokens_ref, grad_ref, bases_ref, lengths_ref, pieces_ref, x_ref, dy_ref, base_ref, other_ref, lens_ref, wide, narrow, x_between,
    dy_between, s_core, s_y, s_relay, s_x, s_x2, s_dy, s_dy2, s_load, s_store, s_len, s_other,
):
    me, blk = lax.axis_index("batch"), lax.axis_index("blk")
    y, core = me // 2, me % 2
    to_core = {"batch": y * 2 + 1 - core}
    to_y = {"batch": (1 - y) * 2 + core}
    x_group, x_blk, x_finish = to_group_copies(tokens_ref, x_between, x_ref, s_x, s_x2, me, blk)
    dy_group, dy_blk, dy_finish = to_group_copies(grad_ref, dy_between, dy_ref, s_dy, s_dy2, me, blk)
    slots = bases_ref.shape[0]

    def load(n):
        return pltpu.make_async_copy(bases_ref.at[n], wide.at[n % 2], s_load.at[n])

    def store(n):
        return pltpu.make_async_copy(narrow.at[n % 2], base_ref.at[n], s_store.at[n])

    def lengths_copy(n, at):
        return pltpu.make_async_remote_copy(
            src_ref=lengths_ref,
            dst_ref=lens_ref.at[at],
            send_sem=s_len.at[0, n],
            recv_sem=s_len.at[1, 4 - n if at is me else n],
            device_id={"batch": (me + n) % 4},
            device_id_type=MESH,
        )

    zl = (blk // 2) % 2

    def share(n):
        return remote(base_ref.at[n], other_ref.at[n], s_other, n, {"blk": blk + 2 - 4 * zl})

    def cast(n):
        load(n).wait()
        if n - 2 >= EARLY:
            store(n - 2).wait()
        narrow[n % 2] = wide[n % 2].astype(BF)
        store(n).start()
        if n + 2 < slots:
            load(n + 2).start()

    def share_now(n):
        store(n).wait()
        share(n).start()

    def copies(c):
        at = pl.ds(3 * c, 3)
        return (
            lambda: remote(master_ref.at[at], pieces_ref.at[0, at], s_core, c, to_core),
            lambda: remote(master_ref.at[at], pieces_ref.at[1, at], s_y, c, to_y),
            lambda: remote(pieces_ref.at[1, at], pieces_ref.at[2, at], s_relay, c, to_core),
        )

    greet([{"batch": (me + n) % 4} for n in (1, 2, 3)] + [{"blk": (blk + n) % 8} for n in range(1, 8)])
    x_group()
    own_lengths = pltpu.make_async_copy(lengths_ref, lens_ref.at[me], s_len.at[0, 0])
    own_lengths.start()
    for n in (1, 2, 3):
        lengths_copy(n, me).start()
    load(0).start()
    load(1).start()
    x_blk(0)
    cast(0)
    cast(1)
    for c in range(3):
        copies(c)[1]().start()
    dy_group()
    for c in range(3):
        copies(c)[0]().start()
    share_now(0)
    share_now(1)
    cast(2)
    share_now(2)
    for n in (1, 2, 3):
        x_blk(n)
    for n in range(3, slots):
        cast(n)
    store(slots - 2).wait()
    store(slots - 1).wait()
    for n in range(4):
        dy_blk(n)
    for c in range(3):
        copies(c)[1]().wait_recv()
        copies(c)[2]().start()
    for c in range(3):
        near, far, relay = copies(c)
        near().wait()
        far().wait_send()
        relay().wait()
    for n in range(EARLY):
        share(n).wait()
    own_lengths.wait()
    for n in (1, 2, 3):
        lengths_copy(n, me).wait_send()
        lengths_copy(n, (me + n) % 4).wait_recv()
    x_finish()
    dy_finish()


def begin(master, tokens, cotangent, bases, lengths):
    hbm = pl.BlockSpec(memory_space=pl.ANY)
    size = tokens.shape[1] // 4
    sems = lambda n: pltpu.SemaphoreType.DMA((2, n))
    return pl.pallas_call(
        begin_kernel,
        in_specs=[hbm] * 4 + [pl.BlockSpec(memory_space=pltpu.VMEM)],
        out_specs=[hbm] * 6,
        out_shape=[
            jax.ShapeDtypeStruct((3,) + master.shape, BF),
            jax.ShapeDtypeStruct((8, size, D), BF),
            jax.ShapeDtypeStruct((8, size, D), BF),
            jax.ShapeDtypeStruct(bases.shape, BF),
            jax.ShapeDtypeStruct((EARLY,) + bases.shape[1:], BF),
            jax.ShapeDtypeStruct((4,) + lengths.shape, jnp.int32),
        ],
        scratch_shapes=[
            pltpu.VMEM((2,) + bases.shape[1:], F32),
            pltpu.VMEM((2,) + bases.shape[1:], BF),
            pltpu.VMEM((8, size, D), BF),
            pltpu.VMEM((8, size, D), BF),
            sems(3),
            sems(3),
            sems(3),
            sems(4),
            sems(8),
            sems(4),
            sems(8),
            pltpu.SemaphoreType.DMA((bases.shape[0],)),
            pltpu.SemaphoreType.DMA((bases.shape[0],)),
            sems(4),
            sems(EARLY),
        ],
        compiler_params=params(collective_id=3, has_side_effects=True),
        name="begin",
    )(master, tokens, cotangent, bases, lengths)


def gather_kernel(
    shard_ref, down_ref, x_ref, rate_ref, lens_ref, attn_ref, downs_ref, xs_ref, outs_ref, cos_ref, sin_ref, start_ref,
    s_local, s_up, s_down, s_up2, s_down2, s_x, s_out,
):
    me, blk = lax.axis_index("batch"), lax.axis_index("blk")
    y, core = me // 2, me % 2
    to_core = {"batch": y * 2 + 1 - core}
    to_y = {"batch": (1 - y) * 2 + core}
    place = ring_place(blk)
    after_me, before_me = {"blk": ring_owner(place + 1)}, {"blk": ring_owner(place - 1)}
    half = shard_ref.shape[0] // 2
    sub = half // 2
    far_slab = (1 - y) * 2 + core

    def ring(t, up, part, second=False):
        owner = ring_owner(place - t) if up else ring_owner(place + t)
        at = pl.ds((0 if up else half) + part * sub, sub)
        target = (downs_ref if second else attn_ref).at[owner, at]
        source = (down_ref if second else shard_ref).at[at] if t == 0 else target
        sems = (s_up2 if up else s_down2) if second else (s_up if up else s_down)
        return remote(source, target, sems, 2 * t + part, after_me if up else before_me)

    def spread(source, whole, sems, c):
        at = pl.ds(4 * c, 4)
        return (
            lambda: remote(source.at[at], whole.at[at, me], sems, c, to_core),
            lambda: remote(source.at[at], whole.at[at, me], sems, 2 + c, to_y),
            lambda: remote(whole.at[at, far_slab], whole.at[at, far_slab], sems, 4 + c, to_core),
        )

    mine = attn_ref.at[:, :, pl.ds(3 * QW, QW)]
    out = (
        lambda: remote(mine, outs_ref.at[0], s_out, 0, to_core),
        lambda: remote(mine, outs_ref.at[1], s_out, 1, to_y),
        lambda: remote(outs_ref.at[1], outs_ref.at[2], s_out, 2, to_core),
    )
    locals_ = [
        pltpu.make_async_copy(shard_ref, attn_ref.at[blk], s_local.at[0]),
        pltpu.make_async_copy(x_ref, xs_ref.at[:, me], s_local.at[1]),
        pltpu.make_async_copy(down_ref, downs_ref.at[blk], s_local.at[2]),
    ]

    lens = [lens_ref[blk // 2, blk % 2, j] for j in range(NDOC)]
    ends = [lens[0]]
    for j in range(1, NDOC):
        ends.append(ends[-1] + lens[j])

    def first_of(places):
        first = jnp.zeros_like(places)
        for j in range(NDOC):
            first += jnp.where(places >= ends[j], lens[j], 0)
        return first

    def starts():
        places = lax.broadcasted_iota(jnp.int32, start_ref.shape, 1)
        start_ref[...] = jnp.where(places >= ends[NDOC - 2], places, first_of(places))

    def table(b):
        lane = lax.broadcasted_iota(jnp.int32, (TILE, VD), 1)
        places = b * TILE + lax.broadcasted_iota(jnp.int32, (TILE, VD), 0)
        angle = (places - first_of(places)).astype(F32) * rate_ref[...]
        sine = jnp.sin(angle)
        at = slice(b * TILE, (b + 1) * TILE)
        cos_ref[at, :] = jnp.cos(angle)
        sin_ref[at, :] = jnp.where(lane % HD < HD // 2, -sine, sine)

    greet((to_core, to_y, after_me, before_me))
    for part in range(2):
        ring(0, True, part).start()
        ring(0, False, part).start()
    for way in (1, 0):
        for c in range(2):
            spread(x_ref, xs_ref, s_x, c)[way]().start()
    for copy in locals_:
        copy.start()

    def relay(c):
        copies = spread(x_ref, xs_ref, s_x, c)
        copies[1]().wait_recv()
        copies[2]().start()

    starts()
    for t in range(1, 7):
        for part in range(2):
            for up in (True, False):
                ring(t - 1, up, part).wait_recv()
                ring(t, up, part).start()
        table(t - 1)
    for part in range(2):
        for up in (True, False):
            ring(0, up, part, True).start()
            ring(6, up, part).wait_recv()
    locals_[0].wait()
    out[1]().start()
    out[0]().start()
    for t in range(1, 7):
        for part in range(2):
            for up in (True, False):
                ring(t - 1, up, part, True).wait_recv()
                ring(t, up, part, True).start()
        if t in (3, 4):
            relay(t - 3)
        if t in (1, 2):
            table(t + 5)
    for part in range(2):
        for up in (True, False):
            ring(6, up, part, True).wait_recv()
    out[1]().wait_recv()
    out[2]().start()
    for t in range(7):
        for part in range(2):
            for up in (True, False):
                ring(t, up, part).wait_send()
                ring(t, up, part, True).wait_send()
    for c in range(2):
        near, far, again = spread(x_ref, xs_ref, s_x, c)
        near().wait()
        far().wait_send()
        again().wait()
    out[0]().wait()
    out[1]().wait_send()
    out[2]().wait()
    for copy in locals_[1:]:
        copy.wait()


def gather(shard, down, x, lens):
    hbm = pl.BlockSpec(memory_space=pl.ANY)
    size = x.shape[1]
    sems = lambda n: pltpu.SemaphoreType.DMA((2, n))
    count = 32 * size
    vmem = pl.BlockSpec(memory_space=pltpu.VMEM)
    rates = jnp.tile(rope_base ** (-2.0 * jnp.arange(HD // 2, dtype=F32) / HD), 4).reshape(1, VD)
    return pl.pallas_call(
        gather_kernel,
        in_specs=[vmem] * 4 + [pl.BlockSpec(memory_space=pltpu.SMEM)],
        out_specs=[hbm] * 4 + [vmem] * 3,
        out_shape=[
            jax.ShapeDtypeStruct((8,) + shard.shape, BF),
            jax.ShapeDtypeStruct((8,) + down.shape, BF),
            jax.ShapeDtypeStruct((8, 4, size, D), BF),
            jax.ShapeDtypeStruct((3, 8, shard.shape[0], QW), BF),
            jax.ShapeDtypeStruct((count, VD), F32),
            jax.ShapeDtypeStruct((count, VD), F32),
            jax.ShapeDtypeStruct((1, count), jnp.int32),
        ],
        scratch_shapes=[pltpu.SemaphoreType.DMA((3,))] + [sems(14)] * 4 + [sems(6), sems(3)],
        compiler_params=params(collective_id=4, has_side_effects=True),
        name="gather",
    )(shard, down, x, rates, lens)


def attention_pieces(me):
    pieces = []
    for matrix in range(4):
        for j in range(HEADS):
            block = HEADS * me + j
            pieces.append((3 * matrix + block // 4, block % 4, HEADS * matrix + j))
    return pieces


def pick_kernel(place_ref, me_ref, own, pieces, attn_ref, ffn_ref, down_ref, sems):
    me = me_ref[0]
    waits = []

    def begin(unit, source, target, sem):
        at = place_ref[unit]
        for other, ref in enumerate((own, pieces.at[0], pieces.at[1], pieces.at[2])):

            @pl.when(at // 9 == other)
            def start():
                pltpu.make_async_copy(source(ref.at[at % 9]), target, sem).start()

        waits.append(pltpu.make_async_copy(source(own.at[0]), target, sem))

    for i, (unit, block, packed) in enumerate(attention_pieces(me)):
        column = pl.multiple_of(block * 128, 128)
        begin(unit, lambda r, c=column: r.at[:, pl.ds(c, 128)], attn_ref.at[:, pl.ds(packed * 128, 128)], sems.at[i])
    for i in range(6):
        unit = 12 + 8 * (i // 2) + 2 * me + i % 2
        target = ffn_ref.at[:, pl.ds(i * UW, UW)] if i < 4 else down_ref.at[:, pl.ds((i - 4) * UW, UW)]
        begin(unit, lambda r: r, target, sems.at[12 + i])
    for wait in waits:
        wait.wait()


def pick_units(place, me, own, pieces):
    rows = own.shape[1]
    hbm = pl.BlockSpec(memory_space=pl.ANY)
    smem = pl.BlockSpec(memory_space=pltpu.SMEM)
    vmem = pl.BlockSpec(memory_space=pltpu.VMEM)
    return pl.pallas_call(
        pick_kernel,
        in_specs=[smem, smem, hbm, hbm],
        out_specs=[vmem, vmem, vmem],
        out_shape=[
            jax.ShapeDtypeStruct((rows, 4 * QW), BF),
            jax.ShapeDtypeStruct((rows, 4 * UW), BF),
            jax.ShapeDtypeStruct((rows, 2 * UW), BF),
        ],
        scratch_shapes=[pltpu.SemaphoreType.DMA((18,))],
        compiler_params=params(),
        name="pick_units",
    )(place, me.reshape(1), own, pieces)


def place_kernel(unit_ref, me_ref, attn, gate_up, down, out_ref, sems):
    me = me_ref[0]
    waits = []
    for i in range(9):
        unit = unit_ref[i]
        f = jnp.maximum(unit - 12, 0)
        for q in range(4):
            block = (unit % 3) * 4 + q
            low = f % 16
            choices = (
                (unit < 12, attn, block // HEADS, (unit // 3) * QW + (block % HEADS) * 128),
                ((unit >= 12) & (unit < 28), gate_up, (low % 8) // 2, (low // 8) * FQ + (low % 2) * UW + q * 128),
                (unit >= 28, down, (f % 8) // 2, (f % 2) * UW + q * 128),
            )
            target, sem = out_ref.at[i, :, pl.ds(q * 128, 128)], sems.at[i, q]
            for chosen, pieces, holder, column in choices:

                @pl.when(chosen)
                def start(pieces=pieces, holder=holder, column=column, target=target, sem=sem):
                    source = pieces.at[holder ^ me, :, pl.ds(pl.multiple_of(column, 128), 128)]
                    pltpu.make_async_copy(source, target, sem).start()

            waits.append(pltpu.make_async_copy(attn.at[0, :, pl.ds(0, 128)], target, sem))
    for wait in waits:
        wait.wait()


def place_units(units, me, attn_pieces, gate_up_pieces, down_pieces):
    rows = attn_pieces.shape[1]
    hbm = pl.BlockSpec(memory_space=pl.ANY)
    smem = pl.BlockSpec(memory_space=pltpu.SMEM)
    return pl.pallas_call(
        place_kernel,
        in_specs=[smem, smem] + [hbm] * 3,
        out_specs=pl.BlockSpec(memory_space=pltpu.VMEM),
        out_shape=jax.ShapeDtypeStruct((9, rows, UW), BF),
        scratch_shapes=[pltpu.SemaphoreType.DMA((9, 4))],
        compiler_params=params(),
        name="place_units",
    )(units, me.reshape(1), attn_pieces, gate_up_pieces, down_pieces)


def turn(values, cosine, sine, lane):
    partner = jnp.where(lane % HD < HD // 2, pltpu.roll(values, 96, 1), pltpu.roll(values, 32, 1))
    return values * cosine + partner * sine


def project_kernel(x_ref, w_ref, gain_ref, cos_ref, sin_ref, n_ref, q_ref, k_ref, v_ref):
    x = x_ref[...].astype(F32)
    r = lax.rsqrt(jnp.mean(x * x, axis=-1, keepdims=True) + norm_epsilon)
    n = (x * r * gain_ref[...]).astype(BF)
    n_ref[...] = n
    lane = lax.broadcasted_iota(jnp.int32, (x.shape[0], VD), 1)
    cosine, sine = cos_ref[...], sin_ref[...]
    out = dot_plain(n, w_ref[...])
    for h in range(HEADS):
        at = slice(h * VD, (h + 1) * VD)
        q = turn(out[:, h * VD : (h + 1) * VD], cosine, sine, lane)
        q_ref[:, at] = (q.astype(BF).astype(F32) * HD**-0.5).astype(BF)
        k = turn(out[:, QW + h * VD : QW + (h + 1) * VD], cosine, sine, lane)
        k_ref[:, at] = k.astype(BF)
    v_ref[...] = out[:, 2 * QW :].astype(BF)


def project(x, weights, gain, cosine, sine):
    count = x.shape[0]
    rows = lambda w: pl.BlockSpec((TILE, w), lambda i: (i, 0))
    fixed = lambda h, w: pl.BlockSpec((h, w), lambda i: (0, 0), pipeline_mode=pl.Buffered(1))
    narrow = jax.ShapeDtypeStruct((count, QW), BF)
    return pl.pallas_call(
        project_kernel,
        grid=(count // TILE,),
        in_specs=[rows(D), fixed(D, 3 * QW), fixed(1, D), rows(VD), rows(VD)],
        out_specs=[rows(D), rows(QW), rows(QW), rows(QW)],
        out_shape=[jax.ShapeDtypeStruct((count, D), BF), narrow, narrow, narrow],
        compiler_params=params(),
        cost_estimate=pl.CostEstimate(
            flops=2 * count * D * 3 * QW, bytes_accessed=count * D * 6 + 6 * D * QW, transcendentals=0
        ),
        name="project",
    )(x, weights, gain, cosine, sine)


def split_halves(q):
    lane = lax.broadcasted_iota(jnp.int32, q.shape, 1)
    zero = jnp.zeros_like(q)
    return jnp.concatenate([jnp.where(lane < HD, q, zero), jnp.where(lane >= HD, q, zero)], axis=0)


def block_mask(j, n, i, start):
    key = j * TILE + lax.broadcasted_iota(jnp.int32, (n * TILE, 2 * TILE), 0)
    query = i * TILE + lax.broadcasted_iota(jnp.int32, (n * TILE, TILE), 1)
    query = jnp.concatenate([query, query], axis=1)
    return (key >= start) & (key <= query)


def over_blocks(low, high, step, carry):
    odd = (high - low) % 2
    carry = lax.fori_loop(low, low + odd, lambda j, c: step(j, 1, c), carry)
    pairs = (high - low) // 2
    return lax.fori_loop(0, pairs, lambda p, c: step(low + odd + 2 * p, 2, c), carry)


def attend_kernel(low_ref, lam_ref, q_ref, k_ref, v_ref, start_ref, gain_ref, a_ref, maps_ref, log_ref, vt_ref):
    i = pl.program_id(1)

    @pl.when(i == 0)
    def turn_values():
        for j in range(vt_ref.shape[0]):
            vt_ref[j] = v_ref[j * TILE : (j + 1) * TILE, :].astype(F32).T.astype(BF)

    q = split_halves(q_ref[...])
    start = jnp.concatenate([start_ref[...], start_ref[...]], axis=1)

    def step(j, n, carry):
        top, mass, total = carry
        keys = k_ref[pl.ds(pl.multiple_of(j * TILE, TILE), n * TILE), :]
        scores = jnp.where(block_mask(j, n, i, start), dot_last(keys, q), masked_fill)
        new = jnp.maximum(top, jnp.max(scores, axis=0, keepdims=True))
        shares = jnp.exp(scores - new)
        keep = jnp.exp(top - new)
        mass = mass * keep + jnp.sum(shares, axis=0, keepdims=True)
        low_shares = shares.astype(BF)
        total = total * keep
        for b in range(n):
            total += dot_plain(vt_ref[j + b], low_shares[b * TILE : (b + 1) * TILE])
        return new, mass, total

    first = (
        jnp.full((1, 2 * TILE), masked_fill, F32),
        jnp.zeros((1, 2 * TILE), F32),
        jnp.zeros((VD, 2 * TILE), F32),
    )
    top, mass, total = over_blocks(low_ref[i], i + 1, step, first)
    maps = total / mass
    one, two = maps[:, :TILE], maps[:, TILE:]
    maps_ref[0, 0] = one
    maps_ref[0, 1] = two
    log_ref[0, 0] = top + jnp.log(mass)
    mixed = one - lam_ref[0] * two
    r = lax.rsqrt(jnp.mean(mixed * mixed, axis=0, keepdims=True) + norm_epsilon)
    a_ref[...] = (mixed * r * gain_ref[...] * (1.0 - lambda_start)).T.astype(BF)


def attend(low, lam, q, k, v, start, gain):
    count = q.shape[0]
    blocks = count // TILE
    smem = pl.BlockSpec(memory_space=pltpu.SMEM)
    return pl.pallas_call(
        attend_kernel,
        grid=(HEADS, blocks),
        in_specs=[
            smem,
            smem,
            pl.BlockSpec((TILE, VD), lambda h, i: (i, h)),
            pl.BlockSpec((count, VD), lambda h, i: (0, h)),
            pl.BlockSpec((count, VD), lambda h, i: (0, h)),
            pl.BlockSpec((1, TILE), lambda h, i: (0, i)),
            pl.BlockSpec((VD, 1), lambda h, i: (0, 0)),
        ],
        out_specs=[
            pl.BlockSpec((TILE, VD), lambda h, i: (i, h)),
            pl.BlockSpec((1, 2, VD, TILE), lambda h, i: (h, 0, 0, i)),
            pl.BlockSpec((1, 1, 1, 2 * TILE), lambda h, i: (h, i, 0, 0)),
        ],
        out_shape=[
            jax.ShapeDtypeStruct((count, QW), BF),
            jax.ShapeDtypeStruct((HEADS, 2, VD, count), F32),
            jax.ShapeDtypeStruct((HEADS, blocks, 1, 2 * TILE), F32),
        ],
        scratch_shapes=[pltpu.VMEM((blocks, VD, TILE), BF)],
        compiler_params=params(),
        cost_estimate=pl.CostEstimate(
            flops=8 * count * count * VD * HEADS, bytes_accessed=count * QW * 16, transcendentals=count * count * HEADS
        ),
        name="attend",
    )(low, lam, q, k, v, start, gain)


def attend_back_kernel(
    low_ref, lam_ref, q_ref, k_ref, v_ref, start_ref, gain_ref, maps_ref, log_ref, da_ref, cosq_ref, sinq_ref,
    cosk_ref, sink_ref, dq_ref, dk_ref, dv_ref, dgain_ref, dlam_ref, kt_ref, dk_sum, dv_sum, dq_sum,
):
    i = pl.program_id(1)
    blocks = kt_ref.shape[0]

    @pl.when(i == 0)
    def begin():
        for j in range(blocks):
            kt_ref[j] = k_ref[j * TILE : (j + 1) * TILE, :].astype(F32).T.astype(BF)
        dk_sum[...] = jnp.zeros_like(dk_sum)
        dv_sum[...] = jnp.zeros_like(dv_sum)
        dgain_ref[...] = jnp.zeros_like(dgain_ref)
        dlam_ref[...] = jnp.zeros_like(dlam_ref)

    lam = lam_ref[0]
    q = split_halves(q_ref[...])
    start = jnp.concatenate([start_ref[...], start_ref[...]], axis=1)
    log_mass = log_ref[0, 0]
    one, two = maps_ref[0, 0], maps_ref[0, 1]
    mixed = one - lam * two
    r = lax.rsqrt(jnp.mean(mixed * mixed, axis=0, keepdims=True) + norm_epsilon)
    t = mixed * r
    da = da_ref[...].T * (1.0 - lambda_start)
    dgain_ref[0] += da * t
    e = da * gain_ref[...]
    dmixed = r * (e - t * jnp.mean(e * t, axis=0, keepdims=True))
    dlam_ref[0] -= jnp.sum(dmixed * two, axis=0, keepdims=True)
    dmaps = jnp.concatenate([dmixed, -lam * dmixed], axis=1).astype(BF)
    maps = jnp.concatenate([one, two], axis=1)
    offset = jnp.sum(dmaps.astype(F32) * maps, axis=0, keepdims=True)
    dq_sum[...] = jnp.zeros_like(dq_sum)

    def step(j, n, carry):
        at = pl.ds(pl.multiple_of(j * TILE, TILE), n * TILE)
        keys, values = k_ref[at, :], v_ref[at, :]
        scores = dot_last(keys, q)
        shares = jnp.where(block_mask(j, n, i, start), jnp.exp(scores - log_mass), 0.0)
        dshares = dot_plain(values, dmaps)
        dscores = (shares * (dshares - offset)).astype(BF)
        dv_sum[at, :] += dot_last(shares.astype(BF), dmaps)
        dk_sum[at, :] += dot_plain(dscores, q)
        dq = dot_plain(kt_ref[j], dscores[:TILE])
        for b in range(1, n):
            dq += dot_plain(kt_ref[j + b], dscores[b * TILE : (b + 1) * TILE])
        dq_sum[...] += dq
        return carry

    over_blocks(low_ref[i], i + 1, step, 0)
    lane = lax.broadcasted_iota(jnp.int32, (TILE, VD), 1)
    dq = jnp.concatenate([dq_sum[:HD, :TILE], dq_sum[HD:, TILE:]], axis=0).T * HD**-0.5
    dq_ref[...] = turn(dq, cosq_ref[...], -sinq_ref[...], lane).astype(BF)

    @pl.when(i == blocks - 1)
    def finish():
        for j in range(blocks):
            at = slice(j * TILE, (j + 1) * TILE)
            dk_ref[at, :] = turn(dk_sum[at, :], cosk_ref[at, :], -sink_ref[at, :], lane).astype(BF)
        dv_ref[...] = dv_sum[...].astype(BF)


def attend_back(low, lam, q, k, v, start, gain, maps, log_mass, da, cosine, sine):
    count = q.shape[0]
    blocks = count // TILE
    smem = pl.BlockSpec(memory_space=pltpu.SMEM)
    tile = pl.BlockSpec((TILE, VD), lambda h, i: (i, h))
    whole = pl.BlockSpec((count, VD), lambda h, i: (0, h))
    table = pl.BlockSpec((TILE, VD), lambda h, i: (i, 0))
    full_table = pl.BlockSpec((count, VD), lambda h, i: (0, 0), pipeline_mode=pl.Buffered(1))
    narrow = jax.ShapeDtypeStruct((count, QW), BF)
    return pl.pallas_call(
        attend_back_kernel,
        grid=(HEADS, blocks),
        in_specs=[
            smem,
            smem,
            tile,
            whole,
            whole,
            pl.BlockSpec((1, TILE), lambda h, i: (0, i)),
            pl.BlockSpec((VD, 1), lambda h, i: (0, 0)),
            pl.BlockSpec((1, 2, VD, TILE), lambda h, i: (h, 0, 0, i)),
            pl.BlockSpec((1, 1, 1, 2 * TILE), lambda h, i: (h, i, 0, 0)),
            tile,
            table,
            table,
            full_table,
            full_table,
        ],
        out_specs=[
            tile,
            whole,
            whole,
            pl.BlockSpec((1, VD, TILE), lambda h, i: (h, 0, 0)),
            pl.BlockSpec((1, 1, TILE), lambda h, i: (h, 0, 0)),
        ],
        out_shape=[
            narrow,
            narrow,
            narrow,
            jax.ShapeDtypeStruct((HEADS, VD, TILE), F32),
            jax.ShapeDtypeStruct((HEADS, 1, TILE), F32),
        ],
        scratch_shapes=[
            pltpu.VMEM((blocks, VD, TILE), BF),
            pltpu.VMEM((count, VD), F32),
            pltpu.VMEM((count, VD), F32),
            pltpu.VMEM((VD, 2 * TILE), F32),
        ],
        compiler_params=params(),
        cost_estimate=pl.CostEstimate(
            flops=20 * count * count * VD * HEADS, bytes_accessed=count * QW * 24, transcendentals=count * count * HEADS
        ),
        name="attend_back",
    )(low, lam, q, k, v, start, gain, maps, log_mass, da, cosine, sine, cosine, sine)


def middle_kernel(
    x_ref, gain_ref, a_ref, w_ref, w_in, a_hbm, n_ref, own_ref, a_in, total, s_a, s_ay, s_ar
):
    i = pl.program_id(0)
    me = lax.axis_index("batch")
    y, core = me // 2, me % 2
    to_core = {"batch": y * 2 + 1 - core}
    to_y = {"batch": (1 - y) * 2 + core}
    blocks = a_in.shape[1]

    def a_copies(b):
        source = a_hbm.at[pl.ds(b * TILE, TILE)]
        return (
            lambda: remote(source, a_in.at[0, b], s_a, b, to_core),
            lambda: remote(source, a_in.at[1, b], s_ay, b, to_y),
            lambda: remote(a_in.at[1, b], a_in.at[2, b], s_ar, b, to_core),
        )

    @pl.when(i == 0)
    def begin():
        greet((to_core, to_y))
        for b in range(blocks):
            a_copies(b)[1]().start()
        for b in range(blocks):
            a_copies(b)[0]().start()

    @pl.when(i < blocks)
    def relay():
        a_copies(i)[1]().wait_recv()
        a_copies(i)[2]().start()

    @pl.when(i >= 1)
    def compute():
        b = i - 1
        a_copies(b)[0]().wait_recv()
        a_copies(b)[2]().wait_recv()
        x1 = x_ref[...].astype(F32) + dot_last(a_ref[...], w_ref[...])
        for other in range(3):
            x1 += dot_last(a_in[other, b], w_in[other])
        total[...] = x1
        r = lax.rsqrt(jnp.mean(x1 * x1, axis=-1, keepdims=True) + norm_epsilon)
        n_ref[...] = (x1 * r * gain_ref[...]).astype(BF)
        part = TILE // 4
        own_ref[0] = total[pl.ds(pl.multiple_of(me * part, part), part), :]

    @pl.when(i == blocks)
    def finish():
        for b in range(blocks):
            for copy in a_copies(b):
                copy().wait_send()


def middle(a, x, attn, others, gain):
    count = x.shape[0]
    blocks = count // TILE
    late = lambda i: (jnp.maximum(i - 1, 0), 0)
    hbm = pl.BlockSpec(memory_space=pl.ANY)
    sems = lambda n: pltpu.SemaphoreType.DMA((2, n))
    return pl.pallas_call(
        middle_kernel,
        grid=(blocks + 1,),
        in_specs=[
            pl.BlockSpec((TILE, D), late),
            pl.BlockSpec((1, D), lambda i: (0, 0)),
            pl.BlockSpec((TILE, QW), late),
            pl.BlockSpec((D, QW), lambda i: (0, 3), pipeline_mode=pl.Buffered(1)),
            pl.BlockSpec((3, D, QW), lambda i: (0, 0, 0), pipeline_mode=pl.Buffered(1)),
            hbm,
        ],
        out_specs=[
            pl.BlockSpec((TILE, D), late),
            pl.BlockSpec((1, TILE // 4, D), lambda i: (jnp.maximum(i - 1, 0), 0, 0)),
        ],
        out_shape=[
            jax.ShapeDtypeStruct((count, D), BF),
            jax.ShapeDtypeStruct((blocks, TILE // 4, D), F32),
        ],
        scratch_shapes=[
            pltpu.VMEM((3, blocks, TILE, QW), BF),
            pltpu.VMEM((TILE, D), F32),
            sems(blocks),
            sems(blocks),
            sems(blocks),
        ],
        compiler_params=params(collective_id=5, has_side_effects=True),
        cost_estimate=pl.CostEstimate(
            flops=2 * count * D * D, bytes_accessed=count * D * 7 + 2 * D * D, transcendentals=0
        ),
        name="middle",
    )(x, gain, a, attn, others, a)


def feed_kernel(
    n_ref, dy0_ref, dy1_ref, dy2_ref, dy3_ref, w_ref, wd_ref, x1_ref, dyo_ref, wo_ref, gain_ref, base_ref, dup_ref, out_ref, dx_ref, low_ref, da_ref, dgain_ref,
    gate_grad_ref, down_grad_ref, other_ref, dy_ref, part, near_in, near, far_in, gathered, gate_sum, down_sum, staged, s_near, s_far, s_y,
    s_core, s_relay, s_grad, s_low, s_other,
):
    i = pl.program_id(0)
    me = lax.axis_index("batch")
    y, core = me // 2, me % 2
    to_core = {"batch": y * 2 + 1 - core}
    to_y = {"batch": (1 - y) * 2 + core}
    blocks = near_in.shape[0]

    def near_copy(b):
        return remote(part.at[b % 3, :, 1 - core], near_in.at[b], s_near, b, to_core)

    blk = lax.axis_index("blk")
    to_pair = {"blk": blk + 2 - 4 * ((blk // 2) % 2)}

    def share(n):
        return remote(base_ref.at[EARLY + n], other_ref.at[n], s_other, n, to_pair)

    def low_copy(b):
        return pltpu.make_async_copy(gathered.at[b], low_ref.at[b], s_low.at[b])

    grads = ((gate_sum, gate_grad_ref), (down_sum, down_grad_ref))
    strip = gate_sum.shape[0] // 4

    def grad_copy(n, which):
        at = pl.ds(pl.multiple_of(n * strip, strip), strip)
        return pltpu.make_async_copy(staged.at[which], grads[which][1].at[at], s_grad.at[which, n])

    def far_copy(b):
        return remote(near.at[b], far_in.at[b], s_far, b, to_y)

    def own_copy(b, sems, device):
        return remote(gathered.at[b, me], gathered.at[b, me], sems, b, device)

    def relay_copy(b):
        slab = (1 - y) * 2 + core
        return remote(gathered.at[b, slab], gathered.at[b, slab], s_relay, b, to_core)

    @pl.when(i == 0)
    def begin():
        greet((to_core, to_y, to_pair))
        for n in range(other_ref.shape[0]):
            share(n).start()
        dgain_ref[...] = jnp.zeros_like(dgain_ref)
        gate_sum[...] = jnp.zeros_like(gate_sum)
        down_sum[...] = jnp.zeros_like(down_sum)

    @pl.when((i >= 1) & (i < blocks + 1))
    def send_far():
        b = i - 1
        near_copy(b).wait_recv()
        both = part[b % 3, 1 - y, core].astype(F32) + near_in[b, 1 - y].astype(F32)
        near[b] = both.astype(BF)
        far_copy(b).start()

    @pl.when((i >= 2) & (i < blocks + 2))
    def send_own():
        b = i - 2
        far_copy(b).wait_recv()
        dn = part[b % 3, y, core].astype(F32) + near_in[b, y].astype(F32) + far_in[b].astype(F32)
        x1 = x1_ref[0]
        r = lax.rsqrt(jnp.mean(x1 * x1, axis=-1, keepdims=True) + norm_epsilon)
        t = x1 * r
        e = dn * gain_ref[...]
        dx = dyo_ref[0].astype(F32) + r * (e - t * jnp.mean(e * t, axis=-1, keepdims=True))
        dgain_ref[...] += jnp.sum(dn * t, axis=0, keepdims=True)
        dx_ref[0] = dx
        gathered[b, me] = dx.astype(BF)
        own_copy(b, s_y, to_y).start()
        own_copy(b, s_core, to_core).start()

    @pl.when((i >= 3) & (i < blocks + 3))
    def send_relay():
        b = i - 3
        own_copy(b, s_y, to_y).wait_recv()
        relay_copy(b).start()

    @pl.when(i >= 4)
    def use():
        b = i - 4
        own_copy(b, s_core, to_core).wait_recv()
        relay_copy(b).wait_recv()
        whole = jnp.concatenate([gathered[b, other] for other in range(4)], axis=0)
        low_copy(b).start()
        da_ref[...] = dot_plain(whole, wo_ref[...])

    @pl.when(i < blocks)
    def compute():
        size = dy0_ref.shape[1]
        slabs = (me, 2 * y + 1 - core, 2 * (1 - y) + core, 2 * (1 - y) + 1 - core)
        for slab, piece in zip(slabs, (dy0_ref, dy1_ref, dy2_ref, dy3_ref)):
            dy_ref[pl.ds(pl.multiple_of(slab * size, size), size), :] = piece[0]
        n, dy = n_ref[...], dy_ref[...]
        wg, wu, wd = w_ref[:, :FQ], w_ref[:, FQ:], wd_ref[...]
        gate = dot_plain(n, wg)
        up = dot_plain(n, wu)
        dhidden = dot_plain(dy, wd)
        share = 1.0 / (1.0 + jnp.exp(-gate))
        silu = gate * share
        hidden = (silu * up).astype(BF)
        dup = (dhidden * silu).astype(BF)
        dgate = (dhidden * up * (share * (1.0 + gate * (1.0 - share)))).astype(BF)
        dup_ref[...] = dup
        dn = (dot_last(dgate, wg) + dot_last(dup, wu)).astype(BF)

        @pl.when(i >= 3)
        def reuse():
            near_copy(i - 3).wait_send()

        for other in range(4):
            part[i % 3, other // 2, other % 2] = dn[other * size : (other + 1) * size]
        near_copy(i).start()
        out_ref[...] = dot_last(hidden, wd).astype(BF)
        for c in range(0, n.shape[1], TILE):
            gate_sum[c : c + TILE, :] += dot_first(n[:, c : c + TILE], dgate)
            down_sum[c : c + TILE, :] += dot_first(dy[:, c : c + TILE], hidden)

    @pl.when(i >= blocks)
    def keep():
        n = i - blocks
        for which in range(2):

            @pl.when(n >= 1)
            def reuse(which=which):
                grad_copy(n - 1, which).wait()

            at = pl.ds(pl.multiple_of(n * strip, strip), strip)
            staged[which] = grads[which][0][at, :].astype(BF)
            grad_copy(n, which).start()

    @pl.when(i == blocks + 3)
    def finish():
        for which in range(2):
            grad_copy(3, which).wait()
        for b in range(blocks - 3, blocks):
            near_copy(b).wait_send()
        for b in range(blocks):
            far_copy(b).wait_send()
            own_copy(b, s_y, to_y).wait_send()
            own_copy(b, s_core, to_core).wait_send()
            relay_copy(b).wait_send()
            low_copy(b).wait()
        for n in range(other_ref.shape[0]):
            share(n).wait()


def feed(n, dy, weights, down, x1, dy_own, attn, gain, base):
    count = n.shape[0]
    blocks = count // TILE
    size = TILE // 4
    late = lambda lag: lambda i: (jnp.clip(i - lag, 0, blocks - 1), 0)
    late3 = lambda lag: lambda i: (jnp.clip(i - lag, 0, blocks - 1), 0, 0)
    rows = lambda w, lag: pl.BlockSpec((TILE, w), late(lag))
    own = pl.BlockSpec((1, size, D), late3(2))
    shape = lambda w, kind=BF: jax.ShapeDtypeStruct((count, w), kind)
    sems = pltpu.SemaphoreType.DMA((2, blocks))
    return pl.pallas_call(
        feed_kernel,
        grid=(blocks + 4,),
        in_specs=[
            rows(D, 0),
            pl.BlockSpec((1, size, D), late3(0)),
            pl.BlockSpec((1, size, D), late3(0)),
            pl.BlockSpec((1, size, D), late3(0)),
            pl.BlockSpec((1, size, D), late3(0)),
            pl.BlockSpec((D, 2 * FQ), lambda i: (0, 0), pipeline_mode=pl.Buffered(1)),
            pl.BlockSpec((D, FQ), lambda i: (0, 0), pipeline_mode=pl.Buffered(1)),
            own,
            own,
            pl.BlockSpec((D, QW), lambda i: (0, 3), pipeline_mode=pl.Buffered(1)),
            pl.BlockSpec((1, D), lambda i: (0, 0)),
            pl.BlockSpec(memory_space=pl.ANY),
        ],
        out_specs=[
            rows(FQ, 0),
            rows(D, 0),
            own,
            pl.BlockSpec(memory_space=pl.ANY),
            rows(QW, 4),
            pl.BlockSpec((1, D), lambda i: (0, 0)),
            pl.BlockSpec(memory_space=pl.ANY),
            pl.BlockSpec(memory_space=pl.ANY),
            pl.BlockSpec(memory_space=pl.ANY),
        ],
        out_shape=[
            shape(FQ),
            shape(D),
            jax.ShapeDtypeStruct((blocks, size, D), F32),
            jax.ShapeDtypeStruct((blocks, 4, size, D), BF),
            shape(QW, F32),
            jax.ShapeDtypeStruct((1, D), F32),
            jax.ShapeDtypeStruct((D, FQ), BF),
            jax.ShapeDtypeStruct((D, FQ), BF),
            jax.ShapeDtypeStruct((base.shape[0] - EARLY,) + base.shape[1:], BF),
        ],
        scratch_shapes=[
            pltpu.VMEM((TILE, D), BF),
            pltpu.VMEM((3, 2, 2, size, D), BF),
            pltpu.VMEM((blocks, 2, size, D), BF),
            pltpu.VMEM((blocks, size, D), BF),
            pltpu.VMEM((blocks, size, D), BF),
            pltpu.VMEM((blocks, 4, size, D), BF),
            pltpu.VMEM((D, FQ), F32),
            pltpu.VMEM((D, FQ), F32),
            pltpu.VMEM((2, D // 4, FQ), BF),
            sems,
            sems,
            sems,
            sems,
            sems,
            pltpu.SemaphoreType.DMA((2, 4)),
            pltpu.SemaphoreType.DMA((blocks,)),
            pltpu.SemaphoreType.DMA((2, base.shape[0] - EARLY)),
        ],
        compiler_params=params(63 * 2**20, collective_id=1, has_side_effects=True),
        cost_estimate=pl.CostEstimate(
            flops=12 * count * D * FQ, bytes_accessed=count * (8 * D + 6 * FQ) + 6 * D * FQ, transcendentals=count * FQ
        ),
        name="feed",
    )(n, *dy, weights, down, x1, dy_own, attn, gain, base)


def return_rows_copies(source, target, sems, me, blk):
    size = source.shape[1]

    def copies(act_local, act_remote):
        for k in range(8):
            here = (me == blk // 2) & (blk == k)
            piece = target.at[blk % 2, pl.ds(pl.multiple_of(me * size, size), size)]

            @pl.when(here)
            def stay():
                act_local(pltpu.make_async_copy(source.at[k], piece, sems.at[0, k]))

            @pl.when(jnp.logical_not(here))
            def go():
                act_remote(
                    pltpu.make_async_remote_copy(
                        src_ref=source.at[k],
                        dst_ref=piece,
                        send_sem=sems.at[0, k],
                        recv_sem=sems.at[1, (blk % 2) * 4 + me],
                        device_id=(blk // 2, k),
                        device_id_type=MESH,
                    )
                )

    def start():
        copies(lambda copy: copy.start(), lambda copy: copy.start())

    def finish():
        copies(lambda copy: copy.wait(), lambda copy: copy.wait_send())
        for i in range(2):
            for other in range(4):

                @pl.when((me != other) | (blk != 2 * me + i))
                def arrived():
                    pltpu.make_async_remote_copy(
                        src_ref=source.at[0],
                        dst_ref=target.at[i, pl.ds(other * size, size)],
                        send_sem=sems.at[0, 0],
                        recv_sem=sems.at[1, 4 * i + other],
                        device_id=(me, blk),
                        device_id_type=MESH,
                    ).wait_recv()

    return start, finish


def collect_kernel(
    gate, up, dqkv, a_own, n1_ref, low_ref, down_ref, out_part_ref, dn1_part_ref, x1_ref, dx1_ref, x_ref, gain_ref, attn_ref, gate_up_ref,
    downs_ref, dx_ref, back_ref, dgain_ref, qkv, out, strips, first_in, second_in, first_sum, second_sum, own, near_in, near, far_in,
    out_rows, s_up, s_down, s_up2, s_down2, s_near, s_own, s_far, s_pieces, s_local, s_back,
    s_strip,
):
    me, blk = lax.axis_index("batch"), lax.axis_index("blk")
    y, core = me // 2, me % 2
    to_core = {"batch": y * 2 + 1 - core}
    to_y = {"batch": (1 - y) * 2 + core}
    place = ring_place(blk)
    after_me, before_me = {"blk": ring_owner(place + 1)}, {"blk": ring_owner(place - 1)}
    part = first_sum.shape[0]
    half = part // 2
    blocks = dx1_ref.shape[0]

    wide = QW + 256
    plans = (
        ((gate, 0, FQ, 0), (up, 0, FQ, FQ)),
        ((qkv, 0, wide, 0), (qkv, wide, 3 * QW - wide, wide), (out, 0, QW, 3 * QW)),
    )
    buffers, totals = (first_in, second_in), (first_sum, second_sum)
    ring_sems = ((s_up, s_down), (s_up2, s_down2))

    def mine(r, t, up_way, p):
        grad, column, width, _ = plans[r][p]
        owner = ring_owner(place - 1 - t) if up_way else ring_owner(place + 1 + t)
        begin = pl.multiple_of(owner * part + (0 if up_way else half), half)
        return grad.at[pl.ds(begin, half), pl.ds(column, width)]

    def landing(r, t, up_way, p):
        _, _, width, to = plans[r][p]
        return buffers[r].at[0 if up_way else 1, t, :, pl.ds(to, width)]

    def ring(r, t, up_way, p):
        source = mine(r, 0, up_way, p) if t == 0 else landing(r, t - 1, up_way, p)
        sems = ring_sems[r][0 if up_way else 1]
        at = len(plans[r]) * t + p
        return remote(source, landing(r, t, up_way, p), sems, at, after_me if up_way else before_me)

    def ring_start(r):
        for p in range(len(plans[r])):
            ring(r, 0, True, p).start()
            ring(r, 0, False, p).start()

    def ring_step(r, t, p):
        _, _, width, to = plans[r][p]
        for up_way in (True, False):
            ring(r, t - 1, up_way, p).wait_recv()
            here = landing(r, t - 1, up_way, p)
            value = (here[...].astype(F32) + mine(r, t, up_way, p)[...].astype(F32)).astype(BF)
            if t < 7:
                here[...] = value
                ring(r, t, up_way, p).start()
            else:
                totals[r][0 if up_way else half : half if up_way else part, to : to + width] = value

    def exchange(source, target, n):
        return (
            lambda: remote(source, target.at[1], s_pieces, 3 * n, to_core),
            lambda: remote(source, target.at[2], s_pieces, 3 * n + 1, to_y),
            lambda: remote(target.at[2], target.at[3], s_pieces, 3 * n + 2, to_core),
            lambda: pltpu.make_async_copy(source, target.at[0], s_local.at[n]),
        )

    exchanges = [exchange(down_ref, downs_ref, 0), exchange(first_sum, gate_up_ref, 1)]
    for p, (_, _, width, to) in enumerate(plans[1]):
        at = pl.ds(to, width)
        exchanges.append(exchange(second_sum.at[:, at], attn_ref.at[:, :, at], 2 + p))

    strip = strips.shape[2]
    count = D // strip
    lefts, rights, results = (n1_ref, low_ref), (dqkv, a_own), (qkv, out)

    def strip_copy(n):
        source = lefts[n // count].at[:, pl.ds((n % count) * strip, strip)]
        return pltpu.make_async_copy(source, strips.at[n % 2], s_strip.at[n])

    def strip_product(n):
        strip_copy(n).wait()
        at = pl.ds((n % count) * strip, strip)
        results[n // count][at, :] = dot_first(strips[n % 2], rights[n // count][...]).astype(BF)
        if n + 2 < 2 * count:
            strip_copy(n + 2).start()

    def spread(n):
        for way in (1, 0, 3):
            exchanges[n][way]().start()

    def relay(n):
        exchanges[n][1]().wait_recv()
        exchanges[n][2]().start()

    parts = (out_part_ref, dn1_part_ref)

    def near_copy(j):
        return remote(parts[j // blocks].at[j % blocks, :, 1 - core], near_in.at[j], s_near, j, to_core)

    def own_copy(j):
        return pltpu.make_async_copy(parts[j // blocks].at[j % blocks, :, core], own.at[j], s_own.at[j])

    def far_copy(j):
        return remote(near.at[j], far_in.at[j], s_far, j, to_y)

    def near_step(j):
        near_copy(j).wait_recv()
        own_copy(j).wait()
        near[j] = (own[j, 1 - y].astype(F32) + near_in[j, 1 - y].astype(F32)).astype(BF)
        far_copy(j).start()

    def far_step(j):
        far_copy(j).wait_recv()
        total = own[j, y].astype(F32) + near_in[j, y].astype(F32) + far_in[j].astype(F32)
        b = j % blocks
        if j < blocks:
            out_rows[b] = (x1_ref[b] + total).astype(BF)
            return
        x = x_ref[b].astype(F32)
        r = lax.rsqrt(jnp.mean(x * x, axis=-1, keepdims=True) + norm_epsilon)
        t = x * r
        e = total * gain_ref[...]
        dx = dx1_ref[b] + r * (e - t * jnp.mean(e * t, axis=-1, keepdims=True))
        dx_ref[b] = dx.astype(BF)
        dgain_ref[...] += jnp.sum(total * t, axis=0, keepdims=True)

    back_start, back_finish = return_rows_copies(out_rows, back_ref, s_back, me, blk)
    dgain_ref[...] = jnp.zeros_like(dgain_ref)
    greet_all()
    ring_start(0)
    for j in range(2 * blocks):
        own_copy(j).start()
        near_copy(j).start()
    spread(0)
    strip_copy(0).start()
    strip_copy(1).start()
    groups = [(r, t, p) for r in range(2) for t in range(1, 8) for p in range(len(plans[r]))]
    for g, (r, t, p) in enumerate(groups):
        ring_step(r, t, p)
        if g < 2 * count:
            strip_product(g)
        if g < 2 * blocks:
            near_step(g)
        if 3 <= g < 2 * blocks + 3:
            far_step(g - 3)
        if (r, t, p) == (0, 6, 1):
            ring_start(1)
            relay(0)
        if (r, t, p) == (0, 7, 1):
            spread(1)
            back_start()
        if (r, t, p) == (1, 5, 0):
            relay(1)
        if (r, t) == (1, 7):
            spread(2 + p)
    for p in range(3):
        relay(2 + p)
    back_finish()
    for n in range(5):
        near_piece, far_piece, relay_piece, local = exchanges[n]
        near_piece().wait()
        far_piece().wait_send()
        relay_piece().wait()
        local().wait()
    for j in range(2 * blocks):
        near_copy(j).wait_send()
        far_copy(j).wait_send()
    for r in range(2):
        for t in range(7):
            for p in range(len(plans[r])):
                ring(r, t, True, p).wait_send()
                ring(r, t, False, p).wait_send()


def collect(gate, up, n1, dqkv, low, a_own, down, out_part, dn1_part, x1, dx1, x, gain):
    part = D // 8
    size = x.shape[1]
    items = 2 * x.shape[0]
    hbm = pl.BlockSpec(memory_space=pl.ANY)
    vmem = pl.BlockSpec(memory_space=pltpu.VMEM)
    sems = lambda n: pltpu.SemaphoreType.DMA((2, n))
    four = lambda width: jax.ShapeDtypeStruct((4, part, width), BF)
    return pl.pallas_call(
        collect_kernel,
        in_specs=[vmem] * 4 + [hbm] * 5 + [vmem] * 4,
        out_specs=[hbm] * 3 + [vmem, hbm, vmem],
        out_shape=[
            four(4 * QW),
            four(2 * FQ),
            four(FQ),
            jax.ShapeDtypeStruct(x.shape, BF),
            jax.ShapeDtypeStruct((2, 4 * size, D), BF),
            jax.ShapeDtypeStruct((1, D), F32),
        ],
        scratch_shapes=[
            pltpu.VMEM((D, 3 * QW), BF),
            pltpu.VMEM((D, QW), BF),
            pltpu.VMEM((2, n1.shape[0], TILE), BF),
            pltpu.VMEM((2, 7, part // 2, 2 * FQ), BF),
            pltpu.VMEM((2, 7, part // 2, 4 * QW), BF),
            pltpu.VMEM((part, 2 * FQ), BF),
            pltpu.VMEM((part, 4 * QW), BF),
            pltpu.VMEM((items, 2, size, D), BF),
            pltpu.VMEM((items, 2, size, D), BF),
            pltpu.VMEM((items, size, D), BF),
            pltpu.VMEM((items, size, D), BF),
            pltpu.VMEM(x.shape, BF),
            sems(14),
            sems(14),
            sems(21),
            sems(21),
            sems(items),
            pltpu.SemaphoreType.DMA((items,)),
            sems(items),
            sems(15),
            pltpu.SemaphoreType.DMA((5,)),
            sems(8),
            pltpu.SemaphoreType.DMA((2 * D // TILE,)),
        ],
        compiler_params=params(63 * 2**20, collective_id=6, has_side_effects=True),
        cost_estimate=pl.CostEstimate(flops=10**11, bytes_accessed=2**25, transcendentals=0),
        name="collect",
    )(gate, up, dqkv, a_own, n1, low, down, out_part, dn1_part, x1, dx1, x, gain)


def rotate_kernel(
    g_ref, base_ref, early_ref, other_ref, first_ref, second_ref, master_ref, rows_ref, small_ref, scale_ref, new_first_ref,
    new_second_ref, new_master_ref, rows_out_ref, small_out_ref, group_small, blk_small, g, base, other, firsts, seconds, masters, g_in, part, x_in, near, z_in, far, p_in, step, steps,
    back, back_in, steps_own, load, store, s_g, s_x, s_z, s_p, s_step, s_back, s_up, s_side, s_rows,
    s_small, s_small2,
):
    blk = lax.axis_index("blk")
    zh, zl, xx = blk // 4, (blk // 2) % 2, blk % 2
    to_x = {"blk": blk + 1 - 2 * xx}
    to_z = {"blk": blk + 4 - 8 * zh}
    to_pair = {"blk": blk + 2 - 4 * zl}
    count = g.shape[0]
    half = UW // 2
    own = pl.ds(pl.multiple_of(zl * half, half), half)
    away = pl.ds(pl.multiple_of((1 - zl) * half, half), half)
    block = 4 * zh + xx
    loads = [
        (g_ref, g), (base_ref, base), (other_ref, other), (first_ref, firsts), (second_ref, seconds), (master_ref, masters),
    ]
    stores = [(firsts, new_first_ref), (seconds, new_second_ref), (masters, new_master_ref)]

    def loading(i, s):
        if i == 2:
            early = isinstance(s, int) and s < EARLY
            source = early_ref.at[s] if early else other_ref.at[jnp.maximum(s - EARLY, 0)]
            return pltpu.make_async_copy(source, other.at[s], load.at[i, s])
        return pltpu.make_async_copy(loads[i][0].at[s], loads[i][1].at[s], load.at[i, s])

    def storing(i, s):
        return pltpu.make_async_copy(stores[i][0].at[s], stores[i][1].at[s], store.at[i, s])

    def send_g(s):
        return remote(g.at[s, :, away], g_in.at[s], s_g, s, to_pair)

    def send_x(s):
        return remote(part.at[s % 3, :, 1 - xx], x_in.at[s], s_x, s, to_x)

    def send_z(s):
        return remote(near.at[s % 3, 1 - zh], z_in.at[s], s_z, s, to_z)

    def send_p(s):
        return remote(far.at[s % 3], p_in.at[s], s_p, s, to_pair)

    def step_pair(s):
        return remote(step.at[s, :, away], steps.at[s, block + 2 * zl], s_step, s, to_pair)

    def step_z(s, a):
        return remote(steps.at[s, block + 2 * a], steps.at[s, block + 2 * a], s_up, 2 * s + a, to_z)

    def step_x(s, a):
        at = 2 * a + xx
        return remote(steps.at[s, at], steps.at[s, at], s_side, 4 * s + a, to_x)

    def send_back(s):
        return remote(back.at[s % 3], back_in.at[s], s_back, s, to_pair)

    for i in range(len(loads)):
        for s in range(count):
            loading(i, s).start()
    rows_start, rows_finish = return_rows_copies(rows_ref, rows_out_ref, s_rows, lax.axis_index("batch"), blk)
    greet_all()
    rows_start()
    for s in range(count):
        loading(0, s).wait()
        send_g(s).start()
    me = lax.axis_index("batch")
    group_small[me] = small_ref[...]

    def small_over(buffer, at, n, size, axis, sems):
        return pltpu.make_async_remote_copy(
            src_ref=buffer.at[at],
            dst_ref=buffer.at[at],
            send_sem=sems.at[0, n],
            recv_sem=sems.at[1, size - n],
            device_id={axis: (at + n) % size},
            device_id_type=MESH,
        )

    def small_from(buffer, at, n, size, axis, sems):
        other = (at + n) % size
        return pltpu.make_async_remote_copy(
            src_ref=buffer.at[other],
            dst_ref=buffer.at[other],
            send_sem=sems.at[0, n],
            recv_sem=sems.at[1, n],
            device_id={axis: other},
            device_id_type=MESH,
        )

    over_group = (group_small, me, 4, "batch", s_small)
    over_blk = (blk_small, blk, 8, "blk", s_small2)

    def small_each(which, act, begin):
        buffer, at, size, axis, sems = which
        for n in range(1, size):
            act(begin(buffer, at, n, size, axis, sems))

    rows = base.shape[1]

    def tick(t, carry):
        def stage(lag, act):
            @pl.when((t >= lag) & (t < count + lag))
            def run():
                act(t - lag)

        def finish(s):
            send_back(s).wait_recv()
            loading(5, s).wait()
            for at, update in ((own, steps_own[s % 2]), (away, back_in[s].astype(F32))):
                value = masters[s, :, at]
                masters[s, :, at] = value - scale_ref[0] * (update + weight_decay * value)
            storing(2, s).start()

        def update(s):
            for a in range(4):
                step_x(s, a).wait_recv()
            whole = jnp.concatenate([steps[s, b] for b in range(8)], axis=0)
            steps_own[s % 2] = dot_plain(base[s], whole)

            @pl.when(s >= 3)
            def reuse():
                send_back(s - 3).wait_send()

            back[s % 3] = dot_plain(other[s], whole).astype(BF)
            send_back(s).start()

        def relay_x(s):
            for a in range(2):
                step_z(s, a).wait_recv()
            for a in range(4):
                step_x(s, a).start()

        def relay_z(s):
            step_pair(s).wait_recv()
            for a in range(2):
                step_z(s, a).start()

        def adam(s):
            send_p(s).wait_recv()
            loading(3, s).wait()
            loading(4, s).wait()
            mine = near[s % 3, zh, zl].astype(F32) + z_in[s, zl].astype(F32)
            for at, turned in ((own, mine), (away, p_in[s].astype(F32))):
                new_first = beta_one * firsts[s, :, at] + (1.0 - beta_one) * turned
                new_second = beta_two * seconds[s, :, at] + (1.0 - beta_two) * turned * turned
                firsts[s, :, at] = new_first
                seconds[s, :, at] = new_second
                moved = new_first / scale_ref[1] / (jnp.sqrt(new_second / scale_ref[2]) + adam_epsilon)
                step[s, :, at] = moved.astype(BF)
            storing(0, s).start()
            storing(1, s).start()
            steps[s, block + 2 * zl] = step[s, :, own]
            step_pair(s).start()

        def send_far(s):
            send_z(s).wait_recv()

            @pl.when(s >= 3)
            def reuse():
                send_p(s - 3).wait_send()

            far[s % 3] = (near[s % 3, zh, 1 - zl].astype(F32) + z_in[s, 1 - zl].astype(F32)).astype(BF)
            send_p(s).start()

        def send_near(s):
            send_x(s).wait_recv()

            @pl.when(s >= 3)
            def reuse():
                send_z(s - 3).wait_send()

            for a in range(2):
                for b in range(2):
                    at = 2 * a + b
                    total = part[s % 3, at, xx].astype(F32) + x_in[s, at].astype(F32)
                    near[s % 3, a, b] = total.astype(BF)
            send_z(s).start()

        def turn_slot(s):
            loading(1, s).wait()
            loading(2, s).wait()
            send_g(s).wait_recv()

            @pl.when(s >= 3)
            def reuse():
                send_x(s - 3).wait_send()

            turned = dot_first(base[s], g[s, :, own]) + dot_first(other[s], g_in[s])
            for b in range(8):
                part[s % 3, b // 2, b % 2] = turned[b * rows : (b + 1) * rows].astype(BF)
            send_x(s).start()

        @pl.when(t == 2)
        def small_start():
            small_each(over_group, lambda copy: copy.start(), small_over)

        @pl.when(t == 8)
        def small_middle():
            small_each(over_group, lambda copy: copy.wait_recv(), small_from)
            total = group_small[0]
            for n in range(1, 4):
                total += group_small[n]
            blk_small[blk] = total
            small_each(over_blk, lambda copy: copy.start(), small_over)

        stage(7, finish)
        stage(6, update)
        stage(5, relay_x)
        stage(4, relay_z)
        stage(3, adam)
        stage(2, send_far)
        stage(1, send_near)
        stage(0, turn_slot)
        return carry

    lax.fori_loop(0, count + 7, tick, 0)
    small_each(over_blk, lambda copy: copy.wait_recv(), small_from)
    small = blk_small[0]
    for n in range(1, 8):
        small += blk_small[n]
    small_each(over_group, lambda copy: copy.wait_send(), small_over)
    small_each(over_blk, lambda copy: copy.wait_send(), small_over)
    small_out_ref[...] = small
    rows_finish()
    for s in range(count):
        send_g(s).wait_send()
        step_pair(s).wait_send()
        for a in range(2):
            step_z(s, a).wait_send()
        for a in range(4):
            step_x(s, a).wait_send()
        for i in range(3):
            storing(i, s).wait()
    for s in range(count - 3, count):
        send_x(s).wait_send()
        send_z(s).wait_send()
        send_p(s).wait_send()
        send_back(s).wait_send()


def rotate_slots(grads, base, early, other, first, second, master, tokens, small, scales):
    count, rows, width = grads.shape
    half = width // 2
    hbm = pl.BlockSpec(memory_space=pl.ANY)
    shape = jax.ShapeDtypeStruct(master.shape, F32)
    sems = lambda n: pltpu.SemaphoreType.DMA((2, n))
    return pl.pallas_call(
        rotate_kernel,
        in_specs=[hbm] * 8 + [pl.BlockSpec(memory_space=pltpu.VMEM), pl.BlockSpec(memory_space=pltpu.SMEM)],
        out_specs=[hbm] * 4 + [pl.BlockSpec(memory_space=pltpu.VMEM)],
        out_shape=[shape] * 3
        + [jax.ShapeDtypeStruct((2, 4 * tokens.shape[1], D), BF), jax.ShapeDtypeStruct(small.shape, F32)],
        scratch_shapes=[
            pltpu.VMEM((4,) + small.shape, F32),
            pltpu.VMEM((8,) + small.shape, F32),
            pltpu.VMEM((count, rows, width), BF),
            pltpu.VMEM((count, rows, D), BF),
            pltpu.VMEM((count, rows, D), BF),
            pltpu.VMEM((count, rows, width), F32),
            pltpu.VMEM((count, rows, width), F32),
            pltpu.VMEM((count, rows, width), F32),
            pltpu.VMEM((count, rows, half), BF),
            pltpu.VMEM((3, 4, 2, rows, half), BF),
            pltpu.VMEM((count, 4, rows, half), BF),
            pltpu.VMEM((3, 2, 2, rows, half), BF),
            pltpu.VMEM((count, 2, rows, half), BF),
            pltpu.VMEM((3, rows, half), BF),
            pltpu.VMEM((count, rows, half), BF),
            pltpu.VMEM((count, rows, width), BF),
            pltpu.VMEM((count, 8, rows, half), BF),
            pltpu.VMEM((3, rows, half), BF),
            pltpu.VMEM((count, rows, half), BF),
            pltpu.VMEM((2, rows, half), F32),
            pltpu.SemaphoreType.DMA((6, count)),
            pltpu.SemaphoreType.DMA((3, count)),
            sems(count),
            sems(count),
            sems(count),
            sems(count),
            sems(count),
            sems(count),
            sems(2 * count),
            sems(4 * count),
            sems(8),
            sems(4),
            sems(8),
        ],
        compiler_params=params(collective_id=2, has_side_effects=True),
        name="rotate_slots",
    )(grads, base, early, other, first, second, master, tokens, small, scales)


def row_groups(
    tokens,
    cotangent,
    lengths,
    unit_owner,
    step_count,
    master,
    first,
    second,
    bases,
    small,
    small_first,
    small_second,
):
    me, blk = lax.axis_index("batch"), lax.axis_index("blk")
    count = tokens.shape[1] * 8
    learn_rate = 2.0 / D**0.5
    slots = lambda array: jnp.transpose(array, (1, 0, 2))
    master_slots = slots(master)

    place = ((unit_owner // 9) ^ me) * 9 + unit_owner % 9
    master_low = master_slots.astype(BF)
    lengths_tile = jnp.pad(lengths, ((0, 8 - lengths.shape[0]), (0, 128 - NDOC)))
    pieces, x_own, dy_own, base, base_early, lens = begin(master_low, tokens, cotangent, slots(bases), lengths_tile)
    attn_shard, gate_up_shard, down_shard = pick_units(place, me, master_low, pieces)
    attn, down, x, other_out, cosine, sine, start = gather(attn_shard, down_shard, x_own, lens)
    low = start.reshape(-1, TILE)[:, 0] // TILE
    down = down.reshape(D, FQ)
    gate_up = lax.all_gather(after(gate_up_shard, attn), "blk", axis=0, tiled=True)
    attn, x = attn.reshape(D, 4 * QW), x.reshape(count, D)
    dy_near, dy_far = swap_core(after(dy_own, attn)), swap_y(after(dy_own, attn))

    gain_one = small[:D].reshape(1, D)
    gain_two = small[D : 2 * D].reshape(1, D)
    head_gain = small[2 * D : 2 * D + VD].reshape(VD, 1)
    mixer, mixer_back = jax.vjp(mix_value, small[2 * D + VD :].reshape(4, HD))
    lam = mixer.reshape(1)

    n1, q, k, v = project(x, attn, gain_one, cosine, sine)
    a_own, maps, log_mass = attend(low, lam, q, k, v, start, head_gain)
    dy = (dy_own, dy_near, dy_far, swap_core(after(dy_far, a_own)))
    n2, x1 = middle(a_own, x, attn, other_out.reshape(3, D, QW), gain_two)
    dup, out_part, dx1, dx1_low, da, gain_two_grad, gate_grad, down_grad, base_other = feed(
        n2, dy, gate_up, down, x1, dy_own, attn, gain_two, base
    )

    down_sums = lax.psum_scatter(down_grad, "blk", scatter_dimension=0, tiled=True)
    dx1_low = dx1_low.reshape(count, D)
    dq, dk, dv, head_gain_sums, mixer_sums = attend_back(
        low, lam, q, k, v, start, head_gain, maps, log_mass, da, cosine, sine
    )
    up_grad = dot_first(n2, after(dup, dq)).astype(BF)
    dqkv = jnp.concatenate([dq, dk, dv], axis=1)
    dn1_part = dot_last(dqkv, attn[:, : 3 * QW]).astype(BF)
    groups = (8, 2, 2, count // 32, D)
    attn_pieces, gate_up_pieces, down_pieces, dx, block_out, gain_one_grad = collect(
        gate_grad, up_grad, n1, dqkv, dx1_low, a_own, down_sums, out_part.reshape(groups), dn1_part.reshape(groups),
        x1, dx1, x_own, gain_one,
    )

    (mixers_grad,) = mixer_back(jnp.sum(mixer_sums))
    small_local = jnp.concatenate(
        [gain_one_grad.reshape(D), gain_two_grad.reshape(D), jnp.sum(head_gain_sums, axis=(0, 2)), mixers_grad.reshape(-1)]
    )
    small_rows = jnp.pad(small_local, (0, 32 * 128 - small_local.shape[0])).reshape(32, 128)

    unit_of = inverse_order(unit_owner)
    units = lax.dynamic_slice_in_dim(unit_of, me * 9, 9)
    grads = place_units(units, me, attn_pieces, gate_up_pieces, down_pieces)

    steps_done = step_count[0].astype(F32)
    scales = jnp.stack([jnp.float32(learn_rate), 1.0 - beta_one**steps_done, 1.0 - beta_two**steps_done])
    new_first, new_second, new_master, input_grad, small_sums = rotate_slots(
        grads, base, base_early, base_other, slots(first), slots(second), master_slots, dx, small_rows, scales
    )
    small_grads = small_sums.reshape(-1)[: small_local.shape[0]]
    new_small_first = beta_one * small_first + (1.0 - beta_one) * small_grads
    new_small_second = beta_two * small_second + (1.0 - beta_two) * small_grads * small_grads
    new_small = small - small_rate * adam_step(new_small_first, new_small_second, steps_done)
    return (
        block_out,
        input_grad,
        slots(new_master),
        slots(new_first),
        slots(new_second),
        small_grads,
        new_small,
        new_small_first,
        new_small_second,
    )


def solution(mesh):
    in_specs = (
        P("batch", "blk", None),
        P("batch", "blk", None),
        P("batch", None),
        P(),
        P(),
        P("blk", "batch", None),
        P("blk", "batch", None),
        P("blk", "batch", None),
        P("blk", "batch", None),
        P(),
        P(),
        P(),
    )
    out_specs = (
        P("batch", "blk", None),
        P("batch", "blk", None),
        P("blk", "batch", None),
        P("blk", "batch", None),
        P("blk", "batch", None),
        P(),
        P(),
        P(),
        P(),
    )
    by_rows = mesh.shape["blk"] == 8 and mesh.shape["batch"] == 4
    body = row_groups if by_rows else any_mesh
    return jax.shard_map(body, mesh=mesh, in_specs=in_specs, out_specs=out_specs, check_vma=False)
```

```python
import functools

import jax
import jax.numpy as jnp
from jax import lax
from jax.experimental import pallas as pl
from jax.experimental.pallas import tpu as pltpu
from jax.sharding import PartitionSpec as P

D = 1536
H = 12
HD = 64
VD = 128
FF = 4096
UW = 512
NDOC = 6
UNITS = 36


norm_epsilon = 1e-05
lambda_start = 0.2
rope_base = 10000.0
masked_fill = -1000000000.0
beta_one = 0.9
beta_two = 0.95
adam_epsilon = 1e-08
weight_decay = 0.01
small_rate = 1.0


def from_behind(shard, axis, by):
    count = lax.axis_size(axis)
    return lax.ppermute(shard, axis, [(i, (i + by) % count) for i in range(count)])


def root_norm(values, gain):
    return (
        values * lax.rsqrt(jnp.mean(values * values, axis=-1, keepdims=True) + norm_epsilon) * gain
    )


def mix_value(mixers):
    return (
        jnp.exp(jnp.sum(mixers[0] * mixers[1]))
        - jnp.exp(jnp.sum(mixers[2] * mixers[3]))
        + lambda_start
    )


def head_mix(maps_out, head_gain, mixer):
    combined = maps_out[:, :, 0] - mixer * maps_out[:, :, 1]
    normed = (
        combined
        * lax.rsqrt(jnp.mean(combined * combined, axis=-1, keepdims=True) + norm_epsilon)
        * head_gain
        * (1.0 - lambda_start)
    )
    rows_count, heads, positions, width = normed.shape
    return jnp.transpose(normed, (0, 2, 1, 3)).reshape(rows_count, positions, heads * width)


def gated_unit(gate, up):
    return jax.nn.silu(gate) * up


def doc_ends(lengths):
    count = lengths.shape[1]
    ends = [lengths[:, 0]]
    for j in range(1, count):
        ends.append(ends[-1] + lengths[:, j])
    return jnp.stack(ends, axis=1)


def document_places(lengths, places):
    ends = doc_ends(lengths)
    starts = ends - lengths
    segment = jnp.sum((places[None, :, None] >= ends[:, None, :]).astype(jnp.int32), axis=2)
    chosen = segment[:, :, None] == jnp.arange(lengths.shape[1], dtype=jnp.int32)[None, None, :]
    offset = jnp.sum(jnp.where(chosen, starts[:, None, :], 0), axis=2)
    return (segment, places[None, :] - offset)


def allowed(seg_query, place_query, seg_key, place_key, last):
    same = seg_query[:, :, None] == seg_key[:, None, :]
    causal = place_key[None, None, :] <= place_query[None, :, None]
    itself = place_key[None, None, :] == place_query[None, :, None]
    return same & causal & ((seg_query[:, :, None] < last) | itself)


def turn_tables(position):
    rates = rope_base ** (-2.0 * jnp.arange(HD // 2, dtype=jnp.float32) / HD)
    angle = position.astype(jnp.float32)[..., None] * rates
    return (jnp.cos(angle), jnp.sin(angle))


def rotate(values, cosine, sine):
    half = values.shape[-1] // 2
    front = values[..., :half]
    back = values[..., half:]
    return jnp.concatenate([front * cosine - back * sine, back * cosine + front * sine], axis=-1)


def adam_step(first_new, second_new, steps_done):
    return (
        first_new
        / (1.0 - beta_one**steps_done)
        / (jnp.sqrt(second_new / (1.0 - beta_two**steps_done)) + adam_epsilon)
    )


def take_units(stacked, order):
    parts = [lax.dynamic_slice_in_dim(stacked, order[i], 1, axis=1) for i in range(UNITS)]
    return jnp.concatenate(parts, axis=1)


def inverse_order(owner):
    numbers = jnp.arange(UNITS, dtype=jnp.int32)
    return jnp.sum(jnp.where(owner[None, :] == numbers[:, None], numbers[None, :], 0), axis=1)


def contract_rows(left, right):
    return lax.dot_general(
        left, right, (((1,), (1,)), ((), ())), preferred_element_type=jnp.float32
    )


def any_mesh(
    tokens,
    cotangent,
    lengths,
    unit_owner,
    step_count,
    master,
    first,
    second,
    bases,
    small,
    small_first,
    small_second,
):
    rows_count, seq_part, width = tokens.shape
    token_count = rows_count * seq_part
    axis_count = lax.axis_size("blk")
    axis_place = lax.axis_index("blk")
    rows_part = master.shape[0]
    scale = HD ** (-0.5)
    highest = lax.Precision.HIGHEST
    learn_rate = 2.0 / D**0.5
    every_slot = lax.all_gather(master.astype(jnp.bfloat16), "batch", axis=1, tiled=True)
    by_unit = take_units(every_slot, unit_owner).reshape(rows_part, UNITS * UW)
    attention_whole = lax.all_gather(by_unit[:, : 4 * D], "blk", axis=0, tiled=True)
    gate_whole = lax.all_gather(by_unit[:, 4 * D : 4 * D + 2 * FF], "blk", axis=0, tiled=True)
    down_whole = lax.all_gather(by_unit[:, 4 * D + 2 * FF :], "blk", axis=0, tiled=True)
    places = axis_place * seq_part + jnp.arange(seq_part, dtype=jnp.int32)
    segment, position = document_places(lengths, places)
    cosine, sine = turn_tables(position)
    cosine = cosine[:, :, None, None, :]
    sine = sine[:, :, None, None, :]
    residual = tokens.astype(jnp.float32)
    gain_one = small[:D]
    gain_two = small[D : 2 * D]
    head_gain = small[2 * D : 2 * D + VD]
    mixer, mixer_back = jax.vjp(mix_value, small[2 * D + VD :].reshape(4, HD))
    normed_exact, norm_one_back = jax.vjp(root_norm, residual, gain_one)
    normed_one = normed_exact.astype(jnp.bfloat16).reshape(token_count, D)
    projected = jnp.dot(normed_one, attention_whole[:, : 3 * D], preferred_element_type=jnp.float32)
    query = rotate(projected[:, :D].reshape(rows_count, seq_part, H, 2, HD), cosine, sine).astype(
        jnp.bfloat16
    )
    key_own = (
        rotate(projected[:, D : 2 * D].reshape(rows_count, seq_part, H, 2, HD), cosine, sine)
        .astype(jnp.bfloat16)
        .reshape(rows_count, seq_part, D)
    )
    value_own = projected[:, 2 * D :].astype(jnp.bfloat16).reshape(rows_count, seq_part, D)
    best = jnp.full((rows_count, H, 2, seq_part), masked_fill, jnp.float32)
    key_piece = lax.all_gather(key_own, "blk", axis=1, tiled=True)
    value_piece = lax.all_gather(value_own, "blk", axis=1, tiled=True)
    count = key_piece.shape[1]
    key_places = jnp.arange(count, dtype=jnp.int32)
    key_segment, unused = document_places(lengths, key_places)
    mask = allowed(segment, places, key_segment, key_places, NDOC - 1)[:, None, None]
    keys = key_piece.reshape(rows_count, count, H, 2, HD)
    values = value_piece.reshape(rows_count, count, H, VD)
    scores = (
        jnp.einsum("rqhcd,rkhcd->rhcqk", query, keys, preferred_element_type=jnp.float32) * scale
    )
    scores = jnp.where(mask, scores, masked_fill)
    top = jnp.maximum(best, jnp.max(scores, axis=-1))
    shares = jnp.where(mask, jnp.exp(scores - top[..., None]), 0.0)
    mass = jnp.sum(shares, axis=-1)
    summed = jnp.einsum(
        "rhcqk,rkhe->rhcqe", shares.astype(jnp.bfloat16), values, preferred_element_type=jnp.float32
    )
    best, mass, summed = (top, mass, summed)
    maps_out = summed / mass[..., None]
    log_mass = best + jnp.log(mass)
    mixed_exact, mix_back = jax.vjp(head_mix, maps_out, head_gain, mixer)
    mixed = mixed_exact.astype(jnp.bfloat16).reshape(token_count, D)
    middle = residual.reshape(token_count, D) + contract_rows(mixed, attention_whole[:, 3 * D :])
    normed_two_exact, norm_two_back = jax.vjp(root_norm, middle, gain_two)
    normed_two = normed_two_exact.astype(jnp.bfloat16)
    gate_up = jnp.dot(normed_two, gate_whole, preferred_element_type=jnp.float32)
    hidden_exact, gated_back = jax.vjp(gated_unit, gate_up[:, :FF], gate_up[:, FF:])
    hidden = hidden_exact.astype(jnp.bfloat16)
    result = middle + contract_rows(hidden, down_whole)
    block_out = result.astype(jnp.bfloat16).reshape(rows_count, seq_part, D)
    output_grad = cotangent.reshape(token_count, D)
    hidden_grad = jnp.dot(output_grad, down_whole, preferred_element_type=jnp.float32)
    gate_grad, up_grad = gated_back(hidden_grad)
    gate_up_grad = jnp.concatenate([gate_grad, up_grad], axis=1).astype(jnp.bfloat16)
    normed_two_grad = contract_rows(gate_up_grad, gate_whole)
    middle_part, gain_two_grad = norm_two_back(normed_two_grad)
    middle_grad = output_grad.astype(jnp.float32) + middle_part
    middle_low = middle_grad.astype(jnp.bfloat16)
    mixed_grad = jnp.dot(
        middle_low, attention_whole[:, 3 * D :], preferred_element_type=jnp.float32
    )
    maps_grad, head_gain_grad, mixer_grad = mix_back(mixed_grad.reshape(rows_count, seq_part, D))
    maps_low = maps_grad.astype(jnp.bfloat16)
    offset_term = jnp.sum(maps_low.astype(jnp.float32) * maps_out, axis=-1)

    def circle(turn_index, carry):
        moving, moving_grad, query_grad = carry
        source = (axis_place - turn_index) % axis_count
        key_places = source * seq_part + jnp.arange(seq_part, dtype=jnp.int32)
        key_segment, unused = document_places(lengths, key_places)
        mask = allowed(segment, places, key_segment, key_places, NDOC - 1)[:, None, None]
        keys = moving[0].astype(jnp.bfloat16).reshape(rows_count, seq_part, H, 2, HD)
        values = moving[1].astype(jnp.bfloat16).reshape(rows_count, seq_part, H, VD)
        scores = (
            jnp.einsum("rqhcd,rkhcd->rhcqk", query, keys, preferred_element_type=jnp.float32)
            * scale
        )
        shares = jnp.where(mask, jnp.exp(scores - log_mass[..., None]), 0.0)
        value_term = jnp.einsum(
            "rhcqk,rhcqe->rkhe",
            shares.astype(jnp.bfloat16),
            maps_low,
            preferred_element_type=jnp.float32,
        )
        share_grad = jnp.einsum(
            "rhcqe,rkhe->rhcqk", maps_low, values, preferred_element_type=jnp.float32
        )
        score_low = (shares * (share_grad - offset_term[..., None])).astype(jnp.bfloat16)
        query_grad = query_grad + jnp.einsum(
            "rhcqk,rkhcd->rqhcd", score_low, keys, preferred_element_type=jnp.float32
        )
        key_term = jnp.einsum(
            "rhcqk,rqhcd->rkhcd", score_low, query, preferred_element_type=jnp.float32
        )
        update = jnp.stack(
            [key_term.reshape(rows_count, seq_part, D), value_term.reshape(rows_count, seq_part, D)]
        )
        moving_grad = moving_grad + update
        moving, moving_grad = (
            from_behind(moving.astype(jnp.bfloat16), "blk", 1).astype(moving.dtype),
            from_behind(moving_grad.astype(jnp.bfloat16), "blk", 1).astype(moving_grad.dtype),
        )
        return (moving, moving_grad, query_grad)

    circle_start = (
        jnp.stack([key_own, value_own]).astype(jnp.float32),
        jnp.zeros((2, rows_count, seq_part, D), jnp.float32),
        jnp.zeros((rows_count, seq_part, H, 2, HD), jnp.float32),
    )
    moving, moving_grad, query_grad = lax.fori_loop(0, axis_count, circle, circle_start)
    key_grad = moving_grad[0].reshape(rows_count, seq_part, H, 2, HD) * scale
    query_pre = rotate(query_grad * scale, cosine, -sine).reshape(token_count, D)
    key_pre = rotate(key_grad, cosine, -sine).reshape(token_count, D)
    projected_grad = jnp.concatenate(
        [query_pre, key_pre, moving_grad[1].reshape(token_count, D)], axis=1
    ).astype(jnp.bfloat16)
    normed_one_grad = contract_rows(projected_grad, attention_whole[:, : 3 * D])
    residual_part, gain_one_grad = norm_one_back(normed_one_grad.reshape(rows_count, seq_part, D))
    input_grad = (middle_grad.reshape(rows_count, seq_part, D) + residual_part).astype(jnp.bfloat16)
    (mixers_grad,) = mixer_back(mixer_grad)
    small_local = jnp.concatenate(
        [gain_one_grad, gain_two_grad, head_gain_grad, mixers_grad.reshape(-1)]
    )
    small_grads = lax.psum(small_local, ("batch", "blk"))
    right_side = jnp.concatenate([projected_grad, mixed, gate_up_grad, hidden], axis=1)
    left_sides = (normed_one, middle_low, normed_two, output_grad)
    bounds = (0, 3 * D, 4 * D, 4 * D + 2 * FF, 4 * D + 3 * FF)
    slot_order = inverse_order(unit_owner)
    parts = []
    for group in range(4):
        left_rows = left_sides[group]
        parts.append(
            lax.dot_general(
                left_rows,
                right_side[:, bounds[group] : bounds[group + 1]],
                (((0,), (0,)), ((), ())),
                preferred_element_type=jnp.float32,
            )
        )
    row_sums = lax.psum_scatter(
        jnp.concatenate(parts, axis=1).astype(jnp.bfloat16), "blk", scatter_dimension=0, tiled=True
    ).astype(jnp.float32)
    placed = take_units(row_sums.reshape(rows_part, UNITS, UW), slot_order)
    grad_slots = lax.psum_scatter(
        placed.astype(jnp.bfloat16), "batch", scatter_dimension=1, tiled=True
    ).astype(jnp.float32)
    columns = bases
    turned = lax.psum_scatter(
        jnp.einsum("ksa,ksn->asn", columns, grad_slots, precision=highest).astype(jnp.bfloat16),
        "blk",
        scatter_dimension=0,
        tiled=True,
    ).astype(jnp.float32)
    steps_done = step_count[0].astype(jnp.float32)
    new_first = beta_one * first + (1.0 - beta_one) * turned
    new_second = beta_two * second + (1.0 - beta_two) * turned * turned
    normalized = adam_step(new_first, new_second, steps_done)
    columns = bases
    update = jnp.zeros_like(master) + jnp.einsum(
        "ksa,asn->ksn",
        columns,
        lax.all_gather(normalized.astype(jnp.bfloat16), "blk", axis=0, tiled=True).astype(
            jnp.float32
        ),
        precision=highest,
    )
    new_master = master - learn_rate * (update + weight_decay * master)
    new_small_first = beta_one * small_first + (1.0 - beta_one) * small_grads
    new_small_second = beta_two * small_second + (1.0 - beta_two) * small_grads * small_grads
    new_small = small - small_rate * adam_step(new_small_first, new_small_second, steps_done)
    return (
        block_out,
        input_grad,
        new_master,
        new_first,
        new_second,
        small_grads,
        new_small,
        new_small_first,
        new_small_second,
    )


BF = jnp.bfloat16
F32 = jnp.float32
TILE = 256
HEADS = 3
QW = HEADS * VD
FQ = FF // 4
EARLY = 3
VMEM_LIMIT = 56 * 2**20


def params(limit=VMEM_LIMIT, **more):
    return pltpu.CompilerParams(vmem_limit_bytes=limit, **more)


def dot_last(left, right):
    return lax.dot_general(left, right, (((1,), (1,)), ((), ())), preferred_element_type=F32)


def dot_first(left, right):
    return lax.dot_general(left, right, (((0,), (0,)), ((), ())), preferred_element_type=F32)


def dot_plain(left, right):
    return jnp.dot(left, right, preferred_element_type=F32)


def swap_core(piece):
    return lax.ppermute(piece, "batch", [(i, i ^ 1) for i in range(4)])


def swap_y(piece):
    return lax.ppermute(piece, "batch", [(i, i ^ 2) for i in range(4)])


def after(values, earlier):
    return lax.optimization_barrier((values, earlier))[0]


def ring_place(blk):
    side = blk % 2
    return (1 - side) * (blk // 2) + side * (7 - blk // 2)


def ring_owner(place):
    place = (place + 16) % 8
    side = place // 4
    return 2 * ((1 - side) * place + side * (7 - place)) + side


MESH = pl.DeviceIdType.MESH


def greet(devices):
    barrier = pltpu.get_barrier_semaphore()
    for device in devices:
        pl.semaphore_signal(barrier, inc=1, device_id=device, device_id_type=MESH)
    pl.semaphore_wait(barrier, len(devices))


def greet_and_rows(devices):
    barrier = pltpu.get_barrier_semaphore()
    me, blk = lax.axis_index("batch"), lax.axis_index("blk")
    for device in devices:
        pl.semaphore_signal(barrier, inc=1, device_id=device, device_id_type=MESH)
    for i in range(2):
        for other in range(4):

            @pl.when((me != other) | (blk != 2 * me + i))
            def signal():
                pl.semaphore_signal(barrier, inc=1, device_id=(other, 2 * me + i), device_id_type=MESH)

    @pl.when(me == blk // 2)
    def seven():
        pl.semaphore_wait(barrier, len(devices) + 7)

    @pl.when(me != blk // 2)
    def eight():
        pl.semaphore_wait(barrier, len(devices) + 8)


def remote(source, target, sems, at, device):
    return pltpu.make_async_remote_copy(
        src_ref=source,
        dst_ref=target,
        send_sem=sems.at[0, at],
        recv_sem=sems.at[1, at],
        device_id=device,
        device_id_type=MESH,
    )


def to_group_copies(source, between, target, s_batch, s_blk, me, blk):
    size = target.shape[1]

    def over_group(n):
        other = (me + n) % 4
        return pltpu.make_async_remote_copy(
            src_ref=source.at[:, pl.ds(pl.multiple_of(other * size, size), size)],
            dst_ref=between.at[pl.ds(2 * me, 2)],
            send_sem=s_batch.at[0, n],
            recv_sem=s_batch.at[1, 4 - n],
            device_id={"batch": other},
            device_id_type=MESH,
        )

    def group_arrival(n):
        other = (me + n) % 4
        return pltpu.make_async_remote_copy(
            src_ref=source.at[:, pl.ds(0, size)],
            dst_ref=between.at[pl.ds(2 * other, 2)],
            send_sem=s_batch.at[0, n],
            recv_sem=s_batch.at[1, n],
            device_id={"batch": other},
            device_id_type=MESH,
        )

    def over_blk(n, i, local, remote_act):
        other = (me + n) % 4
        row = 2 * other + i
        if n == 0:
            piece = source.at[i, pl.ds(pl.multiple_of(me * size, size), size)]
        else:
            piece = between.at[row]

        @pl.when(row == blk)
        def stay():
            local(pltpu.make_async_copy(piece, target.at[blk], s_blk.at[0, 2 * n + i]))

        @pl.when(row != blk)
        def go():
            remote_act(
                pltpu.make_async_remote_copy(
                    src_ref=piece,
                    dst_ref=target.at[blk],
                    send_sem=s_blk.at[0, 2 * n + i],
                    recv_sem=s_blk.at[1, blk],
                    device_id={"blk": row},
                    device_id_type=MESH,
                )
            )

    def start_group():
        for n in (2, 3, 1):
            over_group(n).start()

    def start_blk(n):
        if n:
            group_arrival(n).wait_recv()
        for i in range(2):
            over_blk(n, i, lambda copy: copy.start(), lambda copy: copy.start())

    def finish():
        for n in (1, 2, 3):
            over_group(n).wait_send()
        for n in range(4):
            for i in range(2):
                over_blk(n, i, lambda copy: copy.wait(), lambda copy: copy.wait_send())
        for k in range(8):

            @pl.when(blk != k)
            def arrived():
                pltpu.make_async_remote_copy(
                    src_ref=between.at[0],
                    dst_ref=target.at[k],
                    send_sem=s_blk.at[0, 0],
                    recv_sem=s_blk.at[1, k],
                    device_id={"blk": k},
                    device_id_type=MESH,
                ).wait_recv()

    return start_group, start_blk, finish


def begin_kernel(
    master_ref, tokens_ref, grad_ref, bases_ref, lengths_ref, pieces_ref, x_ref, dy_ref, base_ref, other_ref, lens_ref, wide, narrow, x_between,
    dy_between, s_core, s_y, s_relay, s_x, s_x2, s_dy, s_dy2, s_load, s_store, s_len, s_other,
):
    me, blk = lax.axis_index("batch"), lax.axis_index("blk")
    y, core = me // 2, me % 2
    to_core = {"batch": y * 2 + 1 - core}
    to_y = {"batch": (1 - y) * 2 + core}
    x_group, x_blk, x_finish = to_group_copies(tokens_ref, x_between, x_ref, s_x, s_x2, me, blk)
    dy_group, dy_blk, dy_finish = to_group_copies(grad_ref, dy_between, dy_ref, s_dy, s_dy2, me, blk)
    slots = bases_ref.shape[0]

    def load(n):
        return pltpu.make_async_copy(bases_ref.at[n], wide.at[n % 2], s_load.at[n])

    def store(n):
        return pltpu.make_async_copy(narrow.at[n % 2], base_ref.at[n], s_store.at[n])

    def lengths_copy(n, at):
        return pltpu.make_async_remote_copy(
            src_ref=lengths_ref,
            dst_ref=lens_ref.at[at],
            send_sem=s_len.at[0, n],
            recv_sem=s_len.at[1, 4 - n if at is me else n],
            device_id={"batch": (me + n) % 4},
            device_id_type=MESH,
        )

    zl = (blk // 2) % 2

    def share(n):
        return remote(base_ref.at[n], other_ref.at[n], s_other, n, {"blk": blk + 2 - 4 * zl})

    def cast(n):
        load(n).wait()
        if n - 2 >= EARLY:
            store(n - 2).wait()
        narrow[n % 2] = wide[n % 2].astype(BF)
        store(n).start()
        if n + 2 < slots:
            load(n + 2).start()

    def share_now(n):
        store(n).wait()
        share(n).start()

    def copies(c):
        at = pl.ds(3 * c, 3)
        return (
            lambda: remote(master_ref.at[at], pieces_ref.at[0, at], s_core, c, to_core),
            lambda: remote(master_ref.at[at], pieces_ref.at[1, at], s_y, c, to_y),
            lambda: remote(pieces_ref.at[1, at], pieces_ref.at[2, at], s_relay, c, to_core),
        )

    greet([{"batch": (me + n) % 4} for n in (1, 2, 3)] + [{"blk": (blk + n) % 8} for n in range(1, 8)])
    x_group()
    own_lengths = pltpu.make_async_copy(lengths_ref, lens_ref.at[me], s_len.at[0, 0])
    own_lengths.start()
    for n in (1, 2, 3):
        lengths_copy(n, me).start()
    load(0).start()
    load(1).start()
    x_blk(0)
    cast(0)
    cast(1)
    for c in range(3):
        copies(c)[1]().start()
    dy_group()
    for c in range(3):
        copies(c)[0]().start()
    share_now(0)
    share_now(1)
    cast(2)
    share_now(2)
    for n in (1, 2, 3):
        x_blk(n)
    for n in range(3, slots):
        cast(n)
    store(slots - 2).wait()
    store(slots - 1).wait()
    for n in range(4):
        dy_blk(n)
    for c in range(3):
        copies(c)[1]().wait_recv()
        copies(c)[2]().start()
    for c in range(3):
        near, far, relay = copies(c)
        near().wait()
        far().wait_send()
        relay().wait()
    for n in range(EARLY):
        share(n).wait()
    own_lengths.wait()
    for n in (1, 2, 3):
        lengths_copy(n, me).wait_send()
        lengths_copy(n, (me + n) % 4).wait_recv()
    x_finish()
    dy_finish()


def begin(master, tokens, cotangent, bases, lengths):
    hbm = pl.BlockSpec(memory_space=pl.ANY)
    size = tokens.shape[1] // 4
    sems = lambda n: pltpu.SemaphoreType.DMA((2, n))
    return pl.pallas_call(
        begin_kernel,
        in_specs=[hbm] * 4 + [pl.BlockSpec(memory_space=pltpu.VMEM)],
        out_specs=[hbm] * 6,
        out_shape=[
            jax.ShapeDtypeStruct((3,) + master.shape, BF),
            jax.ShapeDtypeStruct((8, size, D), BF),
            jax.ShapeDtypeStruct((8, size, D), BF),
            jax.ShapeDtypeStruct(bases.shape, BF),
            jax.ShapeDtypeStruct((EARLY,) + bases.shape[1:], BF),
            jax.ShapeDtypeStruct((4,) + lengths.shape, jnp.int32),
        ],
        scratch_shapes=[
            pltpu.VMEM((2,) + bases.shape[1:], F32),
            pltpu.VMEM((2,) + bases.shape[1:], BF),
            pltpu.VMEM((8, size, D), BF),
            pltpu.VMEM((8, size, D), BF),
            sems(3),
            sems(3),
            sems(3),
            sems(4),
            sems(8),
            sems(4),
            sems(8),
            pltpu.SemaphoreType.DMA((bases.shape[0],)),
            pltpu.SemaphoreType.DMA((bases.shape[0],)),
            sems(4),
            sems(EARLY),
        ],
        compiler_params=params(collective_id=3, has_side_effects=True),
        name="begin",
    )(master, tokens, cotangent, bases, lengths)


def gather_kernel(
    shard_ref, down_ref, x_ref, rate_ref, lens_ref, attn_ref, downs_ref, xs_ref, outs_ref, cos_ref, sin_ref, start_ref,
    s_local, s_up, s_down, s_up2, s_down2, s_x, s_out,
):
    me, blk = lax.axis_index("batch"), lax.axis_index("blk")
    y, core = me // 2, me % 2
    to_core = {"batch": y * 2 + 1 - core}
    to_y = {"batch": (1 - y) * 2 + core}
    place = ring_place(blk)
    after_me, before_me = {"blk": ring_owner(place + 1)}, {"blk": ring_owner(place - 1)}
    half = shard_ref.shape[0] // 2
    sub = half // 2
    far_slab = (1 - y) * 2 + core

    def ring(t, up, part, second=False):
        owner = ring_owner(place - t) if up else ring_owner(place + t)
        at = pl.ds((0 if up else half) + part * sub, sub)
        target = (downs_ref if second else attn_ref).at[owner, at]
        source = (down_ref if second else shard_ref).at[at] if t == 0 else target
        sems = (s_up2 if up else s_down2) if second else (s_up if up else s_down)
        return remote(source, target, sems, 2 * t + part, after_me if up else before_me)

    def spread(source, whole, sems, c):
        at = pl.ds(4 * c, 4)
        return (
            lambda: remote(source.at[at], whole.at[at, me], sems, c, to_core),
            lambda: remote(source.at[at], whole.at[at, me], sems, 2 + c, to_y),
            lambda: remote(whole.at[at, far_slab], whole.at[at, far_slab], sems, 4 + c, to_core),
        )

    mine = attn_ref.at[:, :, pl.ds(3 * QW, QW)]
    out = (
        lambda: remote(mine, outs_ref.at[0], s_out, 0, to_core),
        lambda: remote(mine, outs_ref.at[1], s_out, 1, to_y),
        lambda: remote(outs_ref.at[1], outs_ref.at[2], s_out, 2, to_core),
    )
    locals_ = [
        pltpu.make_async_copy(shard_ref, attn_ref.at[blk], s_local.at[0]),
        pltpu.make_async_copy(x_ref, xs_ref.at[:, me], s_local.at[1]),
        pltpu.make_async_copy(down_ref, downs_ref.at[blk], s_local.at[2]),
    ]

    lens = [lens_ref[blk // 2, blk % 2, j] for j in range(NDOC)]
    ends = [lens[0]]
    for j in range(1, NDOC):
        ends.append(ends[-1] + lens[j])

    def first_of(places):
        first = jnp.zeros_like(places)
        for j in range(NDOC):
            first += jnp.where(places >= ends[j], lens[j], 0)
        return first

    def starts():
        places = lax.broadcasted_iota(jnp.int32, start_ref.shape, 1)
        start_ref[...] = jnp.where(places >= ends[NDOC - 2], places, first_of(places))

    def table(b):
        lane = lax.broadcasted_iota(jnp.int32, (TILE, VD), 1)
        places = b * TILE + lax.broadcasted_iota(jnp.int32, (TILE, VD), 0)
        angle = (places - first_of(places)).astype(F32) * rate_ref[...]
        sine = jnp.sin(angle)
        at = slice(b * TILE, (b + 1) * TILE)
        cos_ref[at, :] = jnp.cos(angle)
        sin_ref[at, :] = jnp.where(lane % HD < HD // 2, -sine, sine)

    greet((to_core, to_y, after_me, before_me))
    for part in range(2):
        ring(0, True, part).start()
        ring(0, False, part).start()
    for way in (1, 0):
        for c in range(2):
            spread(x_ref, xs_ref, s_x, c)[way]().start()
    for copy in locals_:
        copy.start()

    def relay(c):
        copies = spread(x_ref, xs_ref, s_x, c)
        copies[1]().wait_recv()
        copies[2]().start()

    starts()
    for t in range(1, 7):
        for part in range(2):
            for up in (True, False):
                ring(t - 1, up, part).wait_recv()
                ring(t, up, part).start()
        table(t - 1)
    for part in range(2):
        for up in (True, False):
            ring(0, up, part, True).start()
            ring(6, up, part).wait_recv()
    locals_[0].wait()
    out[1]().start()
    out[0]().start()
    for t in range(1, 7):
        for part in range(2):
            for up in (True, False):
                ring(t - 1, up, part, True).wait_recv()
                ring(t, up, part, True).start()
        if t in (3, 4):
            relay(t - 3)
        if t in (1, 2):
            table(t + 5)
    for part in range(2):
        for up in (True, False):
            ring(6, up, part, True).wait_recv()
    out[1]().wait_recv()
    out[2]().start()
    for t in range(7):
        for part in range(2):
            for up in (True, False):
                ring(t, up, part).wait_send()
                ring(t, up, part, True).wait_send()
    for c in range(2):
        near, far, again = spread(x_ref, xs_ref, s_x, c)
        near().wait()
        far().wait_send()
        again().wait()
    out[0]().wait()
    out[1]().wait_send()
    out[2]().wait()
    for copy in locals_[1:]:
        copy.wait()


def gather(shard, down, x, lens):
    hbm = pl.BlockSpec(memory_space=pl.ANY)
    size = x.shape[1]
    sems = lambda n: pltpu.SemaphoreType.DMA((2, n))
    count = 32 * size
    vmem = pl.BlockSpec(memory_space=pltpu.VMEM)
    rates = jnp.tile(rope_base ** (-2.0 * jnp.arange(HD // 2, dtype=F32) / HD), 4).reshape(1, VD)
    return pl.pallas_call(
        gather_kernel,
        in_specs=[vmem] * 4 + [pl.BlockSpec(memory_space=pltpu.SMEM)],
        out_specs=[hbm] * 4 + [vmem] * 3,
        out_shape=[
            jax.ShapeDtypeStruct((8,) + shard.shape, BF),
            jax.ShapeDtypeStruct((8,) + down.shape, BF),
            jax.ShapeDtypeStruct((8, 4, size, D), BF),
            jax.ShapeDtypeStruct((3, 8, shard.shape[0], QW), BF),
            jax.ShapeDtypeStruct((count, VD), F32),
            jax.ShapeDtypeStruct((count, VD), F32),
            jax.ShapeDtypeStruct((1, count), jnp.int32),
        ],
        scratch_shapes=[pltpu.SemaphoreType.DMA((3,))] + [sems(14)] * 4 + [sems(6), sems(3)],
        compiler_params=params(collective_id=4, has_side_effects=True),
        name="gather",
    )(shard, down, x, rates, lens)


def attention_pieces(me):
    pieces = []
    for matrix in range(4):
        for j in range(HEADS):
            block = HEADS * me + j
            pieces.append((3 * matrix + block // 4, block % 4, HEADS * matrix + j))
    return pieces


def pick_kernel(place_ref, me_ref, own, pieces, attn_ref, ffn_ref, down_ref, sems):
    me = me_ref[0]
    waits = []

    def begin(unit, source, target, sem):
        at = place_ref[unit]
        for other, ref in enumerate((own, pieces.at[0], pieces.at[1], pieces.at[2])):

            @pl.when(at // 9 == other)
            def start():
                pltpu.make_async_copy(source(ref.at[at % 9]), target, sem).start()

        waits.append(pltpu.make_async_copy(source(own.at[0]), target, sem))

    for i, (unit, block, packed) in enumerate(attention_pieces(me)):
        column = pl.multiple_of(block * 128, 128)
        begin(unit, lambda r, c=column: r.at[:, pl.ds(c, 128)], attn_ref.at[:, pl.ds(packed * 128, 128)], sems.at[i])
    for i in range(6):
        unit = 12 + 8 * (i // 2) + 2 * me + i % 2
        target = ffn_ref.at[:, pl.ds(i * UW, UW)] if i < 4 else down_ref.at[:, pl.ds((i - 4) * UW, UW)]
        begin(unit, lambda r: r, target, sems.at[12 + i])
    for wait in waits:
        wait.wait()


def pick_units(place, me, own, pieces):
    rows = own.shape[1]
    hbm = pl.BlockSpec(memory_space=pl.ANY)
    smem = pl.BlockSpec(memory_space=pltpu.SMEM)
    vmem = pl.BlockSpec(memory_space=pltpu.VMEM)
    return pl.pallas_call(
        pick_kernel,
        in_specs=[smem, smem, hbm, hbm],
        out_specs=[vmem, vmem, vmem],
        out_shape=[
            jax.ShapeDtypeStruct((rows, 4 * QW), BF),
            jax.ShapeDtypeStruct((rows, 4 * UW), BF),
            jax.ShapeDtypeStruct((rows, 2 * UW), BF),
        ],
        scratch_shapes=[pltpu.SemaphoreType.DMA((18,))],
        compiler_params=params(),
        name="pick_units",
    )(place, me.reshape(1), own, pieces)


def place_kernel(unit_ref, me_ref, attn, gate_up, down, out_ref, sems):
    me = me_ref[0]
    waits = []
    for i in range(9):
        unit = unit_ref[i]
        f = jnp.maximum(unit - 12, 0)
        for q in range(4):
            block = (unit % 3) * 4 + q
            low = f % 16
            choices = (
                (unit < 12, attn, block // HEADS, (unit // 3) * QW + (block % HEADS) * 128),
                ((unit >= 12) & (unit < 28), gate_up, (low % 8) // 2, (low // 8) * FQ + (low % 2) * UW + q * 128),
                (unit >= 28, down, (f % 8) // 2, (f % 2) * UW + q * 128),
            )
            target, sem = out_ref.at[i, :, pl.ds(q * 128, 128)], sems.at[i, q]
            for chosen, pieces, holder, column in choices:

                @pl.when(chosen)
                def start(pieces=pieces, holder=holder, column=column, target=target, sem=sem):
                    source = pieces.at[holder ^ me, :, pl.ds(pl.multiple_of(column, 128), 128)]
                    pltpu.make_async_copy(source, target, sem).start()

            waits.append(pltpu.make_async_copy(attn.at[0, :, pl.ds(0, 128)], target, sem))
    for wait in waits:
        wait.wait()


def place_units(units, me, attn_pieces, gate_up_pieces, down_pieces):
    rows = attn_pieces.shape[1]
    hbm = pl.BlockSpec(memory_space=pl.ANY)
    smem = pl.BlockSpec(memory_space=pltpu.SMEM)
    return pl.pallas_call(
        place_kernel,
        in_specs=[smem, smem] + [hbm] * 3,
        out_specs=pl.BlockSpec(memory_space=pltpu.VMEM),
        out_shape=jax.ShapeDtypeStruct((9, rows, UW), BF),
        scratch_shapes=[pltpu.SemaphoreType.DMA((9, 4))],
        compiler_params=params(),
        name="place_units",
    )(units, me.reshape(1), attn_pieces, gate_up_pieces, down_pieces)


def turn(values, cosine, sine, lane):
    partner = jnp.where(lane % HD < HD // 2, pltpu.roll(values, 96, 1), pltpu.roll(values, 32, 1))
    return values * cosine + partner * sine


def project_kernel(x_ref, w_ref, gain_ref, cos_ref, sin_ref, n_ref, q_ref, k_ref, v_ref):
    x = x_ref[...].astype(F32)
    r = lax.rsqrt(jnp.mean(x * x, axis=-1, keepdims=True) + norm_epsilon)
    n = (x * r * gain_ref[...]).astype(BF)
    n_ref[...] = n
    lane = lax.broadcasted_iota(jnp.int32, (x.shape[0], VD), 1)
    cosine, sine = cos_ref[...], sin_ref[...]
    out = dot_plain(n, w_ref[...])
    for h in range(HEADS):
        at = slice(h * VD, (h + 1) * VD)
        q = turn(out[:, h * VD : (h + 1) * VD], cosine, sine, lane)
        q_ref[:, at] = (q.astype(BF).astype(F32) * HD**-0.5).astype(BF)
        k = turn(out[:, QW + h * VD : QW + (h + 1) * VD], cosine, sine, lane)
        k_ref[:, at] = k.astype(BF)
    v_ref[...] = out[:, 2 * QW :].astype(BF)


def project(x, weights, gain, cosine, sine):
    count = x.shape[0]
    rows = lambda w: pl.BlockSpec((TILE, w), lambda i: (i, 0))
    fixed = lambda h, w: pl.BlockSpec((h, w), lambda i: (0, 0), pipeline_mode=pl.Buffered(1))
    narrow = jax.ShapeDtypeStruct((count, QW), BF)
    return pl.pallas_call(
        project_kernel,
        grid=(count // TILE,),
        in_specs=[rows(D), fixed(D, 3 * QW), fixed(1, D), rows(VD), rows(VD)],
        out_specs=[rows(D), rows(QW), rows(QW), rows(QW)],
        out_shape=[jax.ShapeDtypeStruct((count, D), BF), narrow, narrow, narrow],
        compiler_params=params(),
        cost_estimate=pl.CostEstimate(
            flops=2 * count * D * 3 * QW, bytes_accessed=count * D * 6 + 6 * D * QW, transcendentals=0
        ),
        name="project",
    )(x, weights, gain, cosine, sine)


def split_halves(q):
    lane = lax.broadcasted_iota(jnp.int32, q.shape, 1)
    zero = jnp.zeros_like(q)
    return jnp.concatenate([jnp.where(lane < HD, q, zero), jnp.where(lane >= HD, q, zero)], axis=0)


def block_mask(j, n, i, start):
    key = j * TILE + lax.broadcasted_iota(jnp.int32, (n * TILE, 2 * TILE), 0)
    query = i * TILE + lax.broadcasted_iota(jnp.int32, (n * TILE, TILE), 1)
    query = jnp.concatenate([query, query], axis=1)
    return (key >= start) & (key <= query)


def over_blocks(low, high, step, carry):
    odd = (high - low) % 2
    carry = lax.fori_loop(low, low + odd, lambda j, c: step(j, 1, c), carry)
    pairs = (high - low) // 2
    return lax.fori_loop(0, pairs, lambda p, c: step(low + odd + 2 * p, 2, c), carry)


def attend_kernel(low_ref, lam_ref, q_ref, k_ref, v_ref, start_ref, gain_ref, a_ref, maps_ref, log_ref, vt_ref):
    i = pl.program_id(1)

    @pl.when(i == 0)
    def turn_values():
        for j in range(vt_ref.shape[0]):
            vt_ref[j] = v_ref[j * TILE : (j + 1) * TILE, :].astype(F32).T.astype(BF)

    q = split_halves(q_ref[...])
    start = jnp.concatenate([start_ref[...], start_ref[...]], axis=1)

    def step(j, n, carry):
        top, mass, total = carry
        keys = k_ref[pl.ds(pl.multiple_of(j * TILE, TILE), n * TILE), :]
        scores = jnp.where(block_mask(j, n, i, start), dot_last(keys, q), masked_fill)
        new = jnp.maximum(top, jnp.max(scores, axis=0, keepdims=True))
        shares = jnp.exp(scores - new)
        keep = jnp.exp(top - new)
        mass = mass * keep + jnp.sum(shares, axis=0, keepdims=True)
        low_shares = shares.astype(BF)
        total = total * keep
        for b in range(n):
            total += dot_plain(vt_ref[j + b], low_shares[b * TILE : (b + 1) * TILE])
        return new, mass, total

    first = (
        jnp.full((1, 2 * TILE), masked_fill, F32),
        jnp.zeros((1, 2 * TILE), F32),
        jnp.zeros((VD, 2 * TILE), F32),
    )
    top, mass, total = over_blocks(low_ref[i], i + 1, step, first)
    maps = total / mass
    one, two = maps[:, :TILE], maps[:, TILE:]
    maps_ref[0, 0] = one
    maps_ref[0, 1] = two
    log_ref[0, 0] = top + jnp.log(mass)
    mixed = one - lam_ref[0] * two
    r = lax.rsqrt(jnp.mean(mixed * mixed, axis=0, keepdims=True) + norm_epsilon)
    a_ref[...] = (mixed * r * gain_ref[...] * (1.0 - lambda_start)).T.astype(BF)


def attend(low, lam, q, k, v, start, gain):
    count = q.shape[0]
    blocks = count // TILE
    smem = pl.BlockSpec(memory_space=pltpu.SMEM)
    return pl.pallas_call(
        attend_kernel,
        grid=(HEADS, blocks),
        in_specs=[
            smem,
            smem,
            pl.BlockSpec((TILE, VD), lambda h, i: (i, h)),
            pl.BlockSpec((count, VD), lambda h, i: (0, h)),
            pl.BlockSpec((count, VD), lambda h, i: (0, h)),
            pl.BlockSpec((1, TILE), lambda h, i: (0, i)),
            pl.BlockSpec((VD, 1), lambda h, i: (0, 0)),
        ],
        out_specs=[
            pl.BlockSpec((TILE, VD), lambda h, i: (i, h)),
            pl.BlockSpec((1, 2, VD, TILE), lambda h, i: (h, 0, 0, i)),
            pl.BlockSpec((1, 1, 1, 2 * TILE), lambda h, i: (h, i, 0, 0)),
        ],
        out_shape=[
            jax.ShapeDtypeStruct((count, QW), BF),
            jax.ShapeDtypeStruct((HEADS, 2, VD, count), F32),
            jax.ShapeDtypeStruct((HEADS, blocks, 1, 2 * TILE), F32),
        ],
        scratch_shapes=[pltpu.VMEM((blocks, VD, TILE), BF)],
        compiler_params=params(),
        cost_estimate=pl.CostEstimate(
            flops=8 * count * count * VD * HEADS, bytes_accessed=count * QW * 16, transcendentals=count * count * HEADS
        ),
        name="attend",
    )(low, lam, q, k, v, start, gain)


def attend_back_kernel(
    low_ref, lam_ref, q_ref, k_ref, v_ref, start_ref, gain_ref, maps_ref, log_ref, da_ref, cosq_ref, sinq_ref,
    cosk_ref, sink_ref, dq_ref, dk_ref, dv_ref, dgain_ref, dlam_ref, kt_ref, dk_sum, dv_sum, dq_sum,
):
    i = pl.program_id(1)
    blocks = kt_ref.shape[0]

    @pl.when(i == 0)
    def begin():
        for j in range(blocks):
            kt_ref[j] = k_ref[j * TILE : (j + 1) * TILE, :].astype(F32).T.astype(BF)
        dk_sum[...] = jnp.zeros_like(dk_sum)
        dv_sum[...] = jnp.zeros_like(dv_sum)
        dgain_ref[...] = jnp.zeros_like(dgain_ref)
        dlam_ref[...] = jnp.zeros_like(dlam_ref)

    lam = lam_ref[0]
    q = split_halves(q_ref[...])
    start = jnp.concatenate([start_ref[...], start_ref[...]], axis=1)
    log_mass = log_ref[0, 0]
    one, two = maps_ref[0, 0], maps_ref[0, 1]
    mixed = one - lam * two
    r = lax.rsqrt(jnp.mean(mixed * mixed, axis=0, keepdims=True) + norm_epsilon)
    t = mixed * r
    da = da_ref[...].T * (1.0 - lambda_start)
    dgain_ref[0] += da * t
    e = da * gain_ref[...]
    dmixed = r * (e - t * jnp.mean(e * t, axis=0, keepdims=True))
    dlam_ref[0] -= jnp.sum(dmixed * two, axis=0, keepdims=True)
    dmaps = jnp.concatenate([dmixed, -lam * dmixed], axis=1).astype(BF)
    maps = jnp.concatenate([one, two], axis=1)
    offset = jnp.sum(dmaps.astype(F32) * maps, axis=0, keepdims=True)
    dq_sum[...] = jnp.zeros_like(dq_sum)

    def step(j, n, carry):
        at = pl.ds(pl.multiple_of(j * TILE, TILE), n * TILE)
        keys, values = k_ref[at, :], v_ref[at, :]
        scores = dot_last(keys, q)
        shares = jnp.where(block_mask(j, n, i, start), jnp.exp(scores - log_mass), 0.0)
        dshares = dot_plain(values, dmaps)
        dscores = (shares * (dshares - offset)).astype(BF)
        dv_sum[at, :] += dot_last(shares.astype(BF), dmaps)
        dk_sum[at, :] += dot_plain(dscores, q)
        dq = dot_plain(kt_ref[j], dscores[:TILE])
        for b in range(1, n):
            dq += dot_plain(kt_ref[j + b], dscores[b * TILE : (b + 1) * TILE])
        dq_sum[...] += dq
        return carry

    over_blocks(low_ref[i], i + 1, step, 0)
    lane = lax.broadcasted_iota(jnp.int32, (TILE, VD), 1)
    dq = jnp.concatenate([dq_sum[:HD, :TILE], dq_sum[HD:, TILE:]], axis=0).T * HD**-0.5
    dq_ref[...] = turn(dq, cosq_ref[...], -sinq_ref[...], lane).astype(BF)

    @pl.when(i == blocks - 1)
    def finish():
        for j in range(blocks):
            at = slice(j * TILE, (j + 1) * TILE)
            dk_ref[at, :] = turn(dk_sum[at, :], cosk_ref[at, :], -sink_ref[at, :], lane).astype(BF)
        dv_ref[...] = dv_sum[...].astype(BF)


def attend_back(low, lam, q, k, v, start, gain, maps, log_mass, da, cosine, sine):
    count = q.shape[0]
    blocks = count // TILE
    smem = pl.BlockSpec(memory_space=pltpu.SMEM)
    tile = pl.BlockSpec((TILE, VD), lambda h, i: (i, h))
    whole = pl.BlockSpec((count, VD), lambda h, i: (0, h))
    table = pl.BlockSpec((TILE, VD), lambda h, i: (i, 0))
    full_table = pl.BlockSpec((count, VD), lambda h, i: (0, 0), pipeline_mode=pl.Buffered(1))
    narrow = jax.ShapeDtypeStruct((count, QW), BF)
    return pl.pallas_call(
        attend_back_kernel,
        grid=(HEADS, blocks),
        in_specs=[
            smem,
            smem,
            tile,
            whole,
            whole,
            pl.BlockSpec((1, TILE), lambda h, i: (0, i)),
            pl.BlockSpec((VD, 1), lambda h, i: (0, 0)),
            pl.BlockSpec((1, 2, VD, TILE), lambda h, i: (h, 0, 0, i)),
            pl.BlockSpec((1, 1, 1, 2 * TILE), lambda h, i: (h, i, 0, 0)),
            tile,
            table,
            table,
            full_table,
            full_table,
        ],
        out_specs=[
            tile,
            whole,
            whole,
            pl.BlockSpec((1, VD, TILE), lambda h, i: (h, 0, 0)),
            pl.BlockSpec((1, 1, TILE), lambda h, i: (h, 0, 0)),
        ],
        out_shape=[
            narrow,
            narrow,
            narrow,
            jax.ShapeDtypeStruct((HEADS, VD, TILE), F32),
            jax.ShapeDtypeStruct((HEADS, 1, TILE), F32),
        ],
        scratch_shapes=[
            pltpu.VMEM((blocks, VD, TILE), BF),
            pltpu.VMEM((count, VD), F32),
            pltpu.VMEM((count, VD), F32),
            pltpu.VMEM((VD, 2 * TILE), F32),
        ],
        compiler_params=params(),
        cost_estimate=pl.CostEstimate(
            flops=20 * count * count * VD * HEADS, bytes_accessed=count * QW * 24, transcendentals=count * count * HEADS
        ),
        name="attend_back",
    )(low, lam, q, k, v, start, gain, maps, log_mass, da, cosine, sine, cosine, sine)


def middle_kernel(
    x_ref, gain_ref, a_ref, w_ref, w_in, a_hbm, n_ref, own_ref, a_in, total, s_a, s_ay, s_ar
):
    i = pl.program_id(0)
    me = lax.axis_index("batch")
    y, core = me // 2, me % 2
    to_core = {"batch": y * 2 + 1 - core}
    to_y = {"batch": (1 - y) * 2 + core}
    blocks = a_in.shape[1]

    def a_copies(b):
        source = a_hbm.at[pl.ds(b * TILE, TILE)]
        return (
            lambda: remote(source, a_in.at[0, b], s_a, b, to_core),
            lambda: remote(source, a_in.at[1, b], s_ay, b, to_y),
            lambda: remote(a_in.at[1, b], a_in.at[2, b], s_ar, b, to_core),
        )

    @pl.when(i == 0)
    def begin():
        greet((to_core, to_y))
        for b in range(blocks):
            a_copies(b)[1]().start()
        for b in range(blocks):
            a_copies(b)[0]().start()

    @pl.when(i < blocks)
    def relay():
        a_copies(i)[1]().wait_recv()
        a_copies(i)[2]().start()

    @pl.when(i >= 1)
    def compute():
        b = i - 1
        a_copies(b)[0]().wait_recv()
        a_copies(b)[2]().wait_recv()
        x1 = x_ref[...].astype(F32) + dot_last(a_ref[...], w_ref[...])
        for other in range(3):
            x1 += dot_last(a_in[other, b], w_in[other])
        total[...] = x1
        r = lax.rsqrt(jnp.mean(x1 * x1, axis=-1, keepdims=True) + norm_epsilon)
        n_ref[...] = (x1 * r * gain_ref[...]).astype(BF)
        part = TILE // 4
        own_ref[0] = total[pl.ds(pl.multiple_of(me * part, part), part), :]

    @pl.when(i == blocks)
    def finish():
        for b in range(blocks):
            for copy in a_copies(b):
                copy().wait_send()


def middle(a, x, attn, others, gain):
    count = x.shape[0]
    blocks = count // TILE
    late = lambda i: (jnp.maximum(i - 1, 0), 0)
    hbm = pl.BlockSpec(memory_space=pl.ANY)
    sems = lambda n: pltpu.SemaphoreType.DMA((2, n))
    return pl.pallas_call(
        middle_kernel,
        grid=(blocks + 1,),
        in_specs=[
            pl.BlockSpec((TILE, D), late),
            pl.BlockSpec((1, D), lambda i: (0, 0)),
            pl.BlockSpec((TILE, QW), late),
            pl.BlockSpec((D, QW), lambda i: (0, 3), pipeline_mode=pl.Buffered(1)),
            pl.BlockSpec((3, D, QW), lambda i: (0, 0, 0), pipeline_mode=pl.Buffered(1)),
            hbm,
        ],
        out_specs=[
            pl.BlockSpec((TILE, D), late),
            pl.BlockSpec((1, TILE // 4, D), lambda i: (jnp.maximum(i - 1, 0), 0, 0)),
        ],
        out_shape=[
            jax.ShapeDtypeStruct((count, D), BF),
            jax.ShapeDtypeStruct((blocks, TILE // 4, D), F32),
        ],
        scratch_shapes=[
            pltpu.VMEM((3, blocks, TILE, QW), BF),
            pltpu.VMEM((TILE, D), F32),
            sems(blocks),
            sems(blocks),
            sems(blocks),
        ],
        compiler_params=params(collective_id=5, has_side_effects=True),
        cost_estimate=pl.CostEstimate(
            flops=2 * count * D * D, bytes_accessed=count * D * 7 + 2 * D * D, transcendentals=0
        ),
        name="middle",
    )(x, gain, a, attn, others, a)


def feed_kernel(
    n_ref, dy0_ref, dy1_ref, dy2_ref, dy3_ref, w_ref, wd_ref, x1_ref, dyo_ref, wo_ref, gain_ref, base_ref, dup_ref, out_ref, dx_ref, low_ref, da_ref, dgain_ref,
    gate_grad_ref, down_grad_ref, other_ref, dy_ref, part, near_in, near, far_in, gathered, gate_sum, down_sum, staged, s_near, s_far, s_y,
    s_core, s_relay, s_grad, s_low, s_other,
):
    i = pl.program_id(0)
    me = lax.axis_index("batch")
    y, core = me // 2, me % 2
    to_core = {"batch": y * 2 + 1 - core}
    to_y = {"batch": (1 - y) * 2 + core}
    blocks = near_in.shape[0]

    def near_copy(b):
        return remote(part.at[b % 3, :, 1 - core], near_in.at[b], s_near, b, to_core)

    blk = lax.axis_index("blk")
    to_pair = {"blk": blk + 2 - 4 * ((blk // 2) % 2)}

    def share(n):
        return remote(base_ref.at[EARLY + n], other_ref.at[n], s_other, n, to_pair)

    def low_copy(b):
        return pltpu.make_async_copy(gathered.at[b], low_ref.at[b], s_low.at[b])

    grads = ((gate_sum, gate_grad_ref), (down_sum, down_grad_ref))
    strip = gate_sum.shape[0] // 4

    def grad_copy(n, which):
        at = pl.ds(pl.multiple_of(n * strip, strip), strip)
        return pltpu.make_async_copy(staged.at[which], grads[which][1].at[at], s_grad.at[which, n])

    def far_copy(b):
        return remote(near.at[b], far_in.at[b], s_far, b, to_y)

    def own_copy(b, sems, device):
        return remote(gathered.at[b, me], gathered.at[b, me], sems, b, device)

    def relay_copy(b):
        slab = (1 - y) * 2 + core
        return remote(gathered.at[b, slab], gathered.at[b, slab], s_relay, b, to_core)

    @pl.when(i == 0)
    def begin():
        greet((to_core, to_y, to_pair))
        for n in range(other_ref.shape[0]):
            share(n).start()
        dgain_ref[...] = jnp.zeros_like(dgain_ref)
        gate_sum[...] = jnp.zeros_like(gate_sum)
        down_sum[...] = jnp.zeros_like(down_sum)

    @pl.when((i >= 1) & (i < blocks + 1))
    def send_far():
        b = i - 1
        near_copy(b).wait_recv()
        both = part[b % 3, 1 - y, core].astype(F32) + near_in[b, 1 - y].astype(F32)
        near[b] = both.astype(BF)
        far_copy(b).start()

    @pl.when((i >= 2) & (i < blocks + 2))
    def send_own():
        b = i - 2
        far_copy(b).wait_recv()
        dn = part[b % 3, y, core].astype(F32) + near_in[b, y].astype(F32) + far_in[b].astype(F32)
        x1 = x1_ref[0]
        r = lax.rsqrt(jnp.mean(x1 * x1, axis=-1, keepdims=True) + norm_epsilon)
        t = x1 * r
        e = dn * gain_ref[...]
        dx = dyo_ref[0].astype(F32) + r * (e - t * jnp.mean(e * t, axis=-1, keepdims=True))
        dgain_ref[...] += jnp.sum(dn * t, axis=0, keepdims=True)
        dx_ref[0] = dx
        gathered[b, me] = dx.astype(BF)
        own_copy(b, s_y, to_y).start()
        own_copy(b, s_core, to_core).start()

    @pl.when((i >= 3) & (i < blocks + 3))
    def send_relay():
        b = i - 3
        own_copy(b, s_y, to_y).wait_recv()
        relay_copy(b).start()

    @pl.when(i >= 4)
    def use():
        b = i - 4
        own_copy(b, s_core, to_core).wait_recv()
        relay_copy(b).wait_recv()
        whole = jnp.concatenate([gathered[b, other] for other in range(4)], axis=0)
        low_copy(b).start()
        da_ref[...] = dot_plain(whole, wo_ref[...])

    @pl.when(i < blocks)
    def compute():
        size = dy0_ref.shape[1]
        slabs = (me, 2 * y + 1 - core, 2 * (1 - y) + core, 2 * (1 - y) + 1 - core)
        for slab, piece in zip(slabs, (dy0_ref, dy1_ref, dy2_ref, dy3_ref)):
            dy_ref[pl.ds(pl.multiple_of(slab * size, size), size), :] = piece[0]
        n, dy = n_ref[...], dy_ref[...]
        wg, wu, wd = w_ref[:, :FQ], w_ref[:, FQ:], wd_ref[...]
        gate = dot_plain(n, wg)
        up = dot_plain(n, wu)
        dhidden = dot_plain(dy, wd)
        share = 1.0 / (1.0 + jnp.exp(-gate))
        silu = gate * share
        hidden = (silu * up).astype(BF)
        dup = (dhidden * silu).astype(BF)
        dgate = (dhidden * up * (share * (1.0 + gate * (1.0 - share)))).astype(BF)
        dup_ref[...] = dup
        dn = (dot_last(dgate, wg) + dot_last(dup, wu)).astype(BF)

        @pl.when(i >= 3)
        def reuse():
            near_copy(i - 3).wait_send()

        for other in range(4):
            part[i % 3, other // 2, other % 2] = dn[other * size : (other + 1) * size]
        near_copy(i).start()
        out_ref[...] = dot_last(hidden, wd).astype(BF)
        for c in range(0, n.shape[1], TILE):
            gate_sum[c : c + TILE, :] += dot_first(n[:, c : c + TILE], dgate)
            down_sum[c : c + TILE, :] += dot_first(dy[:, c : c + TILE], hidden)

    @pl.when(i >= blocks)
    def keep():
        n = i - blocks
        for which in range(2):

            @pl.when(n >= 1)
            def reuse(which=which):
                grad_copy(n - 1, which).wait()

            at = pl.ds(pl.multiple_of(n * strip, strip), strip)
            staged[which] = grads[which][0][at, :].astype(BF)
            grad_copy(n, which).start()

    @pl.when(i == blocks + 3)
    def finish():
        for which in range(2):
            grad_copy(3, which).wait()
        for b in range(blocks - 3, blocks):
            near_copy(b).wait_send()
        for b in range(blocks):
            far_copy(b).wait_send()
            own_copy(b, s_y, to_y).wait_send()
            own_copy(b, s_core, to_core).wait_send()
            relay_copy(b).wait_send()
            low_copy(b).wait()
        for n in range(other_ref.shape[0]):
            share(n).wait()


def feed(n, dy, weights, down, x1, dy_own, attn, gain, base):
    count = n.shape[0]
    blocks = count // TILE
    size = TILE // 4
    late = lambda lag: lambda i: (jnp.clip(i - lag, 0, blocks - 1), 0)
    late3 = lambda lag: lambda i: (jnp.clip(i - lag, 0, blocks - 1), 0, 0)
    rows = lambda w, lag: pl.BlockSpec((TILE, w), late(lag))
    own = pl.BlockSpec((1, size, D), late3(2))
    shape = lambda w, kind=BF: jax.ShapeDtypeStruct((count, w), kind)
    sems = pltpu.SemaphoreType.DMA((2, blocks))
    return pl.pallas_call(
        feed_kernel,
        grid=(blocks + 4,),
        in_specs=[
            rows(D, 0),
            pl.BlockSpec((1, size, D), late3(0)),
            pl.BlockSpec((1, size, D), late3(0)),
            pl.BlockSpec((1, size, D), late3(0)),
            pl.BlockSpec((1, size, D), late3(0)),
            pl.BlockSpec((D, 2 * FQ), lambda i: (0, 0), pipeline_mode=pl.Buffered(1)),
            pl.BlockSpec((D, FQ), lambda i: (0, 0), pipeline_mode=pl.Buffered(1)),
            own,
            own,
            pl.BlockSpec((D, QW), lambda i: (0, 3), pipeline_mode=pl.Buffered(1)),
            pl.BlockSpec((1, D), lambda i: (0, 0)),
            pl.BlockSpec(memory_space=pl.ANY),
        ],
        out_specs=[
            rows(FQ, 0),
            rows(D, 0),
            own,
            pl.BlockSpec(memory_space=pl.ANY),
            rows(QW, 4),
            pl.BlockSpec((1, D), lambda i: (0, 0)),
            pl.BlockSpec(memory_space=pl.ANY),
            pl.BlockSpec(memory_space=pl.ANY),
            pl.BlockSpec(memory_space=pl.ANY),
        ],
        out_shape=[
            shape(FQ),
            shape(D),
            jax.ShapeDtypeStruct((blocks, size, D), F32),
            jax.ShapeDtypeStruct((blocks, 4, size, D), BF),
            shape(QW, F32),
            jax.ShapeDtypeStruct((1, D), F32),
            jax.ShapeDtypeStruct((D, FQ), BF),
            jax.ShapeDtypeStruct((D, FQ), BF),
            jax.ShapeDtypeStruct((base.shape[0] - EARLY,) + base.shape[1:], BF),
        ],
        scratch_shapes=[
            pltpu.VMEM((TILE, D), BF),
            pltpu.VMEM((3, 2, 2, size, D), BF),
            pltpu.VMEM((blocks, 2, size, D), BF),
            pltpu.VMEM((blocks, size, D), BF),
            pltpu.VMEM((blocks, size, D), BF),
            pltpu.VMEM((blocks, 4, size, D), BF),
            pltpu.VMEM((D, FQ), F32),
            pltpu.VMEM((D, FQ), F32),
            pltpu.VMEM((2, D // 4, FQ), BF),
            sems,
            sems,
            sems,
            sems,
            sems,
            pltpu.SemaphoreType.DMA((2, 4)),
            pltpu.SemaphoreType.DMA((blocks,)),
            pltpu.SemaphoreType.DMA((2, base.shape[0] - EARLY)),
        ],
        compiler_params=params(63 * 2**20, collective_id=1, has_side_effects=True),
        cost_estimate=pl.CostEstimate(
            flops=12 * count * D * FQ, bytes_accessed=count * (8 * D + 6 * FQ) + 6 * D * FQ, transcendentals=count * FQ
        ),
        name="feed",
    )(n, *dy, weights, down, x1, dy_own, attn, gain, base)


def return_rows_copies(source, target, sems, me, blk):
    size = source.shape[1]

    def copies(act_local, act_remote):
        for k in range(8):
            here = (me == blk // 2) & (blk == k)
            piece = target.at[blk % 2, pl.ds(pl.multiple_of(me * size, size), size)]

            @pl.when(here)
            def stay():
                act_local(pltpu.make_async_copy(source.at[k], piece, sems.at[0, k]))

            @pl.when(jnp.logical_not(here))
            def go():
                act_remote(
                    pltpu.make_async_remote_copy(
                        src_ref=source.at[k],
                        dst_ref=piece,
                        send_sem=sems.at[0, k],
                        recv_sem=sems.at[1, (blk % 2) * 4 + me],
                        device_id=(blk // 2, k),
                        device_id_type=MESH,
                    )
                )

    def start():
        copies(lambda copy: copy.start(), lambda copy: copy.start())

    def finish():
        copies(lambda copy: copy.wait(), lambda copy: copy.wait_send())
        for i in range(2):
            for other in range(4):

                @pl.when((me != other) | (blk != 2 * me + i))
                def arrived():
                    pltpu.make_async_remote_copy(
                        src_ref=source.at[0],
                        dst_ref=target.at[i, pl.ds(other * size, size)],
                        send_sem=sems.at[0, 0],
                        recv_sem=sems.at[1, 4 * i + other],
                        device_id=(me, blk),
                        device_id_type=MESH,
                    ).wait_recv()

    return start, finish


def collect_kernel(
    gate, up, dqkv, a_own, n1_ref, low_ref, down_ref, out_part_ref, dn1_part_ref, x1_ref, dx1_ref, x_ref, gain_ref, attn_ref, gate_up_ref,
    downs_ref, dx_ref, back_ref, dgain_ref, qkv, out, strips, first_in, second_in, first_sum, second_sum, own, near_in, near, far_in,
    out_rows, s_up, s_down, s_up2, s_down2, s_near, s_own, s_far, s_pieces, s_local, s_back,
    s_strip,
):
    me, blk = lax.axis_index("batch"), lax.axis_index("blk")
    y, core = me // 2, me % 2
    to_core = {"batch": y * 2 + 1 - core}
    to_y = {"batch": (1 - y) * 2 + core}
    place = ring_place(blk)
    after_me, before_me = {"blk": ring_owner(place + 1)}, {"blk": ring_owner(place - 1)}
    part = first_sum.shape[0]
    half = part // 2
    blocks = dx1_ref.shape[0]

    wide = QW + 256
    plans = (
        ((gate, 0, FQ, 0), (up, 0, FQ, FQ)),
        ((qkv, 0, wide, 0), (qkv, wide, 3 * QW - wide, wide), (out, 0, QW, 3 * QW)),
    )
    buffers, totals = (first_in, second_in), (first_sum, second_sum)
    ring_sems = ((s_up, s_down), (s_up2, s_down2))

    def mine(r, t, up_way, p):
        grad, column, width, _ = plans[r][p]
        owner = ring_owner(place - 1 - t) if up_way else ring_owner(place + 1 + t)
        begin = pl.multiple_of(owner * part + (0 if up_way else half), half)
        return grad.at[pl.ds(begin, half), pl.ds(column, width)]

    def landing(r, t, up_way, p):
        _, _, width, to = plans[r][p]
        return buffers[r].at[0 if up_way else 1, t, :, pl.ds(to, width)]

    def ring(r, t, up_way, p):
        source = mine(r, 0, up_way, p) if t == 0 else landing(r, t - 1, up_way, p)
        sems = ring_sems[r][0 if up_way else 1]
        at = len(plans[r]) * t + p
        return remote(source, landing(r, t, up_way, p), sems, at, after_me if up_way else before_me)

    def ring_start(r):
        for p in range(len(plans[r])):
            ring(r, 0, True, p).start()
            ring(r, 0, False, p).start()

    def ring_step(r, t, p):
        _, _, width, to = plans[r][p]
        for up_way in (True, False):
            ring(r, t - 1, up_way, p).wait_recv()
            here = landing(r, t - 1, up_way, p)
            value = (here[...].astype(F32) + mine(r, t, up_way, p)[...].astype(F32)).astype(BF)
            if t < 7:
                here[...] = value
                ring(r, t, up_way, p).start()
            else:
                totals[r][0 if up_way else half : half if up_way else part, to : to + width] = value

    def exchange(source, target, n):
        return (
            lambda: remote(source, target.at[1], s_pieces, 3 * n, to_core),
            lambda: remote(source, target.at[2], s_pieces, 3 * n + 1, to_y),
            lambda: remote(target.at[2], target.at[3], s_pieces, 3 * n + 2, to_core),
            lambda: pltpu.make_async_copy(source, target.at[0], s_local.at[n]),
        )

    exchanges = [exchange(down_ref, downs_ref, 0), exchange(first_sum, gate_up_ref, 1)]
    for p, (_, _, width, to) in enumerate(plans[1]):
        at = pl.ds(to, width)
        exchanges.append(exchange(second_sum.at[:, at], attn_ref.at[:, :, at], 2 + p))

    strip = strips.shape[2]
    count = D // strip
    lefts, rights, results = (n1_ref, low_ref), (dqkv, a_own), (qkv, out)

    def strip_copy(n):
        source = lefts[n // count].at[:, pl.ds((n % count) * strip, strip)]
        return pltpu.make_async_copy(source, strips.at[n % 2], s_strip.at[n])

    def strip_product(n):
        strip_copy(n).wait()
        at = pl.ds((n % count) * strip, strip)
        results[n // count][at, :] = dot_first(strips[n % 2], rights[n // count][...]).astype(BF)
        if n + 2 < 2 * count:
            strip_copy(n + 2).start()

    def spread(n):
        for way in (1, 0, 3):
            exchanges[n][way]().start()

    def relay(n):
        exchanges[n][1]().wait_recv()
        exchanges[n][2]().start()

    parts = (out_part_ref, dn1_part_ref)

    def near_copy(j):
        return remote(parts[j // blocks].at[j % blocks, :, 1 - core], near_in.at[j], s_near, j, to_core)

    def own_copy(j):
        return pltpu.make_async_copy(parts[j // blocks].at[j % blocks, :, core], own.at[j], s_own.at[j])

    def far_copy(j):
        return remote(near.at[j], far_in.at[j], s_far, j, to_y)

    def near_step(j):
        near_copy(j).wait_recv()
        own_copy(j).wait()
        near[j] = (own[j, 1 - y].astype(F32) + near_in[j, 1 - y].astype(F32)).astype(BF)
        far_copy(j).start()

    def far_step(j):
        far_copy(j).wait_recv()
        total = own[j, y].astype(F32) + near_in[j, y].astype(F32) + far_in[j].astype(F32)
        b = j % blocks
        if j < blocks:
            out_rows[b] = (x1_ref[b] + total).astype(BF)
            return
        x = x_ref[b].astype(F32)
        r = lax.rsqrt(jnp.mean(x * x, axis=-1, keepdims=True) + norm_epsilon)
        t = x * r
        e = total * gain_ref[...]
        dx = dx1_ref[b] + r * (e - t * jnp.mean(e * t, axis=-1, keepdims=True))
        dx_ref[b] = dx.astype(BF)
        dgain_ref[...] += jnp.sum(total * t, axis=0, keepdims=True)

    back_start, back_finish = return_rows_copies(out_rows, back_ref, s_back, me, blk)
    dgain_ref[...] = jnp.zeros_like(dgain_ref)
    greet_and_rows((to_core, to_y, after_me, before_me))
    ring_start(0)
    for j in range(2 * blocks):
        own_copy(j).start()
        near_copy(j).start()
    spread(0)
    strip_copy(0).start()
    strip_copy(1).start()
    groups = [(r, t, p) for r in range(2) for t in range(1, 8) for p in range(len(plans[r]))]
    for g, (r, t, p) in enumerate(groups):
        ring_step(r, t, p)
        if g < 2 * count:
            strip_product(g)
        if g < 2 * blocks:
            near_step(g)
        if 3 <= g < 2 * blocks + 3:
            far_step(g - 3)
        if g == blocks + 3:
            back_start()
        if (r, t, p) == (0, 6, 1):
            ring_start(1)
            relay(0)
        if (r, t, p) == (0, 7, 1):
            spread(1)
        if (r, t, p) == (1, 5, 0):
            relay(1)
        if (r, t) == (1, 7):
            spread(2 + p)
    for p in range(3):
        relay(2 + p)
    back_finish()
    for n in range(5):
        near_piece, far_piece, relay_piece, local = exchanges[n]
        near_piece().wait()
        far_piece().wait_send()
        relay_piece().wait()
        local().wait()
    for j in range(2 * blocks):
        near_copy(j).wait_send()
        far_copy(j).wait_send()
    for r in range(2):
        for t in range(7):
            for p in range(len(plans[r])):
                ring(r, t, True, p).wait_send()
                ring(r, t, False, p).wait_send()


def collect(gate, up, n1, dqkv, low, a_own, down, out_part, dn1_part, x1, dx1, x, gain):
    part = D // 8
    size = x.shape[1]
    items = 2 * x.shape[0]
    hbm = pl.BlockSpec(memory_space=pl.ANY)
    vmem = pl.BlockSpec(memory_space=pltpu.VMEM)
    sems = lambda n: pltpu.SemaphoreType.DMA((2, n))
    four = lambda width: jax.ShapeDtypeStruct((4, part, width), BF)
    return pl.pallas_call(
        collect_kernel,
        in_specs=[vmem] * 4 + [hbm] * 5 + [vmem] * 4,
        out_specs=[hbm] * 3 + [vmem, hbm, vmem],
        out_shape=[
            four(4 * QW),
            four(2 * FQ),
            four(FQ),
            jax.ShapeDtypeStruct(x.shape, BF),
            jax.ShapeDtypeStruct((2, 4 * size, D), BF),
            jax.ShapeDtypeStruct((1, D), F32),
        ],
        scratch_shapes=[
            pltpu.VMEM((D, 3 * QW), BF),
            pltpu.VMEM((D, QW), BF),
            pltpu.VMEM((2, n1.shape[0], TILE), BF),
            pltpu.VMEM((2, 7, part // 2, 2 * FQ), BF),
            pltpu.VMEM((2, 7, part // 2, 4 * QW), BF),
            pltpu.VMEM((part, 2 * FQ), BF),
            pltpu.VMEM((part, 4 * QW), BF),
            pltpu.VMEM((items, 2, size, D), BF),
            pltpu.VMEM((items, 2, size, D), BF),
            pltpu.VMEM((items, size, D), BF),
            pltpu.VMEM((items, size, D), BF),
            pltpu.VMEM(x.shape, BF),
            sems(14),
            sems(14),
            sems(21),
            sems(21),
            sems(items),
            pltpu.SemaphoreType.DMA((items,)),
            sems(items),
            sems(15),
            pltpu.SemaphoreType.DMA((5,)),
            sems(8),
            pltpu.SemaphoreType.DMA((2 * D // TILE,)),
        ],
        compiler_params=params(63 * 2**20, collective_id=6, has_side_effects=True),
        cost_estimate=pl.CostEstimate(flops=10**11, bytes_accessed=2**25, transcendentals=0),
        name="collect",
    )(gate, up, dqkv, a_own, n1, low, down, out_part, dn1_part, x1, dx1, x, gain)


def rotate_kernel(
    g_ref, base_ref, early_ref, other_ref, first_ref, second_ref, master_ref, rows_ref, small_ref, scale_ref, new_first_ref,
    new_second_ref, new_master_ref, rows_out_ref, small_out_ref, group_small, blk_small, g, base, other, firsts, seconds, masters, g_in, part, x_in, near, z_in, far, p_in, step, steps,
    back, back_in, steps_own, load, store, s_g, s_x, s_z, s_p, s_step, s_back, s_up, s_side, s_rows,
    s_small, s_small2,
):
    blk = lax.axis_index("blk")
    zh, zl, xx = blk // 4, (blk // 2) % 2, blk % 2
    to_x = {"blk": blk + 1 - 2 * xx}
    to_z = {"blk": blk + 4 - 8 * zh}
    to_pair = {"blk": blk + 2 - 4 * zl}
    count = g.shape[0]
    half = UW // 2
    own = pl.ds(pl.multiple_of(zl * half, half), half)
    away = pl.ds(pl.multiple_of((1 - zl) * half, half), half)
    block = 4 * zh + xx
    loads = [
        (g_ref, g), (base_ref, base), (other_ref, other), (first_ref, firsts), (second_ref, seconds), (master_ref, masters),
    ]
    stores = [(firsts, new_first_ref), (seconds, new_second_ref), (masters, new_master_ref)]

    def loading(i, s):
        if i == 2:
            early = isinstance(s, int) and s < EARLY
            source = early_ref.at[s] if early else other_ref.at[jnp.maximum(s - EARLY, 0)]
            return pltpu.make_async_copy(source, other.at[s], load.at[i, s])
        return pltpu.make_async_copy(loads[i][0].at[s], loads[i][1].at[s], load.at[i, s])

    def storing(i, s):
        return pltpu.make_async_copy(stores[i][0].at[s], stores[i][1].at[s], store.at[i, s])

    def send_g(s):
        return remote(g.at[s, :, away], g_in.at[s], s_g, s, to_pair)

    def send_x(s):
        return remote(part.at[s % 3, :, 1 - xx], x_in.at[s], s_x, s, to_x)

    def send_z(s):
        return remote(near.at[s % 3, 1 - zh], z_in.at[s], s_z, s, to_z)

    def send_p(s):
        return remote(far.at[s % 3], p_in.at[s], s_p, s, to_pair)

    def step_pair(s):
        return remote(step.at[s, :, away], steps.at[s, block + 2 * zl], s_step, s, to_pair)

    def step_z(s, a):
        return remote(steps.at[s, block + 2 * a], steps.at[s, block + 2 * a], s_up, 2 * s + a, to_z)

    def step_x(s, a):
        at = 2 * a + xx
        return remote(steps.at[s, at], steps.at[s, at], s_side, 4 * s + a, to_x)

    def send_back(s):
        return remote(back.at[s % 3], back_in.at[s], s_back, s, to_pair)

    for i in range(len(loads)):
        for s in range(count):
            loading(i, s).start()
    rows_start, rows_finish = return_rows_copies(rows_ref, rows_out_ref, s_rows, lax.axis_index("batch"), blk)
    group = [{"batch": (lax.axis_index("batch") + n) % 4} for n in (1, 2, 3)]
    greet_and_rows(group + [{"blk": (blk + n) % 8} for n in range(1, 8)])
    rows_start()
    for s in range(count):
        loading(0, s).wait()
        send_g(s).start()
    me = lax.axis_index("batch")
    group_small[me] = small_ref[...]

    def small_over(buffer, at, n, size, axis, sems):
        return pltpu.make_async_remote_copy(
            src_ref=buffer.at[at],
            dst_ref=buffer.at[at],
            send_sem=sems.at[0, n],
            recv_sem=sems.at[1, size - n],
            device_id={axis: (at + n) % size},
            device_id_type=MESH,
        )

    def small_from(buffer, at, n, size, axis, sems):
        other = (at + n) % size
        return pltpu.make_async_remote_copy(
            src_ref=buffer.at[other],
            dst_ref=buffer.at[other],
            send_sem=sems.at[0, n],
            recv_sem=sems.at[1, n],
            device_id={axis: other},
            device_id_type=MESH,
        )

    over_group = (group_small, me, 4, "batch", s_small)
    over_blk = (blk_small, blk, 8, "blk", s_small2)

    def small_each(which, act, begin):
        buffer, at, size, axis, sems = which
        for n in range(1, size):
            act(begin(buffer, at, n, size, axis, sems))

    rows = base.shape[1]

    def tick(t, carry):
        def stage(lag, act):
            @pl.when((t >= lag) & (t < count + lag))
            def run():
                act(t - lag)

        def finish(s):
            send_back(s).wait_recv()
            loading(5, s).wait()
            for at, update in ((own, steps_own[s % 2]), (away, back_in[s].astype(F32))):
                value = masters[s, :, at]
                masters[s, :, at] = value - scale_ref[0] * (update + weight_decay * value)
            storing(2, s).start()

        def update(s):
            for a in range(4):
                step_x(s, a).wait_recv()
            whole = jnp.concatenate([steps[s, b] for b in range(8)], axis=0)
            steps_own[s % 2] = dot_plain(base[s], whole)

            @pl.when(s >= 3)
            def reuse():
                send_back(s - 3).wait_send()

            back[s % 3] = dot_plain(other[s], whole).astype(BF)
            send_back(s).start()

        def relay_x(s):
            for a in range(2):
                step_z(s, a).wait_recv()
            for a in range(4):
                step_x(s, a).start()

        def relay_z(s):
            step_pair(s).wait_recv()
            for a in range(2):
                step_z(s, a).start()

        def adam(s):
            send_p(s).wait_recv()
            loading(3, s).wait()
            loading(4, s).wait()
            mine = near[s % 3, zh, zl].astype(F32) + z_in[s, zl].astype(F32)
            for at, turned in ((own, mine), (away, p_in[s].astype(F32))):
                new_first = beta_one * firsts[s, :, at] + (1.0 - beta_one) * turned
                new_second = beta_two * seconds[s, :, at] + (1.0 - beta_two) * turned * turned
                firsts[s, :, at] = new_first
                seconds[s, :, at] = new_second
                moved = new_first / scale_ref[1] / (jnp.sqrt(new_second / scale_ref[2]) + adam_epsilon)
                step[s, :, at] = moved.astype(BF)
            storing(0, s).start()
            storing(1, s).start()
            steps[s, block + 2 * zl] = step[s, :, own]
            step_pair(s).start()

        def send_far(s):
            send_z(s).wait_recv()

            @pl.when(s >= 3)
            def reuse():
                send_p(s - 3).wait_send()

            far[s % 3] = (near[s % 3, zh, 1 - zl].astype(F32) + z_in[s, 1 - zl].astype(F32)).astype(BF)
            send_p(s).start()

        def send_near(s):
            send_x(s).wait_recv()

            @pl.when(s >= 3)
            def reuse():
                send_z(s - 3).wait_send()

            for a in range(2):
                for b in range(2):
                    at = 2 * a + b
                    total = part[s % 3, at, xx].astype(F32) + x_in[s, at].astype(F32)
                    near[s % 3, a, b] = total.astype(BF)
            send_z(s).start()

        def turn_slot(s):
            loading(1, s).wait()
            loading(2, s).wait()
            send_g(s).wait_recv()

            @pl.when(s >= 3)
            def reuse():
                send_x(s - 3).wait_send()

            turned = dot_first(base[s], g[s, :, own]) + dot_first(other[s], g_in[s])
            for b in range(8):
                part[s % 3, b // 2, b % 2] = turned[b * rows : (b + 1) * rows].astype(BF)
            send_x(s).start()

        @pl.when(t == 2)
        def small_start():
            small_each(over_group, lambda copy: copy.start(), small_over)

        @pl.when(t == 8)
        def small_middle():
            small_each(over_group, lambda copy: copy.wait_recv(), small_from)
            total = group_small[0]
            for n in range(1, 4):
                total += group_small[n]
            blk_small[blk] = total
            small_each(over_blk, lambda copy: copy.start(), small_over)

        stage(7, finish)
        stage(6, update)
        stage(5, relay_x)
        stage(4, relay_z)
        stage(3, adam)
        stage(2, send_far)
        stage(1, send_near)
        stage(0, turn_slot)
        return carry

    lax.fori_loop(0, count + 7, tick, 0)
    small_each(over_blk, lambda copy: copy.wait_recv(), small_from)
    small = blk_small[0]
    for n in range(1, 8):
        small += blk_small[n]
    small_each(over_group, lambda copy: copy.wait_send(), small_over)
    small_each(over_blk, lambda copy: copy.wait_send(), small_over)
    small_out_ref[...] = small
    rows_finish()
    for s in range(count):
        send_g(s).wait_send()
        step_pair(s).wait_send()
        for a in range(2):
            step_z(s, a).wait_send()
        for a in range(4):
            step_x(s, a).wait_send()
        for i in range(3):
            storing(i, s).wait()
    for s in range(count - 3, count):
        send_x(s).wait_send()
        send_z(s).wait_send()
        send_p(s).wait_send()
        send_back(s).wait_send()


def rotate_slots(grads, base, early, other, first, second, master, tokens, small, scales):
    count, rows, width = grads.shape
    half = width // 2
    hbm = pl.BlockSpec(memory_space=pl.ANY)
    shape = jax.ShapeDtypeStruct(master.shape, F32)
    sems = lambda n: pltpu.SemaphoreType.DMA((2, n))
    return pl.pallas_call(
        rotate_kernel,
        in_specs=[hbm] * 8 + [pl.BlockSpec(memory_space=pltpu.VMEM), pl.BlockSpec(memory_space=pltpu.SMEM)],
        out_specs=[hbm] * 4 + [pl.BlockSpec(memory_space=pltpu.VMEM)],
        out_shape=[shape] * 3
        + [jax.ShapeDtypeStruct((2, 4 * tokens.shape[1], D), BF), jax.ShapeDtypeStruct(small.shape, F32)],
        scratch_shapes=[
            pltpu.VMEM((4,) + small.shape, F32),
            pltpu.VMEM((8,) + small.shape, F32),
            pltpu.VMEM((count, rows, width), BF),
            pltpu.VMEM((count, rows, D), BF),
            pltpu.VMEM((count, rows, D), BF),
            pltpu.VMEM((count, rows, width), F32),
            pltpu.VMEM((count, rows, width), F32),
            pltpu.VMEM((count, rows, width), F32),
            pltpu.VMEM((count, rows, half), BF),
            pltpu.VMEM((3, 4, 2, rows, half), BF),
            pltpu.VMEM((count, 4, rows, half), BF),
            pltpu.VMEM((3, 2, 2, rows, half), BF),
            pltpu.VMEM((count, 2, rows, half), BF),
            pltpu.VMEM((3, rows, half), BF),
            pltpu.VMEM((count, rows, half), BF),
            pltpu.VMEM((count, rows, width), BF),
            pltpu.VMEM((count, 8, rows, half), BF),
            pltpu.VMEM((3, rows, half), BF),
            pltpu.VMEM((count, rows, half), BF),
            pltpu.VMEM((2, rows, half), F32),
            pltpu.SemaphoreType.DMA((6, count)),
            pltpu.SemaphoreType.DMA((3, count)),
            sems(count),
            sems(count),
            sems(count),
            sems(count),
            sems(count),
            sems(count),
            sems(2 * count),
            sems(4 * count),
            sems(8),
            sems(4),
            sems(8),
        ],
        compiler_params=params(collective_id=2, has_side_effects=True),
        name="rotate_slots",
    )(grads, base, early, other, first, second, master, tokens, small, scales)


def row_groups(
    tokens,
    cotangent,
    lengths,
    unit_owner,
    step_count,
    master,
    first,
    second,
    bases,
    small,
    small_first,
    small_second,
):
    me, blk = lax.axis_index("batch"), lax.axis_index("blk")
    count = tokens.shape[1] * 8
    learn_rate = 2.0 / D**0.5
    slots = lambda array: jnp.transpose(array, (1, 0, 2))
    master_slots = slots(master)

    place = ((unit_owner // 9) ^ me) * 9 + unit_owner % 9
    master_low = master_slots.astype(BF)
    lengths_tile = jnp.pad(lengths, ((0, 8 - lengths.shape[0]), (0, 128 - NDOC)))
    pieces, x_own, dy_own, base, base_early, lens = begin(master_low, tokens, cotangent, slots(bases), lengths_tile)
    attn_shard, gate_up_shard, down_shard = pick_units(place, me, master_low, pieces)
    attn, down, x, other_out, cosine, sine, start = gather(attn_shard, down_shard, x_own, lens)
    low = start.reshape(-1, TILE)[:, 0] // TILE
    down = down.reshape(D, FQ)
    gate_up = lax.all_gather(after(gate_up_shard, attn), "blk", axis=0, tiled=True)
    attn, x = attn.reshape(D, 4 * QW), x.reshape(count, D)
    dy_near, dy_far = swap_core(after(dy_own, attn)), swap_y(after(dy_own, attn))

    gain_one = small[:D].reshape(1, D)
    gain_two = small[D : 2 * D].reshape(1, D)
    head_gain = small[2 * D : 2 * D + VD].reshape(VD, 1)
    mixer, mixer_back = jax.vjp(mix_value, small[2 * D + VD :].reshape(4, HD))
    lam = mixer.reshape(1)

    n1, q, k, v = project(x, attn, gain_one, cosine, sine)
    a_own, maps, log_mass = attend(low, lam, q, k, v, start, head_gain)
    dy = (dy_own, dy_near, dy_far, swap_core(after(dy_far, a_own)))
    n2, x1 = middle(a_own, x, attn, other_out.reshape(3, D, QW), gain_two)
    dup, out_part, dx1, dx1_low, da, gain_two_grad, gate_grad, down_grad, base_other = feed(
        n2, dy, gate_up, down, x1, dy_own, attn, gain_two, base
    )

    down_sums = lax.psum_scatter(down_grad, "blk", scatter_dimension=0, tiled=True)
    dx1_low = dx1_low.reshape(count, D)
    dq, dk, dv, head_gain_sums, mixer_sums = attend_back(
        low, lam, q, k, v, start, head_gain, maps, log_mass, da, cosine, sine
    )
    up_grad = dot_first(n2, after(dup, dq)).astype(BF)
    dqkv = jnp.concatenate([dq, dk, dv], axis=1)
    dn1_part = dot_last(dqkv, attn[:, : 3 * QW]).astype(BF)
    groups = (8, 2, 2, count // 32, D)
    attn_pieces, gate_up_pieces, down_pieces, dx, block_out, gain_one_grad = collect(
        gate_grad, up_grad, n1, dqkv, dx1_low, a_own, down_sums, out_part.reshape(groups), dn1_part.reshape(groups),
        x1, dx1, x_own, gain_one,
    )

    (mixers_grad,) = mixer_back(jnp.sum(mixer_sums))
    small_local = jnp.concatenate(
        [gain_one_grad.reshape(D), gain_two_grad.reshape(D), jnp.sum(head_gain_sums, axis=(0, 2)), mixers_grad.reshape(-1)]
    )
    small_rows = jnp.pad(small_local, (0, 32 * 128 - small_local.shape[0])).reshape(32, 128)

    unit_of = inverse_order(unit_owner)
    units = lax.dynamic_slice_in_dim(unit_of, me * 9, 9)
    grads = place_units(units, me, attn_pieces, gate_up_pieces, down_pieces)

    steps_done = step_count[0].astype(F32)
    scales = jnp.stack([jnp.float32(learn_rate), 1.0 - beta_one**steps_done, 1.0 - beta_two**steps_done])
    new_first, new_second, new_master, input_grad, small_sums = rotate_slots(
        grads, base, base_early, base_other, slots(first), slots(second), master_slots, dx, small_rows, scales
    )
    small_grads = small_sums.reshape(-1)[: small_local.shape[0]]
    new_small_first = beta_one * small_first + (1.0 - beta_one) * small_grads
    new_small_second = beta_two * small_second + (1.0 - beta_two) * small_grads * small_grads
    new_small = small - small_rate * adam_step(new_small_first, new_small_second, steps_done)
    return (
        block_out,
        input_grad,
        slots(new_master),
        slots(new_first),
        slots(new_second),
        small_grads,
        new_small,
        new_small_first,
        new_small_second,
    )


def solution(mesh):
    in_specs = (
        P("batch", "blk", None),
        P("batch", "blk", None),
        P("batch", None),
        P(),
        P(),
        P("blk", "batch", None),
        P("blk", "batch", None),
        P("blk", "batch", None),
        P("blk", "batch", None),
        P(),
        P(),
        P(),
    )
    out_specs = (
        P("batch", "blk", None),
        P("batch", "blk", None),
        P("blk", "batch", None),
        P("blk", "batch", None),
        P("blk", "batch", None),
        P(),
        P(),
        P(),
        P(),
    )
    by_rows = mesh.shape["blk"] == 8 and mesh.shape["batch"] == 4
    body = row_groups if by_rows else any_mesh
    return jax.shard_map(body, mesh=mesh, in_specs=in_specs, out_specs=out_specs, check_vma=False)
```
